32 devices in a mesh: ctx: 8 (over y, x, core), fsdp: 4 (over z).
Axes of the slice: x: 2, y: 2, z: 4, core: 2. Of those that a mesh axis runs over, the one named last changes fastest.
Arguments:
- enc_input: bfloat16 [8, 1024, 768], P('fsdp', 'ctx'), may hold values from -6 to 6
- dec_input: bfloat16 [8, 1024, 768], P('fsdp', 'ctx'), may hold values from -6 to 6
- segments: int32 [8, 1024], P('fsdp', 'ctx'), may hold values from 0 to 7, never falling along the last dimension, each value on 1 to 512 neighbouring positions
- prefix_rows: int32 [8, 8, 20], P('fsdp'), may hold values from 0 to 255
- buckets: int32 [2048], replicated, may hold values from 0 to 31
- memory: bfloat16 [256, 1536], P('fsdp'), may hold values from -3 to 3
- enc_gain: bfloat16 [768], P('fsdp'), may hold values from 0.5 to 1.5
- enc_qkv: bfloat16 [768, 2304], P('fsdp'), may hold values from -0.09375 to 0.09375
- enc_rel: bfloat16 [32, 12], P('fsdp'), may hold values from -3 to 3
- enc_proj: bfloat16 [768, 768], P('fsdp'), may hold values from -1 to 1
- enc_ffnorm: bfloat16 [768], P('fsdp'), may hold values from 0.5 to 1.5
- enc_ffin: bfloat16 [768, 3072], P('fsdp'), may hold values from -0.21875 to 0.21875
- enc_ffout: bfloat16 [3072, 768], P('fsdp'), may hold values from -0.15625 to 0.15625
- dec_gain: bfloat16 [768], P('fsdp'), may hold values from 0.5 to 1.5
- dec_qkv: bfloat16 [768, 2304], P('fsdp'), may hold values from -0.09375 to 0.09375
- dec_rel: bfloat16 [32, 12], P('fsdp'), may hold values from -3 to 3
- dec_proj: bfloat16 [768, 768], P('fsdp'), may hold values from -1 to 1
- cross_gain: bfloat16 [768], P('fsdp'), may hold values from 0.5 to 1.5
- cross_query: bfloat16 [768, 768], P('fsdp'), may hold values from -0.09375 to 0.09375
- cross_kv: bfloat16 [768, 1536], P('fsdp'), may hold values from -0.0625 to 0.0625
- cross_proj: bfloat16 [768, 768], P('fsdp'), may hold values from -1 to 1
- dec_ffnorm: bfloat16 [768], P('fsdp'), may hold values from 0.5 to 1.5
- dec_ffin: bfloat16 [768, 3072], P('fsdp'), may hold values from -0.21875 to 0.21875
- dec_ffout: bfloat16 [3072, 768], P('fsdp'), may hold values from -0.15625 to 0.15625
- enc_cotan: bfloat16 [8, 1024, 768], P('fsdp', 'ctx'), may hold values from -6 to 6
- dec_cotan: bfloat16 [8, 1024, 768], P('fsdp', 'ctx'), may hold values from -6 to 6
Outputs:
- enc_output: bfloat16 [8, 1024, 768], P('fsdp', 'ctx')
- dec_output: bfloat16 [8, 1024, 768], P('fsdp', 'ctx')
- enc_ingrad: float32 [8, 1024, 768], P('fsdp', 'ctx')
- dec_ingrad: float32 [8, 1024, 768], P('fsdp', 'ctx')
- memory_grad: float32 [256, 1536], P('fsdp')
- genc_gain: float32 [768], P('fsdp')
- genc_qkv: float32 [768, 2304], P('fsdp')
- genc_rel: float32 [32, 12], P('fsdp')
- genc_proj: float32 [768, 768], P('fsdp')
- genc_ffnorm: float32 [768], P('fsdp')
- genc_ffin: float32 [768, 3072], P('fsdp')
- genc_ffout: float32 [3072, 768], P('fsdp')
- gdec_gain: float32 [768], P('fsdp')
- gdec_qkv: float32 [768, 2304], P('fsdp')
- gdec_rel: float32 [32, 12], P('fsdp')
- gdec_proj: float32 [768, 768], P('fsdp')
- gcross_gain: float32 [768], P('fsdp')
- gcross_query: float32 [768, 768], P('fsdp')
- gcross_kv: float32 [768, 1536], P('fsdp')
- gcross_proj: float32 [768, 768], P('fsdp')
- gdec_ffnorm: float32 [768], P('fsdp')
- gdec_ffin: float32 [768, 3072], P('fsdp')
- gdec_ffout: float32 [3072, 768], P('fsdp')
The draws below stay inside these ranges and needn't reach their ends.
All inputs are finite; a program needn't handle non-finite values.
Results may differ from the reference program's by a relative error of at most 0.035.
Values may be sent and summed in bfloat16 or wider, within the bound.
A program may use at most 448 MiB of HBM per device.

```python
import math
import jax
import jax.numpy as jnp
import numpy as np
from jax import lax

D = 768
HEADS = 12
HEAD_DIM = 64
FF = 3072
BUCKETS = 32
PREFIX = 20
DOCS = 8
SEQ = 1024
SEQS = 8
MEMROWS = 256


def with_ends(entries, own_key, low, largest):
    longest = entries.shape.index(max(entries.shape))
    spots = []
    for shift in (0, 1):
        where = [jax.random.randint(jax.random.fold_in(own_key, axis), (), 0, length) for axis, length in enumerate(entries.shape)]
        where[longest] = (where[longest] + shift) % entries.shape[longest]
        spots.append(tuple(where))
    return entries.at[spots[0]].set(low).at[spots[1]].set(largest)


def block_scale(key, extent, cuts, least, largest):
    def one(axis_at, parts):
        heights = jax.random.uniform(jax.random.fold_in(jax.random.fold_in(key, 6), axis_at), (parts,), jnp.float32, least / len(cuts), largest / len(cuts))
        return jnp.repeat(jnp.exp(heights), extent[axis_at] // parts).reshape((-1,) + (1,) * (len(extent) - axis_at - 1))

    gain = one(*cuts[0])
    for cut in cuts[1:]:
        gain = gain * one(*cut)
    return gain


def split_up(amount, total, reach, skew):
    weights = [(1 << 20) // math.isqrt(standing ** skew) + 1 for standing in range(2, amount + 1)]
    surplus, given = total - reach - (amount - 1), [1] * (amount - 1)
    while surplus > 0:
        candidates = [i for i in range(amount - 1) if given[i] < reach]
        whole, remaining = sum([weights[i] for i in candidates]), surplus
        for i in candidates:
            extra = min(reach - given[i], max(1, remaining * weights[i] // whole), surplus)
            given[i] = given[i] + extra
            surplus = surplus - extra
    return np.array([reach] + given)


def ragged(rng, amount, total, most, lean):
    if amount == 2:
        one = jax.random.randint(rng, (), max(1, total - most), min(most, total - 1) + 1)
        return jnp.stack([one, total - one])
    tallies = jnp.asarray(split_up(amount, total, most, lean), jnp.int32)
    pairs = (amount - 1) // 2
    donor, taker = tallies[1:1 + 2 * pairs:2], tallies[2:2 + 2 * pairs:2]
    slack = jnp.minimum(donor - 1, most - taker)
    passed = jax.random.randint(jax.random.fold_in(rng, 1), (pairs,), 0, 1 << 20) % (slack + 1)
    tallies = tallies.at[1:1 + 2 * pairs:2].set(donor - passed).at[2:2 + 2 * pairs:2].set(taker + passed)
    return tallies[jax.random.permutation(jax.random.fold_in(rng, 2), amount)]


def noise(key, shape, deviation, bound, shards=(), kind=jnp.bfloat16):
    drawn = jax.random.normal(key, shape, jnp.float32) * deviation
    if len(shards) > 0:
        drawn = block_scale(key, shape, shards, -0.22, 0.18) * drawn
    return jnp.clip(drawn, min=-bound, max=bound).astype(kind)


def setup_inputs(seed: int = 0) -> dict:
    key_of = jax.random.split(jax.random.key(seed), 27)
    enc_input = noise(key_of[0], (SEQS, SEQ, D), 1.0, 6.0, ((0, 4), (1, 8)))
    dec_input = noise(key_of[1], (SEQS, SEQ, D), 1.0, 6.0, ((0, 4), (1, 8)))
    segments = jax.vmap(lambda own: jnp.searchsorted(jnp.cumsum(ragged(own, DOCS, SEQ, SEQ // 2, 2)), jnp.arange(SEQ), side="right"))(jax.random.split(key_of[2], SEQS)).reshape((SEQS, SEQ)).astype(jnp.int32)
    prefix_rows = with_ends(jax.random.randint(key_of[3], (SEQS, DOCS, PREFIX), 0, MEMROWS), jax.random.fold_in(key_of[3], 1), 0, MEMROWS - 1).astype(jnp.int32)
    buckets = with_ends(jax.random.randint(key_of[4], (2 * SEQ,), 0, BUCKETS), jax.random.fold_in(key_of[4], 1), 0, BUCKETS - 1).astype(jnp.int32)
    memory = noise(key_of[5], (MEMROWS, 2 * D), 0.5, 3.0, ((0, 4),))
    enc_gain = jnp.clip(1.0 + 0.1 * jax.random.normal(key_of[6], (D,), jnp.float32), 0.5, 1.5).astype(jnp.bfloat16)
    enc_qkv = noise(key_of[7], (D, 3 * D), (6 * D) ** -0.5, 0.09375, ((0, 4),))
    enc_rel = noise(key_of[8], (BUCKETS, HEADS), 0.7, 3.0, ((0, 4),))
    enc_proj = noise(key_of[9], (D, D), 32 ** -0.5, 1.0, ((0, 4),))
    enc_ffnorm = jnp.clip(1.0 + 0.1 * jax.random.normal(key_of[10], (D,), jnp.float32), 0.5, 1.5).astype(jnp.bfloat16)
    enc_ffin = noise(key_of[11], (D, FF), D ** -0.5, 0.21875, ((0, 4),))
    enc_ffout = noise(key_of[12], (FF, D), (FF // 2) ** -0.5, 0.15625, ((0, 4),))
    dec_gain = jnp.clip(1.0 + 0.1 * jax.random.normal(key_of[13], (D,), jnp.float32), 0.5, 1.5).astype(jnp.bfloat16)
    dec_qkv = noise(key_of[14], (D, 3 * D), (6 * D) ** -0.5, 0.09375, ((0, 4),))
    dec_rel = noise(key_of[15], (BUCKETS, HEADS), 0.7, 3.0, ((0, 4),))
    dec_proj = noise(key_of[16], (D, D), 32 ** -0.5, 1.0, ((0, 4),))
    cross_gain = jnp.clip(1.0 + 0.1 * jax.random.normal(key_of[17], (D,), jnp.float32), 0.5, 1.5).astype(jnp.bfloat16)
    cross_query = noise(key_of[18], (D, D), (6 * D) ** -0.5, 0.09375, ((0, 4),))
    cross_kv = noise(key_of[19], (D, 2 * D), (12 * D) ** -0.5, 0.0625, ((0, 4),))
    cross_proj = noise(key_of[20], (D, D), 32 ** -0.5, 1.0, ((0, 4),))
    dec_ffnorm = jnp.clip(1.0 + 0.1 * jax.random.normal(key_of[21], (D,), jnp.float32), 0.5, 1.5).astype(jnp.bfloat16)
    dec_ffin = noise(key_of[22], (D, FF), D ** -0.5, 0.21875, ((0, 4),))
    dec_ffout = noise(key_of[23], (FF, D), (FF // 2) ** -0.5, 0.15625, ((0, 4),))
    enc_cotan = noise(key_of[24], (SEQS, SEQ, D), 1.0, 6.0, ((0, 4), (1, 8)))
    dec_cotan = noise(key_of[25], (SEQS, SEQ, D), 1.0, 6.0, ((0, 4), (1, 8)))
    return dict(enc_input=enc_input, dec_input=dec_input, segments=segments, prefix_rows=prefix_rows, buckets=buckets, memory=memory, enc_gain=enc_gain, enc_qkv=enc_qkv, enc_rel=enc_rel, enc_proj=enc_proj, enc_ffnorm=enc_ffnorm, enc_ffin=enc_ffin, enc_ffout=enc_ffout, dec_gain=dec_gain, dec_qkv=dec_qkv, dec_rel=dec_rel, dec_proj=dec_proj, cross_gain=cross_gain, cross_query=cross_query, cross_kv=cross_kv, cross_proj=cross_proj, dec_ffnorm=dec_ffnorm, dec_ffin=dec_ffin, dec_ffout=dec_ffout, enc_cotan=enc_cotan, dec_cotan=dec_cotan)


highest = lax.Precision.HIGHEST
masked = -1e+30
epsilon = 1e-06

@jax.custom_vjp
def low(v):
    return lax.optimization_barrier(v.astype(jnp.bfloat16)).astype(jnp.float32)

@jax.custom_vjp
def low_back(v):
    return v

def low_keep(v):
    return (low(v), None)

def low_pass(kept, grad):
    return (grad,)

def back_keep(v):
    return (v, None)

def back_low(kept, grad):
    return (low(grad),)
low.defvjp(low_keep, low_pass)
low_back.defvjp(back_keep, back_low)

def rms_norm(values, gains):
    return values * lax.rsqrt(lax.optimization_barrier(jnp.mean(values * values, axis=-1, keepdims=True)) + epsilon) * gains

def smooth_act(values):
    return jax.nn.gelu(values, approximate=True)

def matmul(former, latter):
    return jnp.dot(former, latter, precision=highest)

def attend(queries, kv_rows, allowed, rel_bias, mem_rows):
    length = queries.shape[0]
    query_heads = queries.reshape(length, HEADS, HEAD_DIM)
    key_heads = kv_rows[:, :D].reshape(-1, HEADS, HEAD_DIM)
    value_heads = kv_rows[:, D:].reshape(-1, HEADS, HEAD_DIM)
    scores = jnp.einsum('qhd,khd->hqk', query_heads, key_heads, precision=highest)
    if rel_bias is not None:
        scores = scores + rel_bias
    scores = jnp.where(allowed[None], scores, masked)
    key_count = scores.shape[-1]
    if mem_rows is not None:
        mem_keys = mem_rows[:, :, :D].reshape(length, PREFIX, HEADS, HEAD_DIM)
        mem_scores = jnp.einsum('qhd,qphd->hqp', query_heads, mem_keys, precision=highest)
        scores = jnp.concatenate([scores, mem_scores], axis=-1)
    weights = low(jax.nn.softmax(low_back(scores), axis=-1))
    result = jnp.einsum('hqk,khd->qhd', weights[..., :key_count], value_heads, precision=highest)
    if mem_rows is not None:
        mem_values = mem_rows[:, :, D:].reshape(length, PREFIX, HEADS, HEAD_DIM)
        result = result + jnp.einsum('hqp,qphd->qhd', weights[..., key_count:], mem_values, precision=highest)
    return result.reshape(length, D)

def sequence_layers(params, enc_rows, dec_rows, seg_rows, prefix_table, buckets):
    memory, enc_gain, enc_qkv, enc_rel, enc_proj, enc_ffnorm, enc_ffin, enc_ffout, dec_gain, dec_qkv, dec_rel, dec_proj, cross_gain, cross_query, cross_kv, cross_proj, dec_ffnorm, dec_ffin, dec_ffout = params
    places = jnp.arange(SEQ, dtype=jnp.int32)
    rel_index = buckets[places[None, :] - places[:, None] + SEQ]
    same_doc = seg_rows[:, None] == seg_rows[None, :]
    causal = same_doc & (places[None, :] <= places[:, None])
    mem_rows = memory[prefix_table[seg_rows]]
    normed = low(rms_norm(enc_rows, enc_gain))
    projected = low(low_back(matmul(normed, enc_qkv)))
    attended = low(low_back(attend(projected[:, :D], projected[:, D:], same_doc, jnp.take(enc_rel.T, rel_index, axis=1), mem_rows)))
    hidden = enc_rows + low_back(matmul(attended, enc_proj))
    normed = low(rms_norm(hidden, enc_ffnorm))
    activated = low(smooth_act(low_back(matmul(normed, enc_ffin))))
    enc_result = hidden + low_back(matmul(activated, enc_ffout))
    normed = low(rms_norm(dec_rows, dec_gain))
    projected = low(low_back(matmul(normed, dec_qkv)))
    attended = low(low_back(attend(projected[:, :D], projected[:, D:], causal, jnp.take(dec_rel.T, rel_index, axis=1), None)))
    hidden = dec_rows + low_back(matmul(attended, dec_proj))
    normed = low(rms_norm(hidden, cross_gain))
    cross_queries = low(low_back(matmul(normed, cross_query)))
    cross_rows = low(low_back(matmul(low(enc_result), cross_kv)))
    attended = low(low_back(attend(cross_queries, cross_rows, same_doc, None, None)))
    hidden = hidden + low_back(matmul(attended, cross_proj))
    normed = low(rms_norm(hidden, dec_ffnorm))
    activated = low(smooth_act(low_back(matmul(normed, dec_ffin))))
    dec_result = hidden + low_back(matmul(activated, dec_ffout))
    return (enc_result, dec_result)

def reference(enc_input, dec_input, segments, prefix_rows, buckets, memory, enc_gain, enc_qkv, enc_rel, enc_proj, enc_ffnorm, enc_ffin, enc_ffout, dec_gain, dec_qkv, dec_rel, dec_proj, cross_gain, cross_query, cross_kv, cross_proj, dec_ffnorm, dec_ffin, dec_ffout, enc_cotan, dec_cotan):
    params = tuple((weight.astype(jnp.float32) for weight in (memory, enc_gain, enc_qkv, enc_rel, enc_proj, enc_ffnorm, enc_ffin, enc_ffout, dec_gain, dec_qkv, dec_rel, dec_proj, cross_gain, cross_query, cross_kv, cross_proj, dec_ffnorm, dec_ffin, dec_ffout)))
    layered = jax.checkpoint(sequence_layers)

    def forward(weights, enc_all, dec_all):

        def one_sequence(members):
            return layered(weights, members[0], members[1], members[2], members[3], buckets)
        return lax.map(one_sequence, (enc_all, dec_all, segments, prefix_rows))
    outputs, backward = jax.vjp(forward, params, enc_input.astype(jnp.float32), dec_input.astype(jnp.float32))
    grads, enc_grad, dec_grad = backward((enc_cotan.astype(jnp.float32), dec_cotan.astype(jnp.float32)))
    return (outputs[0].astype(jnp.bfloat16), outputs[1].astype(jnp.bfloat16), enc_grad, dec_grad, grads[0], grads[1], grads[2], grads[3], grads[4], grads[5], grads[6], grads[7], grads[8], grads[9], grads[10], grads[11], grads[12], grads[13], grads[14], grads[15], grads[16], grads[17], grads[18])
```

```python
import functools

import jax
import jax.numpy as jnp
import numpy as np
from jax import lax
from jax.experimental import pallas as pl
from jax.experimental.pallas import tpu as pltpu
from jax.sharding import Mesh
from jax.sharding import PartitionSpec as P

D = 768
HEADS = 12
DH = 64
BUCKETS = 32
EPS = 1e-06
MASKED = -1e30
TP = 4
HQ = HEADS // TP
QC = HQ * DH
BF = jnp.bfloat16
F32 = jnp.float32
MESH_ID = pl.DeviceIdType.MESH
MB = 1024 * 1024


def mm(a, b):
    return jnp.dot(a, b, preferred_element_type=F32)


def mm_tn(a, b):
    return lax.dot_general(a, b, (((0,), (0,)), ((), ())), preferred_element_type=F32)


def mm_nt(a, b):
    return lax.dot_general(a, b, (((1,), (1,)), ((), ())), preferred_element_type=F32)


def gelu(v):
    return jax.nn.gelu(v, approximate=True)


def gelu_back(pre, grad):
    return jax.vjp(gelu, pre)[1](grad)[0]


def group_ids():
    me = lax.axis_index("tp")
    core = me + 1 - 2 * lax.rem(me, 2)
    across = lax.rem(me + 2, TP)
    far = lax.rem(core + 2, TP)
    return me, core, across, far


def greet(core, across):
    barrier = pltpu.get_barrier_semaphore()
    pl.semaphore_signal(barrier, inc=1, device_id={"tp": core}, device_id_type=MESH_ID)
    pl.semaphore_signal(barrier, inc=1, device_id={"tp": across}, device_id_type=MESH_ID)
    pl.semaphore_wait(barrier, 2)


def send(src, dst, send_sem, recv_sem, peer):
    return pltpu.make_async_remote_copy(
        src_ref=src,
        dst_ref=dst,
        send_sem=send_sem,
        recv_sem=recv_sem,
        device_id={"tp": peer},
        device_id_type=MESH_ID,
    )


def normed(values, gains):
    return values * lax.rsqrt(jnp.mean(values * values, axis=-1, keepdims=True) + EPS) * gains


class Gatherer:
    def __init__(self, buf, sems, chunk, ids):
        self.buf, self.sems, self.chunk, self.ids = buf, sems, chunk, ids
        self.sends = []

    def rows(self, j, owner):
        return self.buf.at[pl.ds(pl.multiple_of((TP * j + owner) * self.chunk, self.chunk), self.chunk)]

    def put(self, j, value):
        me, core, across, far = self.ids
        mine = self.rows(j, me)
        mine[...] = value
        x_copy = send(mine, mine, self.sems.at[0, j], self.sems.at[1, j], across)
        x_copy.start()
        c_copy = send(mine, mine, self.sems.at[2, j], self.sems.at[3, j], core)
        c_copy.start()
        self.sends += [x_copy, c_copy]

    def forward(self, j):
        me, core, across, far = self.ids
        theirs = self.rows(j, across)
        send(theirs, theirs, self.sems.at[0, j], self.sems.at[1, j], across).wait_recv()
        f_copy = send(theirs, theirs, self.sems.at[4, j], self.sems.at[5, j], core)
        f_copy.start()
        self.sends.append(f_copy)

    def finish(self):
        me, core, across, far = self.ids
        for j in range(2):
            a = self.rows(j, core)
            send(a, a, self.sems.at[2, j], self.sems.at[3, j], core).wait_recv()
            b = self.rows(j, far)
            send(b, b, self.sems.at[4, j], self.sems.at[5, j], core).wait_recv()
        for copy in self.sends:
            copy.wait_send()


def gather_kernel(chunk, x_ref, gain_ref, out_ref, sems):
    ids = group_ids()
    greet(ids[1], ids[2])
    g = Gatherer(out_ref, sems, chunk, ids)
    for j in range(2):
        g.put(j, normed(x_ref[j].astype(F32), gain_ref[...]).astype(BF))
    for j in range(2):
        g.forward(j)
    g.finish()


def gather_norm(number, x, gain):
    chunk = x.shape[1]
    return pl.pallas_call(
        functools.partial(gather_kernel, chunk),
        out_shape=jax.ShapeDtypeStruct((2 * TP * chunk, D), BF),
        in_specs=[pl.BlockSpec(memory_space=pltpu.VMEM)] * 2,
        out_specs=pl.BlockSpec(memory_space=pltpu.VMEM),
        scratch_shapes=[pltpu.SemaphoreType.DMA((6, 2))],
        compiler_params=pltpu.CompilerParams(
            collective_id=number, has_side_effects=True, vmem_limit_bytes=24 * MB
        ),
        name="gather_norm",
    )(x, gain)


def stage_kernel(conf, *refs):
    chunk, flips, back, gather = conf
    refs = list(refs)
    pairs = [(refs.pop(0), refs.pop(0), flip) for flip in flips]
    resid_ref = refs.pop(0)
    gain_ref = refs.pop(0) if (back or gather == "norm") else None
    x_ref = refs.pop(0) if back else None
    given_ref = refs.pop(0) if gather == "given" else None
    y_ref = refs.pop(0)
    gath_ref = refs.pop(0) if gather else None
    dgain_ref = refs.pop(0) if back else None
    s_far, r_far, s_x, r_x, s_core, r_core, keep, own, sems = refs[:9]
    gsems = refs[9] if gather else None
    ids = group_ids()
    me, core, across, far = ids

    def partial(owner, store):
        r0 = pl.multiple_of(owner * chunk, chunk)
        r1 = pl.multiple_of((TP + owner) * chunk, chunk)

        @pl.loop(0, D // 256)
        def _(n):
            cols = pl.ds(pl.multiple_of(n * 256, 256), 256)
            total = None
            for a_ref, w_ref, flip in pairs:
                a = jnp.concatenate([a_ref[pl.ds(r0, chunk)], a_ref[pl.ds(r1, chunk)]], axis=0)
                term = mm_nt(a, w_ref[cols, :]) if flip else mm(a, w_ref[:, cols])
                total = term if total is None else total + term
            for j in range(2):
                store(j, cols, total[j * chunk : (j + 1) * chunk])

    def into(ref):
        def store(j, cols, value):
            ref[j, :, cols] = value.astype(ref.dtype)

        return store

    greet(core, across)
    g = Gatherer(gath_ref, gsems, chunk, ids) if gather else None
    if gather == "given":
        for j in range(2):
            g.put(j, given_ref[j])
    partial(far, into(s_far))
    c_far = send(s_far, r_far, sems.at[0], sems.at[1], core)
    c_far.start()
    partial(across, into(keep))
    c_far.wait_recv()
    c_x = []
    for j in range(2):
        s_x[j] = (keep[j] + r_far[j].astype(F32)).astype(BF)
        c_x.append(send(s_x.at[j], r_x.at[j], sems.at[2 + j], sems.at[4 + j], across))
        c_x[j].start()
    partial(core, into(s_core))
    c_core = send(s_core, r_core, sems.at[6], sems.at[7], core)
    c_core.start()
    partial(me, into(own))
    c_core.wait_recv()
    if gather == "given":
        for j in range(2):
            g.forward(j)
    for j in range(2):
        c_x[j].wait_recv()
        total = own[j] + r_core[j].astype(F32) + r_x[j].astype(F32)
        if back:
            x = x_ref[j].astype(F32)
            gains = gain_ref[...]
            r = lax.rsqrt(jnp.mean(x * x, axis=-1, keepdims=True) + EPS)
            scaled = total * gains
            inner = jnp.mean(scaled * x, axis=-1, keepdims=True)
            y = resid_ref[j].astype(F32) + r * scaled - x * (r * r * r * inner)
            dgain = jnp.sum(total * x * r, axis=0, keepdims=True)
            if j == 0:
                dgain_ref[...] = dgain
            else:
                dgain_ref[...] += dgain
        else:
            y = resid_ref[j].astype(F32) + total
        y_ref[j] = y.astype(y_ref.dtype)
        if gather == "norm":
            g.put(j, normed(y, gain_ref[...]).astype(BF))
        elif gather == "low":
            g.put(j, y.astype(BF))
    if gather in ("norm", "low"):
        for j in range(2):
            g.forward(j)
    if gather:
        g.finish()
    c_far.wait_send()
    c_core.wait_send()
    for j in range(2):
        c_x[j].wait_send()


def stage(number, pairs, resid, *, back=None, gather=None, gain=None, given=None, dtype=F32):
    chunk = resid.shape[1]
    operands, flips = [], []
    for a, w, flip in pairs:
        operands += [a, w]
        flips.append(flip)
    operands.append(resid)
    if back:
        operands += [back[1], back[0]]
    elif gather == "norm":
        operands.append(gain)
    if gather == "given":
        operands.append(given)
    outs = [jax.ShapeDtypeStruct((2, chunk, D), dtype)]
    if gather:
        outs.append(jax.ShapeDtypeStruct((2 * TP * chunk, D), BF))
    if back:
        outs.append(jax.ShapeDtypeStruct((1, D), F32))
    half = pltpu.VMEM((2, chunk, D), BF)
    full = pltpu.VMEM((2, chunk, D), F32)
    scratch = [half] * 6 + [full] * 2 + [pltpu.SemaphoreType.DMA((8,))]
    if gather:
        scratch.append(pltpu.SemaphoreType.DMA((6, 2)))
    vmem = pl.BlockSpec(memory_space=pltpu.VMEM)
    return pl.pallas_call(
        functools.partial(stage_kernel, (chunk, tuple(flips), bool(back), gather)),
        out_shape=tuple(outs),
        in_specs=[vmem] * len(operands),
        out_specs=(vmem,) * len(outs),
        scratch_shapes=scratch,
        compiler_params=pltpu.CompilerParams(
            collective_id=number, has_side_effects=True, vmem_limit_bytes=40 * MB
        ),
        name="stage",
    )(*operands)


def attn_fwd_kernel(conf, pos_ref, *refs):
    chunk, q_off, kv_off, keys, extra, bias, causal = conf
    refs = list(refs)
    q_ref, kv_ref, segq_ref, segk_ref = refs[:4]
    refs = refs[4:]
    bvec_ref = refs.pop(0) if bias else None
    mkv_ref = refs.pop(0) if extra else None
    att_ref, p_ref, qs, ks, vs, os = refs[:6]
    toep = refs[6] if bias else None
    h, b = pl.program_id(0), pl.program_id(1)
    length = keys

    @pl.when((h == 0) & (b == 0))
    def _():
        for i in range(HQ):
            qs[i] = q_ref[:, q_off + DH * i : q_off + DH * (i + 1)]
            ks[i, :keys] = kv_ref[:, kv_off + DH * i : kv_off + DH * (i + 1)]
            vs[i, :keys] = kv_ref[:, kv_off + QC + DH * i : kv_off + QC + DH * (i + 1)]
            if extra:
                ks[i, keys:] = mkv_ref[:, DH * i : DH * (i + 1)]
                vs[i, keys:] = mkv_ref[:, QC + DH * i : QC + DH * (i + 1)]

    if bias:

        @pl.when(b == 0)
        def _():
            row = jnp.broadcast_to(bvec_ref[h], (chunk, 2 * length))
            toep[...] = pltpu.roll(row, 0, 1, stride=1, stride_axis=0)

    rows = pl.ds(pl.multiple_of(b * 2 * chunk, 2 * chunk), 2 * chunk)
    s = mm_nt(qs[h, rows], ks[h])
    allowed = segq_ref[rows] == segk_ref[...]
    if bias:
        parts = []
        for u in range(2):
            off = pl.multiple_of(length - pos_ref[2 * b + u], 128)
            parts.append(toep[:, pl.ds(off, keys)])
        biased = s[:, :keys] + jnp.concatenate(parts, axis=0)
        s = jnp.concatenate([biased, s[:, keys:]], axis=1) if extra else biased
    if causal:
        place = lax.broadcasted_iota(jnp.int32, (chunk, 1), 0)
        places = jnp.concatenate([place + pos_ref[2 * b + u] for u in range(2)], axis=0)
        allowed = allowed & (lax.broadcasted_iota(jnp.int32, (1, keys), 1) <= places)
    s = jnp.where(allowed, s, MASKED)
    top = jnp.max(s, axis=-1, keepdims=True)
    e = jnp.exp(s - top)
    p = (e * (1.0 / jnp.sum(e, axis=-1, keepdims=True))).astype(BF)
    p_ref[0] = p
    os[h, rows] = mm(p, vs[h]).astype(BF)

    @pl.when((h == HQ - 1) & (b == pl.num_programs(1) - 1))
    def _():
        for i in range(HQ):
            att_ref[:, DH * i : DH * (i + 1)] = os[i]


def whole(shape):
    return pl.BlockSpec(shape, lambda h, b, pos: (0,) * len(shape))


def attn_fwd(pos, q, kv, segq, segk, bvec, mkv, causal, q_off, kv_off):
    rows, keys = q.shape[0], kv.shape[0]
    chunk = rows // 8
    extra = 0 if mkv is None else mkv.shape[0]
    total = keys + extra
    conf = (chunk, q_off, kv_off, keys, extra, bvec is not None, causal)
    operands = [q, kv, segq, segk]
    operands += [v for v in (bvec, mkv) if v is not None]
    scratch = [
        pltpu.VMEM((HQ, rows, DH), BF),
        pltpu.VMEM((HQ, total, DH), BF),
        pltpu.VMEM((HQ, total, DH), BF),
        pltpu.VMEM((HQ, rows, DH), BF),
    ]
    if bvec is not None:
        scratch.append(pltpu.VMEM((chunk, 2 * keys), F32))
    return pl.pallas_call(
        functools.partial(attn_fwd_kernel, conf),
        out_shape=(
            jax.ShapeDtypeStruct((rows, QC), BF),
            jax.ShapeDtypeStruct((HQ, rows, total), BF),
        ),
        grid_spec=pltpu.PrefetchScalarGridSpec(
            num_scalar_prefetch=1,
            grid=(HQ, rows // (2 * chunk)),
            in_specs=[whole(v.shape) for v in operands],
            out_specs=(
                whole((rows, QC)),
                pl.BlockSpec((1, 2 * chunk, total), lambda h, b, pos: (h, b, 0)),
            ),
            scratch_shapes=scratch,
        ),
        compiler_params=pltpu.CompilerParams(
            dimension_semantics=("arbitrary", "arbitrary"), vmem_limit_bytes=48 * MB
        ),
        cost_estimate=pl.CostEstimate(
            flops=4 * HQ * rows * total * DH,
            bytes_accessed=HQ * rows * total * 2,
            transcendentals=HQ * rows * total,
        ),
        name="attn_fwd",
    )(pos, *operands)


def attn_bwd_kernel(conf, pos_ref, *refs):
    chunk, q_off, kv_off, keys, extra, bias = conf
    refs = list(refs)
    p_ref, q_ref, kv_ref, do_ref, att_ref = refs[:5]
    refs = refs[5:]
    mkv_ref = refs.pop(0) if extra else None
    dq_ref, dkv_ref = refs[:2]
    refs = refs[2:]
    dbvec_ref = refs.pop(0) if bias else None
    dmkv_ref = refs.pop(0) if extra else None
    qs, ks, vs, dos, rds, dqs, dks, dvs = refs[:8]
    diag = refs[8] if bias else None
    h, b = pl.program_id(0), pl.program_id(1)
    last = pl.num_programs(1) - 1
    length = keys

    @pl.when((h == 0) & (b == 0))
    def _():
        for i in range(HQ):
            qs[i] = q_ref[:, q_off + DH * i : q_off + DH * (i + 1)]
            ks[i, :keys] = kv_ref[:, kv_off + DH * i : kv_off + DH * (i + 1)]
            vs[i, :keys] = kv_ref[:, kv_off + QC + DH * i : kv_off + QC + DH * (i + 1)]
            if extra:
                ks[i, keys:] = mkv_ref[:, DH * i : DH * (i + 1)]
                vs[i, keys:] = mkv_ref[:, QC + DH * i : QC + DH * (i + 1)]
            grad = do_ref[:, DH * i : DH * (i + 1)]
            dos[i] = grad
            out = att_ref[:, DH * i : DH * (i + 1)]
            rds[i] = jnp.sum(grad.astype(F32) * out.astype(F32), axis=-1, keepdims=True)

    @pl.when(b == 0)
    def _():
        dks[h] = jnp.zeros(dks.shape[1:], F32)
        dvs[h] = jnp.zeros(dvs.shape[1:], F32)
        if bias:
            diag[...] = jnp.zeros_like(diag)

    rows = pl.ds(pl.multiple_of(b * 2 * chunk, 2 * chunk), 2 * chunk)
    q, grad, p = qs[h, rows], dos[h, rows], p_ref[0]
    dp = mm_nt(grad, vs[h])
    ds = (p.astype(F32) * (dp - rds[h, rows])).astype(BF)
    dqs[h, rows] = mm(ds, ks[h]).astype(BF)
    dks[h] += mm_tn(ds, q)
    dvs[h] += mm_tn(p, grad)
    if bias:
        for u in range(2):
            off = pl.multiple_of(length - pos_ref[2 * b + u], 128)
            diag[:, pl.ds(off, keys)] += ds[u * chunk : (u + 1) * chunk, :keys].astype(F32)

        @pl.when(b == last)
        def _():
            x = diag[...]
            size = chunk
            while size > 1:
                size //= 2
                x = x[:size] + pltpu.roll(x[size:], 2 * length - size, 1)
            dbvec_ref[h] = x

    @pl.when((h == HQ - 1) & (b == last))
    def _():
        for i in range(HQ):
            dq_ref[:, DH * i : DH * (i + 1)] = dqs[i]
            dkv_ref[:, DH * i : DH * (i + 1)] = dks[i, :keys].astype(dkv_ref.dtype)
            dkv_ref[:, QC + DH * i : QC + DH * (i + 1)] = dvs[i, :keys].astype(dkv_ref.dtype)
            if extra:
                dmkv_ref[:, DH * i : DH * (i + 1)] = dks[i, keys:].astype(BF)
                dmkv_ref[:, QC + DH * i : QC + DH * (i + 1)] = dvs[i, keys:].astype(BF)


def attn_bwd(pos, p, q, kv, grad, att, mkv, bias, q_off, kv_off, dtype):
    rows, keys = q.shape[0], kv.shape[0]
    chunk = rows // 8
    extra = 0 if mkv is None else mkv.shape[0]
    total = keys + extra
    conf = (chunk, q_off, kv_off, keys, extra, bias)
    operands = [q, kv, grad, att] + ([mkv] if extra else [])
    outs = [jax.ShapeDtypeStruct((rows, QC), BF), jax.ShapeDtypeStruct((keys, 2 * QC), dtype)]
    if bias:
        outs.append(jax.ShapeDtypeStruct((HQ, 1, 2 * keys), F32))
    if extra:
        outs.append(jax.ShapeDtypeStruct((extra, 2 * QC), BF))
    scratch = [
        pltpu.VMEM((HQ, rows, DH), BF),
        pltpu.VMEM((HQ, total, DH), BF),
        pltpu.VMEM((HQ, total, DH), BF),
        pltpu.VMEM((HQ, rows, DH), BF),
        pltpu.VMEM((HQ, rows, 1), F32),
        pltpu.VMEM((HQ, rows, DH), BF),
        pltpu.VMEM((HQ, total, DH), F32),
        pltpu.VMEM((HQ, total, DH), F32),
    ]
    if bias:
        scratch.append(pltpu.VMEM((chunk, 2 * keys), F32))
    return pl.pallas_call(
        functools.partial(attn_bwd_kernel, conf),
        out_shape=tuple(outs),
        grid_spec=pltpu.PrefetchScalarGridSpec(
            num_scalar_prefetch=1,
            grid=(HQ, rows // (2 * chunk)),
            in_specs=[pl.BlockSpec((1, 2 * chunk, total), lambda h, b, pos: (h, b, 0))]
            + [whole(v.shape) for v in operands],
            out_specs=tuple(whole(v.shape) for v in outs),
            scratch_shapes=scratch,
        ),
        compiler_params=pltpu.CompilerParams(
            dimension_semantics=("arbitrary", "arbitrary"), vmem_limit_bytes=48 * MB
        ),
        cost_estimate=pl.CostEstimate(
            flops=8 * HQ * rows * total * DH,
            bytes_accessed=HQ * rows * total * 2,
            transcendentals=0,
        ),
        name="attn_bwd",
    )(pos, p, *operands)


ALL = ("seq", "part", "tp", "fsdp")
CTX = ("seq", "part", "tp")


def per_device(
    parts,
    planes,
    enc_input,
    dec_input,
    segments,
    prefix_rows,
    buckets,
    memory,
    enc_gain,
    enc_qkv,
    enc_rel,
    enc_proj,
    enc_ffnorm,
    enc_ffin,
    enc_ffout,
    dec_gain,
    dec_qkv,
    dec_rel,
    dec_proj,
    cross_gain,
    cross_query,
    cross_kv,
    cross_proj,
    dec_ffnorm,
    dec_ffin,
    dec_ffout,
    enc_cotan,
    dec_cotan,
):
    seq, part, tp, plane = (lax.axis_index(name) for name in ALL)
    chunk = enc_input.shape[1]
    length = buckets.shape[0] // 2
    docs, prefix = prefix_rows.shape[1:]

    def swap(x):
        mine = lax.dynamic_index_in_dim(x, seq, 0, keepdims=False)
        other = lax.dynamic_index_in_dim(x, 1 - seq, 0, keepdims=False)
        came = lax.ppermute(other, "seq", [(0, 1), (1, 0)])
        first = seq == 0
        return jnp.stack([jnp.where(first, mine, came), jnp.where(first, came, mine)])

    def fetch(x):
        return lax.all_gather(x, "fsdp", axis=0, tiled=True)

    def cols(w, start, width=QC):
        return lax.dynamic_slice_in_dim(w, start + width * tp, width, 1)

    gains = (enc_gain, enc_ffnorm, dec_gain, cross_gain, dec_ffnorm)
    small = jnp.concatenate(list(gains) + [enc_rel.reshape(-1), dec_rel.reshape(-1)])
    small = lax.all_gather(small, "fsdp", axis=0)
    per = enc_gain.shape[0]
    gain_rows = [small[:, per * i : per * (i + 1)].reshape(1, D).astype(F32) for i in range(5)]
    g_enc, g_effn, g_dec, g_cross, g_dffn = gain_rows
    per_rel = enc_rel.size
    rels = [
        small[:, 5 * per + per_rel * i : 5 * per + per_rel * (i + 1)].reshape(BUCKETS, HEADS)
        for i in range(2)
    ]
    onehot = (buckets[:, None] == jnp.arange(BUCKETS, dtype=jnp.int32)[None, :]).astype(BF)

    def bias_vector(rel):
        own = lax.dynamic_slice_in_dim(rel, HQ * tp, HQ, 1)
        return lax.dot_general(
            own, onehot, (((0,), (1,)), ((), ())), preferred_element_type=F32
        ).reshape(HQ, 1, 2 * length)

    def qkv_part(w):
        return jnp.concatenate([cols(w, D * i) for i in range(w.shape[1] // D)], axis=1)

    hidden = enc_ffout.shape[0] // TP

    def ffin_part(w):
        return jnp.concatenate(
            [cols(w, hidden * TP * i, hidden) for i in range(planes)], axis=1
        )

    def ffout_part(w):
        return lax.dynamic_slice_in_dim(w, hidden * tp, hidden, 0)

    w_eqkv = fetch(qkv_part(enc_qkv))
    table = fetch(qkv_part(memory))
    xe, xd = swap(enc_input), swap(dec_input)
    segs = lax.all_gather(segments, CTX, axis=1, tiled=True)
    seg = lax.dynamic_index_in_dim(segs, seq, 0, keepdims=False)
    pairs = [(i * TP + j, j * TP + i) for i in range(TP) for j in range(TP)]
    projs = jnp.stack([enc_proj, dec_proj, cross_proj])
    if planes == TP:
        projs = lax.ppermute(projs, ("tp", "fsdp"), pairs)
    else:
        projs = lax.all_gather(projs, "fsdp", axis=1, tiled=True)
        projs = lax.dynamic_slice_in_dim(projs, QC * tp, QC, 1)
    w_eproj, w_dproj, w_cproj = projs[0], projs[1], projs[2]
    w_dqkv = fetch(qkv_part(dec_qkv))
    w_effin, w_effout = fetch(ffin_part(enc_ffin)), fetch(ffout_part(enc_ffout))
    w_cq, w_ckv = fetch(qkv_part(cross_query)), fetch(qkv_part(cross_kv))
    w_dffin, w_dffout = fetch(ffin_part(dec_ffin)), fetch(ffout_part(dec_ffout))
    xec, xdc = swap(enc_cotan), swap(dec_cotan)

    index = jnp.arange(2 * TP, dtype=jnp.int32)
    pos = ((index // TP) * TP * parts + TP * part + index % TP) * chunk
    segq = lax.dynamic_index_in_dim(seg.reshape(2, parts, TP * chunk), part, 1, keepdims=False)
    segq = segq.reshape(-1, 1)
    segk = seg.reshape(1, length)
    ids = lax.dynamic_index_in_dim(prefix_rows, seq, 0, keepdims=False).reshape(-1)
    extra = -(-(docs * prefix) // 256) * 256
    ids = jnp.concatenate([ids, jnp.full((extra - docs * prefix,), -1, jnp.int32)])
    mem_doc = np.full((extra,), -1, np.int32)
    mem_doc[: docs * prefix] = np.arange(docs * prefix) // prefix
    segk_mem = jnp.concatenate([segk, jnp.asarray(mem_doc)[None]], axis=1)
    pick = (ids[:, None] == jnp.arange(table.shape[0], dtype=jnp.int32)[None, :]).astype(BF)
    mkv = mm(pick, table).astype(BF)

    def spread(kv):
        if parts == 1:
            return kv
        got = lax.all_gather(kv, "part", axis=0)
        return got.reshape(parts, 2, TP * chunk, -1).transpose(1, 0, 2, 3).reshape(length, -1)

    def collect(dkv):
        if parts == 1:
            return dkv
        split = dkv.reshape(2, parts, TP * chunk, -1).transpose(1, 0, 2, 3)
        split = split.reshape(parts * 2 * TP * chunk, -1)
        return lax.psum_scatter(split, "part", scatter_dimension=0, tiled=True).astype(BF)

    def self_attn(rows, bvec, mem, segk_now, causal):
        if parts == 1:
            q, kv, kv_off = rows, rows, QC
        else:
            q, kv, kv_off = rows[:, :QC], spread(rows[:, QC:]), 0
        att, p = attn_fwd(pos, q, kv, segq, segk_now, bvec, mem, causal, 0, kv_off)

        def back(grad):
            got = attn_bwd(
                pos, p, q, kv, grad, att, mem, bvec is not None, 0, kv_off, BF if parts == 1 else F32
            )
            return got[0], collect(got[1]), got[2:]

        return att, back

    def cross_attn(q, kv_rows):
        kv = spread(kv_rows)
        att, p = attn_fwd(pos, q, kv, segq, segk, None, None, False, 0, 0)

        def back(grad):
            got = attn_bwd(pos, p, q, kv, grad, att, None, False, 0, 0, BF if parts == 1 else F32)
            return got[0], collect(got[1])

        return att, back

    en = gather_norm(0, xe, g_enc)
    e_rows = mm(en, w_eqkv).astype(BF)
    e_att, e_back = self_attn(e_rows, bias_vector(rels[0]), mkv, segk_mem, False)
    e_mid, e_fn = stage(2, [(e_att, w_eproj, False)], xe, gather="norm", gain=g_effn)
    dn = gather_norm(1, xd, g_dec)
    d_rows = mm(dn, w_dqkv).astype(BF)
    d_att, d_back = self_attn(d_rows, bias_vector(rels[1]), None, segk, True)
    e_pre = mm(e_fn, w_effin)
    e_act = gelu(e_pre).astype(BF)
    e_low, e_gath = stage(3, [(e_act, w_effout, False)], e_mid, gather="low", dtype=BF)
    d_mid, c_n = stage(4, [(d_att, w_dproj, False)], xd, gather="norm", gain=g_cross)
    c_q = mm(c_n, w_cq).astype(BF)
    c_kv = mm(e_gath, w_ckv).astype(BF)
    c_att, c_back = cross_attn(c_q, c_kv)
    d_cross, d_fn = stage(5, [(c_att, w_cproj, False)], d_mid, gather="norm", gain=g_dffn)
    d_pre = mm(d_fn, w_dffin)
    d_act = gelu(d_pre).astype(BF)
    d_low, up_g = stage(
        6, [(d_act, w_dffout, False)], d_cross, gather="given", given=xdc, dtype=BF
    )
    enc_output, dec_output = swap(e_low), swap(d_low)

    def ff_back(number, up, up_rows, fn, act, pre, w_in, w_out, mid, gain):
        d_out = mm_tn(act, up_rows).astype(BF)
        pre_grad = gelu_back(pre, mm_nt(up_rows, w_out)).astype(BF)
        d_in = mm_tn(fn, pre_grad).astype(BF)
        got = stage(number, [(pre_grad, w_in, True)], up, back=(mid, gain), gather="low")
        return got, d_in, d_out

    (up, up_g, dg_dffn), g_dffin, g_dffout = ff_back(
        7, xdc, up_g, d_fn, d_act, d_pre, w_dffin, w_dffout, d_cross, g_dffn
    )
    g_cproj = mm_tn(c_att, up_g).astype(BF)
    c_dq, c_dkv = c_back(mm_nt(up_g, w_cproj).astype(BF))
    g_cq = mm_tn(c_n, c_dq).astype(BF)
    g_ckv = mm_tn(e_gath, c_dkv).astype(BF)
    e_up, e_up_g = stage(8, [(c_dkv, w_ckv, True)], xec, gather="low")
    up, up_g, dg_cross = stage(
        9, [(c_dq, w_cq, True)], up, back=(d_mid, g_cross), gather="low"
    )
    g_dproj = mm_tn(d_att, up_g).astype(BF)
    d_dq, d_dkv, (d_dbv,) = d_back(mm_nt(up_g, w_dproj).astype(BF))
    g_dqkv = jnp.concatenate([mm_tn(dn, d_dq), mm_tn(dn, d_dkv)], axis=1).astype(BF)
    d_in, dg_dec = stage(
        10,
        [(d_dq, w_dqkv[:, :QC], True), (d_dkv, w_dqkv[:, QC:], True)],
        up,
        back=(xd, g_dec),
    )
    (e_up, e_up_g, dg_effn), g_effin, g_effout = ff_back(
        11, e_up, e_up_g, e_fn, e_act, e_pre, w_effin, w_effout, e_mid, g_effn
    )
    g_eproj = mm_tn(e_att, e_up_g).astype(BF)
    e_dq, e_dkv, (e_dbv, d_mkv) = e_back(mm_nt(e_up_g, w_eproj).astype(BF))
    g_eqkv = jnp.concatenate([mm_tn(en, e_dq), mm_tn(en, e_dkv)], axis=1).astype(BF)
    g_table = mm_tn(pick, d_mkv).astype(BF)
    e_in, dg_enc = stage(
        12,
        [(e_dq, w_eqkv[:, :QC], True), (e_dkv, w_eqkv[:, QC:], True)],
        e_up,
        back=(xe, g_enc),
    )
    enc_ingrad = swap(e_in.astype(BF)).astype(F32)
    dec_ingrad = swap(d_in.astype(BF)).astype(F32)

    split = 2 * parts

    def reduce_rows(g):
        return lax.psum_scatter(
            g, ("fsdp", "seq", "part"), scatter_dimension=0, tiled=True
        )

    def gather_rows(g):
        got = lax.all_gather(g, CTX, axis=0)
        return got.reshape((split, TP) + g.shape)

    def by_cols(got, width):
        rows = got.shape[2]
        got = got.reshape(split, TP, rows, -1, width).transpose(0, 2, 3, 1, 4)
        return got.reshape(split * rows, -1).astype(F32)

    def by_rows(got):
        return got.transpose(1, 0, 2, 3).reshape(-1, D).astype(F32)

    red = functools.partial(reduce_rows)
    r_dffin, r_dffout, r_cq, r_ckv = red(g_dffin), red(g_dffout), red(g_cq), red(g_ckv)
    r_dqkv, r_effin, r_effout = red(g_dqkv), red(g_effin), red(g_effout)
    r_eqkv, r_table = red(g_eqkv), red(g_table)
    g_projs = [g_eproj, g_dproj, g_cproj]
    if planes == TP:
        r_projs = red(jnp.concatenate(g_projs, axis=1))
        r_projs = lax.ppermute(r_projs, ("tp", "fsdp"), pairs)
        r_projs = gather_rows(r_projs)
        o_projs = [by_rows(r_projs[..., D * i : D * (i + 1)]) for i in range(3)]
    else:
        o_projs = []
        for g in g_projs:
            full = lax.dynamic_update_slice_in_dim(jnp.zeros((D, D), BF), g, QC * tp, 0)
            full = lax.psum_scatter(full, "fsdp", scatter_dimension=0, tiled=True)
            o_projs.append(lax.psum(full.astype(F32), CTX))
    o_eproj, o_dproj, o_cproj = o_projs
    o_dffin = by_cols(gather_rows(r_dffin), hidden)
    o_dffout = by_rows(gather_rows(r_dffout))
    o_cq = by_cols(gather_rows(r_cq), QC)
    o_ckv = by_cols(gather_rows(r_ckv), QC)
    o_dqkv = by_cols(gather_rows(r_dqkv), QC)
    o_effin = by_cols(gather_rows(r_effin), hidden)
    o_effout = by_rows(gather_rows(r_effout))
    o_eqkv = by_cols(gather_rows(r_eqkv), QC)
    o_table = by_cols(gather_rows(r_table), QC)

    def rel_grad(dbv):
        own = lax.dot_general(
            onehot.astype(F32),
            dbv.reshape(HQ, -1),
            (((0,), (1,)), ((), ())),
            precision=lax.Precision.HIGHEST,
            preferred_element_type=F32,
        )
        return lax.dynamic_update_slice_in_dim(jnp.zeros((BUCKETS, HEADS), F32), own, HQ * tp, 1)

    tiny = [dg_enc, dg_effn, dg_dec, dg_cross, dg_dffn]
    tiny = jnp.concatenate([v.reshape(planes, -1) for v in tiny] + [
        rel_grad(v).reshape(planes, -1) for v in (e_dbv, d_dbv)
    ], axis=1)
    tiny = lax.psum(tiny, ALL)
    tiny = lax.dynamic_index_in_dim(tiny, plane, 0, keepdims=False)
    o_gains = [tiny[per * i : per * (i + 1)] for i in range(5)]
    o_rels = [
        tiny[5 * per + per_rel * i : 5 * per + per_rel * (i + 1)].reshape(-1, HEADS)
        for i in range(2)
    ]
    return (
        enc_output,
        dec_output,
        enc_ingrad,
        dec_ingrad,
        o_table,
        o_gains[0],
        o_eqkv,
        o_rels[0],
        o_eproj,
        o_gains[1],
        o_effin,
        o_effout,
        o_gains[2],
        o_dqkv,
        o_rels[1],
        o_dproj,
        o_gains[3],
        o_cq,
        o_ckv,
        o_cproj,
        o_gains[4],
        o_dffin,
        o_dffout,
    )


def solution(mesh):
    ctx, planes = mesh.shape["ctx"], mesh.shape["fsdp"]
    parts = ctx // (2 * TP)
    inner = Mesh(np.asarray(mesh.devices).reshape(2, parts, TP, planes), ALL)
    rows3 = P("fsdp", CTX, None)
    mat, vec = P("fsdp", None), P("fsdp")
    args = (
        (rows3, rows3, P("fsdp", CTX), P("fsdp", None, None), P(), mat)
        + (vec, mat, mat, mat, vec, mat, mat)
        + (vec, mat, mat, mat)
        + (vec, mat, mat, mat)
        + (vec, mat, mat)
        + (rows3, rows3)
    )
    outs = (
        (rows3, rows3, rows3, rows3, mat)
        + (vec, mat, mat, mat, vec, mat, mat)
        + (vec, mat, mat, mat)
        + (vec, mat, mat, mat)
        + (vec, mat, mat)
    )
    return jax.shard_map(
        functools.partial(per_device, parts, planes),
        mesh=inner,
        in_specs=args,
        out_specs=outs,
        check_vma=False,
    )
```

```python
import collections
import functools

import jax
import jax.numpy as jnp
import numpy as np
from jax import lax
from jax.experimental import pallas as pl
from jax.experimental.pallas import tpu as pltpu
from jax.sharding import Mesh
from jax.sharding import PartitionSpec as P

D = 768
HEADS = 12
DH = 64
BUCKETS = 32
EPS = 1e-06
MASKED = -1e30
TP = 4
HQ = HEADS // TP
QC = HQ * DH
BF = jnp.bfloat16
F32 = jnp.float32
MESH_ID = pl.DeviceIdType.MESH
MB = 1024 * 1024
VMEM_LIMIT = 60 * MB


def mm(a, b):
    return jnp.dot(a, b, preferred_element_type=F32)


def mm_tn(a, b):
    return lax.dot_general(a, b, (((0,), (0,)), ((), ())), preferred_element_type=F32)


def mm_nt(a, b):
    return lax.dot_general(a, b, (((1,), (1,)), ((), ())), preferred_element_type=F32)


def gelu(v):
    return jax.nn.gelu(v, approximate=True)


def gelu_back(pre, grad):
    return jax.vjp(gelu, pre)[1](grad)[0]


def group_ids():
    me = lax.axis_index("tp")
    core = me + 1 - 2 * lax.rem(me, 2)
    across = lax.rem(me + 2, TP)
    far = lax.rem(core + 2, TP)
    return me, core, across, far


def send(src, dst, send_sem, recv_sem, peer):
    return pltpu.make_async_remote_copy(
        src_ref=src,
        dst_ref=dst,
        send_sem=send_sem,
        recv_sem=recv_sem,
        device_id={"tp": peer},
        device_id_type=MESH_ID,
    )


def normed(values, gains):
    return values * lax.rsqrt(jnp.mean(values * values, axis=-1, keepdims=True) + EPS) * gains


class Gatherer:
    def __init__(self, buf, stage, sems, chunk, ids):
        self.buf, self.stage, self.sems, self.chunk, self.ids = buf, stage, sems, chunk, ids
        self.sends, self.own = [], []

    def rows(self, j, owner):
        return self.buf.at[pl.ds(pl.multiple_of((TP * j + owner) * self.chunk, self.chunk), self.chunk)]

    def put(self, j, value):
        me, core, across, far = self.ids
        mine = self.stage.at[j]
        mine[...] = value
        x_copy = send(mine, self.rows(j, me), self.sems.at[0, j], self.sems.at[1, j], across)
        x_copy.start()
        c_copy = send(mine, self.rows(j, me), self.sems.at[2, j], self.sems.at[3, j], core)
        c_copy.start()
        self.sends += [x_copy, c_copy]
        own = pltpu.make_async_copy(mine, self.rows(j, me), self.sems.at[6, j])
        own.start()
        self.own.append(own)

    def forward(self, j):
        me, core, across, far = self.ids
        theirs = self.rows(j, across)
        send(theirs, theirs, self.sems.at[0, j], self.sems.at[1, j], across).wait_recv()
        f_copy = send(theirs, theirs, self.sems.at[4, j], self.sems.at[5, j], core)
        f_copy.start()
        self.sends.append(f_copy)

    def finish(self):
        me, core, across, far = self.ids
        for j in range(2):
            a = self.rows(j, core)
            send(a, a, self.sems.at[2, j], self.sems.at[3, j], core).wait_recv()
            b = self.rows(j, far)
            send(b, b, self.sems.at[4, j], self.sems.at[5, j], core).wait_recv()
        for copy in self.sends:
            copy.wait_send()
        for copy in self.own:
            copy.wait()


Job = collections.namedtuple("Job", ["axis", "src_axis", "dst_axis", "local", "src", "shape", "finish"])


def gather_job(axis, src, size=2, at=0):
    shape = src.shape[:at] + (size,) + src.shape[at:]
    return Job(axis, None, at, True, src, shape, None)


def total_job(axis, src, size=2):
    return gather_job(axis, src, size)._replace(finish="sum")


def deal_job(axis, src):
    return Job(axis, 0, 0, True, src, src.shape, "sum")


def swap_job(src, at=0, add=False):
    shape = src.shape[:at] + src.shape[at + 1 :]
    return Job("seq", at, None, add, src, shape, "add" if add else None)


def turn_job(src):
    return Job("turn", None, None, True, src, src.shape, None)


def block_job(src):
    return Job("ctx", 0, 0, True, src, (2 * TP,) + src.shape[1:], None)


def last_job(src, width):
    return gather_job("core", src, 2, 2)._replace(finish=("layout", width))


def result_of(job):
    if job.finish == "sum":
        return job.shape[1:], job.src.dtype
    if isinstance(job.finish, tuple):
        seqs, halves, cores, rows, cols = job.shape
        if job.finish[1]:
            return (seqs * rows, halves * cores * cols), F32
        return (seqs * halves * cores * rows, cols), F32
    return job.shape, job.src.dtype


def entry(ref, axis, index):
    return ref if axis is None else ref.at[(slice(None),) * axis + (index,)]


class Shipper:
    def __init__(self, jobs, planes, srcs, outs, scratch, sems):
        self.jobs, self.planes, self.srcs, self.outs, self.sems = jobs, planes, srcs, outs, sems
        self.tp, self.seq, self.plane = (lax.axis_index(n) for n in ("tp", "seq", "fsdp"))
        self.dsts, self.bounce, self.made = [], [], []
        for job, out in zip(jobs, outs):
            if job.finish:
                self.dsts.append(scratch.pop(0))
                self.bounce.append(scratch.pop(0) if job.finish == "add" else None)
                self.made.append(scratch.pop(0) if job.finish != "add" else None)
            else:
                self.dsts.append(out)
                self.bounce.append(scratch.pop(0) if job.local else None)
                self.made.append(None)

    @staticmethod
    def scratch(jobs):
        shapes = []
        for job in jobs:
            dtype = job.src.dtype
            if job.finish:
                shapes.append(pltpu.VMEM(job.shape, dtype))
                if job.finish == "add":
                    shapes.append(pltpu.VMEM(job.shape, dtype))
                else:
                    shapes.append(pltpu.VMEM(*result_of(job)))
            elif job.local:
                drop = job.dst_axis
                own = job.shape if drop is None else job.shape[:drop] + job.shape[drop + 1 :]
                shapes.append(pltpu.VMEM(own, dtype))
        return shapes

    @staticmethod
    def count(jobs, planes):
        return sum(2 * Shipper.n_peers(job, planes) + 2 for job in jobs)

    @staticmethod
    def n_peers(job, planes):
        return {"fsdp": planes - 1, "ctx": 2 * TP - 1}.get(job.axis, 1)

    def coord(self, axis):
        half = self.tp // 2
        return {
            "fsdp": self.plane,
            "seq": self.seq,
            "across": half,
            "core": self.tp - 2 * half,
            "ctx": TP * self.seq + self.tp,
            "turn": None,
        }[axis]

    def peers(self, axis):
        if axis == "fsdp":
            n, z = self.planes, self.plane
            for k in range(1, n):
                to = lax.rem(z + k, n)
                yield to, {"fsdp": to}, lax.rem(z + (n - k), n)
        elif axis == "ctx":
            for k in range(1, 2 * TP):
                to = lax.rem(self.seq + k // TP, 2)
                to_tp = lax.rem(self.tp + k % TP, TP)
                from_seq = lax.rem(self.seq + (2 - k // TP), 2)
                from_tp = lax.rem(self.tp + (TP - k % TP), TP)
                yield to, {"seq": to, "tp": to_tp}, TP * from_seq + from_tp
        elif axis == "seq":
            yield 1 - self.seq, {"seq": 1 - self.seq}, 1 - self.seq
        elif axis == "turn":
            yield None, {"fsdp": self.tp, "tp": self.plane}, None
        else:
            to = lax.rem(self.tp + 2, TP) if axis == "across" else self.tp + 1 - 2 * lax.rem(self.tp, 2)
            other = 1 - self.coord(axis)
            yield other, {"tp": to}, other

    def greet(self, always=("core", "across")):
        axes = list(always) + sorted({job.axis for job in self.jobs} - set(always))
        barrier = pltpu.get_barrier_semaphore()
        total = 0
        for axis in axes:
            for _, device, _ in self.peers(axis):
                if axis == "turn":
                    continue
                pl.semaphore_signal(barrier, inc=1, device_id=device, device_id_type=MESH_ID)
                total += 1
        if "turn" in axes:
            moves = self.plane != self.tp

            @pl.when(moves)
            def _():
                for _, device, _ in self.peers("turn"):
                    pl.semaphore_signal(barrier, inc=1, device_id=device, device_id_type=MESH_ID)
                pl.semaphore_wait(barrier, total + 1)

            @pl.when(jnp.logical_not(moves))
            def _():
                pl.semaphore_wait(barrier, total)
        else:
            pl.semaphore_wait(barrier, total)

    def each(self, act_remote, act_local):
        base = 0
        for n, (job, src, dst) in enumerate(zip(self.jobs, self.srcs, self.dsts)):
            mine = self.coord(job.axis)
            peers = list(self.peers(job.axis))
            for i, (to, device, source) in enumerate(peers):
                sems = (self.sems.at[base + 2 * i], self.sems.at[base + 2 * i + 1])

                def copy_into(slot, to=to, device=device, sems=sems, src=src, dst=dst, job=job):
                    return pltpu.make_async_remote_copy(
                        src_ref=entry(src, job.src_axis, to),
                        dst_ref=entry(dst, job.dst_axis, slot),
                        send_sem=sems[0],
                        recv_sem=sems[1],
                        device_id=device,
                        device_id_type=MESH_ID,
                    )

                def remote(copy_into=copy_into, source=source, mine=mine):
                    act_remote(copy_into, mine, source)

                if job.axis == "turn":
                    pl.when(self.plane != self.tp)(remote)
                else:
                    remote()
            if job.local:
                own = self.seq if job.axis == "ctx" else mine

                def local(n=n, job=job, src=src, dst=dst, own=own, mine=mine, sem=base + 2 * len(peers)):
                    here, there = entry(src, job.src_axis, own), entry(dst, job.dst_axis, mine)
                    bounce = self.bounce[n]
                    if bounce is None:
                        act_local([(here, there)], self.sems.at[sem])
                    elif job.finish == "add":
                        act_local([(here, bounce)], self.sems.at[sem])
                    else:
                        act_local([(here, bounce), (bounce, there)], self.sems.at[sem])

                if job.axis == "turn":
                    pl.when(self.plane == self.tp)(local)
                else:
                    local()
            base += 2 * len(peers) + 2
        return base

    def start(self):
        self.each(
            lambda copy_into, mine, source: copy_into(mine).start(),
            lambda legs, sem: pltpu.make_async_copy(*legs[0], sem).start(),
        )

    def finish(self):
        def turn_round(legs, sem):
            if len(legs) > 1:
                pltpu.make_async_copy(*legs[0], sem).wait()
                pltpu.make_async_copy(*legs[1], sem).start()

        def remote(copy_into, mine, source):
            copy_into(source).wait_recv()
            copy_into(mine).wait_send()

        self.each(lambda *_: None, turn_round)
        self.each(remote, lambda legs, sem: pltpu.make_async_copy(*legs[-1], sem).wait())
        stores, base = [], 0
        for job, dst, bounce, made, out in zip(
            self.jobs, self.dsts, self.bounce, self.made, self.outs
        ):
            base += 2 * self.n_peers(job, self.planes) + 2
            if not job.finish:
                continue
            if job.finish == "add":
                made = bounce

                @pl.loop(0, dst.shape[0])
                def _(i):
                    bounce[i] = (bounce[i].astype(F32) + dst[i].astype(F32)).astype(bounce.dtype)

            elif job.finish == "sum":
                total = dst[0].astype(F32)
                for i in range(1, dst.shape[0]):
                    total = total + dst[i].astype(F32)
                made[...] = total.astype(made.dtype)
            else:
                self.lay_out(dst, made, job.finish[1])
            store = pltpu.make_async_copy(made, out, self.sems.at[base - 1])
            store.start()
            stores.append(store)
        for store in stores:
            store.wait()

    @staticmethod
    def lay_out(src, dst, width):
        seqs, halves, cores, rows, cols = src.shape

        @pl.loop(0, seqs)
        def _(i):
            if not width:
                for q in range(TP):
                    at = pl.multiple_of((q * seqs + i) * rows, rows)
                    dst[pl.ds(at, rows)] = src[i, q // 2, q % 2].astype(F32)
            else:
                at = pl.multiple_of(i * rows, rows)
                for n in range(cols // width):
                    span = slice(n * width, (n + 1) * width)
                    parts = [src[i, q // 2, q % 2, :, span].astype(F32) for q in range(TP)]
                    block = slice(n * width * TP, (n + 1) * width * TP)
                    dst[pl.ds(at, rows), block] = jnp.concatenate(parts, axis=1)


HBM_SPEC = pl.BlockSpec(memory_space=pltpu.HBM)


class Loaded:
    def __init__(self, src, dst, sem):
        self.copy, self.ref, self.waited = pltpu.make_async_copy(src, dst, sem), dst, False
        self.copy.start()

    def get(self):
        if not self.waited:
            self.copy.wait()
            self.waited = True
        return self.ref


def call_with_jobs(kernel, number, planes, jobs, operands, outs, scratch, name, cost):
    n_in, n_out, n_job = len(operands), len(outs), len(jobs)
    n_sems = max(Shipper.count(jobs, planes), 1)
    plain = [job._replace(src=jax.ShapeDtypeStruct(job.src.shape, job.src.dtype)) for job in jobs]
    job_scratch = Shipper.scratch(jobs)

    def body(*refs):
        ins, refs = refs[:n_in], refs[n_in:]
        srcs, refs = refs[:n_job], refs[n_job:]
        results, refs = refs[:n_out], refs[n_out:]
        dsts, refs = refs[:n_job], refs[n_job:]
        sems, in_sems, refs = refs[0], refs[1], list(refs[2:])
        loaded = [Loaded(src, refs.pop(0), in_sems.at[i]) for i, src in enumerate(ins)]
        own = [refs.pop(0) for _ in job_scratch]
        shipper = Shipper(plain, planes, srcs, dsts, own, sems)
        kernel(shipper, loaded, list(results), refs)

    results = [result_of(job) for job in jobs]
    got = pl.pallas_call(
        body,
        out_shape=tuple(outs) + tuple(jax.ShapeDtypeStruct(*r) for r in results),
        in_specs=[HBM_SPEC] * (n_in + n_job),
        out_specs=(HBM_SPEC,) * (n_out + n_job),
        scratch_shapes=[
            pltpu.SemaphoreType.DMA((n_sems,)),
            pltpu.SemaphoreType.DMA((max(n_in, 1),)),
        ]
        + [pltpu.VMEM(v.shape, v.dtype) for v in operands]
        + job_scratch
        + scratch,
        compiler_params=pltpu.CompilerParams(
            collective_id=number, has_side_effects=True, vmem_limit_bytes=VMEM_LIMIT
        ),
        cost_estimate=pl.CostEstimate(flops=cost, bytes_accessed=8 * MB, transcendentals=0),
        name=name,
    )(*operands, *[job.src for job in jobs])
    return got[:n_out], list(got[n_out:])


def ship(number, planes, jobs):
    def kernel(shipper, ins, outs, scratch):
        shipper.greet(())
        shipper.start()
        shipper.finish()

    return call_with_jobs(kernel, number, planes, jobs, [], [], [], "ship", 0)[1]


def gather_norm(number, planes, x, gain, jobs):
    chunk = x.shape[1]

    def kernel(shipper, ins, outs, scratch):
        shipper.greet()
        shipper.start()
        x_ref, gain_ref = (v.get() for v in ins)
        g = Gatherer(outs[0], scratch[0], scratch[1], chunk, group_ids())
        for j in range(2):
            g.put(j, normed(x_ref[j].astype(F32), gain_ref[...]).astype(BF))
        for j in range(2):
            g.forward(j)
        g.finish()
        shipper.finish()

    outs = [jax.ShapeDtypeStruct((2 * TP * chunk, D), BF)]
    scratch = [pltpu.VMEM((2, chunk, D), BF), pltpu.SemaphoreType.DMA((7, 2))]
    got, moved = call_with_jobs(
        kernel, number, planes, jobs, [x, gain], outs, scratch, "gather_norm", 10**6
    )
    return got[0], moved


def stage_kernel(conf, shipper, ins, outs, scratch):
    chunk, flips, back, gather = conf
    pairs = [(ins.pop(0), ins.pop(0), flip) for flip in flips]
    resid_in = ins.pop(0)
    gain_in = ins.pop(0) if (back or gather == "norm") else None
    x_in = ins.pop(0) if back else None
    given_in = ins.pop(0) if gather == "given" else None
    y_out = outs.pop(0)
    gath_ref = outs.pop(0) if gather else None
    dgain_out = outs.pop(0) if back else None
    s_far, r_far, s_x, r_x, s_core, r_core, keep, own, y_ref, sems = scratch[:10]
    scratch = scratch[10:]
    g_stage, g_sems = (scratch.pop(0), scratch.pop(0)) if gather else (None, None)
    dgain_ref = scratch.pop(0) if back else None
    ids = group_ids()
    me, core, across, far = ids

    def partial(owner, store):
        r0 = pl.multiple_of(owner * chunk, chunk)
        r1 = pl.multiple_of((TP + owner) * chunk, chunk)

        @pl.loop(0, D // 256)
        def _(n):
            cols = pl.ds(pl.multiple_of(n * 256, 256), 256)
            total = None
            for a_ref, w_ref, flip in pairs:
                a = jnp.concatenate([a_ref[pl.ds(r0, chunk)], a_ref[pl.ds(r1, chunk)]], axis=0)
                term = mm_nt(a, w_ref[cols, :]) if flip else mm(a, w_ref[:, cols])
                total = term if total is None else total + term
            for j in range(2):
                store(j, cols, total[j * chunk : (j + 1) * chunk])

    def into(ref):
        def store(j, cols, value):
            ref[j, :, cols] = value.astype(ref.dtype)

        return store

    shipper.greet()
    g = Gatherer(gath_ref, g_stage, g_sems, chunk, ids) if gather else None
    if gather == "given":
        given_ref = given_in.get()
        for j in range(2):
            g.put(j, given_ref[j])
    pairs = [(a.get(), w.get(), flip) for a, w, flip in pairs]
    partial(far, into(s_far))
    c_far = send(s_far, r_far, sems.at[0], sems.at[1], core)
    c_far.start()
    partial(across, into(keep))
    c_far.wait_recv()
    c_x = []
    for j in range(2):
        s_x[j] = (keep[j] + r_far[j].astype(F32)).astype(BF)
        c_x.append(send(s_x.at[j], r_x.at[j], sems.at[2 + j], sems.at[4 + j], across))
        c_x[j].start()
    shipper.start()
    partial(core, into(s_core))
    c_core = send(s_core, r_core, sems.at[6], sems.at[7], core)
    c_core.start()
    partial(me, into(own))
    c_core.wait_recv()
    resid_ref = resid_in.get()
    x_ref = x_in.get() if back else None
    gains = gain_in.get()[...] if gain_in else None
    if gather == "given":
        for j in range(2):
            g.forward(j)
    stores = []

    def keep_out(src, dst, sem):
        copy = pltpu.make_async_copy(src, dst, sems.at[sem])
        copy.start()
        stores.append(copy)

    for j in range(2):
        c_x[j].wait_recv()
        total = own[j] + r_core[j].astype(F32) + r_x[j].astype(F32)
        if back:
            x = x_ref[j].astype(F32)
            r = lax.rsqrt(jnp.mean(x * x, axis=-1, keepdims=True) + EPS)
            scaled = total * gains
            inner = jnp.mean(scaled * x, axis=-1, keepdims=True)
            y = resid_ref[j].astype(F32) + r * scaled - x * (r * r * r * inner)
            dgain = jnp.sum(total * x * r, axis=0, keepdims=True)
            if j == 0:
                dgain_ref[...] = dgain
            else:
                dgain_ref[...] += dgain
        else:
            y = resid_ref[j].astype(F32) + total
        y_ref[j] = y.astype(y_ref.dtype)
        if gather == "norm":
            g.put(j, normed(y, gains).astype(BF))
        elif gather == "low":
            g.put(j, y.astype(BF))
        keep_out(y_ref.at[j], y_out.at[j], 8 + j)
    if back:
        keep_out(dgain_ref, dgain_out, 10)
    if gather in ("norm", "low"):
        for j in range(2):
            g.forward(j)
    if gather:
        g.finish()
    c_far.wait_send()
    c_core.wait_send()
    for j in range(2):
        c_x[j].wait_send()
    shipper.finish()
    for copy in stores:
        copy.wait()


def stage(
    number, planes, pairs, resid, *, back=None, gather=None, gain=None, given=None, dtype=F32, jobs=()
):
    chunk = resid.shape[1]
    operands, flips, cost = [], [], 0
    for a, w, flip in pairs:
        operands += [a, w]
        flips.append(flip)
        cost += 2 * a.shape[0] * a.shape[1] * D
    operands.append(resid)
    if back:
        operands += [back[1], back[0]]
    elif gather == "norm":
        operands.append(gain)
    if gather == "given":
        operands.append(given)
    outs = [jax.ShapeDtypeStruct((2, chunk, D), dtype)]
    if gather:
        outs.append(jax.ShapeDtypeStruct((2 * TP * chunk, D), BF))
    if back:
        outs.append(jax.ShapeDtypeStruct((1, D), F32))
    half = pltpu.VMEM((2, chunk, D), BF)
    full = pltpu.VMEM((2, chunk, D), F32)
    scratch = [half] * 6 + [full] * 2 + [
        pltpu.VMEM((2, chunk, D), dtype),
        pltpu.SemaphoreType.DMA((11,)),
    ]
    if gather:
        scratch += [half, pltpu.SemaphoreType.DMA((7, 2))]
    if back:
        scratch.append(pltpu.VMEM((1, D), F32))
    kernel = functools.partial(stage_kernel, (chunk, tuple(flips), bool(back), gather))
    return call_with_jobs(
        kernel, number, planes, list(jobs), operands, outs, scratch, "stage", cost
    )


def attn_fwd_kernel(conf, pos_ref, *refs):
    chunk, q_off, kv_off, keys, extra, bias, causal = conf
    refs = list(refs)
    q_ref, kv_ref, segq_ref, segk_ref = refs[:4]
    refs = refs[4:]
    bvec_ref = refs.pop(0) if bias else None
    mkv_ref = refs.pop(0) if extra else None
    att_ref, p_ref, qs, ks, vs, os = refs[:6]
    toep = refs[6] if bias else None
    h, b = pl.program_id(0), pl.program_id(1)
    length = keys

    @pl.when((h == 0) & (b == 0))
    def _():
        for i in range(HQ):
            qs[i] = q_ref[:, q_off + DH * i : q_off + DH * (i + 1)]
            ks[i, :keys] = kv_ref[:, kv_off + DH * i : kv_off + DH * (i + 1)]
            vs[i, :keys] = kv_ref[:, kv_off + QC + DH * i : kv_off + QC + DH * (i + 1)]
            if extra:
                ks[i, keys:] = mkv_ref[:, DH * i : DH * (i + 1)]
                vs[i, keys:] = mkv_ref[:, QC + DH * i : QC + DH * (i + 1)]

    if bias:

        @pl.when(b == 0)
        def _():
            row = jnp.broadcast_to(bvec_ref[h], (chunk, 2 * length))
            toep[...] = pltpu.roll(row, 0, 1, stride=1, stride_axis=0)

    rows = pl.ds(pl.multiple_of(b * 2 * chunk, 2 * chunk), 2 * chunk)
    s = mm_nt(qs[h, rows], ks[h])
    allowed = segq_ref[rows] == segk_ref[...]
    if bias:
        parts = []
        for u in range(2):
            off = pl.multiple_of(length - pos_ref[2 * b + u], 128)
            parts.append(toep[:, pl.ds(off, keys)])
        biased = s[:, :keys] + jnp.concatenate(parts, axis=0)
        s = jnp.concatenate([biased, s[:, keys:]], axis=1) if extra else biased
    if causal:
        place = lax.broadcasted_iota(jnp.int32, (chunk, 1), 0)
        places = jnp.concatenate([place + pos_ref[2 * b + u] for u in range(2)], axis=0)
        allowed = allowed & (lax.broadcasted_iota(jnp.int32, (1, keys), 1) <= places)
    s = jnp.where(allowed, s, MASKED)
    top = jnp.max(s, axis=-1, keepdims=True)
    e = jnp.exp(s - top)
    p = (e * (1.0 / jnp.sum(e, axis=-1, keepdims=True))).astype(BF)
    p_ref[0] = p
    os[h, rows] = mm(p, vs[h]).astype(BF)

    @pl.when((h == HQ - 1) & (b == pl.num_programs(1) - 1))
    def _():
        for i in range(HQ):
            att_ref[:, DH * i : DH * (i + 1)] = os[i]


def whole(shape):
    return pl.BlockSpec(shape, lambda h, b, pos: (0,) * len(shape))


def attn_fwd(pos, q, kv, segq, segk, bvec, mkv, causal, q_off, kv_off):
    rows, keys = q.shape[0], kv.shape[0]
    chunk = rows // 8
    extra = 0 if mkv is None else mkv.shape[0]
    total = keys + extra
    conf = (chunk, q_off, kv_off, keys, extra, bvec is not None, causal)
    operands = [q, kv, segq, segk]
    operands += [v for v in (bvec, mkv) if v is not None]
    scratch = [
        pltpu.VMEM((HQ, rows, DH), BF),
        pltpu.VMEM((HQ, total, DH), BF),
        pltpu.VMEM((HQ, total, DH), BF),
        pltpu.VMEM((HQ, rows, DH), BF),
    ]
    if bvec is not None:
        scratch.append(pltpu.VMEM((chunk, 2 * keys), F32))
    return pl.pallas_call(
        functools.partial(attn_fwd_kernel, conf),
        out_shape=(
            jax.ShapeDtypeStruct((rows, QC), BF),
            jax.ShapeDtypeStruct((HQ, rows, total), BF),
        ),
        grid_spec=pltpu.PrefetchScalarGridSpec(
            num_scalar_prefetch=1,
            grid=(HQ, rows // (2 * chunk)),
            in_specs=[whole(v.shape) for v in operands],
            out_specs=(
                whole((rows, QC)),
                pl.BlockSpec((1, 2 * chunk, total), lambda h, b, pos: (h, b, 0)),
            ),
            scratch_shapes=scratch,
        ),
        compiler_params=pltpu.CompilerParams(
            dimension_semantics=("arbitrary", "arbitrary"), vmem_limit_bytes=VMEM_LIMIT
        ),
        cost_estimate=pl.CostEstimate(
            flops=4 * HQ * rows * total * DH,
            bytes_accessed=HQ * rows * total * 2,
            transcendentals=HQ * rows * total,
        ),
        name="attn_fwd",
    )(pos, *operands)


def attn_bwd_kernel(conf, pos_ref, *refs):
    chunk, q_off, kv_off, keys, extra, bias = conf
    refs = list(refs)
    p_ref, q_ref, kv_ref, do_ref, att_ref = refs[:5]
    refs = refs[5:]
    mkv_ref = refs.pop(0) if extra else None
    joint = q_ref.shape[1] > QC
    dq_ref = refs.pop(0)
    dkv_ref = dq_ref if joint else refs.pop(0)
    to = QC if joint else 0
    dbvec_ref = refs.pop(0) if bias else None
    dmkv_ref = refs.pop(0) if extra else None
    qs, ks, vs, dos, rds, dqs, dks, dvs = refs[:8]
    diag = refs[8] if bias else None
    h, b = pl.program_id(0), pl.program_id(1)
    last = pl.num_programs(1) - 1
    length = keys

    @pl.when((h == 0) & (b == 0))
    def _():
        for i in range(HQ):
            qs[i] = q_ref[:, q_off + DH * i : q_off + DH * (i + 1)]
            ks[i, :keys] = kv_ref[:, kv_off + DH * i : kv_off + DH * (i + 1)]
            vs[i, :keys] = kv_ref[:, kv_off + QC + DH * i : kv_off + QC + DH * (i + 1)]
            if extra:
                ks[i, keys:] = mkv_ref[:, DH * i : DH * (i + 1)]
                vs[i, keys:] = mkv_ref[:, QC + DH * i : QC + DH * (i + 1)]
            grad = do_ref[:, DH * i : DH * (i + 1)]
            dos[i] = grad
            out = att_ref[:, DH * i : DH * (i + 1)]
            rds[i] = jnp.sum(grad.astype(F32) * out.astype(F32), axis=-1, keepdims=True)

    @pl.when(b == 0)
    def _():
        dks[h] = jnp.zeros(dks.shape[1:], F32)
        dvs[h] = jnp.zeros(dvs.shape[1:], F32)
        if bias:
            diag[...] = jnp.zeros_like(diag)

    rows = pl.ds(pl.multiple_of(b * 2 * chunk, 2 * chunk), 2 * chunk)
    q, grad, p = qs[h, rows], dos[h, rows], p_ref[0]
    dp = mm_nt(grad, vs[h])
    ds = (p.astype(F32) * (dp - rds[h, rows])).astype(BF)
    dqs[h, rows] = mm(ds, ks[h]).astype(BF)
    dks[h] += mm_tn(ds, q)
    dvs[h] += mm_tn(p, grad)
    if bias:
        for u in range(2):
            off = pl.multiple_of(length - pos_ref[2 * b + u], 128)
            diag[:, pl.ds(off, keys)] += ds[u * chunk : (u + 1) * chunk, :keys].astype(F32)

        @pl.when(b == last)
        def _():
            x = diag[...]
            size = chunk
            while size > 1:
                size //= 2
                x = x[:size] + pltpu.roll(x[size:], 2 * length - size, 1)
            dbvec_ref[h] = x

    @pl.when((h == HQ - 1) & (b == last))
    def _():
        for i in range(HQ):
            dq_ref[:, DH * i : DH * (i + 1)] = dqs[i]
            at = to + DH * i
            dkv_ref[:, at : at + DH] = dks[i, :keys].astype(dkv_ref.dtype)
            dkv_ref[:, at + QC : at + QC + DH] = dvs[i, :keys].astype(dkv_ref.dtype)
            if extra:
                dmkv_ref[:, DH * i : DH * (i + 1)] = dks[i, keys:].astype(BF)
                dmkv_ref[:, QC + DH * i : QC + DH * (i + 1)] = dvs[i, keys:].astype(BF)


def attn_bwd(pos, p, q, kv, grad, att, mkv, bias, q_off, kv_off, dtype):
    rows, keys = q.shape[0], kv.shape[0]
    chunk = rows // 8
    extra = 0 if mkv is None else mkv.shape[0]
    total = keys + extra
    conf = (chunk, q_off, kv_off, keys, extra, bias)
    operands = [q, kv, grad, att] + ([mkv] if extra else [])
    if q.shape[1] > QC:
        outs = [jax.ShapeDtypeStruct((rows, 3 * QC), BF)]
    else:
        outs = [jax.ShapeDtypeStruct((rows, QC), BF), jax.ShapeDtypeStruct((keys, 2 * QC), dtype)]
    if bias:
        outs.append(jax.ShapeDtypeStruct((HQ, 1, 2 * keys), F32))
    if extra:
        outs.append(jax.ShapeDtypeStruct((extra, 2 * QC), BF))
    scratch = [
        pltpu.VMEM((HQ, rows, DH), BF),
        pltpu.VMEM((HQ, total, DH), BF),
        pltpu.VMEM((HQ, total, DH), BF),
        pltpu.VMEM((HQ, rows, DH), BF),
        pltpu.VMEM((HQ, rows, 1), F32),
        pltpu.VMEM((HQ, rows, DH), BF),
        pltpu.VMEM((HQ, total, DH), F32),
        pltpu.VMEM((HQ, total, DH), F32),
    ]
    if bias:
        scratch.append(pltpu.VMEM((chunk, 2 * keys), F32))
    return pl.pallas_call(
        functools.partial(attn_bwd_kernel, conf),
        out_shape=tuple(outs),
        grid_spec=pltpu.PrefetchScalarGridSpec(
            num_scalar_prefetch=1,
            grid=(HQ, rows // (2 * chunk)),
            in_specs=[pl.BlockSpec((1, 2 * chunk, total), lambda h, b, pos: (h, b, 0))]
            + [whole(v.shape) for v in operands],
            out_specs=tuple(whole(v.shape) for v in outs),
            scratch_shapes=scratch,
        ),
        compiler_params=pltpu.CompilerParams(
            dimension_semantics=("arbitrary", "arbitrary"), vmem_limit_bytes=VMEM_LIMIT
        ),
        cost_estimate=pl.CostEstimate(
            flops=8 * HQ * rows * total * DH,
            bytes_accessed=HQ * rows * total * 2,
            transcendentals=0,
        ),
        name="attn_bwd",
    )(pos, p, *operands)


ALL = ("seq", "part", "tp", "fsdp")
CTX = ("seq", "part", "tp")


def per_device(
    parts,
    planes,
    enc_input,
    dec_input,
    segments,
    prefix_rows,
    buckets,
    memory,
    enc_gain,
    enc_qkv,
    enc_rel,
    enc_proj,
    enc_ffnorm,
    enc_ffin,
    enc_ffout,
    dec_gain,
    dec_qkv,
    dec_rel,
    dec_proj,
    cross_gain,
    cross_query,
    cross_kv,
    cross_proj,
    dec_ffnorm,
    dec_ffin,
    dec_ffout,
    enc_cotan,
    dec_cotan,
):
    seq, part, tp, plane = (lax.axis_index(name) for name in ALL)
    chunk = enc_input.shape[1]
    length = buckets.shape[0] // 2
    docs, prefix = prefix_rows.shape[1:]

    first = seq == 0
    split = planes * 2

    def joined(x, came):
        mine = lax.dynamic_index_in_dim(x, seq, 0, keepdims=False)
        came = came.astype(x.dtype)
        return jnp.stack([jnp.where(first, mine, came), jnp.where(first, came, mine)])

    def cols(w, start, width=QC):
        return lax.dynamic_slice_in_dim(w, start + width * tp, width, 1)

    def halved(w):
        rows = w.shape[0] // 2
        return lax.dynamic_slice_in_dim(w, rows * seq, rows, 0)

    def qkv_part(w):
        w = halved(w)
        return jnp.concatenate([cols(w, D * i) for i in range(w.shape[1] // D)], axis=1)

    hidden = enc_ffout.shape[0] // TP

    def ffin_part(w):
        w = halved(w)
        return jnp.concatenate(
            [cols(w, hidden * TP * i, hidden) for i in range(planes)], axis=1
        )

    def ffout_part(w):
        rows = hidden // 2
        return lax.dynamic_slice_in_dim(w, hidden * tp + rows * seq, rows, 0)

    def over_planes(w):
        return gather_job("fsdp", w, planes)

    def over_seq(w):
        return gather_job("seq", w, 2, 1)

    def matrix(w):
        return w.reshape(-1, w.shape[-1])

    gains = (enc_gain, enc_ffnorm, dec_gain, cross_gain, dec_ffnorm)
    small = jnp.concatenate(list(gains) + [enc_rel.reshape(-1), dec_rel.reshape(-1)])
    small_size = small.shape[0]
    small = jnp.pad(small.astype(F32), (0, -small_size % 128)).reshape(-1, 128)
    segments = segments.reshape(2, 1, chunk)
    first_jobs = [
        swap_job(enc_input),
        gather_job("fsdp", small, planes),
        over_planes(qkv_part(enc_qkv)),
        over_planes(qkv_part(memory)),
        swap_job(dec_input),
    ]
    if parts == 1:
        first_jobs.append(block_job(segments))
    xe, small, w_eqkv, table, xd, *segs = ship(0, planes, first_jobs)
    xe, xd = joined(enc_input, xe), joined(dec_input, xd)
    if parts == 1:
        seg = segs[0].reshape(-1)
    else:
        segs = lax.all_gather(segments.reshape(2, chunk), CTX, axis=1, tiled=True)
        seg = lax.dynamic_index_in_dim(segs, seq, 0, keepdims=False)
    small = small.reshape(planes, -1)[:, :small_size]
    per = enc_gain.shape[0]
    gain_rows = [small[:, per * i : per * (i + 1)].reshape(1, D) for i in range(5)]
    g_enc, g_effn, g_dec, g_cross, g_dffn = gain_rows
    per_rel = enc_rel.size
    rels = [
        small[:, 5 * per + per_rel * i : 5 * per + per_rel * (i + 1)].reshape(BUCKETS, HEADS)
        for i in range(2)
    ]
    onehot = (buckets[:, None] == jnp.arange(BUCKETS, dtype=jnp.int32)[None, :]).astype(BF)

    def bias_vector(rel):
        own = lax.dynamic_slice_in_dim(rel, HQ * tp, HQ, 1).astype(BF)
        return lax.dot_general(
            own, onehot, (((0,), (1,)), ((), ())), preferred_element_type=F32
        ).reshape(HQ, 1, 2 * length)

    turned = planes == TP

    def proj_jobs(w):
        return [turn_job(w)] if turned else []

    def proj_of(got, w):
        if turned:
            return got.pop()
        full = lax.all_gather(w, "fsdp", axis=0, tiled=True)
        return lax.dynamic_slice_in_dim(full, QC * tp, QC, 0)

    en, (w_eqkv, table, w_dqkv, *got) = gather_norm(
        1,
        planes,
        xe,
        g_enc,
        [over_seq(w_eqkv), over_seq(table), over_planes(qkv_part(dec_qkv))] + proj_jobs(enc_proj),
    )
    w_eproj = proj_of(got, enc_proj)
    w_eqkv, table = matrix(w_eqkv), matrix(table)

    index = jnp.arange(2 * TP, dtype=jnp.int32)
    pos = ((index // TP) * TP * parts + TP * part + index % TP) * chunk
    segq = lax.dynamic_index_in_dim(seg.reshape(2, parts, TP * chunk), part, 1, keepdims=False)
    segq = segq.reshape(-1, 1)
    segk = seg.reshape(1, length)
    ids = lax.dynamic_index_in_dim(prefix_rows, seq, 0, keepdims=False).reshape(-1)
    extra = -(-(docs * prefix) // 256) * 256
    ids = jnp.concatenate([ids, jnp.full((extra - docs * prefix,), -1, jnp.int32)])
    mem_doc = np.full((extra,), -1, np.int32)
    mem_doc[: docs * prefix] = np.arange(docs * prefix) // prefix
    segk_mem = jnp.concatenate([segk, jnp.asarray(mem_doc)[None]], axis=1)
    pick = (ids[:, None] == jnp.arange(table.shape[0], dtype=jnp.int32)[None, :]).astype(BF)
    mkv = mm(pick, table).astype(BF)

    def spread(kv):
        if parts == 1:
            return kv
        got = lax.all_gather(kv, "part", axis=0)
        return got.reshape(parts, 2, TP * chunk, -1).transpose(1, 0, 2, 3).reshape(length, -1)

    def collect(dkv):
        if parts == 1:
            return dkv
        split = dkv.reshape(2, parts, TP * chunk, -1).transpose(1, 0, 2, 3)
        split = split.reshape(parts * 2 * TP * chunk, -1)
        return lax.psum_scatter(split, "part", scatter_dimension=0, tiled=True).astype(BF)

    def self_attn(rows, bvec, mem, segk_now, causal):
        if parts == 1:
            q, kv, kv_off = rows, rows, QC
        else:
            q, kv, kv_off = rows[:, :QC], spread(rows[:, QC:]), 0
        att, p = attn_fwd(pos, q, kv, segq, segk_now, bvec, mem, causal, 0, kv_off)

        def back(grad):
            got = attn_bwd(
                pos, p, q, kv, grad, att, mem, bvec is not None, 0, kv_off, BF if parts == 1 else F32
            )
            if parts == 1:
                return got[0], got[1:]
            return jnp.concatenate([got[0], collect(got[1])], axis=1), got[2:]

        return att, back

    def cross_attn(q, kv_rows):
        kv = spread(kv_rows)
        att, p = attn_fwd(pos, q, kv, segq, segk, None, None, False, 0, 0)

        def back(grad):
            got = attn_bwd(pos, p, q, kv, grad, att, None, False, 0, 0, BF if parts == 1 else F32)
            return got[0], collect(got[1])

        return att, back

    e_rows = mm(en, w_eqkv).astype(BF)
    e_att, e_back = self_attn(e_rows, bias_vector(rels[0]), mkv, segk_mem, False)
    dn, (w_dqkv, w_effin, *got) = gather_norm(
        2,
        planes,
        xd,
        g_dec,
        [over_seq(w_dqkv), over_planes(ffin_part(enc_ffin))] + proj_jobs(dec_proj),
    )
    w_dproj = proj_of(got, dec_proj)
    w_dqkv = matrix(w_dqkv)
    (e_mid, e_fn), (w_effin, w_effout, w_cq, w_ckv) = stage(
        3,
        planes,
        [(e_att, w_eproj, False)],
        xe,
        gather="norm",
        gain=g_effn,
        jobs=[
            over_seq(w_effin),
            over_planes(ffout_part(enc_ffout)),
            over_planes(qkv_part(cross_query)),
            over_planes(qkv_part(cross_kv)),
        ],
    )
    w_effin = matrix(w_effin)
    e_pre = mm(e_fn, w_effin)
    e_act = gelu(e_pre).astype(BF)
    d_rows = mm(dn, w_dqkv).astype(BF)
    d_att, d_back = self_attn(d_rows, bias_vector(rels[1]), None, segk, True)
    (d_mid, c_n), (w_effout, w_cq, w_ckv, w_dffin, *got) = stage(
        4,
        planes,
        [(d_att, w_dproj, False)],
        xd,
        gather="norm",
        gain=g_cross,
        jobs=[
            over_seq(w_effout),
            over_seq(w_cq),
            over_seq(w_ckv),
            over_planes(ffin_part(dec_ffin)),
        ]
        + proj_jobs(cross_proj),
    )
    w_cproj = proj_of(got, cross_proj)
    w_effout, w_cq, w_ckv = matrix(w_effout), matrix(w_cq), matrix(w_ckv)
    (e_low, e_gath), (w_dffin, w_dffout, xdc) = stage(
        5,
        planes,
        [(e_act, w_effout, False)],
        e_mid,
        gather="low",
        dtype=BF,
        jobs=[over_seq(w_dffin), over_planes(ffout_part(dec_ffout)), swap_job(dec_cotan)],
    )
    xdc = joined(dec_cotan, xdc)
    w_dffin = matrix(w_dffin)
    c_q = mm(c_n, w_cq).astype(BF)
    c_kv = mm(e_gath, w_ckv).astype(BF)
    c_att, c_back = cross_attn(c_q, c_kv)
    (d_cross, d_fn), (w_dffout, xec, came) = stage(
        6,
        planes,
        [(c_att, w_cproj, False)],
        d_mid,
        gather="norm",
        gain=g_dffn,
        jobs=[over_seq(w_dffout), swap_job(enc_cotan), swap_job(e_low)],
    )
    xec = joined(enc_cotan, xec)
    enc_output = joined(e_low, came)
    w_dffout = matrix(w_dffout)
    d_pre = mm(d_fn, w_dffin)
    d_act = gelu(d_pre).astype(BF)
    (d_low, up_g), _ = stage(
        7, planes, [(d_act, w_dffout, False)], d_cross, gather="given", given=xdc, dtype=BF
    )

    def pieces(g):
        if parts > 1:
            g = lax.psum(g, "part")
        return g.reshape(planes, 2, g.shape[0] // split, g.shape[1])

    def proj_pieces(g):
        return pieces(g.reshape(2 * QC, D // 2))

    def step1(gs):
        return [swap_job(g, 1, True) for g in gs]

    def step2(gs):
        return [deal_job("fsdp", g) for g in gs]

    def step3(gs):
        return [gather_job("across", g) for g in gs]

    def step4(gs):
        return [gather_job("seq", g) for g in gs]

    def step5(gs, widths):
        return [last_job(g, width) for g, width in zip(gs, widths)]

    ff_widths, qkv_widths, proj_widths = [hidden, 0], [QC, QC], [0]

    def take(got, n):
        out = got[:n]
        del got[:n]
        return out

    def ff_grads(up_rows, fn, act, pre, w_out):
        d_out = mm_tn(act, up_rows).astype(BF)
        pre_grad = gelu_back(pre, mm_nt(up_rows, w_out)).astype(BF)
        d_in = mm_tn(fn, pre_grad).astype(BF)
        return pre_grad, [pieces(d_in), pieces(d_out)]

    pre_grad, g_dff = ff_grads(up_g, d_fn, d_act, d_pre, w_dffout)
    (up, up_g, dg_dffn), got = stage(
        8,
        planes,
        [(pre_grad, w_dffin, True)],
        xdc,
        back=(d_cross, g_dffn),
        gather="low",
        jobs=step1(g_dff) + [swap_job(d_low)],
    )
    dec_output = joined(d_low, got.pop())
    g_dff = got
    c_dq, c_dkv = c_back(mm_nt(up_g, w_cproj).astype(BF))
    g_c = [pieces(mm_tn(c_n, c_dq).astype(BF)), pieces(mm_tn(e_gath, c_dkv).astype(BF))]
    if turned:
        g_c.append(proj_pieces(mm_tn(c_att, up_g).astype(BF)))
    else:
        g_cproj = mm_tn(c_att, up_g).astype(BF)
    (up, up_g, dg_cross), got = stage(
        9,
        planes,
        [(c_dq, w_cq, True)],
        up,
        back=(d_mid, g_cross),
        gather="low",
        jobs=step1(g_c) + step2(g_dff),
    )
    g_c = take(got, len(g_c))
    g_dff = got
    (e_up, e_up_g), got = stage(
        10,
        planes,
        [(c_dkv, w_ckv, True)],
        xec,
        gather="low",
        jobs=step2(g_c) + step3(g_dff),
    )
    g_c = take(got, len(g_c))
    g_dff = got
    d_rows_grad, (d_dbv,) = d_back(mm_nt(up_g, w_dproj).astype(BF))
    g_dqkv = mm_tn(dn, d_rows_grad).astype(BF)
    g_d = [pieces(g_dqkv)]
    if turned:
        g_d.append(proj_pieces(mm_tn(d_att, up_g).astype(BF)))
        turn = [turn_job(g_c.pop())]
    else:
        g_dproj = mm_tn(d_att, up_g).astype(BF)
        turn = []
    (d_in, dg_dec), got = stage(
        11,
        planes,
        [(d_rows_grad, w_dqkv, True)],
        up,
        back=(xd, g_dec),
        jobs=step1(g_d) + step4(g_dff) + step3(g_c) + turn,
    )
    d_in_low = d_in.astype(BF)
    g_d = take(got, len(g_d))
    g_dff, g_c = take(got, 2), take(got, 2)
    g_cp = got
    pre_grad, g_eff = ff_grads(e_up_g, e_fn, e_act, e_pre, w_effout)
    (e_up, e_up_g, dg_effn), got = stage(
        12,
        planes,
        [(pre_grad, w_effin, True)],
        e_up,
        back=(e_mid, g_effn),
        gather="low",
        jobs=step1(g_eff)
        + step5(g_dff, ff_widths)
        + step4(g_c)
        + step3(g_cp)
        + step2(g_d)
        + [swap_job(d_in_low)],
    )
    dec_ingrad = joined(d_in, got.pop())
    g_eff = take(got, 2)
    o_dff, g_c, g_cp = take(got, 2), take(got, 2), take(got, len(g_cp))
    g_d = got
    e_rows_grad, (e_dbv, d_mkv) = e_back(mm_nt(e_up_g, w_eproj).astype(BF))
    if turned:
        g_ep = [proj_pieces(mm_tn(e_att, e_up_g).astype(BF))]
        turn = [turn_job(g_d.pop())]
    else:
        g_eproj = mm_tn(e_att, e_up_g).astype(BF)
        g_ep, turn = [], []
    (e_in, dg_enc), got = stage(
        13,
        planes,
        [(e_rows_grad, w_eqkv, True)],
        e_up,
        back=(xe, g_enc),
        jobs=step2(g_eff) + step5(g_c, qkv_widths) + step4(g_cp) + step3(g_d) + turn + step1(g_ep),
    )
    g_eff = take(got, 2)
    o_c, g_cp, g_d, g_dp = take(got, 2), take(got, len(g_cp)), take(got, 1), take(got, len(turn))
    g_ep = got
    g_eqkv = mm_tn(en, e_rows_grad).astype(BF)
    g_e = [pieces(g_eqkv), pieces(mm_tn(pick, d_mkv).astype(BF))]
    def rel_grad(dbv):
        own = lax.dot_general(
            onehot.astype(F32),
            dbv.reshape(HQ, -1),
            (((0,), (1,)), ((), ())),
            precision=lax.Precision.HIGHEST,
            preferred_element_type=F32,
        )
        return lax.dynamic_update_slice_in_dim(jnp.zeros((BUCKETS, HEADS), F32), own, HQ * tp, 1)

    tiny = [dg_enc, dg_effn, dg_dec, dg_cross, dg_dffn]
    tiny = jnp.concatenate([v.reshape(planes, -1) for v in tiny] + [
        rel_grad(v).reshape(planes, -1) for v in (e_dbv, d_dbv)
    ], axis=1)
    tiny = tiny.reshape(-1, 128)
    if parts > 1:
        tiny = lax.psum(tiny, "part")
    got = ship(
        14,
        planes,
        step1(g_e)
        + step3(g_eff)
        + step5(g_cp, proj_widths)
        + step4(g_d)
        + step3(g_dp)
        + step2(g_ep)
        + [total_job("fsdp", tiny, planes), swap_job(e_in.astype(BF))],
    )
    enc_ingrad = joined(e_in, got.pop())
    tiny = got.pop()
    g_e = take(got, 2)
    g_eff, o_cp, g_d = take(got, 2), take(got, len(g_cp)), take(got, 1)
    g_dp = take(got, len(g_dp))
    g_ep = got
    got = ship(
        15,
        planes,
        step2(g_e)
        + step4(g_eff)
        + step5(g_d, qkv_widths)
        + step4(g_dp)
        + [turn_job(g) for g in g_ep]
        + [total_job("seq", tiny)],
    )
    tiny = got.pop()
    g_e = take(got, 2)
    g_eff, o_d, g_dp, g_ep = take(got, 2), take(got, 1), take(got, len(g_dp)), got
    got = ship(
        16,
        planes,
        step3(g_e + g_ep) + step5(g_eff, ff_widths) + step5(g_dp, proj_widths) + [total_job("across", tiny)],
    )
    tiny = got.pop()
    g_e = take(got, 2 + len(g_ep))
    o_eff, o_dp = take(got, 2), got
    got = ship(17, planes, step4(g_e) + [total_job("core", tiny)])
    tiny = got.pop()
    got = ship(18, planes, step5(got, qkv_widths + proj_widths))
    o_e, o_ep = take(got, 2), got

    def proj_rows(got, g):
        if turned:
            return got[0].reshape(-1, D)
        full = lax.dynamic_update_slice_in_dim(jnp.zeros((D, D), BF), g, QC * tp, 0)
        full = lax.psum_scatter(full, "fsdp", scatter_dimension=0, tiled=True)
        return lax.psum(full.astype(F32), CTX)

    o_eproj = proj_rows(o_ep, None if turned else g_eproj)
    o_dproj = proj_rows(o_dp, None if turned else g_dproj)
    o_cproj = proj_rows(o_cp, None if turned else g_cproj)
    o_dffin, o_dffout = o_dff
    o_effin, o_effout = o_eff
    o_cq, o_ckv = o_c
    (o_dqkv,), (o_eqkv, o_table) = o_d, o_e
    tiny = lax.dynamic_index_in_dim(tiny.reshape(planes, -1), plane, 0, keepdims=False)
    o_gains = [tiny[per * i : per * (i + 1)] for i in range(5)]
    o_rels = [
        tiny[5 * per + per_rel * i : 5 * per + per_rel * (i + 1)].reshape(-1, HEADS)
        for i in range(2)
    ]
    return (
        enc_output,
        dec_output,
        enc_ingrad,
        dec_ingrad,
        o_table,
        o_gains[0],
        o_eqkv,
        o_rels[0],
        o_eproj,
        o_gains[1],
        o_effin,
        o_effout,
        o_gains[2],
        o_dqkv,
        o_rels[1],
        o_dproj,
        o_gains[3],
        o_cq,
        o_ckv,
        o_cproj,
        o_gains[4],
        o_dffin,
        o_dffout,
    )


def solution(mesh):
    ctx, planes = mesh.shape["ctx"], mesh.shape["fsdp"]
    parts = ctx // (2 * TP)
    inner = Mesh(np.asarray(mesh.devices).reshape(2, parts, TP, planes), ALL)
    rows3 = P("fsdp", CTX, None)
    mat, vec = P("fsdp", None), P("fsdp")
    args = (
        (rows3, rows3, P("fsdp", CTX), P("fsdp", None, None), P(), mat)
        + (vec, mat, mat, mat, vec, mat, mat)
        + (vec, mat, mat, mat)
        + (vec, mat, mat, mat)
        + (vec, mat, mat)
        + (rows3, rows3)
    )
    outs = (
        (rows3, rows3, rows3, rows3, mat)
        + (vec, mat, mat, mat, vec, mat, mat)
        + (vec, mat, mat, mat)
        + (vec, mat, mat, mat)
        + (vec, mat, mat)
    )
    return jax.shard_map(
        functools.partial(per_device, parts, planes),
        mesh=inner,
        in_specs=args,
        out_specs=outs,
        check_vma=False,
    )
```

```python
import collections
import functools

import jax
import jax.numpy as jnp
import numpy as np
from jax import lax
from jax.experimental import pallas as pl
from jax.experimental.pallas import tpu as pltpu
from jax.sharding import Mesh
from jax.sharding import PartitionSpec as P

D = 768
HEADS = 12
DH = 64
BUCKETS = 32
EPS = 1e-06
MASKED = -1e30
TP = 4
HQ = HEADS // TP
QC = HQ * DH
BF = jnp.bfloat16
F32 = jnp.float32
MESH_ID = pl.DeviceIdType.MESH
MB = 1024 * 1024
VMEM_LIMIT = 60 * MB
SHARE = (0.25, 0.34, 0.75)


def mm(a, b):
    return jnp.dot(a, b, preferred_element_type=F32)


def mm_tn(a, b):
    return lax.dot_general(a, b, (((0,), (0,)), ((), ())), preferred_element_type=F32)


def mm_nt(a, b):
    return lax.dot_general(a, b, (((1,), (1,)), ((), ())), preferred_element_type=F32)


def gelu(v):
    return jax.nn.gelu(v, approximate=True)


def gelu_back(pre, grad):
    return jax.vjp(gelu, pre)[1](grad)[0]


def group_ids():
    me = lax.axis_index("tp")
    core = me + 1 - 2 * lax.rem(me, 2)
    across = lax.rem(me + 2, TP)
    far = lax.rem(core + 2, TP)
    return me, core, across, far


def send(src, dst, send_sem, recv_sem, peer):
    return pltpu.make_async_remote_copy(
        src_ref=src,
        dst_ref=dst,
        send_sem=send_sem,
        recv_sem=recv_sem,
        device_id={"tp": peer},
        device_id_type=MESH_ID,
    )


def normed(values, gains):
    return values * lax.rsqrt(jnp.mean(values * values, axis=-1, keepdims=True) + EPS) * gains


class Gatherer:
    def __init__(self, buf, stage, sems, chunk, ids):
        self.buf, self.stage, self.sems, self.chunk, self.ids = buf, stage, sems, chunk, ids
        self.sends, self.own = [], []

    def rows(self, j, owner):
        return self.buf.at[pl.ds(pl.multiple_of((TP * j + owner) * self.chunk, self.chunk), self.chunk)]

    def put(self, j, value):
        me, core, across, far = self.ids
        mine = self.stage.at[j]
        mine[...] = value
        x_copy = send(mine, self.rows(j, me), self.sems.at[0, j], self.sems.at[1, j], across)
        x_copy.start()
        c_copy = send(mine, self.rows(j, me), self.sems.at[2, j], self.sems.at[3, j], core)
        c_copy.start()
        self.sends += [x_copy, c_copy]
        own = pltpu.make_async_copy(mine, self.rows(j, me), self.sems.at[6, j])
        own.start()
        self.own.append(own)

    def forward(self, j):
        me, core, across, far = self.ids
        theirs = self.rows(j, across)
        send(theirs, theirs, self.sems.at[0, j], self.sems.at[1, j], across).wait_recv()
        f_copy = send(theirs, theirs, self.sems.at[4, j], self.sems.at[5, j], core)
        f_copy.start()
        self.sends.append(f_copy)

    def finish(self):
        me, core, across, far = self.ids
        for j in range(2):
            a = self.rows(j, core)
            send(a, a, self.sems.at[2, j], self.sems.at[3, j], core).wait_recv()
            b = self.rows(j, far)
            send(b, b, self.sems.at[4, j], self.sems.at[5, j], core).wait_recv()
        for copy in self.sends:
            copy.wait_send()
        for copy in self.own:
            copy.wait()


Job = collections.namedtuple("Job", ["axis", "src_axis", "dst_axis", "local", "src", "shape", "finish"])


def gather_job(axis, src, size=2, at=0):
    shape = src.shape[:at] + (size,) + src.shape[at:]
    return Job(axis, None, at, True, src, shape, None)


def total_job(axis, src, size=2):
    return gather_job(axis, src, size)._replace(finish="sum")


def deal_job(axis, src):
    return Job(axis, 0, 0, True, src, src.shape, "sum")


def swap_job(src, at=0, add=False):
    shape = src.shape[:at] + src.shape[at + 1 :]
    return Job("seq", at, None, add, src, shape, "add" if add else None)


def turn_job(src):
    return Job("turn", None, None, True, src, src.shape, None)


def block_job(src):
    return Job("ctx", 0, 0, True, src, (2 * TP,) + src.shape[1:], None)


def last_job(src, width):
    return gather_job("core", src, 2, 2)._replace(finish=("layout", width))


def result_of(job):
    if job.finish == "sum":
        return job.shape[1:], job.src.dtype
    if isinstance(job.finish, tuple):
        seqs, halves, cores, rows, cols = job.shape
        if job.finish[1]:
            return (seqs * rows, halves * cores * cols), F32
        return (seqs * halves * cores * rows, cols), F32
    return job.shape, job.src.dtype


def entry(ref, axis, index):
    return ref if axis is None else ref.at[(slice(None),) * axis + (index,)]


class Shipper:
    def __init__(self, jobs, planes, srcs, outs, scratch, sems):
        self.jobs, self.planes, self.srcs, self.outs, self.sems = jobs, planes, srcs, outs, sems
        self.tp, self.seq, self.plane = (lax.axis_index(n) for n in ("tp", "seq", "fsdp"))
        self.dsts, self.bounce, self.made = [], [], []
        for job, out in zip(jobs, outs):
            if job.finish:
                self.dsts.append(scratch.pop(0))
                self.bounce.append(scratch.pop(0) if job.finish == "add" else None)
                self.made.append(scratch.pop(0) if job.finish != "add" else None)
            else:
                self.dsts.append(out)
                self.bounce.append(scratch.pop(0) if job.local else None)
                self.made.append(None)

    @staticmethod
    def scratch(jobs):
        shapes = []
        for job in jobs:
            dtype = job.src.dtype
            if job.finish:
                shapes.append(pltpu.VMEM(job.shape, dtype))
                if job.finish == "add":
                    shapes.append(pltpu.VMEM(job.shape, dtype))
                else:
                    shapes.append(pltpu.VMEM(*result_of(job)))
            elif job.local:
                drop = job.dst_axis
                own = job.shape if drop is None else job.shape[:drop] + job.shape[drop + 1 :]
                shapes.append(pltpu.VMEM(own, dtype))
        return shapes

    @staticmethod
    def count(jobs, planes):
        return sum(2 * Shipper.n_peers(job, planes) + 2 for job in jobs)

    @staticmethod
    def n_peers(job, planes):
        return {"fsdp": planes - 1, "ctx": 2 * TP - 1}.get(job.axis, 1)

    def coord(self, axis):
        half = self.tp // 2
        return {
            "fsdp": self.plane,
            "seq": self.seq,
            "across": half,
            "core": self.tp - 2 * half,
            "ctx": TP * self.seq + self.tp,
            "turn": None,
        }[axis]

    def peers(self, axis):
        if axis == "fsdp":
            n, z = self.planes, self.plane
            for k in range(1, n):
                to = lax.rem(z + k, n)
                yield to, {"fsdp": to}, lax.rem(z + (n - k), n)
        elif axis == "ctx":
            for k in range(1, 2 * TP):
                to = lax.rem(self.seq + k // TP, 2)
                to_tp = lax.rem(self.tp + k % TP, TP)
                from_seq = lax.rem(self.seq + (2 - k // TP), 2)
                from_tp = lax.rem(self.tp + (TP - k % TP), TP)
                yield to, {"seq": to, "tp": to_tp}, TP * from_seq + from_tp
        elif axis == "seq":
            yield 1 - self.seq, {"seq": 1 - self.seq}, 1 - self.seq
        elif axis == "turn":
            yield None, {"fsdp": self.tp, "tp": self.plane}, None
        else:
            to = lax.rem(self.tp + 2, TP) if axis == "across" else self.tp + 1 - 2 * lax.rem(self.tp, 2)
            other = 1 - self.coord(axis)
            yield other, {"tp": to}, other

    def greet(self, always=("core", "across")):
        axes = list(always) + sorted({job.axis for job in self.jobs} - set(always))
        barrier = pltpu.get_barrier_semaphore()
        total = 0
        for axis in axes:
            for _, device, _ in self.peers(axis):
                if axis == "turn":
                    continue
                pl.semaphore_signal(barrier, inc=1, device_id=device, device_id_type=MESH_ID)
                total += 1
        if "turn" in axes:
            moves = self.plane != self.tp

            @pl.when(moves)
            def _():
                for _, device, _ in self.peers("turn"):
                    pl.semaphore_signal(barrier, inc=1, device_id=device, device_id_type=MESH_ID)
                pl.semaphore_wait(barrier, total + 1)

            @pl.when(jnp.logical_not(moves))
            def _():
                pl.semaphore_wait(barrier, total)
        else:
            pl.semaphore_wait(barrier, total)

    def each(self, act_remote, act_local):
        base = 0
        for n, (job, src, dst) in enumerate(zip(self.jobs, self.srcs, self.dsts)):
            mine = self.coord(job.axis)
            peers = list(self.peers(job.axis))
            for i, (to, device, source) in enumerate(peers):
                sems = (self.sems.at[base + 2 * i], self.sems.at[base + 2 * i + 1])

                def copy_into(slot, to=to, device=device, sems=sems, src=src, dst=dst, job=job):
                    return pltpu.make_async_remote_copy(
                        src_ref=entry(src, job.src_axis, to),
                        dst_ref=entry(dst, job.dst_axis, slot),
                        send_sem=sems[0],
                        recv_sem=sems[1],
                        device_id=device,
                        device_id_type=MESH_ID,
                    )

                def remote(copy_into=copy_into, source=source, mine=mine):
                    act_remote(copy_into, mine, source)

                if job.axis == "turn":
                    pl.when(self.plane != self.tp)(remote)
                else:
                    remote()
            if job.local:
                own = self.seq if job.axis == "ctx" else mine

                def local(n=n, job=job, src=src, dst=dst, own=own, mine=mine, sem=base + 2 * len(peers)):
                    here, there = entry(src, job.src_axis, own), entry(dst, job.dst_axis, mine)
                    bounce = self.bounce[n]
                    if bounce is None:
                        act_local([(here, there)], self.sems.at[sem])
                    elif job.finish == "add":
                        act_local([(here, bounce)], self.sems.at[sem])
                    else:
                        act_local([(here, bounce), (bounce, there)], self.sems.at[sem])

                if job.axis == "turn":
                    pl.when(self.plane == self.tp)(local)
                else:
                    local()
            base += 2 * len(peers) + 2
        return base

    def start(self):
        self.each(
            lambda copy_into, mine, source: copy_into(mine).start(),
            lambda legs, sem: pltpu.make_async_copy(*legs[0], sem).start(),
        )

    def finish(self):
        def turn_round(legs, sem):
            if len(legs) > 1:
                pltpu.make_async_copy(*legs[0], sem).wait()
                pltpu.make_async_copy(*legs[1], sem).start()

        def remote(copy_into, mine, source):
            copy_into(source).wait_recv()
            copy_into(mine).wait_send()

        self.each(lambda *_: None, turn_round)
        self.each(remote, lambda legs, sem: pltpu.make_async_copy(*legs[-1], sem).wait())
        stores, base = [], 0
        for job, dst, bounce, made, out in zip(
            self.jobs, self.dsts, self.bounce, self.made, self.outs
        ):
            base += 2 * self.n_peers(job, self.planes) + 2
            if not job.finish:
                continue
            if job.finish == "add":
                made = bounce

                @pl.loop(0, dst.shape[0])
                def _(i):
                    bounce[i] = (bounce[i].astype(F32) + dst[i].astype(F32)).astype(bounce.dtype)

            elif job.finish == "sum":
                total = dst[0].astype(F32)
                for i in range(1, dst.shape[0]):
                    total = total + dst[i].astype(F32)
                made[...] = total.astype(made.dtype)
            else:
                self.lay_out(dst, made, job.finish[1])
            store = pltpu.make_async_copy(made, out, self.sems.at[base - 1])
            store.start()
            stores.append(store)
        for store in stores:
            store.wait()

    @staticmethod
    def lay_out(src, dst, width):
        seqs, halves, cores, rows, cols = src.shape

        @pl.loop(0, seqs)
        def _(i):
            if not width:
                for q in range(TP):
                    at = pl.multiple_of((q * seqs + i) * rows, rows)
                    dst[pl.ds(at, rows)] = src[i, q // 2, q % 2].astype(F32)
            else:
                at = pl.multiple_of(i * rows, rows)
                for n in range(cols // width):
                    span = slice(n * width, (n + 1) * width)
                    parts = [src[i, q // 2, q % 2, :, span].astype(F32) for q in range(TP)]
                    block = slice(n * width * TP, (n + 1) * width * TP)
                    dst[pl.ds(at, rows), block] = jnp.concatenate(parts, axis=1)


HBM_SPEC = pl.BlockSpec(memory_space=pltpu.HBM)


class Loaded:
    def __init__(self, src, dst, sem):
        self.copy, self.ref, self.waited = pltpu.make_async_copy(src, dst, sem), dst, False
        self.copy.start()

    def get(self):
        if not self.waited:
            self.copy.wait()
            self.waited = True
        return self.ref


def call_with_jobs(kernel, number, planes, jobs, operands, outs, scratch, name, cost, filler=None):
    filler = filler or Idle()
    jobs = list(jobs)
    n_in, n_out, n_job = len(operands), len(outs), len(jobs)
    n_load, n_raw, n_fill = len(filler.loads), len(filler.raws), len(filler.outs)
    loads, raws = list(filler.loads), list(filler.raws)
    n_sems = max(Shipper.count(jobs, planes), 1)
    plain = [job._replace(src=jax.ShapeDtypeStruct(job.src.shape, job.src.dtype)) for job in jobs]
    job_scratch = Shipper.scratch(jobs)
    n_scratch = len(filler.scratch)

    def body(*refs):
        refs = list(refs)

        def take(n):
            out = refs[:n]
            del refs[:n]
            return out

        ins, srcs, fills, raw = take(n_in), take(n_job), take(n_load), take(n_raw)
        results, dsts, fill_outs = take(n_out), take(n_job), take(n_fill)
        sems, in_sems = take(2)
        loaded = [Loaded(src, refs.pop(0), in_sems.at[i]) for i, src in enumerate(ins)]
        fill_loads = [Loaded(src, refs.pop(0), in_sems.at[n_in + i]) for i, src in enumerate(fills)]
        shipper = Shipper(plain, planes, srcs, dsts, take(len(job_scratch)), sems)
        begin = functools.partial(filler.begin, fill_loads, raw, fill_outs, take(n_scratch))
        kernel(shipper, loaded, list(results), refs, Running(filler, begin))

    results = [result_of(job) for job in jobs]
    got = pl.pallas_call(
        body,
        out_shape=tuple(outs)
        + tuple(jax.ShapeDtypeStruct(*r) for r in results)
        + tuple(filler.outs),
        in_specs=[HBM_SPEC] * (n_in + n_job + n_load + n_raw),
        out_specs=(HBM_SPEC,) * (n_out + n_job + n_fill),
        scratch_shapes=[
            pltpu.SemaphoreType.DMA((n_sems,)),
            pltpu.SemaphoreType.DMA((max(n_in + n_load, 1),)),
        ]
        + [pltpu.VMEM(v.shape, v.dtype) for v in operands + loads]
        + job_scratch
        + list(filler.scratch)
        + scratch,
        compiler_params=pltpu.CompilerParams(
            collective_id=number, has_side_effects=True, vmem_limit_bytes=VMEM_LIMIT
        ),
        cost_estimate=pl.CostEstimate(flops=cost, bytes_accessed=8 * MB, transcendentals=0),
        name=name,
    )(*operands, *[job.src for job in jobs], *loads, *raws)
    return got[:n_out], list(got[n_out : n_out + n_job]), list(got[n_out + n_job :])


class Running:
    def __init__(self, filler, begin):
        self.begin, self.run, self.end = begin, filler.run, filler.end
        self.n_steps, self.done = filler.n_steps, 0

    def advance(self, share):
        high = int(round(share * self.n_steps))
        if high > self.done:
            self.run(self.done, high)
            self.done = high


def ship(number, planes, jobs):
    def kernel(shipper, ins, outs, scratch, filler):
        shipper.greet(())
        shipper.start()
        shipper.finish()

    return call_with_jobs(kernel, number, planes, jobs, [], [], [], "ship", 0)[1]


def gather_norm(number, planes, x, gain, jobs, filler=None):
    chunk = x.shape[1]

    def kernel(shipper, ins, outs, scratch, filler):
        shipper.greet()
        x_ref, gain_ref = (v.get() for v in ins)
        g = Gatherer(outs[0], scratch[0], scratch[1], chunk, group_ids())
        for j in range(2):
            g.put(j, normed(x_ref[j].astype(F32), gain_ref[...]).astype(BF))
        shipper.start()
        filler.begin()
        filler.advance(0.4)
        for j in range(2):
            g.forward(j)
        filler.advance(1.0)
        g.finish()
        filler.end()
        shipper.finish()

    outs = [jax.ShapeDtypeStruct((2 * TP * chunk, D), BF)]
    scratch = [pltpu.VMEM((2, chunk, D), BF), pltpu.SemaphoreType.DMA((7, 2))]
    got, moved, made = call_with_jobs(
        kernel, number, planes, jobs, [x, gain], outs, scratch, "gather_norm", 10**6, filler
    )
    return got[0], moved, made


def stage_kernel(conf, shipper, ins, outs, scratch, filler):
    chunk, flips, back, gather = conf
    pairs = [(ins.pop(0), ins.pop(0), flip) for flip in flips]
    resid_in = ins.pop(0)
    gain_in = ins.pop(0) if (back or gather == "norm") else None
    x_in = ins.pop(0) if back else None
    given_in = ins.pop(0) if gather == "given" else None
    y_out = outs.pop(0)
    gath_ref = outs.pop(0) if gather else None
    dgain_out = outs.pop(0) if back else None
    s_far, r_far, s_x, r_x, s_core, r_core, keep, own, y_ref, sems = scratch[:10]
    scratch = scratch[10:]
    g_stage, g_sems = (scratch.pop(0), scratch.pop(0)) if gather else (None, None)
    dgain_ref = scratch.pop(0) if back else None
    ids = group_ids()
    me, core, across, far = ids

    def partial(owner, store):
        r0 = pl.multiple_of(owner * chunk, chunk)
        r1 = pl.multiple_of((TP + owner) * chunk, chunk)

        @pl.loop(0, D // 256)
        def _(n):
            cols = pl.ds(pl.multiple_of(n * 256, 256), 256)
            total = None
            for a_ref, w_ref, flip in pairs:
                a = jnp.concatenate([a_ref[pl.ds(r0, chunk)], a_ref[pl.ds(r1, chunk)]], axis=0)
                term = mm_nt(a, w_ref[cols, :]) if flip else mm(a, w_ref[:, cols])
                total = term if total is None else total + term
            for j in range(2):
                store(j, cols, total[j * chunk : (j + 1) * chunk])

    def into(ref):
        def store(j, cols, value):
            ref[j, :, cols] = value.astype(ref.dtype)

        return store

    shipper.greet()
    shipper.start()
    g = Gatherer(gath_ref, g_stage, g_sems, chunk, ids) if gather else None
    if gather == "given":
        given_ref = given_in.get()
        for j in range(2):
            g.put(j, given_ref[j])
    pairs = [(a.get(), w.get(), flip) for a, w, flip in pairs]
    partial(far, into(s_far))
    c_far = send(s_far, r_far, sems.at[0], sems.at[1], core)
    c_far.start()
    partial(across, into(keep))
    c_far.wait_recv()
    c_x = []
    for j in range(2):
        s_x[j] = (keep[j] + r_far[j].astype(F32)).astype(BF)
        c_x.append(send(s_x.at[j], r_x.at[j], sems.at[2 + j], sems.at[4 + j], across))
        c_x[j].start()
    partial(core, into(s_core))
    c_core = send(s_core, r_core, sems.at[6], sems.at[7], core)
    c_core.start()
    partial(me, into(own))
    c_core.wait_recv()
    filler.begin()
    filler.advance(SHARE[0])
    resid_ref = resid_in.get()
    x_ref = x_in.get() if back else None
    gains = gain_in.get()[...] if gain_in else None
    if gather == "given":
        for j in range(2):
            g.forward(j)
    stores = []

    def keep_out(src, dst, sem):
        copy = pltpu.make_async_copy(src, dst, sems.at[sem])
        copy.start()
        stores.append(copy)

    for j in range(2):
        c_x[j].wait_recv()
        if j == 1:
            filler.advance(SHARE[1])
        total = own[j] + r_core[j].astype(F32) + r_x[j].astype(F32)
        if back:
            x = x_ref[j].astype(F32)
            r = lax.rsqrt(jnp.mean(x * x, axis=-1, keepdims=True) + EPS)
            scaled = total * gains
            inner = jnp.mean(scaled * x, axis=-1, keepdims=True)
            y = resid_ref[j].astype(F32) + r * scaled - x * (r * r * r * inner)
            dgain = jnp.sum(total * x * r, axis=0, keepdims=True)
            if j == 0:
                dgain_ref[...] = dgain
            else:
                dgain_ref[...] += dgain
        else:
            y = resid_ref[j].astype(F32) + total
        y_ref[j] = y.astype(y_ref.dtype)
        if gather == "norm":
            g.put(j, normed(y, gains).astype(BF))
        elif gather == "low":
            g.put(j, y.astype(BF))
        keep_out(y_ref.at[j], y_out.at[j], 8 + j)
    if back:
        keep_out(dgain_ref, dgain_out, 10)
    if gather in ("norm", "low"):
        filler.advance(SHARE[2])
        for j in range(2):
            g.forward(j)
    filler.advance(1.0)
    if gather:
        g.finish()
    filler.end()
    c_far.wait_send()
    c_core.wait_send()
    for j in range(2):
        c_x[j].wait_send()
    shipper.finish()
    for copy in stores:
        copy.wait()


def stage(
    number, planes, pairs, resid, *, back=None, gather=None, gain=None, given=None, dtype=F32, jobs=(), filler=None
):
    chunk = resid.shape[1]
    operands, flips, cost = [], [], 0
    for a, w, flip in pairs:
        operands += [a, w]
        flips.append(flip)
        cost += 2 * a.shape[0] * a.shape[1] * D
    operands.append(resid)
    if back:
        operands += [back[1], back[0]]
    elif gather == "norm":
        operands.append(gain)
    if gather == "given":
        operands.append(given)
    outs = [jax.ShapeDtypeStruct((2, chunk, D), dtype)]
    if gather:
        outs.append(jax.ShapeDtypeStruct((2 * TP * chunk, D), BF))
    if back:
        outs.append(jax.ShapeDtypeStruct((1, D), F32))
    half = pltpu.VMEM((2, chunk, D), BF)
    full = pltpu.VMEM((2, chunk, D), F32)
    scratch = [half] * 6 + [full] * 2 + [
        pltpu.VMEM((2, chunk, D), dtype),
        pltpu.SemaphoreType.DMA((11,)),
    ]
    if gather:
        scratch += [half, pltpu.SemaphoreType.DMA((7, 2))]
    if back:
        scratch.append(pltpu.VMEM((1, D), F32))
    kernel = functools.partial(stage_kernel, (chunk, tuple(flips), bool(back), gather))
    got, moved, made = call_with_jobs(
        kernel, number, planes, list(jobs), operands, outs, scratch, "stage", cost, filler
    )
    return (got, moved, made) if filler else (got, moved)


class Attention:
    def __init__(self, parts, q, kv, bias, mkv, causal):
        self.parts, self.causal = parts, causal
        self.rows, self.keys = q.shape[0], kv.shape[0]
        self.chunk = self.rows // (2 * TP)
        self.joint = q is kv
        self.extra = 0 if mkv is None else mkv.shape[0]
        self.total = self.keys + self.extra
        self.bias = bias
        self.blocks = self.rows // (2 * self.chunk)
        self.n_steps = HQ * self.blocks
        self.loads = [q] + ([] if self.joint else [kv]) + ([mkv] if self.extra else [])
        self.raws = []

    def heads(self, *widths_dtypes):
        return [pltpu.VMEM((HQ, n, DH), dtype) for n, dtype in widths_dtypes]

    def split_qkv(self, loads, qs, ks, vs):
        q_ref = loads.pop(0).get()
        kv_ref = q_ref if self.joint else loads.pop(0).get()
        at = QC if self.joint else 0
        keys = self.keys
        for i in range(HQ):
            qs[i] = q_ref[:, DH * i : DH * (i + 1)]
            ks[i, :keys] = kv_ref[:, at + DH * i : at + DH * (i + 1)]
            vs[i, :keys] = kv_ref[:, at + QC + DH * i : at + QC + DH * (i + 1)]
        if self.extra:
            mkv_ref = loads.pop(0).get()
            for i in range(HQ):
                ks[i, keys:] = mkv_ref[:, DH * i : DH * (i + 1)]
                vs[i, keys:] = mkv_ref[:, QC + DH * i : QC + DH * (i + 1)]

    def place(self, row_chunk):
        upper = row_chunk // TP
        part = lax.axis_index("part") if self.parts > 1 else 0
        return (upper * (TP * self.parts) + TP * part + (row_chunk - TP * upper)) * self.chunk

    def step_rows(self, i):
        h = i // self.blocks
        b = i - h * self.blocks
        return h, b, pl.ds(pl.multiple_of(b * (2 * self.chunk), 2 * self.chunk), 2 * self.chunk)

    def diagonal(self, b, u):
        return pl.ds(pl.multiple_of(self.keys - self.place(2 * b + u), 128), self.keys)


class AttentionForward(Attention):
    def __init__(self, parts, q, kv, segq, segk, bvec, mkv, causal):
        super().__init__(parts, q, kv, bvec is not None, mkv, causal)
        self.loads += [segq, segk] + ([bvec] if self.bias else [])
        self.outs = [
            jax.ShapeDtypeStruct((self.rows, QC), BF),
            jax.ShapeDtypeStruct((HQ, self.rows, self.total), BF),
        ]
        self.scratch = self.heads((self.rows, BF), (self.total, BF), (self.total, BF), (self.rows, BF))
        self.scratch += [
            pltpu.VMEM((2, 2 * self.chunk, self.total), BF),
            pltpu.VMEM((self.rows, QC), BF),
            pltpu.SemaphoreType.DMA((3,)),
        ]
        if self.bias:
            self.scratch.append(pltpu.VMEM((self.chunk, 2 * self.keys), F32))

    def begin(self, loads, raws, outs, scratch):
        self.att_out, self.p_out = outs
        self.qs, self.ks, self.vs, self.os, self.p_buf, self.att, self.sems = scratch[:7]
        self.toep = scratch[7] if self.bias else None
        loads = list(loads)
        self.split_qkv(loads, self.qs, self.ks, self.vs)
        self.segq, self.segk = loads.pop(0).get(), loads.pop(0).get()
        self.bvec = loads.pop(0).get() if self.bias else None

    def keep(self, i):
        h, b, rows = self.step_rows(i)
        slot = lax.rem(i, 2)
        return pltpu.make_async_copy(self.p_buf.at[slot], self.p_out.at[h, rows], self.sems.at[slot])

    def run(self, low, high):
        keys, chunk = self.keys, self.chunk

        @pl.loop(low, high)
        def _(i):
            h, b, rows = self.step_rows(i)
            slot = lax.rem(i, 2)
            if self.bias:

                @pl.when(b == 0)
                def _():
                    row = jnp.broadcast_to(self.bvec[h], (chunk, 2 * keys))
                    self.toep[...] = pltpu.roll(row, 0, 1, stride=1, stride_axis=0)

            s = mm_nt(self.qs[h, rows], self.ks[h])
            allowed = self.segq[rows] == self.segk[...]
            if self.bias:
                parts = [self.toep[:, self.diagonal(b, u)] for u in range(2)]
                biased = s[:, :keys] + jnp.concatenate(parts, axis=0)
                s = jnp.concatenate([biased, s[:, keys:]], axis=1) if self.extra else biased
            if self.causal:
                row = lax.broadcasted_iota(jnp.int32, (chunk, 1), 0)
                places = jnp.concatenate([row + self.place(2 * b + u) for u in range(2)], axis=0)
                allowed = allowed & (lax.broadcasted_iota(jnp.int32, (1, keys), 1) <= places)
            s = jnp.where(allowed, s, MASKED)
            top = jnp.max(s, axis=-1, keepdims=True)
            e = jnp.exp(s - top)
            p = (e * (1.0 / jnp.sum(e, axis=-1, keepdims=True))).astype(BF)

            @pl.when(i >= 2)
            def _():
                self.keep(i - 2).wait()

            self.p_buf[slot] = p
            self.keep(i).start()
            self.os[h, rows] = mm(p, self.vs[h]).astype(BF)

    def end(self):
        for i in range(HQ):
            self.att[:, DH * i : DH * (i + 1)] = self.os[i]
        out = pltpu.make_async_copy(self.att, self.att_out, self.sems.at[2])
        out.start()
        self.keep(self.n_steps - 2).wait()
        self.keep(self.n_steps - 1).wait()
        out.wait()


class AttentionBackward(Attention):
    def __init__(self, parts, p, q, kv, grad, att, bias, mkv):
        super().__init__(parts, q, kv, bias, mkv, False)
        self.loads += [grad, att]
        self.raws = [p]
        rows, total, keys = self.rows, self.total, self.keys
        if self.joint:
            self.outs = [jax.ShapeDtypeStruct((rows, 3 * QC), BF)]
        else:
            kv_type = BF if parts == 1 else F32
            self.outs = [
                jax.ShapeDtypeStruct((rows, QC), BF),
                jax.ShapeDtypeStruct((keys, 2 * QC), kv_type),
            ]
        if bias:
            self.outs.append(jax.ShapeDtypeStruct((HQ, 1, 2 * keys), F32))
        if self.extra:
            self.outs.append(jax.ShapeDtypeStruct((self.extra, 2 * QC), BF))
        self.scratch = self.heads(
            (rows, BF), (total, BF), (total, BF), (rows, BF), (rows, BF), (total, F32), (total, F32)
        )
        self.scratch += [
            pltpu.VMEM((HQ, rows, 1), F32),
            pltpu.VMEM((2, 2 * self.chunk, total), BF),
            pltpu.SemaphoreType.DMA((2 + len(self.outs),)),
        ]
        self.scratch += [pltpu.VMEM(o.shape, o.dtype) for o in self.outs]
        if bias:
            self.scratch.append(pltpu.VMEM((self.chunk, 2 * keys), F32))

    def fetch(self, i):
        h, b, rows = self.step_rows(i)
        slot = lax.rem(i, 2)
        return pltpu.make_async_copy(self.p_in.at[h, rows], self.p_buf.at[slot], self.sems.at[slot])

    def begin(self, loads, raws, outs, scratch):
        self.results, (self.p_in,) = outs, raws
        scratch, loads = list(scratch), list(loads)
        self.qs, self.ks, self.vs, self.dos, self.dqs, self.dks, self.dvs = scratch[:7]
        self.rds, self.p_buf, self.sems = scratch[7:10]
        self.made = scratch[10 : 10 + len(outs)]
        self.diag = scratch[-1] if self.bias else None
        self.fetch(0).start()
        self.split_qkv(loads, self.qs, self.ks, self.vs)
        do_ref, att_ref = loads.pop(0).get(), loads.pop(0).get()
        for i in range(HQ):
            grad = do_ref[:, DH * i : DH * (i + 1)]
            self.dos[i] = grad
            out = att_ref[:, DH * i : DH * (i + 1)]
            self.rds[i] = jnp.sum(grad.astype(F32) * out.astype(F32), axis=-1, keepdims=True)
        made = list(self.made)
        self.dq = made.pop(0)
        self.dkv = self.dq if self.joint else made.pop(0)
        self.dbvec = made.pop(0) if self.bias else None
        self.dmkv = made.pop(0) if self.extra else None

    def run(self, low, high):
        keys, chunk = self.keys, self.chunk

        @pl.loop(low, high)
        def _(i):
            h, b, rows = self.step_rows(i)
            self.fetch(i).wait()

            @pl.when(i + 1 < self.n_steps)
            def _():
                self.fetch(i + 1).start()

            @pl.when(b == 0)
            def _():
                self.dks[h] = jnp.zeros(self.dks.shape[1:], F32)
                self.dvs[h] = jnp.zeros(self.dvs.shape[1:], F32)
                if self.bias:
                    self.diag[...] = jnp.zeros_like(self.diag)

            q, grad, p = self.qs[h, rows], self.dos[h, rows], self.p_buf[lax.rem(i, 2)]
            dp = mm_nt(grad, self.vs[h])
            ds = (p.astype(F32) * (dp - self.rds[h, rows])).astype(BF)
            self.dqs[h, rows] = mm(ds, self.ks[h]).astype(BF)
            self.dks[h] += mm_tn(ds, q)
            self.dvs[h] += mm_tn(p, grad)
            if self.bias:
                for u in range(2):
                    part = ds[u * chunk : (u + 1) * chunk, :keys]
                    self.diag[:, self.diagonal(b, u)] += part.astype(F32)

                @pl.when(b == self.blocks - 1)
                def _():
                    x = self.diag[...]
                    size = chunk
                    while size > 1:
                        size //= 2
                        x = x[:size] + pltpu.roll(x[size:], 2 * keys - size, 1)
                    self.dbvec[h] = x

    def end(self):
        keys = self.keys
        to = QC if self.joint else 0
        for i in range(HQ):
            self.dq[:, DH * i : DH * (i + 1)] = self.dqs[i]
            at = to + DH * i
            self.dkv[:, at : at + DH] = self.dks[i, :keys].astype(self.dkv.dtype)
            self.dkv[:, at + QC : at + QC + DH] = self.dvs[i, :keys].astype(self.dkv.dtype)
            if self.extra:
                self.dmkv[:, DH * i : DH * (i + 1)] = self.dks[i, keys:].astype(BF)
                self.dmkv[:, QC + DH * i : QC + DH * (i + 1)] = self.dvs[i, keys:].astype(BF)
        copies = [
            pltpu.make_async_copy(src, dst, self.sems.at[2 + n])
            for n, (src, dst) in enumerate(zip(self.made, self.results))
        ]
        for copy in copies:
            copy.start()
        for copy in copies:
            copy.wait()


class Idle:
    n_steps, loads, raws, outs, scratch = 0, [], [], [], []

    def begin(self, loads, raws, outs, scratch):
        pass

    def run(self, low, high):
        pass

    def end(self):
        pass


def attend(number, planes, filler, jobs):
    def kernel(shipper, ins, outs, scratch, filler):
        shipper.greet(())
        shipper.start()
        filler.begin()
        filler.run(0, filler.n_steps)
        filler.end()
        shipper.finish()

    _, moved, made = call_with_jobs(
        kernel, number, planes, jobs, [], [], [], "attend", 4 * 10**9, filler
    )
    return made, moved


ALL = ("seq", "part", "tp", "fsdp")
CTX = ("seq", "part", "tp")


def per_device(
    parts,
    planes,
    enc_input,
    dec_input,
    segments,
    prefix_rows,
    buckets,
    memory,
    enc_gain,
    enc_qkv,
    enc_rel,
    enc_proj,
    enc_ffnorm,
    enc_ffin,
    enc_ffout,
    dec_gain,
    dec_qkv,
    dec_rel,
    dec_proj,
    cross_gain,
    cross_query,
    cross_kv,
    cross_proj,
    dec_ffnorm,
    dec_ffin,
    dec_ffout,
    enc_cotan,
    dec_cotan,
):
    seq, part, tp, plane = (lax.axis_index(name) for name in ALL)
    chunk = enc_input.shape[1]
    length = buckets.shape[0] // 2
    docs, prefix = prefix_rows.shape[1:]

    first = seq == 0
    split = planes * 2

    def joined(x, came):
        mine = lax.dynamic_index_in_dim(x, seq, 0, keepdims=False)
        came = came.astype(x.dtype)
        return jnp.stack([jnp.where(first, mine, came), jnp.where(first, came, mine)])

    def cols(w, start, width=QC):
        return lax.dynamic_slice_in_dim(w, start + width * tp, width, 1)

    def halved(w):
        rows = w.shape[0] // 2
        return lax.dynamic_slice_in_dim(w, rows * seq, rows, 0)

    def qkv_part(w):
        w = halved(w)
        return jnp.concatenate([cols(w, D * i) for i in range(w.shape[1] // D)], axis=1)

    hidden = enc_ffout.shape[0] // TP

    def ffin_part(w):
        w = halved(w)
        return jnp.concatenate(
            [cols(w, hidden * TP * i, hidden) for i in range(planes)], axis=1
        )

    def ffout_part(w):
        rows = hidden // 2
        return lax.dynamic_slice_in_dim(w, hidden * tp + rows * seq, rows, 0)

    def over_planes(w):
        return gather_job("fsdp", w, planes)

    def over_seq(w):
        return gather_job("seq", w, 2, 1)

    def matrix(w):
        return w.reshape(-1, w.shape[-1])

    gains = (enc_gain, enc_ffnorm, dec_gain, cross_gain, dec_ffnorm)
    gain_stack = jnp.stack(gains).astype(F32)
    rel_stack = jnp.stack([enc_rel, dec_rel]).astype(F32)
    segments = segments.reshape(2, 1, chunk)
    first_jobs = [
        swap_job(enc_input),
        gather_job("fsdp", gain_stack, planes),
        gather_job("fsdp", rel_stack, planes),
        over_planes(qkv_part(enc_qkv)),
        over_planes(qkv_part(memory)),
        swap_job(dec_input),
    ]
    if parts == 1:
        first_jobs.append(block_job(segments))
    xe, gain_stack, rel_stack, w_eqkv, table, xd, *segs = ship(0, planes, first_jobs)
    xe, xd = joined(enc_input, xe), joined(dec_input, xd)
    if parts == 1:
        seg = segs[0].reshape(-1)
    else:
        segs = lax.all_gather(segments.reshape(2, chunk), CTX, axis=1, tiled=True)
        seg = lax.dynamic_index_in_dim(segs, seq, 0, keepdims=False)
    per, per_rel = enc_gain.shape[0], enc_rel.size
    g_enc, g_effn, g_dec, g_cross, g_dffn = [
        gain_stack[:, i].reshape(1, D) for i in range(len(gains))
    ]
    rels = [rel_stack[:, i].reshape(BUCKETS, HEADS) for i in range(2)]
    onehot = (buckets[:, None] == jnp.arange(BUCKETS, dtype=jnp.int32)[None, :]).astype(BF)

    def bias_vector(rel):
        own = lax.dynamic_slice_in_dim(rel, HQ * tp, HQ, 1).astype(BF)
        return lax.dot_general(
            own, onehot, (((0,), (1,)), ((), ())), preferred_element_type=F32
        ).reshape(HQ, 1, 2 * length)

    turned = planes == TP

    def proj_jobs(w):
        return [turn_job(w)] if turned else []

    def proj_of(got, w):
        if turned:
            return got.pop()
        full = lax.all_gather(w, "fsdp", axis=0, tiled=True)
        return lax.dynamic_slice_in_dim(full, QC * tp, QC, 0)

    en, (w_eqkv, table, w_dqkv, *got), _ = gather_norm(
        1,
        planes,
        xe,
        g_enc,
        [over_seq(w_eqkv), over_seq(table), over_planes(qkv_part(dec_qkv))] + proj_jobs(enc_proj),
    )
    w_eproj = proj_of(got, enc_proj)
    w_eqkv, table = matrix(w_eqkv), matrix(table)

    segq = lax.dynamic_index_in_dim(seg.reshape(2, parts, TP * chunk), part, 1, keepdims=False)
    segq = segq.reshape(-1, 1)
    segk = seg.reshape(1, length)
    ids = lax.dynamic_index_in_dim(prefix_rows, seq, 0, keepdims=False).reshape(-1)
    extra = -(-(docs * prefix) // 256) * 256
    ids = jnp.concatenate([ids, jnp.full((extra - docs * prefix,), -1, jnp.int32)])
    mem_doc = np.full((extra,), -1, np.int32)
    mem_doc[: docs * prefix] = np.arange(docs * prefix) // prefix
    segk_mem = jnp.concatenate([segk, jnp.asarray(mem_doc)[None]], axis=1)
    pick = (ids[:, None] == jnp.arange(table.shape[0], dtype=jnp.int32)[None, :]).astype(BF)
    mkv = mm(pick, table).astype(BF)

    def spread(kv):
        if parts == 1:
            return kv
        got = lax.all_gather(kv, "part", axis=0)
        return got.reshape(parts, 2, TP * chunk, -1).transpose(1, 0, 2, 3).reshape(length, -1)

    def collect(dkv):
        if parts == 1:
            return dkv
        split = dkv.reshape(2, parts, TP * chunk, -1).transpose(1, 0, 2, 3)
        split = split.reshape(parts * 2 * TP * chunk, -1)
        return lax.psum_scatter(split, "part", scatter_dimension=0, tiled=True).astype(BF)

    def self_kv(rows):
        return (rows, rows) if parts == 1 else (rows[:, :QC], spread(rows[:, QC:]))

    def joint_grad(got):
        if parts == 1:
            return got.pop(0)
        return jnp.concatenate([got.pop(0), collect(got.pop(0))], axis=1)

    e_qkv = self_kv(mm(en, w_eqkv).astype(BF))
    e_fill = AttentionForward(
        parts, *e_qkv, segq, segk_mem, bias_vector(rels[0]), mkv, False
    )
    dn, (w_dqkv, w_effin, w_effout, *got), (e_att, e_p) = gather_norm(
        2,
        planes,
        xd,
        g_dec,
        [
            over_seq(w_dqkv),
            over_planes(ffin_part(enc_ffin)),
            over_planes(ffout_part(enc_ffout)),
        ]
        + proj_jobs(dec_proj),
        e_fill,
    )
    w_dproj = proj_of(got, dec_proj)
    w_dqkv = matrix(w_dqkv)
    d_qkv = self_kv(mm(dn, w_dqkv).astype(BF))
    d_fill = AttentionForward(parts, *d_qkv, segq, segk, bias_vector(rels[1]), None, True)
    (e_mid, e_fn), (w_effin, w_effout, w_cq, w_ckv, w_dffin), (d_att, d_p) = stage(
        3,
        planes,
        [(e_att, w_eproj, False)],
        xe,
        gather="norm",
        gain=g_effn,
        jobs=[
            over_seq(w_effin),
            over_seq(w_effout),
            over_planes(qkv_part(cross_query)),
            over_planes(qkv_part(cross_kv)),
            over_planes(ffin_part(dec_ffin)),
        ],
        filler=d_fill,
    )
    w_effin, w_effout = matrix(w_effin), matrix(w_effout)
    e_pre = mm(e_fn, w_effin)
    e_act = gelu(e_pre).astype(BF)
    (d_mid, c_n), (w_cq, w_ckv, w_dffin, w_dffout, *got) = stage(
        4,
        planes,
        [(d_att, w_dproj, False)],
        xd,
        gather="norm",
        gain=g_cross,
        jobs=[
            over_seq(w_cq),
            over_seq(w_ckv),
            over_seq(w_dffin),
            over_planes(ffout_part(dec_ffout)),
        ]
        + proj_jobs(cross_proj),
    )
    w_cproj = proj_of(got, cross_proj)
    w_cq, w_ckv, w_dffin = matrix(w_cq), matrix(w_ckv), matrix(w_dffin)
    (e_low, e_gath), (w_dffout, xdc, xec) = stage(
        5,
        planes,
        [(e_act, w_effout, False)],
        e_mid,
        gather="low",
        dtype=BF,
        jobs=[over_seq(w_dffout), swap_job(dec_cotan), swap_job(enc_cotan)],
    )
    xdc, xec = joined(dec_cotan, xdc), joined(enc_cotan, xec)
    w_dffout = matrix(w_dffout)
    c_q = mm(c_n, w_cq).astype(BF)
    c_kv = spread(mm(e_gath, w_ckv).astype(BF))
    c_fill = AttentionForward(parts, c_q, c_kv, segq, segk, None, None, False)
    (c_att, c_p), (came,) = attend(19, planes, c_fill, [swap_job(e_low)])
    enc_output = joined(e_low, came)
    (d_cross, d_fn), _ = stage(
        6, planes, [(c_att, w_cproj, False)], d_mid, gather="norm", gain=g_dffn
    )
    d_pre = mm(d_fn, w_dffin)
    d_act = gelu(d_pre).astype(BF)
    (d_low, up_g), _ = stage(
        7, planes, [(d_act, w_dffout, False)], d_cross, gather="given", given=xdc, dtype=BF
    )

    def pieces(g):
        if parts > 1:
            g = lax.psum(g, "part")
        return g.reshape(planes, 2, g.shape[0] // split, g.shape[1])

    def proj_pieces(g):
        return pieces(g.reshape(2 * QC, D // 2))

    def step1(gs):
        return [swap_job(g, 1, True) for g in gs]

    def step2(gs):
        return [deal_job("fsdp", g) for g in gs]

    def step3(gs):
        return [gather_job("across", g) for g in gs]

    def step4(gs):
        return [gather_job("seq", g) for g in gs]

    def step5(gs, widths):
        return [last_job(g, width) for g, width in zip(gs, widths)]

    ff_widths, qkv_widths, proj_widths = [hidden, 0], [QC, QC], [0]

    def take(got, n):
        out = got[:n]
        del got[:n]
        return out

    def ff_grads(up_rows, fn, act, pre, w_out):
        d_out = mm_tn(act, up_rows).astype(BF)
        pre_grad = gelu_back(pre, mm_nt(up_rows, w_out)).astype(BF)
        d_in = mm_tn(fn, pre_grad).astype(BF)
        return pre_grad, [pieces(d_in), pieces(d_out)]

    pre_grad, g_dff = ff_grads(up_g, d_fn, d_act, d_pre, w_dffout)
    (up, up_g, dg_dffn), got = stage(
        8,
        planes,
        [(pre_grad, w_dffin, True)],
        xdc,
        back=(d_cross, g_dffn),
        gather="low",
        jobs=step1(g_dff) + [swap_job(d_low)],
    )
    dec_output = joined(d_low, got.pop())
    c_fill = AttentionBackward(
        parts, c_p, c_q, c_kv, mm_nt(up_g, w_cproj).astype(BF), c_att, False, None
    )
    (c_dq, c_dkv), g_dff = attend(20, planes, c_fill, step2(got))
    c_dkv = collect(c_dkv)
    g_cproj = mm_tn(c_att, up_g).astype(BF)
    g_c = [pieces(mm_tn(c_n, c_dq).astype(BF)), pieces(mm_tn(e_gath, c_dkv).astype(BF))]
    if turned:
        g_c.append(proj_pieces(g_cproj))
    (up, up_g, dg_cross), got = stage(
        9,
        planes,
        [(c_dq, w_cq, True)],
        up,
        back=(d_mid, g_cross),
        gather="low",
        jobs=step3(g_dff) + step1(g_c),
    )
    g_dff, g_c = take(got, 2), got
    d_fill = AttentionBackward(
        parts, d_p, *d_qkv, mm_nt(up_g, w_dproj).astype(BF), d_att, True, None
    )
    g_dproj = mm_tn(d_att, up_g).astype(BF)
    (e_up, e_up_g), got, made = stage(
        10,
        planes,
        [(c_dkv, w_ckv, True)],
        xec,
        gather="low",
        jobs=step4(g_dff) + step2(g_c),
        filler=d_fill,
    )
    g_dff, g_c = take(got, 2), got
    d_rows_grad = joint_grad(made)
    (d_dbv,) = made
    g_d = [pieces(mm_tn(dn, d_rows_grad).astype(BF))]
    turn = []
    if turned:
        g_d.append(proj_pieces(g_dproj))
        turn = [turn_job(g_c.pop())]
    pre_grad, g_eff = ff_grads(e_up_g, e_fn, e_act, e_pre, w_effout)
    (e_up, e_up_g, dg_effn), got = stage(
        12,
        planes,
        [(pre_grad, w_effin, True)],
        e_up,
        back=(e_mid, g_effn),
        gather="low",
        jobs=step5(g_dff, ff_widths) + step1(g_d) + step3(g_c) + turn,
    )
    o_dff, g_d, g_c, g_cp = take(got, 2), take(got, len(g_d)), take(got, 2), got
    e_fill = AttentionBackward(
        parts, e_p, *e_qkv, mm_nt(e_up_g, w_eproj).astype(BF), e_att, True, mkv
    )
    g_eproj = mm_tn(e_att, e_up_g).astype(BF)
    g_ep = [proj_pieces(g_eproj)] if turned else []
    (d_in, dg_dec), got, made = stage(
        11,
        planes,
        [(d_rows_grad, w_dqkv, True)],
        up,
        back=(xd, g_dec),
        jobs=step1(g_eff) + step1(g_ep) + step2(g_d) + step4(g_c) + step3(g_cp),
        filler=e_fill,
    )
    g_eff, g_ep = take(got, 2), take(got, len(g_ep))
    g_d, g_c, g_cp = take(got, len(g_d)), take(got, 2), got
    d_in_low = d_in.astype(BF)
    e_rows_grad = joint_grad(made)
    e_dbv, d_mkv = made
    turn = [turn_job(g_d.pop())] if turned else []
    (e_in, dg_enc), got = stage(
        13,
        planes,
        [(e_rows_grad, w_eqkv, True)],
        e_up,
        back=(xe, g_enc),
        jobs=step2(g_eff)
        + step2(g_ep)
        + step3(g_d)
        + turn
        + step5(g_c, qkv_widths)
        + step4(g_cp)
        + [swap_job(d_in_low)],
    )
    dec_ingrad = joined(d_in, got.pop())
    g_eff, g_ep = take(got, 2), take(got, len(g_ep))
    g_d, g_dp, o_c, g_cp = take(got, 1), take(got, len(turn)), take(got, 2), got
    g_eqkv = mm_tn(en, e_rows_grad).astype(BF)
    g_e = [pieces(g_eqkv), pieces(mm_tn(pick, d_mkv).astype(BF))]
    def rel_grad(dbv):
        own = lax.dot_general(
            onehot.astype(F32),
            dbv.reshape(HQ, -1),
            (((0,), (1,)), ((), ())),
            precision=lax.Precision.HIGHEST,
            preferred_element_type=F32,
        )
        return lax.dynamic_update_slice_in_dim(jnp.zeros((BUCKETS, HEADS), F32), own, HQ * tp, 1)

    tiny = [dg_enc, dg_effn, dg_dec, dg_cross, dg_dffn]
    tiny = jnp.concatenate([v.reshape(planes, -1) for v in tiny] + [
        rel_grad(v).reshape(planes, -1) for v in (e_dbv, d_dbv)
    ], axis=1)
    tiny = tiny.reshape(-1, 128)
    if parts > 1:
        tiny = lax.psum(tiny, "part")
    got = ship(
        14,
        planes,
        step1(g_e)
        + step3(g_eff)
        + [turn_job(g) for g in g_ep]
        + step4(g_d)
        + step3(g_dp)
        + step5(g_cp, proj_widths)
        + [total_job("fsdp", tiny, planes), swap_job(e_in.astype(BF))],
    )
    enc_ingrad = joined(e_in, got.pop())
    tiny = got.pop()
    g_e, g_eff, g_ep = take(got, 2), take(got, 2), take(got, len(g_ep))
    g_d, g_dp, o_cp = take(got, 1), take(got, len(g_dp)), got
    got = ship(
        15,
        planes,
        step2(g_e)
        + step4(g_eff)
        + step3(g_ep)
        + step5(g_d, qkv_widths)
        + step4(g_dp)
        + [total_job("seq", tiny)],
    )
    tiny = got.pop()
    g_e, g_eff, g_ep = take(got, 2), take(got, 2), take(got, len(g_ep))
    o_d, g_dp = take(got, 1), got
    got = ship(
        16,
        planes,
        step3(g_e)
        + step5(g_eff, ff_widths)
        + step4(g_ep)
        + step5(g_dp, proj_widths)
        + [total_job("across", tiny)],
    )
    tiny = got.pop()
    g_e, o_eff, g_ep, o_dp = take(got, 2), take(got, 2), take(got, len(g_ep)), got
    got = ship(17, planes, step4(g_e) + step5(g_ep, proj_widths) + [total_job("core", tiny)])
    tiny = got.pop()
    g_e, o_ep = take(got, 2), got
    o_e = ship(18, planes, step5(g_e, qkv_widths))

    def proj_rows(got, g):
        if turned:
            return got[0].reshape(-1, D)
        full = lax.dynamic_update_slice_in_dim(jnp.zeros((D, D), BF), g, QC * tp, 0)
        full = lax.psum_scatter(full, "fsdp", scatter_dimension=0, tiled=True)
        return lax.psum(full.astype(F32), CTX)

    o_eproj = proj_rows(o_ep, g_eproj)
    o_dproj = proj_rows(o_dp, g_dproj)
    o_cproj = proj_rows(o_cp, g_cproj)
    o_dffin, o_dffout = o_dff
    o_effin, o_effout = o_eff
    o_cq, o_ckv = o_c
    (o_dqkv,), (o_eqkv, o_table) = o_d, o_e
    tiny = lax.dynamic_index_in_dim(tiny.reshape(planes, -1), plane, 0, keepdims=False)
    o_gains = [tiny[per * i : per * (i + 1)] for i in range(5)]
    o_rels = [
        tiny[5 * per + per_rel * i : 5 * per + per_rel * (i + 1)].reshape(-1, HEADS)
        for i in range(2)
    ]
    return (
        enc_output,
        dec_output,
        enc_ingrad,
        dec_ingrad,
        o_table,
        o_gains[0],
        o_eqkv,
        o_rels[0],
        o_eproj,
        o_gains[1],
        o_effin,
        o_effout,
        o_gains[2],
        o_dqkv,
        o_rels[1],
        o_dproj,
        o_gains[3],
        o_cq,
        o_ckv,
        o_cproj,
        o_gains[4],
        o_dffin,
        o_dffout,
    )


def solution(mesh):
    ctx, planes = mesh.shape["ctx"], mesh.shape["fsdp"]
    parts = ctx // (2 * TP)
    inner = Mesh(np.asarray(mesh.devices).reshape(2, parts, TP, planes), ALL)
    rows3 = P("fsdp", CTX, None)
    mat, vec = P("fsdp", None), P("fsdp")
    args = (
        (rows3, rows3, P("fsdp", CTX), P("fsdp", None, None), P(), mat)
        + (vec, mat, mat, mat, vec, mat, mat)
        + (vec, mat, mat, mat)
        + (vec, mat, mat, mat)
        + (vec, mat, mat)
        + (rows3, rows3)
    )
    outs = (
        (rows3, rows3, rows3, rows3, mat)
        + (vec, mat, mat, mat, vec, mat, mat)
        + (vec, mat, mat, mat)
        + (vec, mat, mat, mat)
        + (vec, mat, mat)
    )
    return jax.shard_map(
        functools.partial(per_device, parts, planes),
        mesh=inner,
        in_specs=args,
        out_specs=outs,
        check_vma=False,
    )
```

```python
import collections
import functools

import jax
import jax.numpy as jnp
import numpy as np
from jax import lax
from jax.experimental import pallas as pl
from jax.experimental.pallas import tpu as pltpu
from jax.sharding import Mesh
from jax.sharding import PartitionSpec as P

D = 768
HEADS = 12
DH = 64
BUCKETS = 32
EPS = 1e-06
MASKED = -1e30
TP = 4
HQ = HEADS // TP
QC = HQ * DH
BF = jnp.bfloat16
F32 = jnp.float32
MESH_ID = pl.DeviceIdType.MESH
MB = 1024 * 1024
VMEM_LIMIT = 60 * MB
SHARE = (0.25, 0.34, 0.75)


def mm(a, b):
    return jnp.dot(a, b, preferred_element_type=F32)


def mm_tn(a, b):
    return lax.dot_general(a, b, (((0,), (0,)), ((), ())), preferred_element_type=F32)


def mm_nt(a, b):
    return lax.dot_general(a, b, (((1,), (1,)), ((), ())), preferred_element_type=F32)


def gelu(v):
    return jax.nn.gelu(v, approximate=True)


def gelu_back(pre, grad):
    return jax.vjp(gelu, pre)[1](grad)[0]


def group_ids():
    me = lax.axis_index("tp")
    core = me + 1 - 2 * lax.rem(me, 2)
    across = lax.rem(me + 2, TP)
    far = lax.rem(core + 2, TP)
    return me, core, across, far


def send(src, dst, send_sem, recv_sem, peer):
    return pltpu.make_async_remote_copy(
        src_ref=src,
        dst_ref=dst,
        send_sem=send_sem,
        recv_sem=recv_sem,
        device_id={"tp": peer},
        device_id_type=MESH_ID,
    )


def normed(values, gains):
    return values * lax.rsqrt(jnp.mean(values * values, axis=-1, keepdims=True) + EPS) * gains


class Gatherer:
    def __init__(self, buf, stage, sems, chunk, ids):
        self.buf, self.stage, self.sems, self.chunk, self.ids = buf, stage, sems, chunk, ids
        self.sends, self.own = [], []

    def rows(self, j, owner):
        return self.buf.at[pl.ds(pl.multiple_of((TP * j + owner) * self.chunk, self.chunk), self.chunk)]

    def put(self, j, value):
        me, core, across, far = self.ids
        mine = self.stage.at[j]
        mine[...] = value
        x_copy = send(mine, self.rows(j, me), self.sems.at[0, j], self.sems.at[1, j], across)
        x_copy.start()
        c_copy = send(mine, self.rows(j, me), self.sems.at[2, j], self.sems.at[3, j], core)
        c_copy.start()
        self.sends += [x_copy, c_copy]
        own = pltpu.make_async_copy(mine, self.rows(j, me), self.sems.at[6, j])
        own.start()
        self.own.append(own)

    def forward(self, j):
        me, core, across, far = self.ids
        theirs = self.rows(j, across)
        send(theirs, theirs, self.sems.at[0, j], self.sems.at[1, j], across).wait_recv()
        f_copy = send(theirs, theirs, self.sems.at[4, j], self.sems.at[5, j], core)
        f_copy.start()
        self.sends.append(f_copy)

    def finish(self):
        me, core, across, far = self.ids
        for j in range(2):
            a = self.rows(j, core)
            send(a, a, self.sems.at[2, j], self.sems.at[3, j], core).wait_recv()
            b = self.rows(j, far)
            send(b, b, self.sems.at[4, j], self.sems.at[5, j], core).wait_recv()
        for copy in self.sends:
            copy.wait_send()
        for copy in self.own:
            copy.wait()


Job = collections.namedtuple("Job", ["axis", "src_axis", "dst_axis", "local", "src", "shape", "finish"])


def gather_job(axis, src, size=2, at=0):
    shape = src.shape[:at] + (size,) + src.shape[at:]
    return Job(axis, None, at, True, src, shape, None)


def total_job(axis, src, size=2):
    return gather_job(axis, src, size)._replace(finish="sum")


def deal_job(axis, src):
    return Job(axis, 0, 0, True, src, src.shape, "sum")


def swap_job(src, at=0, add=False):
    if at == "cols":
        shape = src.shape[:-1] + (src.shape[-1] // 2,)
    else:
        shape = src.shape[:at] + src.shape[at + 1 :]
    return Job("seq", at, None, add, src, shape, "add" if add else None)


def turn_job(src):
    return Job("turn", None, None, True, src, src.shape, None)


def block_job(src):
    return Job("ctx", 0, 0, True, src, (2 * TP,) + src.shape[1:], None)


def last_job(src, width):
    return gather_job("core", src, 2, 2)._replace(finish=("layout", width))


def result_of(job):
    if job.finish == "sum":
        return job.shape[1:], job.src.dtype
    if isinstance(job.finish, tuple):
        seqs, halves, cores, rows, cols = job.shape
        if job.finish[1] < 0:
            return (halves * cores * rows, seqs * cols), F32
        if job.finish[1]:
            return (seqs * rows, halves * cores * cols), F32
        return (seqs * halves * cores * rows, cols), F32
    return job.shape, job.src.dtype


def entry(ref, axis, index):
    if axis == "cols":
        half = ref.shape[-1] // 2
        return ref.at[:, :, pl.ds(pl.multiple_of(index * half, half), half)]
    return ref if axis is None else ref.at[(slice(None),) * axis + (index,)]


class Shipper:
    def __init__(self, jobs, planes, srcs, outs, scratch, sems):
        self.jobs, self.planes, self.srcs, self.outs, self.sems = jobs, planes, srcs, outs, sems
        self.tp, self.seq, self.plane = (lax.axis_index(n) for n in ("tp", "seq", "fsdp"))
        self.dsts, self.bounce, self.made = [], [], []
        for job, out in zip(jobs, outs):
            if job.finish:
                self.dsts.append(scratch.pop(0))
                self.bounce.append(scratch.pop(0) if job.finish == "add" else None)
                self.made.append(scratch.pop(0) if job.finish != "add" else None)
            else:
                self.dsts.append(out)
                self.bounce.append(scratch.pop(0) if job.local else None)
                self.made.append(None)

    @staticmethod
    def scratch(jobs):
        shapes = []
        for job in jobs:
            dtype = job.src.dtype
            if job.finish:
                shapes.append(pltpu.VMEM(job.shape, dtype))
                if job.finish == "add":
                    shapes.append(pltpu.VMEM(job.shape, dtype))
                else:
                    shapes.append(pltpu.VMEM(*result_of(job)))
            elif job.local:
                drop = job.dst_axis
                own = job.shape if drop is None else job.shape[:drop] + job.shape[drop + 1 :]
                shapes.append(pltpu.VMEM(own, dtype))
        return shapes

    @staticmethod
    def count(jobs, planes):
        return sum(2 * Shipper.n_peers(job, planes) + 2 for job in jobs)

    @staticmethod
    def n_peers(job, planes):
        return {"fsdp": planes - 1, "ctx": 2 * TP - 1}.get(job.axis, 1)

    def coord(self, axis):
        half = self.tp // 2
        return {
            "fsdp": self.plane,
            "seq": self.seq,
            "across": half,
            "core": self.tp - 2 * half,
            "ctx": TP * self.seq + self.tp,
            "turn": None,
        }[axis]

    def peers(self, axis):
        if axis == "fsdp":
            n, z = self.planes, self.plane
            for k in range(1, n):
                to = lax.rem(z + k, n)
                yield to, {"fsdp": to}, lax.rem(z + (n - k), n)
        elif axis == "ctx":
            for k in range(1, 2 * TP):
                to = lax.rem(self.seq + k // TP, 2)
                to_tp = lax.rem(self.tp + k % TP, TP)
                from_seq = lax.rem(self.seq + (2 - k // TP), 2)
                from_tp = lax.rem(self.tp + (TP - k % TP), TP)
                yield to, {"seq": to, "tp": to_tp}, TP * from_seq + from_tp
        elif axis == "seq":
            yield 1 - self.seq, {"seq": 1 - self.seq}, 1 - self.seq
        elif axis == "turn":
            yield None, {"fsdp": self.tp, "tp": self.plane}, None
        else:
            to = lax.rem(self.tp + 2, TP) if axis == "across" else self.tp + 1 - 2 * lax.rem(self.tp, 2)
            other = 1 - self.coord(axis)
            yield other, {"tp": to}, other

    def signal(self, always=("core", "across")):
        axes = list(always) + sorted({job.axis for job in self.jobs} - set(always))
        barrier = pltpu.get_barrier_semaphore()
        self.expected, self.turns = 0, "turn" in axes
        for axis in axes:
            for _, device, _ in self.peers(axis):
                if axis == "turn":

                    @pl.when(self.plane != self.tp)
                    def _():
                        pl.semaphore_signal(
                            barrier, inc=1, device_id=device, device_id_type=MESH_ID
                        )

                    continue
                pl.semaphore_signal(barrier, inc=1, device_id=device, device_id_type=MESH_ID)
                self.expected += 1

    def met(self):
        barrier = pltpu.get_barrier_semaphore()
        if self.turns:
            moves = self.plane != self.tp

            @pl.when(moves)
            def _():
                pl.semaphore_wait(barrier, self.expected + 1)

            @pl.when(jnp.logical_not(moves))
            def _():
                pl.semaphore_wait(barrier, self.expected)
        else:
            pl.semaphore_wait(barrier, self.expected)

    def greet(self, always=("core", "across")):
        self.signal(always)
        self.met()

    def each(self, act_remote, act_local):
        base = 0
        for n, (job, src, dst) in enumerate(zip(self.jobs, self.srcs, self.dsts)):
            mine = self.coord(job.axis)
            peers = list(self.peers(job.axis))
            for i, (to, device, source) in enumerate(peers):
                sems = (self.sems.at[base + 2 * i], self.sems.at[base + 2 * i + 1])

                def copy_into(slot, to=to, device=device, sems=sems, src=src, dst=dst, job=job):
                    return pltpu.make_async_remote_copy(
                        src_ref=entry(src, job.src_axis, to),
                        dst_ref=entry(dst, job.dst_axis, slot),
                        send_sem=sems[0],
                        recv_sem=sems[1],
                        device_id=device,
                        device_id_type=MESH_ID,
                    )

                def remote(copy_into=copy_into, source=source, mine=mine):
                    act_remote(copy_into, mine, source)

                if job.axis == "turn":
                    pl.when(self.plane != self.tp)(remote)
                else:
                    remote()
            if job.local:
                own = self.seq if job.axis == "ctx" else mine

                def local(n=n, job=job, src=src, dst=dst, own=own, mine=mine, sem=base + 2 * len(peers)):
                    here, there = entry(src, job.src_axis, own), entry(dst, job.dst_axis, mine)
                    bounce = self.bounce[n]
                    if bounce is None:
                        act_local([(here, there)], self.sems.at[sem])
                    elif job.finish == "add":
                        act_local([(here, bounce)], self.sems.at[sem])
                    else:
                        act_local([(here, bounce), (bounce, there)], self.sems.at[sem])

                if job.axis == "turn":
                    pl.when(self.plane == self.tp)(local)
                else:
                    local()
            base += 2 * len(peers) + 2
        return base

    def start(self):
        self.each(
            lambda copy_into, mine, source: copy_into(mine).start(),
            lambda legs, sem: pltpu.make_async_copy(*legs[0], sem).start(),
        )

    def finish(self):
        def turn_round(legs, sem):
            if len(legs) > 1:
                pltpu.make_async_copy(*legs[0], sem).wait()
                pltpu.make_async_copy(*legs[1], sem).start()

        def remote(copy_into, mine, source):
            copy_into(source).wait_recv()
            copy_into(mine).wait_send()

        self.each(lambda *_: None, turn_round)
        self.each(remote, lambda legs, sem: pltpu.make_async_copy(*legs[-1], sem).wait())
        stores, base = [], 0
        for job, dst, bounce, made, out in zip(
            self.jobs, self.dsts, self.bounce, self.made, self.outs
        ):
            base += 2 * self.n_peers(job, self.planes) + 2
            if not job.finish:
                continue
            if job.finish == "add":
                made = bounce

                @pl.loop(0, dst.shape[0])
                def _(i):
                    bounce[i] = (bounce[i].astype(F32) + dst[i].astype(F32)).astype(bounce.dtype)

            elif job.finish == "sum":
                total = dst[0].astype(F32)
                for i in range(1, dst.shape[0]):
                    total = total + dst[i].astype(F32)
                made[...] = total.astype(made.dtype)
            else:
                self.lay_out(dst, made, job.finish[1])
            store = pltpu.make_async_copy(made, out, self.sems.at[base - 1])
            store.start()
            stores.append(store)
        for store in stores:
            store.wait()

    @staticmethod
    def lay_out(src, dst, width):
        seqs, halves, cores, rows, cols = src.shape
        if width < 0:
            for i in range(seqs):
                for q in range(TP):
                    block = slice(i * cols, (i + 1) * cols)
                    dst[q * rows : (q + 1) * rows, block] = src[i, q // 2, q % 2].astype(F32)
            return

        @pl.loop(0, seqs)
        def _(i):
            if not width:
                for q in range(TP):
                    at = pl.multiple_of((q * seqs + i) * rows, rows)
                    dst[pl.ds(at, rows)] = src[i, q // 2, q % 2].astype(F32)
            else:
                at = pl.multiple_of(i * rows, rows)
                for n in range(cols // width):
                    span = slice(n * width, (n + 1) * width)
                    parts = [src[i, q // 2, q % 2, :, span].astype(F32) for q in range(TP)]
                    block = slice(n * width * TP, (n + 1) * width * TP)
                    dst[pl.ds(at, rows), block] = jnp.concatenate(parts, axis=1)


HBM_SPEC = pl.BlockSpec(memory_space=pltpu.HBM)


class Loaded:
    def __init__(self, src, dst, sem, start=True):
        self.copy, self.ref, self.waited = pltpu.make_async_copy(src, dst, sem), dst, False
        if start:
            self.copy.start()

    def get(self):
        if not self.waited:
            self.copy.wait()
            self.waited = True
        return self.ref


class LoadedRows:
    def __init__(self, src, dst, sems, chunk):
        self.src, self.ref, self.sems, self.chunk = src, dst, sems, chunk

    def copies(self, owner, slot):
        for j in range(2):
            at = pl.multiple_of((TP * j + owner) * self.chunk, self.chunk)
            rows = pl.ds(at, self.chunk)
            yield pltpu.make_async_copy(
                self.src.at[rows], self.ref.at[rows], self.sems.at[2 * slot + j]
            )

    def start(self, owners):
        for slot, owner in enumerate(owners):
            for copy in self.copies(owner, slot):
                copy.start()

    def wait(self, owner, slot):
        for copy in self.copies(owner, slot):
            copy.wait()


def call_with_jobs(
    kernel, number, planes, jobs, operands, outs, scratch, name, cost, filler=None, by_rows=()
):
    filler = filler or Idle()
    jobs = list(jobs)
    n_in, n_out, n_job = len(operands), len(outs), len(jobs)
    n_load, n_raw, n_fill = len(filler.loads), len(filler.raws), len(filler.outs)
    loads, raws = list(filler.loads), list(filler.raws)
    n_sems = max(Shipper.count(jobs, planes), 1)
    plain = [job._replace(src=jax.ShapeDtypeStruct(job.src.shape, job.src.dtype)) for job in jobs]
    job_scratch = Shipper.scratch(jobs)
    n_scratch = len(filler.scratch)

    def body(*refs):
        refs = list(refs)

        def take(n):
            out = refs[:n]
            del refs[:n]
            return out

        ins, srcs, fills, raw = take(n_in), take(n_job), take(n_load), take(n_raw)
        results, dsts, fill_outs = take(n_out), take(n_job), take(n_fill)
        sems, in_sems, row_sems = take(3)
        loaded = []
        for i, src in enumerate(ins):
            if i in by_rows:
                rows = row_sems.at[by_rows.index(i)]
                loaded.append(LoadedRows(src, refs.pop(0), rows, src.shape[0] // (2 * TP)))
            else:
                loaded.append(Loaded(src, refs.pop(0), in_sems.at[i]))
        fill_loads = [
            Loaded(src, refs.pop(0), in_sems.at[n_in + i], False) for i, src in enumerate(fills)
        ]
        shipper = Shipper(plain, planes, srcs, dsts, take(len(job_scratch)), sems)
        begin = functools.partial(filler.begin, fill_loads, raw, fill_outs, take(n_scratch))
        kernel(shipper, loaded, list(results), refs, Running(filler, begin, fill_loads))

    results = [result_of(job) for job in jobs]
    got = pl.pallas_call(
        body,
        out_shape=tuple(outs)
        + tuple(jax.ShapeDtypeStruct(*r) for r in results)
        + tuple(filler.outs),
        in_specs=[HBM_SPEC] * (n_in + n_job + n_load + n_raw),
        out_specs=(HBM_SPEC,) * (n_out + n_job + n_fill),
        scratch_shapes=[
            pltpu.SemaphoreType.DMA((n_sems,)),
            pltpu.SemaphoreType.DMA((max(n_in + n_load, 1),)),
            pltpu.SemaphoreType.DMA((max(len(by_rows), 1), 2 * TP)),
        ]
        + [pltpu.VMEM(v.shape, v.dtype) for v in operands + loads]
        + job_scratch
        + list(filler.scratch)
        + scratch,
        compiler_params=pltpu.CompilerParams(
            collective_id=number, has_side_effects=True, vmem_limit_bytes=VMEM_LIMIT
        ),
        cost_estimate=pl.CostEstimate(flops=cost, bytes_accessed=8 * MB, transcendentals=0),
        name=name,
    )(*operands, *[job.src for job in jobs], *loads, *raws)
    return got[:n_out], list(got[n_out : n_out + n_job]), list(got[n_out + n_job :])


class Running:
    def __init__(self, filler, begin, loads):
        self.begin, self.run, self.end, self.loads = begin, filler.run, filler.end, loads
        self.n_steps, self.done = filler.n_steps, 0

    def prefetch(self):
        for load in self.loads:
            load.copy.start()

    def advance(self, share):
        high = int(round(share * self.n_steps))
        if high > self.done:
            self.run(self.done, high)
            self.done = high


def ship(number, planes, jobs):
    def kernel(shipper, ins, outs, scratch, filler):
        shipper.greet(())
        shipper.start()
        shipper.finish()

    return call_with_jobs(kernel, number, planes, jobs, [], [], [], "ship", 0)[1]


def gather_norm(number, planes, x, gain, jobs, filler=None):
    chunk = x.shape[1]

    def kernel(shipper, ins, outs, scratch, filler):
        shipper.signal()
        x_ref, gain_ref = (v.get() for v in ins)
        shipper.met()
        shipper.start()
        g = Gatherer(outs[0], scratch[0], scratch[1], chunk, group_ids())
        for j in range(2):
            g.put(j, normed(x_ref[j].astype(F32), gain_ref[...]).astype(BF))
        filler.prefetch()
        filler.begin()
        filler.advance(0.4)
        for j in range(2):
            g.forward(j)
        filler.advance(1.0)
        filler.end()
        g.finish()
        shipper.finish()

    outs = [jax.ShapeDtypeStruct((2 * TP * chunk, D), BF)]
    scratch = [pltpu.VMEM((2, chunk, D), BF), pltpu.SemaphoreType.DMA((7, 2))]
    got, moved, made = call_with_jobs(
        kernel, number, planes, jobs, [x, gain], outs, scratch, "gather_norm", 10**6, filler
    )
    return got[0], moved, made


GELU_C = float(np.sqrt(2.0 / np.pi))


def gelu_parts(v):
    tanh = jnp.tanh(GELU_C * (v + 0.044715 * v * v * v))
    return tanh, 0.5 * (1.0 + tanh)


def gelu_slope(v):
    tanh, half = gelu_parts(v)
    return half + 0.5 * v * (1.0 - tanh * tanh) * (GELU_C * (1.0 + 3 * 0.044715 * v * v))


class Rows:
    n_operands, n_outs, n_scratch = 1, 0, 0

    def __init__(self, ins, outs, scratch, chunk):
        self.rows, self.chunk = ins.pop(0), chunk
        self.by_rows = [self.rows]

    def prepare(self):
        self.ref = self.rows.ref

    def make(self, pair, slot):
        pass

    def finish(self):
        pass

    def pick(self, ref, pair):
        return jnp.concatenate([ref[rows] for rows in pair], axis=0)


class MadeRows(Rows):
    def write(self, index, ref, out, slot, pair):
        for j, rows in enumerate(pair):
            copy = pltpu.make_async_copy(ref.at[rows], out.at[rows], self.sems.at[index, 2 * slot + j])
            copy.start()
            self.copies.append(copy)

    def finish(self):
        for copy in self.copies:
            copy.wait()

    def tiles(self, body):
        @pl.loop(0, self.ref.shape[1] // 256)
        def _(n):
            body(pl.ds(pl.multiple_of(n * 256, 256), 256))


class FeedForward(MadeRows):
    n_operands, n_outs, n_scratch = 2, 2, 3

    def __init__(self, ins, outs, scratch, chunk):
        self.rows, self.w_in, self.chunk, self.copies = ins.pop(0), ins.pop(0), chunk, []
        self.by_rows = [self.rows]
        self.pre_out, self.act_out = outs.pop(0), outs.pop(0)
        self.pre, self.ref, self.sems = scratch.pop(0), scratch.pop(0), scratch.pop(0)

    @staticmethod
    def extras(n_rows, width):
        shapes = [((n_rows, width), F32), ((n_rows, width), BF)]
        scratch = [pltpu.VMEM(*v) for v in shapes] + [pltpu.SemaphoreType.DMA((2, 2 * TP))]
        return [jax.ShapeDtypeStruct(*v) for v in shapes], scratch

    def prepare(self):
        self.w_in = self.w_in.get()

    def make(self, pair, slot):
        x = self.pick(self.rows.ref, pair)

        def tile(cols):
            v = mm(x, self.w_in[:, cols])
            act = (v * gelu_parts(v)[1]).astype(BF)
            for j, rows in enumerate(pair):
                self.pre[rows, cols] = v[j * self.chunk : (j + 1) * self.chunk]
                self.ref[rows, cols] = act[j * self.chunk : (j + 1) * self.chunk]

        self.tiles(tile)
        self.write(0, self.pre, self.pre_out, slot, pair)
        self.write(1, self.ref, self.act_out, slot, pair)


class FeedForwardBack(MadeRows):
    n_operands, n_outs, n_scratch = 3, 1, 2

    def __init__(self, ins, outs, scratch, chunk):
        self.rows, self.pre, self.w_out = ins.pop(0), ins.pop(0), ins.pop(0)
        self.chunk, self.copies = chunk, []
        self.by_rows = [self.rows, self.pre]
        self.out, self.ref, self.sems = outs.pop(0), scratch.pop(0), scratch.pop(0)

    @staticmethod
    def extras(n_rows, width):
        shape = ((n_rows, width), BF)
        scratch = [pltpu.VMEM(*shape), pltpu.SemaphoreType.DMA((1, 2 * TP))]
        return [jax.ShapeDtypeStruct(*shape)], scratch

    def prepare(self):
        self.w_out = self.w_out.get()

    def make(self, pair, slot):
        x = self.pick(self.rows.ref, pair)

        def tile(cols):
            grad = mm_nt(x, self.w_out[cols, :])
            for j, rows in enumerate(pair):
                back = gelu_slope(self.pre.ref[rows, cols]) * grad[j * self.chunk : (j + 1) * self.chunk]
                self.ref[rows, cols] = back.astype(BF)

        self.tiles(tile)
        self.write(0, self.ref, self.out, slot, pair)


def stage_kernel(conf, shipper, ins, outs, scratch, filler):
    chunk, maker, flip, back, gather = conf
    made_outs = [outs.pop() for _ in range(maker.n_outs)][::-1]
    made_scratch = [scratch.pop() for _ in range(maker.n_scratch)][::-1]
    left = maker(ins, made_outs, made_scratch, chunk)
    w_in = ins.pop(0)
    resid_in = ins.pop(0)
    gain_in = ins.pop(0) if (back or gather == "norm") else None
    x_in = ins.pop(0) if back else None
    given_in = ins.pop(0) if gather == "given" else None
    y_out = outs.pop(0)
    gath_ref = outs.pop(0) if gather else None
    dgain_out = outs.pop(0) if back else None
    s_far, r_far, s_x, r_x, s_core, r_core, keep, own, y_ref, sems = scratch[:10]
    scratch = scratch[10:]
    g_stage, g_sems = (scratch.pop(0), scratch.pop(0)) if gather else (None, None)
    dgain_ref = scratch.pop(0) if back else None
    ids = group_ids()
    me, core, across, far = ids
    slots = [0, 1, 2, 3]

    def partial(owner, store):
        slot = slots.pop(0)
        for rows in left.by_rows:
            rows.wait(owner, slot)
        pair = [
            pl.ds(pl.multiple_of((TP * j + owner) * chunk, chunk), chunk) for j in range(2)
        ]
        left.make(pair, slot)
        a = left.pick(left.ref, pair)

        @pl.loop(0, D // 256)
        def _(n):
            cols = pl.ds(pl.multiple_of(n * 256, 256), 256)
            total = mm_nt(a, w_ref[cols, :]) if flip else mm(a, w_ref[:, cols])
            for j in range(2):
                store(j, cols, total[j * chunk : (j + 1) * chunk])

    def into(ref):
        def store(j, cols, value):
            ref[j, :, cols] = value.astype(ref.dtype)

        return store

    order = (far, across, core, me)
    for rows in left.by_rows:
        rows.start(order)
    shipper.signal()
    left.prepare()
    w_ref = w_in.get()
    partial(far, into(s_far))
    shipper.met()
    c_far = send(s_far, r_far, sems.at[0], sems.at[1], core)
    c_far.start()
    shipper.start()
    g = Gatherer(gath_ref, g_stage, g_sems, chunk, ids) if gather else None
    if gather == "given":
        given_ref = given_in.get()
        for j in range(2):
            g.put(j, given_ref[j])
    partial(across, into(keep))
    filler.prefetch()
    c_far.wait_recv()
    c_x = []
    for j in range(2):
        s_x[j] = (keep[j] + r_far[j].astype(F32)).astype(BF)
        c_x.append(send(s_x.at[j], r_x.at[j], sems.at[2 + j], sems.at[4 + j], across))
        c_x[j].start()
    partial(core, into(s_core))
    c_core = send(s_core, r_core, sems.at[6], sems.at[7], core)
    c_core.start()
    partial(me, into(own))
    c_core.wait_recv()
    filler.begin()
    filler.advance(SHARE[0])
    resid_ref = resid_in.get()
    x_ref = x_in.get() if back else None
    gains = gain_in.get()[...] if gain_in else None
    if gather == "given":
        for j in range(2):
            g.forward(j)
    stores = []

    def keep_out(src, dst, sem):
        copy = pltpu.make_async_copy(src, dst, sems.at[sem])
        copy.start()
        stores.append(copy)

    for j in range(2):
        c_x[j].wait_recv()
        if j == 1:
            filler.advance(SHARE[1])
        total = own[j] + r_core[j].astype(F32) + r_x[j].astype(F32)
        if back:
            x = x_ref[j].astype(F32)
            r = lax.rsqrt(jnp.mean(x * x, axis=-1, keepdims=True) + EPS)
            scaled = total * gains
            inner = jnp.mean(scaled * x, axis=-1, keepdims=True)
            y = resid_ref[j].astype(F32) + r * scaled - x * (r * r * r * inner)
            dgain = jnp.sum(total * x * r, axis=0, keepdims=True)
            if j == 0:
                dgain_ref[...] = dgain
            else:
                dgain_ref[...] += dgain
        else:
            y = resid_ref[j].astype(F32) + total
        y_ref[j] = y.astype(y_ref.dtype)
        if gather == "norm":
            g.put(j, normed(y, gains).astype(BF))
        elif gather == "low":
            g.put(j, y.astype(BF))
        keep_out(y_ref.at[j], y_out.at[j], 8 + j)
    if back:
        keep_out(dgain_ref, dgain_out, 10)
    if gather in ("norm", "low"):
        filler.advance(SHARE[2])
        for j in range(2):
            g.forward(j)
    filler.advance(1.0)
    filler.end()
    if gather:
        g.finish()
    c_far.wait_send()
    c_core.wait_send()
    for j in range(2):
        c_x[j].wait_send()
    shipper.finish()
    for copy in stores:
        copy.wait()
    left.finish()


def stage(
    number,
    planes,
    left,
    weight,
    resid,
    *,
    flip=False,
    maker=Rows,
    back=None,
    gather=None,
    gain=None,
    given=None,
    dtype=F32,
    jobs=(),
    filler=None,
):
    chunk = resid.shape[1]
    operands = list(left) + [weight]
    cost = 4 * left[0].shape[0] * D * D
    by_rows = {Rows: (0,), FeedForward: (0,), FeedForwardBack: (0, 1)}[maker]
    operands.append(resid)
    if back:
        operands += [back[1], back[0]]
    elif gather == "norm":
        operands.append(gain)
    if gather == "given":
        operands.append(given)
    outs = [jax.ShapeDtypeStruct((2, chunk, D), dtype)]
    if gather:
        outs.append(jax.ShapeDtypeStruct((2 * TP * chunk, D), BF))
    if back:
        outs.append(jax.ShapeDtypeStruct((1, D), F32))
    half = pltpu.VMEM((2, chunk, D), BF)
    full = pltpu.VMEM((2, chunk, D), F32)
    scratch = [half] * 6 + [full] * 2 + [
        pltpu.VMEM((2, chunk, D), dtype),
        pltpu.SemaphoreType.DMA((11,)),
    ]
    if gather:
        scratch += [half, pltpu.SemaphoreType.DMA((7, 2))]
    if back:
        scratch.append(pltpu.VMEM((1, D), F32))
    if maker is not Rows:
        width = weight.shape[1] if flip else weight.shape[0]
        more, more_scratch = maker.extras(2 * TP * chunk, width)
        outs += more
        scratch += more_scratch
    kernel = functools.partial(stage_kernel, (chunk, maker, flip, bool(back), gather))
    got, moved, made = call_with_jobs(
        kernel,
        number,
        planes,
        list(jobs),
        operands,
        outs,
        scratch,
        "stage",
        cost,
        filler,
        by_rows,
    )
    return (got, moved, made) if filler else (got, moved)


class Attention:
    def __init__(self, parts, q, kv, bias, mkv, causal):
        self.parts, self.causal = parts, causal
        self.q_shape, self.kv_shape = q.shape, kv.shape
        self.rows, self.keys = q.shape[0], kv.shape[0]
        self.chunk = self.rows // (2 * TP)
        self.joint = q is kv
        self.extra = 0 if mkv is None else mkv.shape[0]
        self.total = self.keys + self.extra
        self.bias = bias
        self.blocks = self.rows // (2 * self.chunk)
        self.n_steps = HQ * self.blocks
        self.loads = [q] + ([] if self.joint else [kv])
        self.mem = [mkv] if self.extra else []
        self.raws = []

    def heads(self, *widths_dtypes):
        return [pltpu.VMEM((HQ, n, DH), dtype) for n, dtype in widths_dtypes]

    def split_qkv(self, q_ref, kv_ref, loads, qs, ks, vs):
        at = QC if self.joint else 0
        keys = self.keys
        for i in range(HQ):
            qs[i] = q_ref[:, DH * i : DH * (i + 1)]
            ks[i, :keys] = kv_ref[:, at + DH * i : at + DH * (i + 1)]
            vs[i, :keys] = kv_ref[:, at + QC + DH * i : at + QC + DH * (i + 1)]
        if self.extra:
            mkv_ref = loads.pop(0).get()
            for i in range(HQ):
                ks[i, keys:] = mkv_ref[:, DH * i : DH * (i + 1)]
                vs[i, keys:] = mkv_ref[:, QC + DH * i : QC + DH * (i + 1)]

    def place(self, row_chunk):
        upper = row_chunk // TP
        part = lax.axis_index("part") if self.parts > 1 else 0
        return (upper * (TP * self.parts) + TP * part + (row_chunk - TP * upper)) * self.chunk

    def step_rows(self, i):
        h = i // self.blocks
        b = i - h * self.blocks
        return h, b, pl.ds(pl.multiple_of(b * (2 * self.chunk), 2 * self.chunk), 2 * self.chunk)

    def diagonal(self, b, u):
        return pl.ds(pl.multiple_of(self.keys - self.place(2 * b + u), 128), self.keys)


class AttentionForward(Attention):
    def __init__(self, parts, q, kv, segq, segk, bvec, mkv, causal, products=None):
        super().__init__(parts, q, kv, bvec is not None, mkv, causal)
        self.products = products
        if products:
            self.loads = [v for pair in products for v in pair]
        self.loads += self.mem + [segq, segk] + ([bvec] if self.bias else [])
        self.outs = [
            jax.ShapeDtypeStruct((self.rows, QC), BF),
            jax.ShapeDtypeStruct((HQ, self.rows, self.total), BF),
        ]
        self.scratch = self.heads((self.rows, BF), (self.total, BF), (self.total, BF), (self.rows, BF))
        self.scratch += [
            pltpu.VMEM((2, 2 * self.chunk, self.total), BF),
            pltpu.VMEM((self.rows, QC), BF),
            pltpu.SemaphoreType.DMA((5,)),
        ]
        if self.bias:
            self.scratch.append(pltpu.VMEM((self.chunk, 2 * self.keys), F32))
        if products:
            for x, w in products:
                self.outs.append(jax.ShapeDtypeStruct((x.shape[0], w.shape[1]), BF))
                self.scratch.append(pltpu.VMEM((x.shape[0], w.shape[1]), BF))

    def begin(self, loads, raws, outs, scratch):
        self.att_out, self.p_out = outs[:2]
        self.qs, self.ks, self.vs, self.os, self.p_buf, self.att, self.sems = scratch[:7]
        self.toep = scratch[7] if self.bias else None
        loads = list(loads)
        self.copies = []
        if self.products:
            made = scratch[-len(self.products) :]
            for n, (out, to) in enumerate(zip(made, outs[2:])):
                x, w = loads.pop(0).get(), loads.pop(0).get()

                @pl.loop(0, x.shape[0] // 256)
                def _(r):
                    rows = pl.ds(pl.multiple_of(r * 256, 256), 256)
                    out[rows] = mm(x[rows], w[...]).astype(BF)

                self.copies.append(pltpu.make_async_copy(out, to, self.sems.at[3 + n]))
                self.copies[-1].start()
            q_ref, kv_ref = made[0], made[-1]
        else:
            q_ref = loads.pop(0).get()
            kv_ref = q_ref if self.joint else loads.pop(0).get()
        self.split_qkv(q_ref, kv_ref, loads, self.qs, self.ks, self.vs)
        self.segq, self.segk = loads.pop(0).get(), loads.pop(0).get()
        self.bvec = loads.pop(0).get() if self.bias else None

    def keep(self, i):
        h, b, rows = self.step_rows(i)
        slot = lax.rem(i, 2)
        return pltpu.make_async_copy(self.p_buf.at[slot], self.p_out.at[h, rows], self.sems.at[slot])

    def run(self, low, high):
        keys, chunk = self.keys, self.chunk

        @pl.loop(low, high)
        def _(i):
            h, b, rows = self.step_rows(i)
            slot = lax.rem(i, 2)
            if self.bias:

                @pl.when(b == 0)
                def _():
                    row = jnp.broadcast_to(self.bvec[h], (chunk, 2 * keys))
                    self.toep[...] = pltpu.roll(row, 0, 1, stride=1, stride_axis=0)

            s = mm_nt(self.qs[h, rows], self.ks[h])
            allowed = self.segq[rows] == self.segk[...]
            if self.bias:
                parts = [self.toep[:, self.diagonal(b, u)] for u in range(2)]
                biased = s[:, :keys] + jnp.concatenate(parts, axis=0)
                s = jnp.concatenate([biased, s[:, keys:]], axis=1) if self.extra else biased
            if self.causal:
                row = lax.broadcasted_iota(jnp.int32, (chunk, 1), 0)
                places = jnp.concatenate([row + self.place(2 * b + u) for u in range(2)], axis=0)
                allowed = allowed & (lax.broadcasted_iota(jnp.int32, (1, keys), 1) <= places)
            s = jnp.where(allowed, s, MASKED)
            top = jnp.max(s, axis=-1, keepdims=True)
            e = jnp.exp(s - top)
            p = (e * (1.0 / jnp.sum(e, axis=-1, keepdims=True))).astype(BF)

            @pl.when(i >= 2)
            def _():
                self.keep(i - 2).wait()

            self.p_buf[slot] = p
            self.keep(i).start()
            self.os[h, rows] = mm(p, self.vs[h]).astype(BF)

    def end(self):
        for i in range(HQ):
            self.att[:, DH * i : DH * (i + 1)] = self.os[i]
        out = pltpu.make_async_copy(self.att, self.att_out, self.sems.at[2])
        out.start()
        self.keep(self.n_steps - 2).wait()
        self.keep(self.n_steps - 1).wait()
        out.wait()
        for copy in self.copies:
            copy.wait()


class AttentionBackward(Attention):
    def __init__(self, parts, p, q, kv, up, w_proj, att, bias, mkv, xs, proj=True):
        super().__init__(parts, q, kv, bias, mkv, False)
        self.xs, self.proj = xs if parts == 1 else [], proj
        self.loads += self.mem + [up, w_proj, att] + self.xs
        self.raws = [p]
        rows, total, keys = self.rows, self.total, self.keys
        if self.joint:
            self.outs = [jax.ShapeDtypeStruct((rows, 3 * QC), BF)]
        else:
            kv_type = BF if parts == 1 else F32
            self.outs = [
                jax.ShapeDtypeStruct((rows, QC), BF),
                jax.ShapeDtypeStruct((keys, 2 * QC), kv_type),
            ]
        if bias:
            self.outs.append(jax.ShapeDtypeStruct((HQ, 1, 2 * keys), F32))
        if self.extra:
            self.outs.append(jax.ShapeDtypeStruct((self.extra, 2 * QC), BF))
        if proj:
            self.outs.append(jax.ShapeDtypeStruct((QC, D), BF))
        for n in range(len(self.xs)):
            self.outs.append(jax.ShapeDtypeStruct((D, self.outs[n].shape[1]), BF))
        self.scratch = self.heads(
            (rows, BF), (total, BF), (total, BF), (rows, BF), (rows, BF), (total, F32), (total, F32)
        )
        self.scratch += [
            pltpu.VMEM((HQ, rows, 1), F32),
            pltpu.VMEM((2, 2 * self.chunk, total), BF),
            pltpu.SemaphoreType.DMA((2 + len(self.outs),)),
        ]
        self.scratch += [pltpu.VMEM(o.shape, o.dtype) for o in self.outs]
        if bias:
            self.scratch.append(pltpu.VMEM((self.chunk, 2 * keys), F32))

    def fetch(self, i):
        h, b, rows = self.step_rows(i)
        slot = lax.rem(i, 2)
        return pltpu.make_async_copy(self.p_in.at[h, rows], self.p_buf.at[slot], self.sems.at[slot])

    def begin(self, loads, raws, outs, scratch):
        self.results, (self.p_in,) = outs, raws
        scratch, loads = list(scratch), list(loads)
        self.qs, self.ks, self.vs, self.dos, self.dqs, self.dks, self.dvs = scratch[:7]
        self.rds, self.p_buf, self.sems = scratch[7:10]
        self.made = scratch[10 : 10 + len(outs)]
        self.diag = scratch[-1] if self.bias else None
        self.fetch(0).start()
        q_ref = loads.pop(0).get()
        kv_ref = q_ref if self.joint else loads.pop(0).get()
        self.split_qkv(q_ref, kv_ref, loads, self.qs, self.ks, self.vs)
        up_ref, w_ref, att_ref = (loads.pop(0).get() for _ in range(3))

        @pl.loop(0, self.rows // 256)
        def _(r):
            rows = pl.ds(pl.multiple_of(r * 256, 256), 256)
            grads = mm_nt(up_ref[rows], w_ref[...]).astype(BF)
            att = att_ref[rows]
            for i in range(HQ):
                span = slice(DH * i, DH * (i + 1))
                self.dos[i, rows] = grads[:, span]
                dots = grads[:, span].astype(F32) * att[:, span].astype(F32)
                self.rds[i, rows] = jnp.sum(dots, axis=-1, keepdims=True)

        made = list(self.made)
        self.dq = made.pop(0)
        self.dkv = self.dq if self.joint else made.pop(0)
        self.dbvec = made.pop(0) if self.bias else None
        self.dmkv = made.pop(0) if self.extra else None
        g_proj = made.pop(0) if self.proj else None
        self.g_rows, self.x_loads = made, loads
        if self.proj:

            @pl.loop(0, D // 256)
            def _(n):
                cols = pl.ds(pl.multiple_of(n * 256, 256), 256)
                g_proj[:, cols] = mm_tn(att_ref[...], up_ref[:, cols]).astype(BF)

    def run(self, low, high):
        keys, chunk = self.keys, self.chunk

        @pl.loop(low, high)
        def _(i):
            h, b, rows = self.step_rows(i)
            self.fetch(i).wait()

            @pl.when(i + 1 < self.n_steps)
            def _():
                self.fetch(i + 1).start()

            @pl.when(b == 0)
            def _():
                self.dks[h] = jnp.zeros(self.dks.shape[1:], F32)
                self.dvs[h] = jnp.zeros(self.dvs.shape[1:], F32)
                if self.bias:
                    self.diag[...] = jnp.zeros_like(self.diag)

            q, grad, p = self.qs[h, rows], self.dos[h, rows], self.p_buf[lax.rem(i, 2)]
            dp = mm_nt(grad, self.vs[h])
            ds = (p.astype(F32) * (dp - self.rds[h, rows])).astype(BF)
            self.dqs[h, rows] = mm(ds, self.ks[h]).astype(BF)
            self.dks[h] += mm_tn(ds, q)
            self.dvs[h] += mm_tn(p, grad)
            if self.bias:
                for u in range(2):
                    part = ds[u * chunk : (u + 1) * chunk, :keys]
                    self.diag[:, self.diagonal(b, u)] += part.astype(F32)

                @pl.when(b == self.blocks - 1)
                def _():
                    x = self.diag[...]
                    size = chunk
                    while size > 1:
                        size //= 2
                        x = x[:size] + pltpu.roll(x[size:], 2 * keys - size, 1)
                    self.dbvec[h] = x

    def end(self):
        keys = self.keys
        to = QC if self.joint else 0
        for i in range(HQ):
            self.dq[:, DH * i : DH * (i + 1)] = self.dqs[i]
            at = to + DH * i
            self.dkv[:, at : at + DH] = self.dks[i, :keys].astype(self.dkv.dtype)
            self.dkv[:, at + QC : at + QC + DH] = self.dvs[i, :keys].astype(self.dkv.dtype)
            if self.extra:
                self.dmkv[:, DH * i : DH * (i + 1)] = self.dks[i, keys:].astype(BF)
                self.dmkv[:, QC + DH * i : QC + DH * (i + 1)] = self.dvs[i, keys:].astype(BF)
        for load, out, grad in zip(self.x_loads, self.g_rows, (self.dq, self.dkv)):
            x_ref = load.get()

            @pl.loop(0, D // 256)
            def _(n):
                cols = pl.ds(pl.multiple_of(n * 256, 256), 256)
                out[cols] = mm_tn(x_ref[:, cols], grad[...]).astype(BF)

        copies = [
            pltpu.make_async_copy(src, dst, self.sems.at[2 + n])
            for n, (src, dst) in enumerate(zip(self.made, self.results))
        ]
        for copy in copies:
            copy.start()
        for copy in copies:
            copy.wait()


class Idle:
    n_steps, loads, raws, outs, scratch = 0, [], [], [], []

    def begin(self, loads, raws, outs, scratch):
        pass

    def run(self, low, high):
        pass

    def end(self):
        pass


def attend(number, planes, filler, jobs):
    def kernel(shipper, ins, outs, scratch, filler):
        filler.prefetch()
        shipper.greet(())
        shipper.start()
        filler.begin()
        filler.run(0, filler.n_steps)
        filler.end()
        shipper.finish()

    _, moved, made = call_with_jobs(
        kernel, number, planes, jobs, [], [], [], "attend", 4 * 10**9, filler
    )
    return made, moved


class Chain:
    def __init__(self, value, steps):
        self.value, self.steps = value, steps


ALL = ("seq", "part", "tp", "fsdp")
CTX = ("seq", "part", "tp")


def per_device(
    parts,
    planes,
    enc_input,
    dec_input,
    segments,
    prefix_rows,
    buckets,
    memory,
    enc_gain,
    enc_qkv,
    enc_rel,
    enc_proj,
    enc_ffnorm,
    enc_ffin,
    enc_ffout,
    dec_gain,
    dec_qkv,
    dec_rel,
    dec_proj,
    cross_gain,
    cross_query,
    cross_kv,
    cross_proj,
    dec_ffnorm,
    dec_ffin,
    dec_ffout,
    enc_cotan,
    dec_cotan,
):
    seq, part, tp, plane = (lax.axis_index(name) for name in ALL)
    chunk = enc_input.shape[1]
    length = buckets.shape[0] // 2
    docs, prefix = prefix_rows.shape[1:]

    first = seq == 0
    split = planes * 2

    def joined(x, came):
        mine = lax.dynamic_index_in_dim(x, seq, 0, keepdims=False)
        came = came.astype(x.dtype)
        return jnp.stack([jnp.where(first, mine, came), jnp.where(first, came, mine)])

    def cols(w, start, width=QC):
        return lax.dynamic_slice_in_dim(w, start + width * tp, width, 1)

    def halved(w):
        rows = w.shape[0] // 2
        return lax.dynamic_slice_in_dim(w, rows * seq, rows, 0)

    def qkv_part(w):
        w = halved(w)
        return jnp.concatenate([cols(w, D * i) for i in range(w.shape[1] // D)], axis=1)

    hidden = enc_ffout.shape[0] // TP

    def ffin_part(w):
        w = halved(w)
        return jnp.concatenate(
            [cols(w, hidden * TP * i, hidden) for i in range(planes)], axis=1
        )

    def ffout_part(w):
        rows = hidden // 2
        return lax.dynamic_slice_in_dim(w, hidden * tp + rows * seq, rows, 0)

    def over_planes(w):
        return gather_job("fsdp", w, planes)

    def over_seq(w):
        return gather_job("seq", w, 2, 1)

    def matrix(w):
        return w.reshape(-1, w.shape[-1])

    gains = (enc_gain, enc_ffnorm, dec_gain, cross_gain, dec_ffnorm)
    gain_stack = jnp.stack(gains).astype(F32)
    rel_stack = jnp.stack([enc_rel, dec_rel]).astype(F32)
    segments = segments.reshape(2, 1, chunk)
    first_jobs = [
        swap_job(enc_input),
        gather_job("fsdp", gain_stack, planes),
        gather_job("fsdp", rel_stack, planes),
        over_planes(qkv_part(enc_qkv)),
        over_planes(qkv_part(memory)),
        swap_job(dec_input),
    ]
    if parts == 1:
        first_jobs.append(block_job(segments))
    xe, gain_stack, rel_stack, w_eqkv, table, xd, *segs = ship(0, planes, first_jobs)
    xe, xd = joined(enc_input, xe), joined(dec_input, xd)
    if parts == 1:
        seg = segs[0].reshape(-1)
    else:
        segs = lax.all_gather(segments.reshape(2, chunk), CTX, axis=1, tiled=True)
        seg = lax.dynamic_index_in_dim(segs, seq, 0, keepdims=False)
    per, per_rel = enc_gain.shape[0], enc_rel.size
    g_enc, g_effn, g_dec, g_cross, g_dffn = [
        gain_stack[:, i].reshape(1, D) for i in range(len(gains))
    ]
    rels = [rel_stack[:, i].reshape(BUCKETS, HEADS) for i in range(2)]
    onehot = (buckets[:, None] == jnp.arange(BUCKETS, dtype=jnp.int32)[None, :]).astype(BF)

    def bias_vector(rel):
        own = lax.dynamic_slice_in_dim(rel, HQ * tp, HQ, 1).astype(BF)
        return lax.dot_general(
            own, onehot, (((0,), (1,)), ((), ())), preferred_element_type=F32
        ).reshape(HQ, 1, 2 * length)

    turned = planes == TP

    def proj_jobs(w):
        return [turn_job(w)] if turned else []

    def proj_of(got, w):
        if turned:
            return got.pop()
        full = lax.all_gather(w, "fsdp", axis=0, tiled=True)
        return lax.dynamic_slice_in_dim(full, QC * tp, QC, 0)

    en, (w_eqkv, table, w_dqkv, *got), _ = gather_norm(
        1,
        planes,
        xe,
        g_enc,
        [over_seq(w_eqkv), over_seq(table), over_planes(qkv_part(dec_qkv))] + proj_jobs(enc_proj),
    )
    w_eproj = proj_of(got, enc_proj)
    w_eqkv, table = matrix(w_eqkv), matrix(table)

    segq = lax.dynamic_index_in_dim(seg.reshape(2, parts, TP * chunk), part, 1, keepdims=False)
    segq = segq.reshape(-1, 1)
    segk = seg.reshape(1, length)
    ids = lax.dynamic_index_in_dim(prefix_rows, seq, 0, keepdims=False).reshape(-1)
    extra = -(-(docs * prefix) // 256) * 256
    ids = jnp.concatenate([ids, jnp.full((extra - docs * prefix,), -1, jnp.int32)])
    mem_doc = np.full((extra,), -1, np.int32)
    mem_doc[: docs * prefix] = np.arange(docs * prefix) // prefix
    segk_mem = jnp.concatenate([segk, jnp.asarray(mem_doc)[None]], axis=1)
    pick = (ids[:, None] == jnp.arange(table.shape[0], dtype=jnp.int32)[None, :]).astype(BF)
    mkv = mm(pick, table).astype(BF)

    def spread(kv):
        if parts == 1:
            return kv
        got = lax.all_gather(kv, "part", axis=0)
        return got.reshape(parts, 2, TP * chunk, -1).transpose(1, 0, 2, 3).reshape(length, -1)

    def collect(dkv):
        if parts == 1:
            return dkv
        split = dkv.reshape(2, parts, TP * chunk, -1).transpose(1, 0, 2, 3)
        split = split.reshape(parts * 2 * TP * chunk, -1)
        return lax.psum_scatter(split, "part", scatter_dimension=0, tiled=True).astype(BF)

    def self_kv(rows):
        return (rows, rows) if parts == 1 else (rows[:, :QC], spread(rows[:, QC:]))

    def joint_grad(got):
        if parts == 1:
            return got.pop(0)
        return jnp.concatenate([got.pop(0), collect(got.pop(0))], axis=1)

    def self_fill(x, w, segk_now, bvec, mem, causal):
        if parts == 1:
            rows = jax.ShapeDtypeStruct((x.shape[0], w.shape[1]), BF)
            return AttentionForward(
                parts, rows, rows, segq, segk_now, bvec, mem, causal, [(x, w)]
            ), None
        rows = self_kv(mm(x, w).astype(BF))
        return AttentionForward(parts, *rows, segq, segk_now, bvec, mem, causal), rows

    def self_made(got, rows):
        return got[0], got[1], rows or (got[2], got[2])

    e_fill, e_qkv = self_fill(en, w_eqkv, segk_mem, bias_vector(rels[0]), mkv, False)
    dn, (w_dqkv, w_effin, *got), made = gather_norm(
        2,
        planes,
        xd,
        g_dec,
        [
            over_seq(w_dqkv),
            over_planes(ffin_part(enc_ffin)),
        ]
        + proj_jobs(dec_proj),
        e_fill,
    )
    e_att, e_p, e_qkv = self_made(made, e_qkv)
    w_dproj = proj_of(got, dec_proj)
    w_dqkv = matrix(w_dqkv)
    d_fill, d_qkv = self_fill(dn, w_dqkv, segk, bias_vector(rels[1]), None, True)
    (e_mid, e_fn), (w_effin, w_effout, w_cq, w_ckv), made = stage(
        3,
        planes,
        [e_att],
        w_eproj,
        xe,
        gather="norm",
        gain=g_effn,
        jobs=[
            over_seq(w_effin),
            over_planes(ffout_part(enc_ffout)),
            over_planes(qkv_part(cross_query)),
            over_planes(qkv_part(cross_kv)),
        ],
        filler=d_fill,
    )
    d_att, d_p, d_qkv = self_made(made, d_qkv)
    w_effin = matrix(w_effin)
    (d_mid, c_n), (w_effout, w_cq, w_ckv, w_dffin, *got) = stage(
        4,
        planes,
        [d_att],
        w_dproj,
        xd,
        gather="norm",
        gain=g_cross,
        jobs=[
            over_seq(w_effout),
            over_seq(w_cq),
            over_seq(w_ckv),
            over_planes(ffin_part(dec_ffin)),
        ]
        + proj_jobs(cross_proj),
    )
    w_cproj = proj_of(got, cross_proj)
    w_effout, w_cq, w_ckv = matrix(w_effout), matrix(w_cq), matrix(w_ckv)
    (e_low, e_gath, e_pre, e_act), (w_dffin, w_dffout, xdc) = stage(
        5,
        planes,
        [e_fn, w_effin],
        w_effout,
        e_mid,
        maker=FeedForward,
        gather="low",
        dtype=BF,
        jobs=[over_seq(w_dffin), over_planes(ffout_part(dec_ffout)), swap_job(dec_cotan)],
    )
    xdc = joined(dec_cotan, xdc)
    w_dffin = matrix(w_dffin)
    products = None
    if parts == 1:
        c_q = jax.ShapeDtypeStruct((c_n.shape[0], QC), BF)
        c_kv = jax.ShapeDtypeStruct((e_gath.shape[0], 2 * QC), BF)
        products = [(c_n, w_cq), (e_gath, w_ckv)]
    else:
        c_q = mm(c_n, w_cq).astype(BF)
        c_kv = spread(mm(e_gath, w_ckv).astype(BF))
    c_fill = AttentionForward(parts, c_q, c_kv, segq, segk, None, None, False, products)
    (c_att, c_p, *made), (w_dffout,) = attend(19, planes, c_fill, [over_seq(w_dffout)])
    if parts == 1:
        c_q, c_kv = made
    w_dffout = matrix(w_dffout)
    (d_cross, d_fn), (came, xec) = stage(
        6,
        planes,
        [c_att],
        w_cproj,
        d_mid,
        gather="norm",
        gain=g_dffn,
        jobs=[swap_job(e_low), swap_job(enc_cotan)],
    )
    enc_output, xec = joined(e_low, came), joined(enc_cotan, xec)
    (d_low, up_g, d_pre, d_act), _ = stage(
        7,
        planes,
        [d_fn, w_dffin],
        w_dffout,
        d_cross,
        maker=FeedForward,
        gather="given",
        given=xdc,
        dtype=BF,
    )

    def pieces(g):
        if parts > 1:
            g = lax.psum(g, "part")
        return g.reshape(planes, 2, g.shape[0] // split, g.shape[1])

    def to_ctx(width):
        return [
            lambda g: gather_job("across", g),
            lambda g: gather_job("seq", g),
            lambda g: last_job(g, width),
        ]

    def chain(g, width):
        steps = [lambda g: swap_job(g, 1, True), lambda g: deal_job("fsdp", g)]
        return Chain(pieces(g), steps + to_ctx(width))

    def proj_chain(g):
        if not turned:
            return Chain(g, [])
        steps = [lambda g: swap_job(g, "cols", True), lambda g: deal_job("fsdp", g), turn_job]
        return Chain(g.reshape(planes, -1, D), steps + to_ctx(-1))

    def steps_of(chains):
        return [c.steps[0](c.value) for c in chains if c.steps]

    def settle(chains, got):
        got = list(got)
        for c in chains:
            if c.steps:
                c.value = got.pop(0)
                c.steps.pop(0)
        return got

    k_dffout = chain(mm_tn(d_act, up_g).astype(BF), 0)
    moving = [k_dffout]
    (up, up_rows, dg_dffn, pre_grad), got = stage(
        8,
        planes,
        [up_g, d_pre, w_dffout],
        w_dffin,
        xdc,
        flip=True,
        maker=FeedForwardBack,
        back=(d_cross, g_dffn),
        gather="low",
        jobs=steps_of(moving) + [swap_job(d_low)],
    )
    (came,) = settle(moving, got)
    dec_output = joined(d_low, came)
    k_dffin = chain(mm_tn(d_fn, pre_grad).astype(BF), hidden)
    c_fill = AttentionBackward(
        parts, c_p, c_q, c_kv, up_rows, w_cproj, c_att, False, None, [c_n, e_gath]
    )
    moving = [k_dffin, k_dffout]
    (c_dq, c_dkv, g_cproj, *made), got = attend(20, planes, c_fill, steps_of(moving))
    settle(moving, got)
    c_dkv = collect(c_dkv)
    if parts > 1:
        made = [mm_tn(c_n, c_dq).astype(BF), mm_tn(e_gath, c_dkv).astype(BF)]
    k_cproj, k_cq, k_ckv = proj_chain(g_cproj), chain(made[0], QC), chain(made[1], QC)
    moving = [k_dffin, k_dffout, k_cq, k_ckv, k_cproj]
    (up, up_rows, dg_cross), got = stage(
        9,
        planes,
        [c_dq],
        w_cq,
        up,
        flip=True,
        back=(d_mid, g_cross),
        gather="low",
        jobs=steps_of(moving),
    )
    settle(moving, got)

    def self_grads(made, x):
        grad = joint_grad(made)
        g_rows = made.pop() if parts == 1 else mm_tn(x, grad).astype(BF)
        return grad, chain(g_rows, QC), made

    d_fill = AttentionBackward(
        parts, d_p, *d_qkv, up_rows, w_dproj, d_att, True, None, [dn]
    )
    (e_up, e_up_rows), got, made = stage(
        10,
        planes,
        [c_dkv],
        w_ckv,
        xec,
        flip=True,
        gather="low",
        jobs=steps_of(moving),
        filler=d_fill,
    )
    settle(moving, got)
    d_rows_grad, k_dqkv, (d_dbv, g_dproj) = self_grads(made, dn)
    k_dproj = proj_chain(g_dproj)
    k_effout = chain(mm_tn(e_act, e_up_rows).astype(BF), 0)
    moving = [k_dffout, k_cq, k_ckv, k_cproj, k_dqkv, k_dproj, k_effout]
    (e_up, e_up_rows, dg_effn, pre_grad), got = stage(
        12,
        planes,
        [e_up_rows, e_pre, w_effout],
        w_effin,
        e_up,
        flip=True,
        maker=FeedForwardBack,
        back=(e_mid, g_effn),
        gather="low",
        jobs=steps_of(moving),
    )
    settle(moving, got)
    k_effin = chain(mm_tn(e_fn, pre_grad).astype(BF), hidden)
    e_fill = AttentionBackward(
        parts, e_p, *e_qkv, e_up_rows, w_eproj, e_att, True, mkv, [en], False
    )
    k_eproj = proj_chain(mm_tn(e_att, e_up_rows).astype(BF))
    moving = [k_dffin, k_cq, k_ckv, k_cproj, k_dqkv, k_dproj, k_effout, k_effin, k_eproj]
    (d_in, dg_dec), got, made = stage(
        11,
        planes,
        [d_rows_grad],
        w_dqkv,
        up,
        flip=True,
        back=(xd, g_dec),
        jobs=steps_of(moving),
        filler=e_fill,
    )
    settle(moving, got)
    e_rows_grad, k_eqkv, (e_dbv, d_mkv) = self_grads(made, en)
    k_table = chain(mm_tn(pick, d_mkv).astype(BF), QC)
    moving += [k_eqkv, k_table]
    (e_in, dg_enc), got = stage(
        13,
        planes,
        [e_rows_grad],
        w_eqkv,
        e_up,
        flip=True,
        back=(xe, g_enc),
        jobs=steps_of(moving) + [swap_job(d_in.astype(BF))],
    )
    (came,) = settle(moving, got)
    dec_ingrad = joined(d_in, came)
    def rel_grad(dbv):
        own = lax.dot_general(
            onehot.astype(F32),
            dbv.reshape(HQ, -1),
            (((0,), (1,)), ((), ())),
            precision=lax.Precision.HIGHEST,
            preferred_element_type=F32,
        )
        return lax.dynamic_update_slice_in_dim(jnp.zeros((BUCKETS, HEADS), F32), own, HQ * tp, 1)

    tiny = [dg_enc, dg_effn, dg_dec, dg_cross, dg_dffn]
    tiny = jnp.concatenate([v.reshape(planes, -1) for v in tiny] + [
        rel_grad(v).reshape(planes, -1) for v in (e_dbv, d_dbv)
    ], axis=1)
    tiny = tiny.reshape(-1, 128)
    if parts > 1:
        tiny = lax.psum(tiny, "part")
    swapped = [swap_job(e_in.astype(BF))]
    for number, axis in enumerate(("fsdp", "seq", "across", "core", None)):
        if axis is None and not steps_of(moving):
            break
        total = [total_job(axis, tiny, planes if axis == "fsdp" else 2)] if axis else []
        got = ship(14 + number, planes, total + swapped + steps_of(moving))
        if axis:
            tiny, *got = got
        if swapped:
            enc_ingrad = joined(e_in, got.pop(0))
            swapped = []
        settle(moving, got)

    def proj_rows(k):
        if turned:
            return k.value
        full = lax.dynamic_update_slice_in_dim(jnp.zeros((D, D), BF), k.value, QC * tp, 0)
        full = lax.psum_scatter(full, "fsdp", scatter_dimension=0, tiled=True)
        return lax.psum(full.astype(F32), CTX)

    o_eproj, o_dproj, o_cproj = (proj_rows(k) for k in (k_eproj, k_dproj, k_cproj))
    o_dffin, o_dffout, o_effin, o_effout, o_cq, o_ckv, o_dqkv, o_eqkv, o_table = (
        k.value
        for k in (k_dffin, k_dffout, k_effin, k_effout, k_cq, k_ckv, k_dqkv, k_eqkv, k_table)
    )
    tiny = lax.dynamic_index_in_dim(tiny.reshape(planes, -1), plane, 0, keepdims=False)
    o_gains = [tiny[per * i : per * (i + 1)] for i in range(5)]
    o_rels = [
        tiny[5 * per + per_rel * i : 5 * per + per_rel * (i + 1)].reshape(-1, HEADS)
        for i in range(2)
    ]
    return (
        enc_output,
        dec_output,
        enc_ingrad,
        dec_ingrad,
        o_table,
        o_gains[0],
        o_eqkv,
        o_rels[0],
        o_eproj,
        o_gains[1],
        o_effin,
        o_effout,
        o_gains[2],
        o_dqkv,
        o_rels[1],
        o_dproj,
        o_gains[3],
        o_cq,
        o_ckv,
        o_cproj,
        o_gains[4],
        o_dffin,
        o_dffout,
    )


def solution(mesh):
    ctx, planes = mesh.shape["ctx"], mesh.shape["fsdp"]
    parts = ctx // (2 * TP)
    inner = Mesh(np.asarray(mesh.devices).reshape(2, parts, TP, planes), ALL)
    rows3 = P("fsdp", CTX, None)
    mat, vec = P("fsdp", None), P("fsdp")
    args = (
        (rows3, rows3, P("fsdp", CTX), P("fsdp", None, None), P(), mat)
        + (vec, mat, mat, mat, vec, mat, mat)
        + (vec, mat, mat, mat)
        + (vec, mat, mat, mat)
        + (vec, mat, mat)
        + (rows3, rows3)
    )
    outs = (
        (rows3, rows3, rows3, rows3, mat)
        + (vec, mat, mat, mat, vec, mat, mat)
        + (vec, mat, mat, mat)
        + (vec, mat, mat, mat)
        + (vec, mat, mat)
    )
    return jax.shard_map(
        functools.partial(per_device, parts, planes),
        mesh=inner,
        in_specs=args,
        out_specs=outs,
        check_vma=False,
    )
```

```python
import collections
import functools

import jax
import jax.numpy as jnp
import numpy as np
from jax import lax
from jax.experimental import pallas as pl
from jax.experimental.pallas import tpu as pltpu
from jax.sharding import Mesh
from jax.sharding import PartitionSpec as P

D = 768
HEADS = 12
DH = 64
BUCKETS = 32
EPS = 1e-06
MASKED = -1e30
TP = 4
HQ = HEADS // TP
QC = HQ * DH
BF = jnp.bfloat16
F32 = jnp.float32
MESH_ID = pl.DeviceIdType.MESH
MB = 1024 * 1024
VMEM_LIMIT = 60 * MB
SHARE = (0.25, 0.34, 0.75)


def mm(a, b):
    return jnp.dot(a, b, preferred_element_type=F32)


def mm_tn(a, b):
    return lax.dot_general(a, b, (((0,), (0,)), ((), ())), preferred_element_type=F32)


def mm_nt(a, b):
    return lax.dot_general(a, b, (((1,), (1,)), ((), ())), preferred_element_type=F32)


def gelu(v):
    return jax.nn.gelu(v, approximate=True)


def gelu_back(pre, grad):
    return jax.vjp(gelu, pre)[1](grad)[0]


def group_ids():
    me = lax.axis_index("tp")
    core = me + 1 - 2 * lax.rem(me, 2)
    across = lax.rem(me + 2, TP)
    far = lax.rem(core + 2, TP)
    return me, core, across, far


def send(src, dst, send_sem, recv_sem, peer):
    return pltpu.make_async_remote_copy(
        src_ref=src,
        dst_ref=dst,
        send_sem=send_sem,
        recv_sem=recv_sem,
        device_id={"tp": peer},
        device_id_type=MESH_ID,
    )


def normed(values, gains):
    return values * lax.rsqrt(jnp.mean(values * values, axis=-1, keepdims=True) + EPS) * gains


class Gatherer:
    def __init__(self, buf, stage, sems, chunk, ids):
        self.buf, self.stage, self.sems, self.chunk, self.ids = buf, stage, sems, chunk, ids
        self.sends, self.own = [], []

    def rows(self, j, owner):
        return self.buf.at[pl.ds(pl.multiple_of((TP * j + owner) * self.chunk, self.chunk), self.chunk)]

    def put(self, j, value):
        me, core, across, far = self.ids
        mine = self.stage.at[j]
        mine[...] = value
        x_copy = send(mine, self.rows(j, me), self.sems.at[0, j], self.sems.at[1, j], across)
        x_copy.start()
        c_copy = send(mine, self.rows(j, me), self.sems.at[2, j], self.sems.at[3, j], core)
        c_copy.start()
        self.sends += [x_copy, c_copy]
        own = pltpu.make_async_copy(mine, self.rows(j, me), self.sems.at[6, j])
        own.start()
        self.own.append(own)

    def forward(self, j):
        me, core, across, far = self.ids
        theirs = self.rows(j, across)
        send(theirs, theirs, self.sems.at[0, j], self.sems.at[1, j], across).wait_recv()
        f_copy = send(theirs, theirs, self.sems.at[4, j], self.sems.at[5, j], core)
        f_copy.start()
        self.sends.append(f_copy)

    def finish(self):
        me, core, across, far = self.ids
        for j in range(2):
            a = self.rows(j, core)
            send(a, a, self.sems.at[2, j], self.sems.at[3, j], core).wait_recv()
            b = self.rows(j, far)
            send(b, b, self.sems.at[4, j], self.sems.at[5, j], core).wait_recv()
        for copy in self.sends:
            copy.wait_send()
        for copy in self.own:
            copy.wait()


Job = collections.namedtuple("Job", ["axis", "src_axis", "dst_axis", "local", "src", "shape", "finish"])


def gather_job(axis, src, size=2, at=0):
    shape = src.shape[:at] + (size,) + src.shape[at:]
    return Job(axis, None, at, True, src, shape, None)


def total_job(axis, src, size=2):
    return gather_job(axis, src, size)._replace(finish="sum")


def deal_job(axis, src):
    return Job(axis, 0, 0, True, src, src.shape, "sum")


def swap_job(src, at=0, add=False):
    if at == "cols":
        shape = src.shape[:-1] + (src.shape[-1] // 2,)
    else:
        shape = src.shape[:at] + src.shape[at + 1 :]
    return Job("seq", at, None, add, src, shape, "add" if add else None)


def turn_job(src):
    return Job("turn", None, None, True, src, src.shape, None)


def block_job(src):
    return Job("ctx", 0, 0, True, src, (2 * TP,) + src.shape[1:], None)


def spread_job(src, add=False):
    return Job("all", None, None, True, src, (2, 2, 2) + src.shape, "sum3" if add else None)


def result_of(job):
    skip = {"sum": 1, "sum3": 3}.get(job.finish, 0)
    return job.shape[skip:], job.src.dtype


def entry(ref, axis, index):
    if axis == "cols":
        half = ref.shape[-1] // 2
        return ref.at[:, :, pl.ds(pl.multiple_of(index * half, half), half)]
    return ref if axis is None else ref.at[(slice(None),) * axis + (index,)]


class Shipper:
    def __init__(self, jobs, planes, srcs, outs, scratch, sems):
        self.jobs, self.planes, self.srcs, self.outs, self.sems = jobs, planes, srcs, outs, sems
        self.tp, self.seq, self.plane = (lax.axis_index(n) for n in ("tp", "seq", "fsdp"))
        self.dsts, self.bounce, self.made = [], [], []
        for job, out in zip(jobs, outs):
            if job.finish:
                self.dsts.append(scratch.pop(0))
                self.bounce.append(scratch.pop(0) if job.finish == "add" else None)
                self.made.append(scratch.pop(0) if job.finish != "add" else None)
            else:
                self.dsts.append(out)
                self.bounce.append(scratch.pop(0) if job.local else None)
                self.made.append(None)

    @staticmethod
    def scratch(jobs):
        shapes = []
        for job in jobs:
            dtype = job.src.dtype
            if job.finish:
                shapes.append(pltpu.VMEM(job.shape, dtype))
                if job.finish == "add":
                    shapes.append(pltpu.VMEM(job.shape, dtype))
                else:
                    shapes.append(pltpu.VMEM(*result_of(job)))
            elif job.axis == "all":
                shapes.append(pltpu.VMEM(job.src.shape, dtype))
            elif job.local:
                drop = job.dst_axis
                own = job.shape if drop is None else job.shape[:drop] + job.shape[drop + 1 :]
                shapes.append(pltpu.VMEM(own, dtype))
        return shapes

    @staticmethod
    def count(jobs, planes):
        return sum(2 * Shipper.n_peers(job, planes) + 2 for job in jobs)

    @staticmethod
    def n_peers(job, planes):
        return {"fsdp": planes - 1, "ctx": 2 * TP - 1, "all": 2 * TP - 1}.get(job.axis, 1)

    def coord(self, axis):
        half = self.tp // 2
        return {
            "fsdp": self.plane,
            "seq": self.seq,
            "across": half,
            "core": self.tp - 2 * half,
            "ctx": TP * self.seq + self.tp,
            "turn": None,
        }[axis]

    def peers(self, axis):
        if axis == "fsdp":
            n, z = self.planes, self.plane
            for k in range(1, n):
                to = lax.rem(z + k, n)
                yield to, {"fsdp": to}, lax.rem(z + (n - k), n)
        elif axis == "ctx":
            for k in range(1, 2 * TP):
                to = lax.rem(self.seq + k // TP, 2)
                to_tp = lax.rem(self.tp + k % TP, TP)
                from_seq = lax.rem(self.seq + (2 - k // TP), 2)
                from_tp = lax.rem(self.tp + (TP - k % TP), TP)
                yield to, {"seq": to, "tp": to_tp}, TP * from_seq + from_tp
        elif axis == "seq":
            yield 1 - self.seq, {"seq": 1 - self.seq}, 1 - self.seq
        elif axis == "turn":
            yield None, {"fsdp": self.tp, "tp": self.plane}, None
        else:
            to = lax.rem(self.tp + 2, TP) if axis == "across" else self.tp + 1 - 2 * lax.rem(self.tp, 2)
            other = 1 - self.coord(axis)
            yield other, {"tp": to}, other

    def signal(self, always=("core", "across")):
        wanted = {job.axis for job in self.jobs}
        if "all" in wanted:
            wanted = (wanted - {"all"}) | {"seq", "across", "core"}
        axes = list(always) + sorted(wanted - set(always))
        barrier = pltpu.get_barrier_semaphore()
        self.expected, self.turns = 0, "turn" in axes
        for axis in axes:
            for _, device, _ in self.peers(axis):
                if axis == "turn":

                    @pl.when(self.plane != self.tp)
                    def _():
                        pl.semaphore_signal(
                            barrier, inc=1, device_id=device, device_id_type=MESH_ID
                        )

                    continue
                pl.semaphore_signal(barrier, inc=1, device_id=device, device_id_type=MESH_ID)
                self.expected += 1

    def met(self):
        barrier = pltpu.get_barrier_semaphore()
        if self.turns:
            moves = self.plane != self.tp

            @pl.when(moves)
            def _():
                pl.semaphore_wait(barrier, self.expected + 1)

            @pl.when(jnp.logical_not(moves))
            def _():
                pl.semaphore_wait(barrier, self.expected)
        else:
            pl.semaphore_wait(barrier, self.expected)

    def greet(self, always=("core", "across")):
        self.signal(always)
        self.met()

    def each(self, act_remote, act_local):
        base = 0
        for n, (job, src, dst) in enumerate(zip(self.jobs, self.srcs, self.dsts)):
            if job.axis == "all":
                base += 2 * self.n_peers(job, self.planes) + 2
                continue
            mine = self.coord(job.axis)
            peers = list(self.peers(job.axis))
            for i, (to, device, source) in enumerate(peers):
                sems = (self.sems.at[base + 2 * i], self.sems.at[base + 2 * i + 1])

                def copy_into(slot, to=to, device=device, sems=sems, src=src, dst=dst, job=job):
                    return pltpu.make_async_remote_copy(
                        src_ref=entry(src, job.src_axis, to),
                        dst_ref=entry(dst, job.dst_axis, slot),
                        send_sem=sems[0],
                        recv_sem=sems[1],
                        device_id=device,
                        device_id_type=MESH_ID,
                    )

                def remote(copy_into=copy_into, source=source, mine=mine):
                    act_remote(copy_into, mine, source)

                if job.axis == "turn":
                    pl.when(self.plane != self.tp)(remote)
                else:
                    remote()
            if job.local:
                own = self.seq if job.axis == "ctx" else mine

                def local(n=n, job=job, src=src, dst=dst, own=own, mine=mine, sem=base + 2 * len(peers)):
                    here, there = entry(src, job.src_axis, own), entry(dst, job.dst_axis, mine)
                    bounce = self.bounce[n]
                    if bounce is None:
                        act_local([(here, there)], self.sems.at[sem])
                    elif job.finish == "add":
                        act_local([(here, bounce)], self.sems.at[sem])
                    else:
                        act_local([(here, bounce), (bounce, there)], self.sems.at[sem])

                if job.axis == "turn":
                    pl.when(self.plane == self.tp)(local)
                else:
                    local()
            base += 2 * len(peers) + 2
        return base

    def spreads(self):
        s, x, c = self.coord("seq"), self.coord("across"), self.coord("core")
        seq, across, core = (next(self.peers(axis))[1] for axis in ("seq", "across", "core"))
        moves = [
            ((s, x, c), across, (s, 1 - x, c)),
            ((s, x, c), seq, (1 - s, x, c)),
            ((s, x, c), core, (s, x, 1 - c)),
            ((s, 1 - x, c), seq, (1 - s, 1 - x, c)),
            ((s, 1 - x, c), core, (s, 1 - x, 1 - c)),
            ((1 - s, x, c), core, (1 - s, x, 1 - c)),
            ((1 - s, 1 - x, c), core, (1 - s, 1 - x, 1 - c)),
        ]
        base = 0
        for job, src, dst, bounce in zip(self.jobs, self.srcs, self.dsts, self.bounce):
            if job.axis == "all":

                def copy(k, arrives=False, src=src, dst=dst, base=base):
                    what, device, other = moves[k]
                    return pltpu.make_async_remote_copy(
                        src_ref=src if k < 3 else dst.at[what],
                        dst_ref=dst.at[other if arrives else what],
                        send_sem=self.sems.at[base + 2 * k],
                        recv_sem=self.sems.at[base + 2 * k + 1],
                        device_id=device,
                        device_id_type=MESH_ID,
                    )

                own = dst.at[s, x, c]
                legs = [(src, own)] if bounce is None else [(src, bounce), (bounce, own)]
                legs = [
                    pltpu.make_async_copy(*leg, self.sems.at[base + 14 + n])
                    for n, leg in enumerate(legs)
                ]
                yield copy, legs
            base += 2 * self.n_peers(job, self.planes) + 2

    def start_spreads(self):
        for copy, legs in self.spreads():
            for k in range(3):
                copy(k).start()
            legs[0].start()

    def finish_spreads(self):
        jobs = list(self.spreads())
        for copy, legs in jobs:
            if len(legs) > 1:
                legs[0].wait()
                legs[1].start()
        for first, then in ((0, (3, 4)), (1, (5,)), (3, (6,))):
            for copy, legs in jobs:
                copy(first, True).wait_recv()
                for k in then:
                    copy(k).start()
        for copy, legs in jobs:
            for k in (2, 4, 5, 6):
                copy(k, True).wait_recv()
            for k in range(7):
                copy(k).wait_send()
            legs[-1].wait()

    def start(self):
        if any(job.axis == "all" for job in self.jobs):
            self.start_spreads()
        self.each(
            lambda copy_into, mine, source: copy_into(mine).start(),
            lambda legs, sem: pltpu.make_async_copy(*legs[0], sem).start(),
        )

    def finish(self):
        def turn_round(legs, sem):
            if len(legs) > 1:
                pltpu.make_async_copy(*legs[0], sem).wait()
                pltpu.make_async_copy(*legs[1], sem).start()

        def remote(copy_into, mine, source):
            copy_into(source).wait_recv()
            copy_into(mine).wait_send()

        if any(job.axis == "all" for job in self.jobs):
            self.finish_spreads()
        self.each(lambda *_: None, turn_round)
        self.each(remote, lambda legs, sem: pltpu.make_async_copy(*legs[-1], sem).wait())
        stores, base = [], 0
        for job, dst, bounce, made, out in zip(
            self.jobs, self.dsts, self.bounce, self.made, self.outs
        ):
            base += 2 * self.n_peers(job, self.planes) + 2
            if not job.finish:
                continue
            if job.finish == "add":
                made = bounce

                @pl.loop(0, dst.shape[0])
                def _(i):
                    bounce[i] = (bounce[i].astype(F32) + dst[i].astype(F32)).astype(bounce.dtype)

            else:
                pieces = [dst.at[i] for i in range(dst.shape[0])]
                if job.finish == "sum3":
                    pieces = [dst.at[i, j, k] for i in range(2) for j in range(2) for k in range(2)]
                total = pieces[0][...].astype(F32)
                for piece in pieces[1:]:
                    total = total + piece[...].astype(F32)
                made[...] = total.astype(made.dtype)
            store = pltpu.make_async_copy(made, out, self.sems.at[base - 1])
            store.start()
            stores.append(store)
        for store in stores:
            store.wait()


def lay_out(src, dst, width):
    seqs, halves, cores, rows, cols = src.shape
    if width < 0:
        for i in range(seqs):
            for q in range(TP):
                block = slice(i * cols, (i + 1) * cols)
                dst[q * rows : (q + 1) * rows, block] = src[i, q // 2, q % 2].astype(F32)
        return

    @pl.loop(0, seqs)
    def _(i):
        if not width:
            for q in range(TP):
                at = pl.multiple_of((q * seqs + i) * rows, rows)
                dst[pl.ds(at, rows)] = src[i, q // 2, q % 2].astype(F32)
        else:
            at = pl.multiple_of(i * rows, rows)
            for n in range(cols // width):
                span = slice(n * width, (n + 1) * width)
                parts = [src[i, q // 2, q % 2, :, span].astype(F32) for q in range(TP)]
                block = slice(n * width * TP, (n + 1) * width * TP)
                dst[pl.ds(at, rows), block] = jnp.concatenate(parts, axis=1)


def laid_out(pieces, widths):
    shapes = []
    for p, width in zip(pieces, widths):
        seqs, halves, cores, rows, cols = p.shape
        if width < 0:
            shapes.append((halves * cores * rows, seqs * cols))
        elif width:
            shapes.append((seqs * rows, halves * cores * cols))
        else:
            shapes.append((seqs * halves * cores * rows, cols))
    n = len(pieces)

    def body(*refs):
        srcs, outs, got, made, sems = refs[:n], refs[n : 2 * n], refs[2 * n : 3 * n], refs[3 * n : 4 * n], refs[4 * n]
        loads = [pltpu.make_async_copy(srcs[i], got[i], sems.at[0, i]) for i in range(n)]
        stores = [pltpu.make_async_copy(made[i], outs[i], sems.at[1, i]) for i in range(n)]
        for load in loads:
            load.start()
        for i in range(n):
            loads[i].wait()
            lay_out(got[i], made[i], widths[i])
            stores[i].start()
        for store in stores:
            store.wait()

    return pl.pallas_call(
        body,
        out_shape=tuple(jax.ShapeDtypeStruct(shape, F32) for shape in shapes),
        in_specs=[HBM_SPEC] * n,
        out_specs=(HBM_SPEC,) * n,
        scratch_shapes=[pltpu.VMEM(p.shape, p.dtype) for p in pieces]
        + [pltpu.VMEM(shape, F32) for shape in shapes]
        + [pltpu.SemaphoreType.DMA((2, n))],
        compiler_params=pltpu.CompilerParams(vmem_limit_bytes=VMEM_LIMIT),
        name="lay_out",
    )(*pieces)


HBM_SPEC = pl.BlockSpec(memory_space=pltpu.HBM)


class Loaded:
    def __init__(self, src, dst, sem, start=True):
        self.copy, self.ref, self.waited = pltpu.make_async_copy(src, dst, sem), dst, False
        if start:
            self.copy.start()

    def get(self):
        if not self.waited:
            self.copy.wait()
            self.waited = True
        return self.ref


class LoadedRows:
    def __init__(self, src, dst, sems, chunk):
        self.src, self.ref, self.sems, self.chunk = src, dst, sems, chunk

    def copies(self, owner, slot):
        for j in range(2):
            at = pl.multiple_of((TP * j + owner) * self.chunk, self.chunk)
            rows = pl.ds(at, self.chunk)
            yield pltpu.make_async_copy(
                self.src.at[rows], self.ref.at[rows], self.sems.at[2 * slot + j]
            )

    def start(self, owners):
        for slot, owner in enumerate(owners):
            for copy in self.copies(owner, slot):
                copy.start()

    def wait(self, owner, slot):
        for copy in self.copies(owner, slot):
            copy.wait()


def call_with_jobs(
    kernel, number, planes, jobs, operands, outs, scratch, name, cost, filler=None, by_rows=()
):
    filler = filler or Idle()
    jobs = list(jobs)
    n_in, n_out, n_job = len(operands), len(outs), len(jobs)
    n_load, n_raw, n_fill = len(filler.loads), len(filler.raws), len(filler.outs)
    loads, raws = list(filler.loads), list(filler.raws)
    n_sems = max(Shipper.count(jobs, planes), 1)
    plain = [job._replace(src=jax.ShapeDtypeStruct(job.src.shape, job.src.dtype)) for job in jobs]
    job_scratch = Shipper.scratch(jobs)
    n_scratch = len(filler.scratch)

    def body(*refs):
        refs = list(refs)

        def take(n):
            out = refs[:n]
            del refs[:n]
            return out

        ins, srcs, fills, raw = take(n_in), take(n_job), take(n_load), take(n_raw)
        results, dsts, fill_outs = take(n_out), take(n_job), take(n_fill)
        sems, in_sems, row_sems = take(3)
        loaded = []
        for i, src in enumerate(ins):
            if i in by_rows:
                rows = row_sems.at[by_rows.index(i)]
                loaded.append(LoadedRows(src, refs.pop(0), rows, src.shape[0] // (2 * TP)))
            else:
                loaded.append(Loaded(src, refs.pop(0), in_sems.at[i]))
        fill_loads = [
            Loaded(src, refs.pop(0), in_sems.at[n_in + i], False) for i, src in enumerate(fills)
        ]
        shipper = Shipper(plain, planes, srcs, dsts, take(len(job_scratch)), sems)
        begin = functools.partial(filler.begin, fill_loads, raw, fill_outs, take(n_scratch))
        kernel(shipper, loaded, list(results), refs, Running(filler, begin, fill_loads))

    results = [result_of(job) for job in jobs]
    got = pl.pallas_call(
        body,
        out_shape=tuple(outs)
        + tuple(jax.ShapeDtypeStruct(*r) for r in results)
        + tuple(filler.outs),
        in_specs=[HBM_SPEC] * (n_in + n_job + n_load + n_raw),
        out_specs=(HBM_SPEC,) * (n_out + n_job + n_fill),
        scratch_shapes=[
            pltpu.SemaphoreType.DMA((n_sems,)),
            pltpu.SemaphoreType.DMA((max(n_in + n_load, 1),)),
            pltpu.SemaphoreType.DMA((max(len(by_rows), 1), 2 * TP)),
        ]
        + [pltpu.VMEM(v.shape, v.dtype) for v in operands + loads]
        + job_scratch
        + list(filler.scratch)
        + scratch,
        compiler_params=pltpu.CompilerParams(
            collective_id=number, has_side_effects=True, vmem_limit_bytes=VMEM_LIMIT
        ),
        cost_estimate=pl.CostEstimate(flops=cost, bytes_accessed=8 * MB, transcendentals=0),
        name=name,
    )(*operands, *[job.src for job in jobs], *loads, *raws)
    return got[:n_out], list(got[n_out : n_out + n_job]), list(got[n_out + n_job :])


class Running:
    def __init__(self, filler, begin, loads):
        self.begin, self.run, self.end, self.loads = begin, filler.run, filler.end, loads
        self.n_steps, self.done = filler.n_steps, 0

    def prefetch(self):
        for load in self.loads:
            load.copy.start()

    def advance(self, share):
        high = int(round(share * self.n_steps))
        if high > self.done:
            self.run(self.done, high)
            self.done = high


def ship(number, planes, jobs):
    def kernel(shipper, ins, outs, scratch, filler):
        shipper.greet(())
        shipper.start()
        shipper.finish()

    return call_with_jobs(kernel, number, planes, jobs, [], [], [], "ship", 0)[1]


class GatherNormed:
    by_rows = ()

    def __init__(self, x, gain):
        self.chunk = x.shape[1]
        self.operands, self.cost = [x, gain], 10**6
        self.outs = [jax.ShapeDtypeStruct((2 * TP * self.chunk, D), BF)]
        self.scratch = [pltpu.VMEM((2, self.chunk, D), BF), pltpu.SemaphoreType.DMA((7, 2))]

    def bind(self, ins, outs, scratch):
        self.x, self.gain = ins
        self.g = Gatherer(outs[0], scratch[0], scratch[1], self.chunk, group_ids())

    def load(self):
        pass

    def first(self, met):
        x_ref, gain_ref = self.x.get(), self.gain.get()
        met()
        for j in range(2):
            self.g.put(j, normed(x_ref[j].astype(F32), gain_ref[...]).astype(BF))

    def second(self, between):
        between()

    def third(self):
        for j in range(2):
            self.g.forward(j)

    def last(self):
        self.g.finish()


GELU_C = float(np.sqrt(2.0 / np.pi))


def gelu_parts(v):
    tanh = jnp.tanh(GELU_C * (v + 0.044715 * v * v * v))
    return tanh, 0.5 * (1.0 + tanh)


def gelu_slope(v):
    tanh, half = gelu_parts(v)
    return half + 0.5 * v * (1.0 - tanh * tanh) * (GELU_C * (1.0 + 3 * 0.044715 * v * v))


class Rows:
    n_operands, n_outs, n_scratch = 1, 0, 0

    def __init__(self, ins, outs, scratch, chunk):
        self.rows, self.chunk = ins.pop(0), chunk
        self.by_rows = [self.rows]

    def prepare(self):
        self.ref = self.rows.ref

    def make(self, pair, slot):
        pass

    def finish(self):
        pass

    def pick(self, ref, pair):
        return jnp.concatenate([ref[rows] for rows in pair], axis=0)


class MadeRows(Rows):
    def write(self, index, ref, out, slot, pair):
        for j, rows in enumerate(pair):
            copy = pltpu.make_async_copy(ref.at[rows], out.at[rows], self.sems.at[index, 2 * slot + j])
            copy.start()
            self.copies.append(copy)

    def finish(self):
        for copy in self.copies:
            copy.wait()

    def tiles(self, body):
        @pl.loop(0, self.ref.shape[1] // 256)
        def _(n):
            body(pl.ds(pl.multiple_of(n * 256, 256), 256))


class FeedForward(MadeRows):
    n_operands, n_outs, n_scratch = 2, 2, 3

    def __init__(self, ins, outs, scratch, chunk):
        self.rows, self.w_in, self.chunk, self.copies = ins.pop(0), ins.pop(0), chunk, []
        self.by_rows = [self.rows]
        self.pre_out, self.act_out = outs.pop(0), outs.pop(0)
        self.pre, self.ref, self.sems = scratch.pop(0), scratch.pop(0), scratch.pop(0)

    @staticmethod
    def extras(n_rows, width):
        shapes = [((n_rows, width), F32), ((n_rows, width), BF)]
        scratch = [pltpu.VMEM(*v) for v in shapes] + [pltpu.SemaphoreType.DMA((2, 2 * TP))]
        return [jax.ShapeDtypeStruct(*v) for v in shapes], scratch

    def prepare(self):
        self.w_in = self.w_in.get()

    def make(self, pair, slot):
        x = self.pick(self.rows.ref, pair)

        def tile(cols):
            v = mm(x, self.w_in[:, cols])
            act = (v * gelu_parts(v)[1]).astype(BF)
            for j, rows in enumerate(pair):
                self.pre[rows, cols] = v[j * self.chunk : (j + 1) * self.chunk]
                self.ref[rows, cols] = act[j * self.chunk : (j + 1) * self.chunk]

        self.tiles(tile)
        self.write(0, self.pre, self.pre_out, slot, pair)
        self.write(1, self.ref, self.act_out, slot, pair)


class FeedForwardBack(MadeRows):
    n_operands, n_outs, n_scratch = 3, 1, 2

    def __init__(self, ins, outs, scratch, chunk):
        self.rows, self.pre, self.w_out = ins.pop(0), ins.pop(0), ins.pop(0)
        self.chunk, self.copies = chunk, []
        self.by_rows = [self.rows, self.pre]
        self.out, self.ref, self.sems = outs.pop(0), scratch.pop(0), scratch.pop(0)

    @staticmethod
    def extras(n_rows, width):
        shape = ((n_rows, width), BF)
        scratch = [pltpu.VMEM(*shape), pltpu.SemaphoreType.DMA((1, 2 * TP))]
        return [jax.ShapeDtypeStruct(*shape)], scratch

    def prepare(self):
        self.w_out = self.w_out.get()

    def make(self, pair, slot):
        x = self.pick(self.rows.ref, pair)

        def tile(cols):
            grad = mm_nt(x, self.w_out[cols, :])
            for j, rows in enumerate(pair):
                back = gelu_slope(self.pre.ref[rows, cols]) * grad[j * self.chunk : (j + 1) * self.chunk]
                self.ref[rows, cols] = back.astype(BF)

        self.tiles(tile)
        self.write(0, self.ref, self.out, slot, pair)


class Stage:
    def __init__(
        self,
        left,
        weight,
        resid,
        *,
        flip=False,
        maker=Rows,
        back=None,
        gather=None,
        gain=None,
        given=None,
        dtype=F32,
        low=False,
    ):
        self.maker, self.flip, self.back, self.gather, self.low = maker, flip, bool(back), gather, low
        self.chunk = chunk = resid.shape[1]
        self.operands = list(left) + [weight, resid]
        self.cost = 4 * left[0].shape[0] * D * D
        self.by_rows = {Rows: (0,), FeedForward: (0,), FeedForwardBack: (0, 1)}[maker]
        if back:
            self.operands += [back[1], back[0]]
        elif gather == "norm":
            self.operands.append(gain)
        if gather == "given":
            self.operands.append(given)
        self.outs = [jax.ShapeDtypeStruct((2, chunk, D), dtype)]
        if gather:
            self.outs.append(jax.ShapeDtypeStruct((2 * TP * chunk, D), BF))
        if back:
            self.outs.append(jax.ShapeDtypeStruct((1, D), F32))
        half = pltpu.VMEM((2, chunk, D), BF)
        full = pltpu.VMEM((2, chunk, D), F32)
        self.scratch = [half] * 6 + [full] * 2
        self.scratch += [pltpu.VMEM((2, chunk, D), dtype), pltpu.SemaphoreType.DMA((13,))]
        if gather:
            self.scratch += [half, pltpu.SemaphoreType.DMA((7, 2))]
        if back:
            self.scratch.append(pltpu.VMEM((1, D), F32))
        if low:
            self.outs.append(jax.ShapeDtypeStruct((2, chunk, D), BF))
            self.scratch.append(half)
        if maker is not Rows:
            width = weight.shape[1] if flip else weight.shape[0]
            more, more_scratch = maker.extras(2 * TP * chunk, width)
            self.outs += more
            self.scratch += more_scratch

    def bind(self, ins, outs, scratch):
        maker = self.maker
        made_outs = [outs.pop() for _ in range(maker.n_outs)][::-1]
        made_scratch = [scratch.pop() for _ in range(maker.n_scratch)][::-1]
        self.left = maker(ins, made_outs, made_scratch, self.chunk)
        self.w_in, self.resid_in = ins.pop(0), ins.pop(0)
        self.gain_in = ins.pop(0) if (self.back or self.gather == "norm") else None
        self.x_in = ins.pop(0) if self.back else None
        self.given_in = ins.pop(0) if self.gather == "given" else None
        self.y_out = outs.pop(0)
        gath_ref = outs.pop(0) if self.gather else None
        self.dgain_out = outs.pop(0) if self.back else None
        self.low_out = outs.pop(0) if self.low else None
        self.s_far, self.r_far, self.s_x, self.r_x, self.s_core, self.r_core = scratch[:6]
        self.keep, self.own, self.y_ref, self.sems = scratch[6:10]
        scratch = scratch[10:]
        self.ids = group_ids()
        self.g = None
        if self.gather:
            self.g = Gatherer(gath_ref, scratch.pop(0), scratch.pop(0), self.chunk, self.ids)
        self.dgain_ref = scratch.pop(0) if self.back else None
        self.low_ref = scratch.pop(0) if self.low else None
        self.slots, self.stores = [0, 1, 2, 3], []

    def load(self):
        me, core, across, far = self.ids
        for rows in self.left.by_rows:
            rows.start((far, across, core, me))

    def partial(self, owner, ref):
        slot, chunk, left = self.slots.pop(0), self.chunk, self.left
        for rows in left.by_rows:
            rows.wait(owner, slot)
        pair = [
            pl.ds(pl.multiple_of((TP * j + owner) * chunk, chunk), chunk) for j in range(2)
        ]
        left.make(pair, slot)
        a = left.pick(left.ref, pair)

        @pl.loop(0, D // 256)
        def _(n):
            cols = pl.ds(pl.multiple_of(n * 256, 256), 256)
            total = mm_nt(a, self.w_ref[cols, :]) if self.flip else mm(a, self.w_ref[:, cols])
            for j in range(2):
                ref[j, :, cols] = total[j * chunk : (j + 1) * chunk].astype(ref.dtype)

    def first(self, met):
        me, core, across, far = self.ids
        sems = self.sems
        self.left.prepare()
        self.w_ref = self.w_in.get()
        self.partial(far, self.s_far)
        met()
        self.c_far = send(self.s_far, self.r_far, sems.at[0], sems.at[1], core)
        self.c_far.start()
        if self.gather == "given":
            given_ref = self.given_in.get()
            for j in range(2):
                self.g.put(j, given_ref[j])
        self.partial(across, self.keep)
        self.c_far.wait_recv()
        self.c_x = []
        for j in range(2):
            self.s_x[j] = (self.keep[j] + self.r_far[j].astype(F32)).astype(BF)
            copy = send(self.s_x.at[j], self.r_x.at[j], sems.at[2 + j], sems.at[4 + j], across)
            copy.start()
            self.c_x.append(copy)
        self.partial(core, self.s_core)
        self.c_core = send(self.s_core, self.r_core, sems.at[6], sems.at[7], core)
        self.c_core.start()
        self.partial(me, self.own)

    def keep_out(self, src, dst, sem):
        copy = pltpu.make_async_copy(src, dst, self.sems.at[sem])
        copy.start()
        self.stores.append(copy)

    def second(self, between):
        self.c_core.wait_recv()
        resid_ref = self.resid_in.get()
        x_ref = self.x_in.get() if self.back else None
        gains = self.gain_in.get()[...] if self.gain_in else None
        if self.gather == "given":
            for j in range(2):
                self.g.forward(j)
        for j in range(2):
            self.c_x[j].wait_recv()
            if j == 1:
                between()
            total = self.own[j] + self.r_core[j].astype(F32) + self.r_x[j].astype(F32)
            if self.back:
                x = x_ref[j].astype(F32)
                r = lax.rsqrt(jnp.mean(x * x, axis=-1, keepdims=True) + EPS)
                scaled = total * gains
                inner = jnp.mean(scaled * x, axis=-1, keepdims=True)
                y = resid_ref[j].astype(F32) + r * scaled - x * (r * r * r * inner)
                dgain = jnp.sum(total * x * r, axis=0, keepdims=True)
                if j == 0:
                    self.dgain_ref[...] = dgain
                else:
                    self.dgain_ref[...] += dgain
            else:
                y = resid_ref[j].astype(F32) + total
            if self.gather == "norm":
                self.g.put(j, normed(y, gains).astype(BF))
            elif self.gather == "low":
                self.g.put(j, y.astype(BF))
            self.y_ref[j] = y.astype(self.y_ref.dtype)
            self.keep_out(self.y_ref.at[j], self.y_out.at[j], 8 + j)
            if self.low:
                self.low_ref[j] = y.astype(BF)
                self.keep_out(self.low_ref.at[j], self.low_out.at[j], 11 + j)
        if self.back:
            self.keep_out(self.dgain_ref, self.dgain_out, 10)

    def third(self):
        if self.gather in ("norm", "low"):
            for j in range(2):
                self.g.forward(j)

    def last(self):
        if self.gather:
            self.g.finish()
        for copy in [self.c_far, self.c_core] + self.c_x:
            copy.wait_send()
        for copy in self.stores:
            copy.wait()
        self.left.finish()


def stage(number, planes, stages, jobs=(), filler=None):
    operands = [v for st in stages for v in st.operands]
    outs = [v for st in stages for v in st.outs]
    scratch = [v for st in stages for v in st.scratch]
    by_rows, base = [], 0
    for st in stages:
        by_rows += [base + i for i in st.by_rows]
        base += len(st.operands)

    def kernel(shipper, ins, results, refs, filler):
        for st in stages:
            parts = []
            for have, n in ((ins, st.operands), (results, st.outs), (refs, st.scratch)):
                parts.append(have[: len(n)])
                del have[: len(n)]
            st.bind(*parts)
            st.load()
        shipper.signal()

        def met():
            shipper.met()
            shipper.start()

        for n, st in enumerate(stages):
            st.first(met if n == 0 else (lambda: None))
        filler.prefetch()
        filler.begin()
        filler.advance(SHARE[0])
        for n, st in enumerate(stages):
            st.second(lambda: filler.advance(SHARE[1]) if n == 0 else None)
        filler.advance(SHARE[2])
        for st in stages:
            st.third()
        filler.advance(1.0)
        filler.end()
        for st in stages:
            st.last()
        shipper.finish()

    cost = sum(st.cost for st in stages)
    got, moved, made = call_with_jobs(
        kernel, number, planes, jobs, operands, outs, scratch, "stage", cost, filler, tuple(by_rows)
    )
    got = list(got)
    each = []
    for st in stages:
        each.append(got[: len(st.outs)])
        del got[: len(st.outs)]
    return each, moved, made


class Attention:
    def __init__(self, parts, q, kv, bias, mkv, causal):
        self.parts, self.causal = parts, causal
        self.q_shape, self.kv_shape = q.shape, kv.shape
        self.rows, self.keys = q.shape[0], kv.shape[0]
        self.chunk = self.rows // (2 * TP)
        self.joint = q is kv
        self.extra = 0 if mkv is None else mkv.shape[0]
        self.total = self.keys + self.extra
        self.bias = bias
        self.size = 2 * self.chunk
        self.blocks = self.rows // self.size
        self.n_steps = 2 * HQ
        self.loads = [q] + ([] if self.joint else [kv])
        self.mem = [mkv] if self.extra else []
        self.raws = []

    def heads(self, *widths_dtypes):
        return [pltpu.VMEM((HQ, n, DH), dtype) for n, dtype in widths_dtypes]

    def split_qkv(self, q_ref, kv_ref, loads, qs, ks, vs):
        at = QC if self.joint else 0
        keys = self.keys
        for i in range(HQ):
            qs[i] = q_ref[:, DH * i : DH * (i + 1)]
            ks[i, :keys] = kv_ref[:, at + DH * i : at + DH * (i + 1)]
            vs[i, :keys] = kv_ref[:, at + QC + DH * i : at + QC + DH * (i + 1)]
        if self.extra:
            mkv_ref = loads.pop(0).get()
            for i in range(HQ):
                ks[i, keys:] = mkv_ref[:, DH * i : DH * (i + 1)]
                vs[i, keys:] = mkv_ref[:, QC + DH * i : QC + DH * (i + 1)]

    def place(self, row_chunk):
        upper = row_chunk // TP
        part = lax.axis_index("part") if self.parts > 1 else 0
        return (upper * (TP * self.parts) + TP * part + (row_chunk - TP * upper)) * self.chunk

    def halves(self, low, high):
        for half in range(2):
            first = max(low - HQ * half, 0)
            last = min(high - HQ * half, HQ)
            if first < last:
                n = self.blocks // 2
                yield half, range(half * n, (half + 1) * n), first, last

    def width(self, b):
        if self.causal and self.parts == 1:
            return (b + 1) * self.size
        return self.total

    def block(self, b):
        return pl.ds(b * self.size, self.size)

    def diagonal(self, b, u):
        keys = min(self.width(b), self.keys)
        start = self.keys - self.place(2 * b + u)
        return pl.ds(start if isinstance(start, int) else pl.multiple_of(start, 128), keys)


class AttentionForward(Attention):
    def __init__(self, parts, q, kv, segq, segk, bvec, mkv, causal, products=None):
        super().__init__(parts, q, kv, bvec is not None, mkv, causal)
        self.products = products
        if products:
            self.loads = [v for pair in products for v in pair]
        self.loads += self.mem + [segq, segk] + ([bvec] if self.bias else [])
        self.outs = [
            jax.ShapeDtypeStruct((self.rows, QC), BF),
            jax.ShapeDtypeStruct((HQ, self.rows, self.total), BF),
        ]
        self.scratch = self.heads((self.rows, BF), (self.total, BF), (self.total, BF), (self.rows, BF))
        self.scratch += [
            pltpu.VMEM((self.blocks, self.size, self.total), BF),
            pltpu.VMEM((self.rows, QC), BF),
            pltpu.SemaphoreType.DMA((3 + self.blocks,)),
        ]
        if self.bias:
            self.scratch.append(pltpu.VMEM((self.chunk, 2 * self.keys), F32))
        if products:
            for x, w in products:
                self.outs.append(jax.ShapeDtypeStruct((x.shape[0], w.shape[1]), BF))
                self.scratch.append(pltpu.VMEM((x.shape[0], w.shape[1]), BF))

    def begin(self, loads, raws, outs, scratch):
        self.att_out, self.p_out = outs[:2]
        self.qs, self.ks, self.vs, self.os, self.p_buf, self.att, self.sems = scratch[:7]
        self.toep = scratch[7] if self.bias else None
        loads = list(loads)
        self.copies = []
        if self.products:
            made = scratch[-len(self.products) :]
            for n, (out, to) in enumerate(zip(made, outs[2:])):
                x, w = loads.pop(0).get(), loads.pop(0).get()

                @pl.loop(0, x.shape[0] // 256)
                def _(r):
                    rows = pl.ds(pl.multiple_of(r * 256, 256), 256)
                    out[rows] = mm(x[rows], w[...]).astype(BF)

                self.copies.append(pltpu.make_async_copy(out, to, self.sems.at[1 + n]))
                self.copies[-1].start()
            q_ref, kv_ref = made[0], made[-1]
        else:
            q_ref = loads.pop(0).get()
            kv_ref = q_ref if self.joint else loads.pop(0).get()
        self.split_qkv(q_ref, kv_ref, loads, self.qs, self.ks, self.vs)
        self.segq, self.segk = loads.pop(0).get(), loads.pop(0).get()
        self.bvec = loads.pop(0).get() if self.bias else None

    def keep(self, h, b):
        wide = pl.ds(0, self.width(b))
        return pltpu.make_async_copy(
            self.p_buf.at[b, :, wide], self.p_out.at[h, self.block(b), wide], self.sems.at[3 + b]
        )

    def one_block(self, h, b):
        wide, chunk, rows = self.width(b), self.chunk, self.block(b)
        keys = min(wide, self.keys)
        s = mm_nt(self.qs[h, rows], self.ks[h, :wide])
        if self.bias:
            parts = [self.toep[:, self.diagonal(b, u)] for u in range(2)]
            biased = s[:, :keys] + jnp.concatenate(parts, axis=0)
            s = jnp.concatenate([biased, s[:, keys:]], axis=1) if self.extra else biased
        allowed = self.segq[rows] == self.segk[:, :wide]
        s = jnp.where(allowed, s, MASKED)
        if self.causal:
            row = lax.broadcasted_iota(jnp.int32, (chunk, 1), 0)
            places = jnp.concatenate([row + self.place(2 * b + u) for u in range(2)], axis=0)
            seen = wide - self.size if self.parts == 1 else 0
            later = lax.broadcasted_iota(jnp.int32, (1, wide - seen), 1) + seen
            last = jnp.where(later <= places, s[:, seen:], MASKED)
            s = jnp.concatenate([s[:, :seen], last], axis=1) if seen else last
        top = jnp.max(s, axis=-1, keepdims=True)
        e = jnp.exp(s - top)
        p = (e * (1.0 / jnp.sum(e, axis=-1, keepdims=True))).astype(BF)
        self.p_buf[b, :, :wide] = p
        self.os[h, rows] = mm(p, self.vs[h, :wide]).astype(BF)

    def run(self, low, high):
        for half, blocks, first, last in self.halves(low, high):

            @pl.loop(first, last)
            def _(h):
                if self.bias:
                    row = jnp.broadcast_to(self.bvec[h], (self.chunk, 2 * self.keys))
                    self.toep[...] = pltpu.roll(row, 0, 1, stride=1, stride_axis=0)

                @pl.when(h > 0)
                def _():
                    for b in blocks:
                        self.keep(h - 1, b).wait()

                for b in blocks:
                    self.one_block(h, b)
                for b in blocks:
                    self.keep(h, b).start()

    def end(self):
        for i in range(HQ):
            self.att[:, DH * i : DH * (i + 1)] = self.os[i]
        out = pltpu.make_async_copy(self.att, self.att_out, self.sems.at[0])
        out.start()
        for b in range(self.blocks):
            self.keep(HQ - 1, b).wait()
        out.wait()
        for copy in self.copies:
            copy.wait()


class AttentionBackward(Attention):
    def __init__(self, parts, p, q, kv, up, w_proj, att, bias, mkv, xs, proj=True, causal=False):
        super().__init__(parts, q, kv, bias, mkv, causal)
        self.xs, self.proj = xs if parts == 1 else [], proj
        self.loads += self.mem + [up, w_proj, att] + self.xs
        self.raws = [p]
        rows, total, keys = self.rows, self.total, self.keys
        if self.joint:
            self.outs = [jax.ShapeDtypeStruct((rows, 3 * QC), BF)]
        else:
            kv_type = BF if parts == 1 else F32
            self.outs = [
                jax.ShapeDtypeStruct((rows, QC), BF),
                jax.ShapeDtypeStruct((keys, 2 * QC), kv_type),
            ]
        if bias:
            self.outs.append(jax.ShapeDtypeStruct((HQ, 1, 2 * keys), F32))
        if self.extra:
            self.outs.append(jax.ShapeDtypeStruct((self.extra, 2 * QC), BF))
        if proj:
            self.outs.append(jax.ShapeDtypeStruct((QC, D), BF))
        for n in range(len(self.xs)):
            self.outs.append(jax.ShapeDtypeStruct((D, self.outs[n].shape[1]), BF))
        self.scratch = self.heads(
            (rows, BF), (total, BF), (total, BF), (rows, BF), (rows, BF), (total, F32), (total, F32)
        )
        self.scratch += [
            pltpu.VMEM((HQ, rows, 1), F32),
            pltpu.VMEM((self.blocks, self.size, total), BF),
            pltpu.SemaphoreType.DMA((self.blocks + len(self.outs),)),
        ]
        self.scratch += [pltpu.VMEM(o.shape, o.dtype) for o in self.outs]
        if bias:
            self.scratch.append(pltpu.VMEM((HQ, self.chunk, 2 * keys), F32))

    def fetch(self, h, b):
        n = self.blocks // 2
        slot = n * lax.rem(h + (b // n) * HQ, 2) + b % n
        wide = pl.ds(0, self.width(b))
        return pltpu.make_async_copy(
            self.p_in.at[h, self.block(b), wide], self.p_buf.at[slot, :, wide], self.sems.at[slot]
        )

    def begin(self, loads, raws, outs, scratch):
        self.results, (self.p_in,) = outs, raws
        scratch, loads = list(scratch), list(loads)
        self.qs, self.ks, self.vs, self.dos, self.dqs, self.dks, self.dvs = scratch[:7]
        self.rds, self.p_buf, self.sems = scratch[7:10]
        self.made = scratch[10 : 10 + len(outs)]
        self.diag = scratch[-1] if self.bias else None
        for b in range(self.blocks // 2):
            self.fetch(0, b).start()
        q_ref = loads.pop(0).get()
        kv_ref = q_ref if self.joint else loads.pop(0).get()
        self.split_qkv(q_ref, kv_ref, loads, self.qs, self.ks, self.vs)
        up_ref, w_ref, att_ref = (loads.pop(0).get() for _ in range(3))

        @pl.loop(0, self.rows // 256)
        def _(r):
            rows = pl.ds(pl.multiple_of(r * 256, 256), 256)
            grads = mm_nt(up_ref[rows], w_ref[...]).astype(BF)
            att = att_ref[rows]
            for i in range(HQ):
                span = slice(DH * i, DH * (i + 1))
                self.dos[i, rows] = grads[:, span]
                dots = grads[:, span].astype(F32) * att[:, span].astype(F32)
                self.rds[i, rows] = jnp.sum(dots, axis=-1, keepdims=True)

        made = list(self.made)
        self.dq = made.pop(0)
        self.dkv = self.dq if self.joint else made.pop(0)
        self.dbvec = made.pop(0) if self.bias else None
        self.dmkv = made.pop(0) if self.extra else None
        g_proj = made.pop(0) if self.proj else None
        self.g_rows, self.x_loads = made, loads
        if self.proj:

            @pl.loop(0, D // 256)
            def _(n):
                cols = pl.ds(pl.multiple_of(n * 256, 256), 256)
                g_proj[:, cols] = mm_tn(att_ref[...], up_ref[:, cols]).astype(BF)

    def run(self, low, high):
        keys, chunk, n = self.keys, self.chunk, self.blocks // 2
        for half, blocks, first, last in self.halves(low, high):

            @pl.loop(first, last)
            def _(h):
                for b in blocks:
                    self.fetch(h, b).wait()

                @pl.when(h + 1 < HQ)
                def _():
                    for b in blocks:
                        self.fetch(h + 1, b).start()

                if half == 0:

                    @pl.when(h + 1 == HQ)
                    def _():
                        for b in range(n, 2 * n):
                            self.fetch(0, b).start()

                    self.dks[h] = jnp.zeros(self.dks.shape[1:], F32)
                    self.dvs[h] = jnp.zeros(self.dvs.shape[1:], F32)
                    if self.bias:
                        self.diag[h] = jnp.zeros(self.diag.shape[1:], F32)
                for b in blocks:
                    wide, rows = self.width(b), self.block(b)
                    slot = n * lax.rem(h + half * HQ, 2) + b % n
                    q, grad, p = self.qs[h, rows], self.dos[h, rows], self.p_buf[slot, :, :wide]
                    dp = mm_nt(grad, self.vs[h, :wide])
                    ds = (p.astype(F32) * (dp - self.rds[h, rows])).astype(BF)
                    self.dqs[h, rows] = mm(ds, self.ks[h, :wide]).astype(BF)
                    self.dks[h, :wide] += mm_tn(ds, q)
                    self.dvs[h, :wide] += mm_tn(p, grad)
                    if self.bias:
                        for u in range(2):
                            part = ds[u * chunk : (u + 1) * chunk, : min(wide, keys)]
                            self.diag[h, :, self.diagonal(b, u)] += part.astype(F32)
                if self.bias and half == 1:
                    x = self.diag[h]
                    size = chunk
                    while size > 1:
                        size //= 2
                        x = x[:size] + pltpu.roll(x[size:], 2 * keys - size, 1)
                    self.dbvec[h] = x

    def end(self):
        keys = self.keys
        to = QC if self.joint else 0
        for i in range(HQ):
            self.dq[:, DH * i : DH * (i + 1)] = self.dqs[i]
            at = to + DH * i
            self.dkv[:, at : at + DH] = self.dks[i, :keys].astype(self.dkv.dtype)
            self.dkv[:, at + QC : at + QC + DH] = self.dvs[i, :keys].astype(self.dkv.dtype)
            if self.extra:
                self.dmkv[:, DH * i : DH * (i + 1)] = self.dks[i, keys:].astype(BF)
                self.dmkv[:, QC + DH * i : QC + DH * (i + 1)] = self.dvs[i, keys:].astype(BF)
        for load, out, grad in zip(self.x_loads, self.g_rows, (self.dq, self.dkv)):
            x_ref = load.get()

            @pl.loop(0, D // 256)
            def _(n):
                cols = pl.ds(pl.multiple_of(n * 256, 256), 256)
                out[cols] = mm_tn(x_ref[:, cols], grad[...]).astype(BF)

        copies = [
            pltpu.make_async_copy(src, dst, self.sems.at[self.blocks + n])
            for n, (src, dst) in enumerate(zip(self.made, self.results))
        ]
        for copy in copies:
            copy.start()
        for copy in copies:
            copy.wait()


class Idle:
    n_steps, loads, raws, outs, scratch = 0, [], [], [], []

    def begin(self, loads, raws, outs, scratch):
        pass

    def run(self, low, high):
        pass

    def end(self):
        pass


def attend(number, planes, filler, jobs):
    def kernel(shipper, ins, outs, scratch, filler):
        filler.prefetch()
        shipper.greet(())
        shipper.start()
        filler.begin()
        filler.run(0, filler.n_steps)
        filler.end()
        shipper.finish()

    _, moved, made = call_with_jobs(
        kernel, number, planes, jobs, [], [], [], "attend", 4 * 10**9, filler
    )
    return made, moved


class Chain:
    def __init__(self, value, steps, width):
        self.value, self.steps, self.width = value, steps, width


ALL = ("seq", "part", "tp", "fsdp")
CTX = ("seq", "part", "tp")


def per_device(
    parts,
    planes,
    enc_input,
    dec_input,
    segments,
    prefix_rows,
    buckets,
    memory,
    enc_gain,
    enc_qkv,
    enc_rel,
    enc_proj,
    enc_ffnorm,
    enc_ffin,
    enc_ffout,
    dec_gain,
    dec_qkv,
    dec_rel,
    dec_proj,
    cross_gain,
    cross_query,
    cross_kv,
    cross_proj,
    dec_ffnorm,
    dec_ffin,
    dec_ffout,
    enc_cotan,
    dec_cotan,
):
    seq, part, tp, plane = (lax.axis_index(name) for name in ALL)
    chunk = enc_input.shape[1]
    length = buckets.shape[0] // 2
    docs, prefix = prefix_rows.shape[1:]

    first = seq == 0
    split = planes * 2

    def joined(x, came):
        mine = lax.dynamic_index_in_dim(x, seq, 0, keepdims=False)
        came = came.astype(x.dtype)
        return jnp.stack([jnp.where(first, mine, came), jnp.where(first, came, mine)])

    def cols(w, start, width=QC):
        return lax.dynamic_slice_in_dim(w, start + width * tp, width, 1)

    def halved(w):
        rows = w.shape[0] // 2
        return lax.dynamic_slice_in_dim(w, rows * seq, rows, 0)

    def qkv_part(w):
        w = halved(w)
        return jnp.concatenate([cols(w, D * i) for i in range(w.shape[1] // D)], axis=1)

    hidden = enc_ffout.shape[0] // TP

    def ffin_part(w):
        w = halved(w)
        return jnp.concatenate(
            [cols(w, hidden * TP * i, hidden) for i in range(planes)], axis=1
        )

    def ffout_part(w):
        rows = hidden // 2
        return lax.dynamic_slice_in_dim(w, hidden * tp + rows * seq, rows, 0)

    def over_planes(w):
        return gather_job("fsdp", w, planes)

    def over_seq(w):
        return gather_job("seq", w, 2, 1)

    def matrix(w):
        return w.reshape(-1, w.shape[-1])

    gains = (enc_gain, enc_ffnorm, dec_gain, cross_gain, dec_ffnorm)
    which = jnp.arange(len(gains), dtype=jnp.int32)[:, None]
    gain_stack = sum(jnp.where(which == i, v.astype(F32)[None], 0.0) for i, v in enumerate(gains))
    which = jnp.arange(2, dtype=jnp.int32)[:, None, None]
    rel_stack = jnp.where(which == 0, enc_rel.astype(F32)[None], dec_rel.astype(F32)[None])
    segments = segments.reshape(2, 1, chunk)
    first_jobs = [
        swap_job(enc_input),
        gather_job("fsdp", gain_stack, planes),
        gather_job("fsdp", rel_stack, planes),
        over_planes(qkv_part(enc_qkv)),
        over_planes(qkv_part(memory)),
        swap_job(dec_input),
    ]
    if parts == 1:
        first_jobs.append(block_job(segments))
    xe, gain_stack, rel_stack, w_eqkv, table, xd, *segs = ship(0, planes, first_jobs)
    xe, xd = joined(enc_input, xe), joined(dec_input, xd)
    if parts == 1:
        seg = segs[0].reshape(-1)
    else:
        segs = lax.all_gather(segments.reshape(2, chunk), CTX, axis=1, tiled=True)
        seg = lax.dynamic_index_in_dim(segs, seq, 0, keepdims=False)
    per, per_rel = enc_gain.shape[0], enc_rel.size
    g_enc, g_effn, g_dec, g_cross, g_dffn = [
        gain_stack[:, i].reshape(1, D) for i in range(len(gains))
    ]
    rels = [rel_stack[:, i].reshape(BUCKETS, HEADS) for i in range(2)]
    onehot = (buckets[:, None] == jnp.arange(BUCKETS, dtype=jnp.int32)[None, :]).astype(BF)

    def bias_vector(rel):
        own = lax.dynamic_slice_in_dim(rel, HQ * tp, HQ, 1).astype(BF)
        return lax.dot_general(
            own, onehot, (((0,), (1,)), ((), ())), preferred_element_type=F32
        ).reshape(HQ, 1, 2 * length)

    turned = planes == TP

    def proj_jobs(w):
        return [turn_job(w)] if turned else []

    def proj_of(got, w):
        if turned:
            return got.pop()
        full = lax.all_gather(w, "fsdp", axis=0, tiled=True)
        return lax.dynamic_slice_in_dim(full, QC * tp, QC, 0)

    ((en,), (dn,)), (w_eqkv, table, w_dqkv, w_effin), _ = stage(
        1,
        planes,
        [GatherNormed(xe, g_enc), GatherNormed(xd, g_dec)],
        jobs=[
            over_seq(w_eqkv),
            over_seq(table),
            over_planes(qkv_part(dec_qkv)),
            over_planes(ffin_part(enc_ffin)),
        ],
    )
    w_eqkv, table = matrix(w_eqkv), matrix(table)

    segq = lax.dynamic_index_in_dim(seg.reshape(2, parts, TP * chunk), part, 1, keepdims=False)
    segq = segq.reshape(-1, 1)
    segk = seg.reshape(1, length)
    ids = lax.dynamic_index_in_dim(prefix_rows, seq, 0, keepdims=False).reshape(-1)
    extra = -(-(docs * prefix) // 256) * 256
    ids = jnp.concatenate([ids, jnp.full((extra - docs * prefix,), -1, jnp.int32)])
    mem_doc = np.full((extra,), -1, np.int32)
    mem_doc[: docs * prefix] = np.arange(docs * prefix) // prefix
    segk_mem = jnp.concatenate([segk, jnp.asarray(mem_doc)[None]], axis=1)
    pick = (ids[:, None] == jnp.arange(table.shape[0], dtype=jnp.int32)[None, :]).astype(BF)
    mkv = mm(pick, table).astype(BF)

    def spread(kv):
        if parts == 1:
            return kv
        got = lax.all_gather(kv, "part", axis=0)
        return got.reshape(parts, 2, TP * chunk, -1).transpose(1, 0, 2, 3).reshape(length, -1)

    def collect(dkv):
        if parts == 1:
            return dkv
        split = dkv.reshape(2, parts, TP * chunk, -1).transpose(1, 0, 2, 3)
        split = split.reshape(parts * 2 * TP * chunk, -1)
        return lax.psum_scatter(split, "part", scatter_dimension=0, tiled=True).astype(BF)

    def self_kv(rows):
        return (rows, rows) if parts == 1 else (rows[:, :QC], spread(rows[:, QC:]))

    def joint_grad(got):
        if parts == 1:
            return got.pop(0)
        return jnp.concatenate([got.pop(0), collect(got.pop(0))], axis=1)

    def self_fill(x, w, segk_now, bvec, mem, causal):
        if parts == 1:
            rows = jax.ShapeDtypeStruct((x.shape[0], w.shape[1]), BF)
            return AttentionForward(
                parts, rows, rows, segq, segk_now, bvec, mem, causal, [(x, w)]
            ), None
        rows = self_kv(mm(x, w).astype(BF))
        return AttentionForward(parts, *rows, segq, segk_now, bvec, mem, causal), rows

    def self_made(got, rows):
        return got[0], got[1], rows or (got[2], got[2])

    e_fill, e_qkv = self_fill(en, w_eqkv, segk_mem, bias_vector(rels[0]), mkv, False)
    made, (w_dqkv, w_effin, w_effout, *got) = attend(
        2,
        planes,
        e_fill,
        [over_seq(w_dqkv), over_seq(w_effin), over_planes(ffout_part(enc_ffout))]
        + proj_jobs(enc_proj),
    )
    e_att, e_p, e_qkv = self_made(made, e_qkv)
    w_eproj = proj_of(got, enc_proj)
    w_dqkv, w_effin = matrix(w_dqkv), matrix(w_effin)
    d_fill, d_qkv = self_fill(dn, w_dqkv, segk, bias_vector(rels[1]), None, True)
    ((e_mid, e_fn),), (w_effout, w_cq, w_ckv, *got), made = stage(
        3,
        planes,
        [Stage([e_att], w_eproj, xe, gather="norm", gain=g_effn)],
        [
            over_seq(w_effout),
            over_planes(qkv_part(cross_query)),
            over_planes(qkv_part(cross_kv)),
        ]
        + proj_jobs(dec_proj),
        d_fill,
    )
    d_att, d_p, d_qkv = self_made(made, d_qkv)
    w_dproj = proj_of(got, dec_proj)
    w_effout = matrix(w_effout)
    ((d_mid, c_n), (e_low, e_gath, e_pre, e_act)), moved, _ = stage(
        4,
        planes,
        [
            Stage([d_att], w_dproj, xd, gather="norm", gain=g_cross),
            Stage(
                [e_fn, w_effin], w_effout, e_mid, maker=FeedForward, gather="low", dtype=BF
            ),
        ],
        [
            over_seq(w_cq),
            over_seq(w_ckv),
            over_planes(ffin_part(dec_ffin)),
            over_planes(ffout_part(dec_ffout)),
            swap_job(dec_cotan),
        ]
        + proj_jobs(cross_proj),
    )
    w_cq, w_ckv, w_dffin, w_dffout, xdc, *got = moved
    w_cproj = proj_of(got, cross_proj)
    w_cq, w_ckv = matrix(w_cq), matrix(w_ckv)
    xdc = joined(dec_cotan, xdc)
    products = None
    if parts == 1:
        c_q = jax.ShapeDtypeStruct((c_n.shape[0], QC), BF)
        c_kv = jax.ShapeDtypeStruct((e_gath.shape[0], 2 * QC), BF)
        products = [(c_n, w_cq), (e_gath, w_ckv)]
    else:
        c_q = mm(c_n, w_cq).astype(BF)
        c_kv = spread(mm(e_gath, w_ckv).astype(BF))
    c_fill = AttentionForward(parts, c_q, c_kv, segq, segk, None, None, False, products)
    (c_att, c_p, *made), (w_dffin,) = attend(5, planes, c_fill, [over_seq(w_dffin)])
    if parts == 1:
        c_q, c_kv = made
    ((d_cross, d_fn),), (w_dffout, came, xec), _ = stage(
        6,
        planes,
        [Stage([c_att], w_cproj, d_mid, gather="norm", gain=g_dffn)],
        [over_seq(w_dffout), swap_job(e_low), swap_job(enc_cotan)],
    )
    enc_output, xec = joined(e_low, came), joined(enc_cotan, xec)
    w_dffin, w_dffout = matrix(w_dffin), matrix(w_dffout)
    ((d_low, up_g, d_pre, d_act),), _, _ = stage(
        7,
        planes,
        [
            Stage(
                [d_fn, w_dffin],
                w_dffout,
                d_cross,
                maker=FeedForward,
                gather="given",
                given=xdc,
                dtype=BF,
            )
        ],
    )

    def pieces(g):
        if parts > 1:
            g = lax.psum(g, "part")
        return g.reshape(planes, 2, g.shape[0] // split, g.shape[1])

    to_ctx = [
        lambda g: gather_job("across", g),
        lambda g: gather_job("seq", g),
        lambda g: gather_job("core", g, 2, 2),
    ]
    to_ctx_seq = [
        lambda g: gather_job("seq", g),
        lambda g: gather_job("across", g, 2, 1),
        lambda g: gather_job("core", g, 2, 2),
    ]

    def chain(g, width, seq_first=False):
        steps = [lambda g: swap_job(g, 1, True), lambda g: deal_job("fsdp", g)]
        return Chain(pieces(g), steps + (to_ctx_seq if seq_first else to_ctx), width)

    def proj_chain(g):
        if not turned:
            return Chain(g, [], -1)
        steps = [lambda g: swap_job(g, "cols", True), lambda g: deal_job("fsdp", g), turn_job]
        return Chain(g.reshape(planes, -1, D), steps + to_ctx, -1)

    def steps_of(chains):
        return [c.steps[0](c.value) for c in chains if c.steps]

    def hurry(chains):
        for c in chains:
            if len(c.steps) == 3:
                c.steps = [spread_job]

    def settle(chains, got):
        got = list(got)
        for c in chains:
            if c.steps:
                c.value = got.pop(0)
                c.steps.pop(0)
        return got

    k_dffout = chain(mm_tn(d_act, up_g).astype(BF), 0, True)
    moving = [k_dffout]
    ((up, up_rows, dg_dffn, pre_grad),), got, _ = stage(
        8,
        planes,
        [
            Stage(
                [up_g, d_pre, w_dffout],
                w_dffin,
                xdc,
                flip=True,
                maker=FeedForwardBack,
                back=(d_cross, g_dffn),
                gather="low",
            )
        ],
        steps_of(moving) + [swap_job(d_low)],
    )
    (came,) = settle(moving, got)
    dec_output = joined(d_low, came)
    k_dffin = chain(mm_tn(d_fn, pre_grad).astype(BF), hidden, True)
    c_fill = AttentionBackward(
        parts, c_p, c_q, c_kv, up_rows, w_cproj, c_att, False, None, [c_n, e_gath]
    )
    moving = [k_dffin, k_dffout]
    (c_dq, c_dkv, g_cproj, *made), got = attend(9, planes, c_fill, steps_of(moving))
    settle(moving, got)
    c_dkv = collect(c_dkv)
    if parts > 1:
        made = [mm_tn(c_n, c_dq).astype(BF), mm_tn(e_gath, c_dkv).astype(BF)]
    k_cproj, k_cq, k_ckv = proj_chain(g_cproj), chain(made[0], QC), chain(made[1], QC)
    moving = [k_dffin, k_dffout, k_cq, k_ckv, k_cproj]
    ((e_up, e_up_rows), (up, up_rows, dg_cross)), got, _ = stage(
        10,
        planes,
        [
            Stage([c_dkv], w_ckv, xec, flip=True, gather="low"),
            Stage([c_dq], w_cq, up, flip=True, back=(d_mid, g_cross), gather="low"),
        ],
        steps_of(moving),
    )
    settle(moving, got)

    def self_grads(made, x):
        grad = joint_grad(made)
        g_rows = made.pop() if parts == 1 else mm_tn(x, grad).astype(BF)
        return grad, chain(g_rows, QC), made

    d_fill = AttentionBackward(
        parts, d_p, *d_qkv, up_rows, w_dproj, d_att, True, None, [dn], causal=True
    )
    k_effout = chain(mm_tn(e_act, e_up_rows).astype(BF), 0, True)
    moving = [k_dffin, k_dffout, k_cq, k_ckv, k_cproj, k_effout]
    ((e_up, e_up_rows, dg_effn, pre_grad),), got, made = stage(
        12,
        planes,
        [
            Stage(
                [e_up_rows, e_pre, w_effout],
                w_effin,
                e_up,
                flip=True,
                maker=FeedForwardBack,
                back=(e_mid, g_effn),
                gather="low",
            )
        ],
        steps_of(moving),
        d_fill,
    )
    settle(moving, got)
    d_rows_grad, k_dqkv, (d_dbv, g_dproj) = self_grads(made, dn)
    k_dproj = proj_chain(g_dproj)
    k_effin = chain(mm_tn(e_fn, pre_grad).astype(BF), hidden)
    k_eproj = proj_chain(mm_tn(e_att, e_up_rows).astype(BF))
    e_fill = AttentionBackward(
        parts, e_p, *e_qkv, e_up_rows, w_eproj, e_att, True, mkv, [en], False
    )
    moving += [k_dqkv, k_dproj, k_effin, k_eproj]
    ((d_in, dg_dec, d_in_low),), got, made = stage(
        11,
        planes,
        [Stage([d_rows_grad], w_dqkv, up, flip=True, back=(xd, g_dec), low=True)],
        steps_of(moving),
        e_fill,
    )
    settle(moving, got)
    e_rows_grad, k_eqkv, (e_dbv, d_mkv) = self_grads(made, en)
    k_table = chain(mm_tn(pick, d_mkv).astype(BF), QC)
    moving += [k_eqkv, k_table]
    ((e_in, dg_enc, e_in_low),), got, _ = stage(
        13,
        planes,
        [Stage([e_rows_grad], w_eqkv, e_up, flip=True, back=(xe, g_enc), low=True)],
        steps_of(moving) + [swap_job(d_in_low)],
    )
    (came,) = settle(moving, got)
    dec_ingrad = joined(d_in, came)

    def rel_grads(*dbvs):
        own = lax.dot_general(
            onehot.astype(F32),
            jnp.concatenate(dbvs, axis=0).reshape(len(dbvs) * HQ, -1),
            (((0,), (1,)), ((), ())),
            precision=lax.Precision.HIGHEST,
            preferred_element_type=F32,
        )
        heads = jnp.arange(HEADS, dtype=jnp.int32)[None, :] // HQ == tp
        return [
            jnp.where(heads, jnp.tile(own[:, HQ * i : HQ * (i + 1)], (1, TP)), 0.0)
            for i in range(len(dbvs))
        ]

    tiny = [v.reshape(planes, -1) for v in (dg_enc, dg_effn, dg_dec, dg_cross, dg_dffn)]
    tiny += [v.reshape(planes, -1) for v in rel_grads(e_dbv, d_dbv)]
    tiny = jnp.concatenate(tiny, axis=1).reshape(-1, 128)
    if parts > 1:
        tiny = lax.psum(tiny, "part")
    hurry(moving)
    tiny, came, *got = ship(
        14,
        planes,
        [total_job("fsdp", tiny, planes), swap_job(e_in_low)] + steps_of(moving),
    )
    enc_ingrad = joined(e_in, came)
    settle(moving, got)
    hurry(moving)
    tiny, *got = ship(15, planes, [spread_job(tiny, True)] + steps_of(moving))
    settle(moving, got)

    def proj_rows(k):
        full = lax.dynamic_update_slice_in_dim(jnp.zeros((D, D), BF), k.value, QC * tp, 0)
        full = lax.psum_scatter(full, "fsdp", scatter_dimension=0, tiled=True)
        return lax.psum(full.astype(F32), CTX)

    ready = [k_dffin, k_dffout, k_effin, k_effout, k_cq, k_ckv, k_dqkv, k_eqkv, k_table]
    k_projs = [k_eproj, k_dproj, k_cproj]
    if turned:
        ready += k_projs
    results = laid_out([k.value for k in ready], [k.width for k in ready])
    o_eproj, o_dproj, o_cproj = results[9:] if turned else [proj_rows(k) for k in k_projs]
    o_dffin, o_dffout, o_effin, o_effout, o_cq, o_ckv, o_dqkv, o_eqkv, o_table = results[:9]
    tiny = lax.dynamic_index_in_dim(tiny.reshape(planes, -1), plane, 0, keepdims=False)
    o_gains = [tiny[per * i : per * (i + 1)] for i in range(5)]
    o_rels = [
        tiny[5 * per + per_rel * i : 5 * per + per_rel * (i + 1)].reshape(-1, HEADS)
        for i in range(2)
    ]
    return (
        enc_output,
        dec_output,
        enc_ingrad,
        dec_ingrad,
        o_table,
        o_gains[0],
        o_eqkv,
        o_rels[0],
        o_eproj,
        o_gains[1],
        o_effin,
        o_effout,
        o_gains[2],
        o_dqkv,
        o_rels[1],
        o_dproj,
        o_gains[3],
        o_cq,
        o_ckv,
        o_cproj,
        o_gains[4],
        o_dffin,
        o_dffout,
    )


def solution(mesh):
    ctx, planes = mesh.shape["ctx"], mesh.shape["fsdp"]
    parts = ctx // (2 * TP)
    inner = Mesh(np.asarray(mesh.devices).reshape(2, parts, TP, planes), ALL)
    rows3 = P("fsdp", CTX, None)
    mat, vec = P("fsdp", None), P("fsdp")
    args = (
        (rows3, rows3, P("fsdp", CTX), P("fsdp", None, None), P(), mat)
        + (vec, mat, mat, mat, vec, mat, mat)
        + (vec, mat, mat, mat)
        + (vec, mat, mat, mat)
        + (vec, mat, mat)
        + (rows3, rows3)
    )
    outs = (
        (rows3, rows3, rows3, rows3, mat)
        + (vec, mat, mat, mat, vec, mat, mat)
        + (vec, mat, mat, mat)
        + (vec, mat, mat, mat)
        + (vec, mat, mat)
    )
    return jax.shard_map(
        functools.partial(per_device, parts, planes),
        mesh=inner,
        in_specs=args,
        out_specs=outs,
        check_vma=False,
    )
```

```python
import collections
import functools

import jax
import jax.numpy as jnp
import numpy as np
from jax import lax
from jax.experimental import pallas as pl
from jax.experimental.pallas import tpu as pltpu
from jax.sharding import Mesh
from jax.sharding import PartitionSpec as P

D = 768
HEADS = 12
DH = 64
BUCKETS = 32
EPS = 1e-06
MASKED = -1e30
TP = 4
HQ = HEADS // TP
QC = HQ * DH
BF = jnp.bfloat16
F32 = jnp.float32
MESH_ID = pl.DeviceIdType.MESH
MB = 1024 * 1024
VMEM_LIMIT = 60 * MB
SHARE = (0.25, 0.34, 0.75)


def mm(a, b):
    return jnp.dot(a, b, preferred_element_type=F32)


def mm_tn(a, b):
    return lax.dot_general(a, b, (((0,), (0,)), ((), ())), preferred_element_type=F32)


def mm_nt(a, b):
    return lax.dot_general(a, b, (((1,), (1,)), ((), ())), preferred_element_type=F32)


def gelu(v):
    return jax.nn.gelu(v, approximate=True)


def gelu_back(pre, grad):
    return jax.vjp(gelu, pre)[1](grad)[0]


def group_ids():
    me = lax.axis_index("tp")
    core = me + 1 - 2 * lax.rem(me, 2)
    across = lax.rem(me + 2, TP)
    far = lax.rem(core + 2, TP)
    return me, core, across, far


def send(src, dst, send_sem, recv_sem, peer):
    return pltpu.make_async_remote_copy(
        src_ref=src,
        dst_ref=dst,
        send_sem=send_sem,
        recv_sem=recv_sem,
        device_id={"tp": peer},
        device_id_type=MESH_ID,
    )


def normed(values, gains):
    return values * lax.rsqrt(jnp.mean(values * values, axis=-1, keepdims=True) + EPS) * gains


class Gatherer:
    def __init__(self, buf, stage, sems, chunk, ids):
        self.buf, self.stage, self.sems, self.chunk, self.ids = buf, stage, sems, chunk, ids
        self.sends, self.own = [], []

    def rows(self, j, owner):
        return self.buf.at[pl.ds(pl.multiple_of((TP * j + owner) * self.chunk, self.chunk), self.chunk)]

    def put(self, j, value):
        me, core, across, far = self.ids
        mine = self.stage.at[j]
        mine[...] = value
        x_copy = send(mine, self.rows(j, me), self.sems.at[0, j], self.sems.at[1, j], across)
        x_copy.start()
        c_copy = send(mine, self.rows(j, me), self.sems.at[2, j], self.sems.at[3, j], core)
        c_copy.start()
        self.sends += [x_copy, c_copy]
        own = pltpu.make_async_copy(mine, self.rows(j, me), self.sems.at[6, j])
        own.start()
        self.own.append(own)

    def forward(self, j):
        me, core, across, far = self.ids
        theirs = self.rows(j, across)
        send(theirs, theirs, self.sems.at[0, j], self.sems.at[1, j], across).wait_recv()
        f_copy = send(theirs, theirs, self.sems.at[4, j], self.sems.at[5, j], core)
        f_copy.start()
        self.sends.append(f_copy)

    def finish(self):
        me, core, across, far = self.ids
        for j in range(2):
            a = self.rows(j, core)
            send(a, a, self.sems.at[2, j], self.sems.at[3, j], core).wait_recv()
            b = self.rows(j, far)
            send(b, b, self.sems.at[4, j], self.sems.at[5, j], core).wait_recv()
        for copy in self.sends:
            copy.wait_send()
        for copy in self.own:
            copy.wait()


Job = collections.namedtuple("Job", ["axis", "src_axis", "dst_axis", "local", "src", "shape", "finish"])


def gather_job(axis, src, size=2, at=0):
    shape = src.shape[:at] + (size,) + src.shape[at:]
    return Job(axis, None, at, True, src, shape, None)


def total_job(axis, src, size=2):
    return gather_job(axis, src, size)._replace(finish="sum")


def deal_job(axis, src):
    return Job(axis, 0, 0, True, src, src.shape, "sum")


def swap_job(src, at=0, add=False):
    if at == "cols":
        shape = src.shape[:-1] + (src.shape[-1] // 2,)
    else:
        shape = src.shape[:at] + src.shape[at + 1 :]
    return Job("seq", at, None, add, src, shape, "add" if add else None)


def turn_job(src):
    return Job("turn", None, None, True, src, src.shape, None)


def block_job(src):
    return Job("ctx", 0, 0, True, src, (2 * TP,) + src.shape[1:], None)


def spread_job(src, add=False):
    return Job("all", None, None, True, src, (2, 2, 2) + src.shape, "sum3" if add else None)


def result_of(job):
    skip = {"sum": 1, "sum3": 3}.get(job.finish, 0)
    return job.shape[skip:], job.src.dtype


def entry(ref, axis, index):
    if axis == "cols":
        half = ref.shape[-1] // 2
        return ref.at[:, :, pl.ds(pl.multiple_of(index * half, half), half)]
    return ref if axis is None else ref.at[(slice(None),) * axis + (index,)]


class Shipper:
    def __init__(self, jobs, planes, srcs, outs, scratch, sems):
        self.jobs, self.planes, self.srcs, self.outs, self.sems = jobs, planes, srcs, outs, sems
        self.tp, self.seq, self.plane = (lax.axis_index(n) for n in ("tp", "seq", "fsdp"))
        self.dsts, self.bounce, self.made = [], [], []
        for job, out in zip(jobs, outs):
            if job.finish:
                self.dsts.append(scratch.pop(0))
                self.bounce.append(scratch.pop(0) if job.finish == "add" else None)
                self.made.append(scratch.pop(0) if job.finish != "add" else None)
            else:
                self.dsts.append(out)
                self.bounce.append(scratch.pop(0) if job.local else None)
                self.made.append(None)

    @staticmethod
    def scratch(jobs):
        shapes = []
        for job in jobs:
            dtype = job.src.dtype
            if job.finish:
                shapes.append(pltpu.VMEM(job.shape, dtype))
                if job.finish == "add":
                    shapes.append(pltpu.VMEM(job.shape, dtype))
                else:
                    shapes.append(pltpu.VMEM(*result_of(job)))
            elif job.axis == "all":
                shapes.append(pltpu.VMEM(job.src.shape, dtype))
            elif job.local:
                drop = job.dst_axis
                own = job.shape if drop is None else job.shape[:drop] + job.shape[drop + 1 :]
                shapes.append(pltpu.VMEM(own, dtype))
        return shapes

    @staticmethod
    def count(jobs, planes):
        return sum(2 * Shipper.n_peers(job, planes) + 2 for job in jobs)

    @staticmethod
    def n_peers(job, planes):
        return {"fsdp": planes - 1, "ctx": 2 * TP - 1, "all": 2 * TP - 1}.get(job.axis, 1)

    def coord(self, axis):
        half = self.tp // 2
        return {
            "fsdp": self.plane,
            "seq": self.seq,
            "across": half,
            "core": self.tp - 2 * half,
            "ctx": TP * self.seq + self.tp,
            "turn": None,
        }[axis]

    def peers(self, axis):
        if axis == "fsdp":
            n, z = self.planes, self.plane
            for k in range(1, n):
                to = lax.rem(z + k, n)
                yield to, {"fsdp": to}, lax.rem(z + (n - k), n)
        elif axis == "ctx":
            for k in range(1, 2 * TP):
                to = lax.rem(self.seq + k // TP, 2)
                to_tp = lax.rem(self.tp + k % TP, TP)
                from_seq = lax.rem(self.seq + (2 - k // TP), 2)
                from_tp = lax.rem(self.tp + (TP - k % TP), TP)
                yield to, {"seq": to, "tp": to_tp}, TP * from_seq + from_tp
        elif axis == "seq":
            yield 1 - self.seq, {"seq": 1 - self.seq}, 1 - self.seq
        elif axis == "turn":
            yield None, {"fsdp": self.tp, "tp": self.plane}, None
        else:
            to = lax.rem(self.tp + 2, TP) if axis == "across" else self.tp + 1 - 2 * lax.rem(self.tp, 2)
            other = 1 - self.coord(axis)
            yield other, {"tp": to}, other

    def signal(self, always=("core", "across")):
        wanted = {job.axis for job in self.jobs}
        if "all" in wanted:
            wanted = (wanted - {"all"}) | {"seq", "across", "core"}
        axes = list(always) + sorted(wanted - set(always))
        barrier = pltpu.get_barrier_semaphore()
        self.expected, self.turns = 0, "turn" in axes
        for axis in axes:
            for _, device, _ in self.peers(axis):
                if axis == "turn":

                    @pl.when(self.plane != self.tp)
                    def _():
                        pl.semaphore_signal(
                            barrier, inc=1, device_id=device, device_id_type=MESH_ID
                        )

                    continue
                pl.semaphore_signal(barrier, inc=1, device_id=device, device_id_type=MESH_ID)
                self.expected += 1

    def met(self):
        barrier = pltpu.get_barrier_semaphore()
        if self.turns:
            moves = self.plane != self.tp

            @pl.when(moves)
            def _():
                pl.semaphore_wait(barrier, self.expected + 1)

            @pl.when(jnp.logical_not(moves))
            def _():
                pl.semaphore_wait(barrier, self.expected)
        else:
            pl.semaphore_wait(barrier, self.expected)

    def greet(self, always=("core", "across")):
        self.signal(always)
        self.met()

    def each(self, act_remote, act_local):
        base = 0
        for n, (job, src, dst) in enumerate(zip(self.jobs, self.srcs, self.dsts)):
            if job.axis == "all":
                base += 2 * self.n_peers(job, self.planes) + 2
                continue
            mine = self.coord(job.axis)
            peers = list(self.peers(job.axis))
            for i, (to, device, source) in enumerate(peers):
                sems = (self.sems.at[base + 2 * i], self.sems.at[base + 2 * i + 1])

                def copy_into(slot, to=to, device=device, sems=sems, src=src, dst=dst, job=job):
                    return pltpu.make_async_remote_copy(
                        src_ref=entry(src, job.src_axis, to),
                        dst_ref=entry(dst, job.dst_axis, slot),
                        send_sem=sems[0],
                        recv_sem=sems[1],
                        device_id=device,
                        device_id_type=MESH_ID,
                    )

                def remote(copy_into=copy_into, source=source, mine=mine):
                    act_remote(copy_into, mine, source)

                if job.axis == "turn":
                    pl.when(self.plane != self.tp)(remote)
                else:
                    remote()
            if job.local:
                own = self.seq if job.axis == "ctx" else mine

                def local(n=n, job=job, src=src, dst=dst, own=own, mine=mine, sem=base + 2 * len(peers)):
                    here, there = entry(src, job.src_axis, own), entry(dst, job.dst_axis, mine)
                    bounce = self.bounce[n]
                    if bounce is None:
                        act_local([(here, there)], self.sems.at[sem])
                    elif job.finish == "add":
                        act_local([(here, bounce)], self.sems.at[sem])
                    else:
                        act_local([(here, bounce), (bounce, there)], self.sems.at[sem])

                if job.axis == "turn":
                    pl.when(self.plane == self.tp)(local)
                else:
                    local()
            base += 2 * len(peers) + 2
        return base

    def spreads(self):
        s, x, c = self.coord("seq"), self.coord("across"), self.coord("core")
        seq, across, core = (next(self.peers(axis))[1] for axis in ("seq", "across", "core"))
        moves = [
            ((s, x, c), across, (s, 1 - x, c)),
            ((s, x, c), seq, (1 - s, x, c)),
            ((s, x, c), core, (s, x, 1 - c)),
            ((s, 1 - x, c), seq, (1 - s, 1 - x, c)),
            ((s, 1 - x, c), core, (s, 1 - x, 1 - c)),
            ((1 - s, x, c), core, (1 - s, x, 1 - c)),
            ((1 - s, 1 - x, c), core, (1 - s, 1 - x, 1 - c)),
        ]
        base = 0
        for job, src, dst, bounce in zip(self.jobs, self.srcs, self.dsts, self.bounce):
            if job.axis == "all":

                def copy(k, arrives=False, src=src, dst=dst, base=base):
                    what, device, other = moves[k]
                    return pltpu.make_async_remote_copy(
                        src_ref=src if k < 3 else dst.at[what],
                        dst_ref=dst.at[other if arrives else what],
                        send_sem=self.sems.at[base + 2 * k],
                        recv_sem=self.sems.at[base + 2 * k + 1],
                        device_id=device,
                        device_id_type=MESH_ID,
                    )

                own = dst.at[s, x, c]
                legs = [(src, own)] if bounce is None else [(src, bounce), (bounce, own)]
                legs = [
                    pltpu.make_async_copy(*leg, self.sems.at[base + 14 + n])
                    for n, leg in enumerate(legs)
                ]
                yield copy, legs
            base += 2 * self.n_peers(job, self.planes) + 2

    def start_spreads(self):
        for copy, legs in self.spreads():
            for k in range(3):
                copy(k).start()
            legs[0].start()

    def finish_spreads(self):
        jobs = list(self.spreads())
        for copy, legs in jobs:
            if len(legs) > 1:
                legs[0].wait()
                legs[1].start()
        for first, then in ((0, (3, 4)), (1, (5,)), (3, (6,))):
            for copy, legs in jobs:
                copy(first, True).wait_recv()
                for k in then:
                    copy(k).start()
        for copy, legs in jobs:
            for k in (2, 4, 5, 6):
                copy(k, True).wait_recv()
            for k in range(7):
                copy(k).wait_send()
            legs[-1].wait()

    def start(self):
        if any(job.axis == "all" for job in self.jobs):
            self.start_spreads()
        self.each(
            lambda copy_into, mine, source: copy_into(mine).start(),
            lambda legs, sem: pltpu.make_async_copy(*legs[0], sem).start(),
        )

    def finish(self):
        def turn_round(legs, sem):
            if len(legs) > 1:
                pltpu.make_async_copy(*legs[0], sem).wait()
                pltpu.make_async_copy(*legs[1], sem).start()

        def remote(copy_into, mine, source):
            copy_into(source).wait_recv()
            copy_into(mine).wait_send()

        if any(job.axis == "all" for job in self.jobs):
            self.finish_spreads()
        self.each(lambda *_: None, turn_round)
        self.each(remote, lambda legs, sem: pltpu.make_async_copy(*legs[-1], sem).wait())
        stores, base = [], 0
        for job, dst, bounce, made, out in zip(
            self.jobs, self.dsts, self.bounce, self.made, self.outs
        ):
            base += 2 * self.n_peers(job, self.planes) + 2
            if not job.finish:
                continue
            if job.finish == "add":
                made = bounce

                @pl.loop(0, dst.shape[0])
                def _(i):
                    bounce[i] = (bounce[i].astype(F32) + dst[i].astype(F32)).astype(bounce.dtype)

            else:
                pieces = [dst.at[i] for i in range(dst.shape[0])]
                if job.finish == "sum3":
                    pieces = [dst.at[i, j, k] for i in range(2) for j in range(2) for k in range(2)]
                total = pieces[0][...].astype(F32)
                for piece in pieces[1:]:
                    total = total + piece[...].astype(F32)
                made[...] = total.astype(made.dtype)
            store = pltpu.make_async_copy(made, out, self.sems.at[base - 1])
            store.start()
            stores.append(store)
        for store in stores:
            store.wait()


def lay_out(src, dst, width):
    seqs, halves, cores, rows, cols = src.shape
    if width < 0:
        for i in range(seqs):
            for q in range(TP):
                block = slice(i * cols, (i + 1) * cols)
                dst[q * rows : (q + 1) * rows, block] = src[i, q // 2, q % 2].astype(F32)
        return

    @pl.loop(0, seqs)
    def _(i):
        if not width:
            for q in range(TP):
                at = pl.multiple_of((q * seqs + i) * rows, rows)
                dst[pl.ds(at, rows)] = src[i, q // 2, q % 2].astype(F32)
        else:
            at = pl.multiple_of(i * rows, rows)
            for n in range(cols // width):
                span = slice(n * width, (n + 1) * width)
                parts = [src[i, q // 2, q % 2, :, span].astype(F32) for q in range(TP)]
                block = slice(n * width * TP, (n + 1) * width * TP)
                dst[pl.ds(at, rows), block] = jnp.concatenate(parts, axis=1)


def laid_out(pieces, widths):
    shapes = []
    for p, width in zip(pieces, widths):
        seqs, halves, cores, rows, cols = p.shape
        if width < 0:
            shapes.append((halves * cores * rows, seqs * cols))
        elif width:
            shapes.append((seqs * rows, halves * cores * cols))
        else:
            shapes.append((seqs * halves * cores * rows, cols))
    n = len(pieces)

    def body(*refs):
        srcs, outs, got, made, sems = refs[:n], refs[n : 2 * n], refs[2 * n : 3 * n], refs[3 * n : 4 * n], refs[4 * n]
        loads = [pltpu.make_async_copy(srcs[i], got[i], sems.at[0, i]) for i in range(n)]
        stores = [pltpu.make_async_copy(made[i], outs[i], sems.at[1, i]) for i in range(n)]
        for load in loads:
            load.start()
        for i in range(n):
            loads[i].wait()
            lay_out(got[i], made[i], widths[i])
            stores[i].start()
        for store in stores:
            store.wait()

    return pl.pallas_call(
        body,
        out_shape=tuple(jax.ShapeDtypeStruct(shape, F32) for shape in shapes),
        in_specs=[HBM_SPEC] * n,
        out_specs=(HBM_SPEC,) * n,
        scratch_shapes=[pltpu.VMEM(p.shape, p.dtype) for p in pieces]
        + [pltpu.VMEM(shape, F32) for shape in shapes]
        + [pltpu.SemaphoreType.DMA((2, n))],
        compiler_params=pltpu.CompilerParams(vmem_limit_bytes=VMEM_LIMIT),
        name="lay_out",
    )(*pieces)


HBM_SPEC = pl.BlockSpec(memory_space=pltpu.HBM)


class Loaded:
    def __init__(self, src, dst, sem, start=True):
        self.copy, self.ref, self.waited = pltpu.make_async_copy(src, dst, sem), dst, False
        if start:
            self.copy.start()

    def get(self):
        if not self.waited:
            self.copy.wait()
            self.waited = True
        return self.ref


class LoadedRows:
    def __init__(self, src, dst, sems, chunk):
        self.src, self.ref, self.sems, self.chunk = src, dst, sems, chunk

    def copies(self, owner, slot):
        for j in range(2):
            at = pl.multiple_of((TP * j + owner) * self.chunk, self.chunk)
            rows = pl.ds(at, self.chunk)
            yield pltpu.make_async_copy(
                self.src.at[rows], self.ref.at[rows], self.sems.at[2 * slot + j]
            )

    def start(self, owners):
        for slot, owner in enumerate(owners):
            for copy in self.copies(owner, slot):
                copy.start()

    def wait(self, owner, slot):
        for copy in self.copies(owner, slot):
            copy.wait()


def call_with_jobs(
    kernel, number, planes, jobs, operands, outs, scratch, name, cost, filler=None, by_rows=()
):
    filler = filler or Idle()
    jobs = list(jobs)
    n_in, n_out, n_job = len(operands), len(outs), len(jobs)
    n_load, n_raw, n_fill = len(filler.loads), len(filler.raws), len(filler.outs)
    loads, raws = list(filler.loads), list(filler.raws)
    n_sems = max(Shipper.count(jobs, planes), 1)
    plain = [job._replace(src=jax.ShapeDtypeStruct(job.src.shape, job.src.dtype)) for job in jobs]
    job_scratch = Shipper.scratch(jobs)
    n_scratch = len(filler.scratch)

    def body(*refs):
        refs = list(refs)

        def take(n):
            out = refs[:n]
            del refs[:n]
            return out

        ins, srcs, fills, raw = take(n_in), take(n_job), take(n_load), take(n_raw)
        results, dsts, fill_outs = take(n_out), take(n_job), take(n_fill)
        sems, in_sems, row_sems = take(3)
        loaded = []
        for i, src in enumerate(ins):
            if i in by_rows:
                rows = row_sems.at[by_rows.index(i)]
                loaded.append(LoadedRows(src, refs.pop(0), rows, src.shape[0] // (2 * TP)))
            else:
                loaded.append(Loaded(src, refs.pop(0), in_sems.at[i]))
        fill_loads = [
            Loaded(src, refs.pop(0), in_sems.at[n_in + i], False) for i, src in enumerate(fills)
        ]
        shipper = Shipper(plain, planes, srcs, dsts, take(len(job_scratch)), sems)
        begin = functools.partial(filler.begin, fill_loads, raw, fill_outs, take(n_scratch))
        kernel(shipper, loaded, list(results), refs, Running(filler, begin, fill_loads))

    results = [result_of(job) for job in jobs]
    got = pl.pallas_call(
        body,
        out_shape=tuple(outs)
        + tuple(jax.ShapeDtypeStruct(*r) for r in results)
        + tuple(filler.outs),
        in_specs=[HBM_SPEC] * (n_in + n_job + n_load + n_raw),
        out_specs=(HBM_SPEC,) * (n_out + n_job + n_fill),
        scratch_shapes=[
            pltpu.SemaphoreType.DMA((n_sems,)),
            pltpu.SemaphoreType.DMA((max(n_in + n_load, 1),)),
            pltpu.SemaphoreType.DMA((max(len(by_rows), 1), 2 * TP)),
        ]
        + [pltpu.VMEM(v.shape, v.dtype) for v in operands + loads]
        + job_scratch
        + list(filler.scratch)
        + scratch,
        compiler_params=pltpu.CompilerParams(
            collective_id=number, has_side_effects=True, vmem_limit_bytes=VMEM_LIMIT
        ),
        cost_estimate=pl.CostEstimate(flops=cost, bytes_accessed=8 * MB, transcendentals=0),
        name=name,
    )(*operands, *[job.src for job in jobs], *loads, *raws)
    return got[:n_out], list(got[n_out : n_out + n_job]), list(got[n_out + n_job :])


class Running:
    def __init__(self, filler, begin, loads):
        self.begin, self.run, self.end, self.loads = begin, filler.run, filler.end, loads
        self.n_steps, self.done = filler.n_steps, 0

    def prefetch(self):
        for load in self.loads:
            load.copy.start()

    def advance(self, share):
        high = int(round(share * self.n_steps))
        if high > self.done:
            self.run(self.done, high)
            self.done = high


def ship(number, planes, jobs):
    def kernel(shipper, ins, outs, scratch, filler):
        shipper.greet(())
        shipper.start()
        shipper.finish()

    return call_with_jobs(kernel, number, planes, jobs, [], [], [], "ship", 0)[1]


class GatherNormed:
    by_rows = ()

    def __init__(self, x, gain):
        self.chunk = x.shape[1]
        self.operands, self.cost = [x, gain], 10**6
        self.outs = [jax.ShapeDtypeStruct((2 * TP * self.chunk, D), BF)]
        self.scratch = [pltpu.VMEM((2, self.chunk, D), BF), pltpu.SemaphoreType.DMA((7, 2))]

    def bind(self, ins, outs, scratch):
        self.x, self.gain = ins
        self.g = Gatherer(outs[0], scratch[0], scratch[1], self.chunk, group_ids())

    def load(self):
        pass

    def first(self, met):
        x_ref, gain_ref = self.x.get(), self.gain.get()
        met()
        for j in range(2):
            self.g.put(j, normed(x_ref[j].astype(F32), gain_ref[...]).astype(BF))

    def second(self, between):
        between()

    def third(self):
        for j in range(2):
            self.g.forward(j)

    def last(self):
        self.g.finish()


GELU_C = float(np.sqrt(2.0 / np.pi))


def gelu_parts(v):
    tanh = jnp.tanh(GELU_C * (v + 0.044715 * v * v * v))
    return tanh, 0.5 * (1.0 + tanh)


def gelu_slope(v):
    tanh, half = gelu_parts(v)
    return half + 0.5 * v * (1.0 - tanh * tanh) * (GELU_C * (1.0 + 3 * 0.044715 * v * v))


class Rows:
    n_operands, n_outs, n_scratch = 1, 0, 0

    def __init__(self, ins, outs, scratch, chunk):
        self.rows, self.chunk = ins.pop(0), chunk
        self.by_rows = [self.rows]

    def prepare(self):
        self.ref = self.rows.ref

    def make(self, pair, slot):
        pass

    def finish(self):
        pass

    def pick(self, ref, pair):
        return jnp.concatenate([ref[rows] for rows in pair], axis=0)


class MadeRows(Rows):
    def write(self, index, ref, out, slot, pair):
        for j, rows in enumerate(pair):
            copy = pltpu.make_async_copy(ref.at[rows], out.at[rows], self.sems.at[index, 2 * slot + j])
            copy.start()
            self.copies.append(copy)

    def finish(self):
        for copy in self.copies:
            copy.wait()

    def tiles(self, body):
        @pl.loop(0, self.ref.shape[1] // 256)
        def _(n):
            body(pl.ds(pl.multiple_of(n * 256, 256), 256))


class FeedForward(MadeRows):
    n_operands, n_outs, n_scratch = 2, 2, 3

    def __init__(self, ins, outs, scratch, chunk):
        self.rows, self.w_in, self.chunk, self.copies = ins.pop(0), ins.pop(0), chunk, []
        self.by_rows = [self.rows]
        self.pre_out, self.act_out = outs.pop(0), outs.pop(0)
        self.pre, self.ref, self.sems = scratch.pop(0), scratch.pop(0), scratch.pop(0)

    @staticmethod
    def extras(n_rows, width):
        shapes = [((n_rows, width), F32), ((n_rows, width), BF)]
        scratch = [pltpu.VMEM(*v) for v in shapes] + [pltpu.SemaphoreType.DMA((2, 2 * TP))]
        return [jax.ShapeDtypeStruct(*v) for v in shapes], scratch

    def prepare(self):
        self.w_in = self.w_in.get()

    def make(self, pair, slot):
        x = self.pick(self.rows.ref, pair)

        def tile(cols):
            v = mm(x, self.w_in[:, cols])
            act = (v * gelu_parts(v)[1]).astype(BF)
            for j, rows in enumerate(pair):
                self.pre[rows, cols] = v[j * self.chunk : (j + 1) * self.chunk]
                self.ref[rows, cols] = act[j * self.chunk : (j + 1) * self.chunk]

        self.tiles(tile)
        self.write(0, self.pre, self.pre_out, slot, pair)
        self.write(1, self.ref, self.act_out, slot, pair)


class FeedForwardBack(MadeRows):
    n_operands, n_outs, n_scratch = 3, 1, 2

    def __init__(self, ins, outs, scratch, chunk):
        self.rows, self.pre, self.w_out = ins.pop(0), ins.pop(0), ins.pop(0)
        self.chunk, self.copies = chunk, []
        self.by_rows = [self.rows, self.pre]
        self.out, self.ref, self.sems = outs.pop(0), scratch.pop(0), scratch.pop(0)

    @staticmethod
    def extras(n_rows, width):
        shape = ((n_rows, width), BF)
        scratch = [pltpu.VMEM(*shape), pltpu.SemaphoreType.DMA((1, 2 * TP))]
        return [jax.ShapeDtypeStruct(*shape)], scratch

    def prepare(self):
        self.w_out = self.w_out.get()

    def make(self, pair, slot):
        x = self.pick(self.rows.ref, pair)

        def tile(cols):
            grad = mm_nt(x, self.w_out[cols, :])
            for j, rows in enumerate(pair):
                back = gelu_slope(self.pre.ref[rows, cols]) * grad[j * self.chunk : (j + 1) * self.chunk]
                self.ref[rows, cols] = back.astype(BF)

        self.tiles(tile)
        self.write(0, self.ref, self.out, slot, pair)


class Stage:
    def __init__(
        self,
        left,
        weight,
        resid,
        *,
        flip=False,
        maker=Rows,
        back=None,
        gather=None,
        gain=None,
        given=None,
        dtype=F32,
        low=False,
    ):
        self.maker, self.flip, self.back, self.gather, self.low = maker, flip, bool(back), gather, low
        self.chunk = chunk = resid.shape[1]
        self.operands = list(left) + [weight, resid]
        self.cost = 4 * left[0].shape[0] * D * D
        self.by_rows = {Rows: (0,), FeedForward: (0,), FeedForwardBack: (0, 1)}[maker]
        if back:
            self.operands += [back[1], back[0]]
        elif gather == "norm":
            self.operands.append(gain)
        if gather == "given":
            self.operands.append(given)
        self.outs = [jax.ShapeDtypeStruct((2, chunk, D), dtype)]
        if gather:
            self.outs.append(jax.ShapeDtypeStruct((2 * TP * chunk, D), BF))
        if back:
            self.outs.append(jax.ShapeDtypeStruct((1, D), F32))
        half = pltpu.VMEM((2, chunk, D), BF)
        full = pltpu.VMEM((2, chunk, D), F32)
        self.scratch = [half] * 6 + [full] * 2
        self.scratch += [pltpu.VMEM((2, chunk, D), dtype), pltpu.SemaphoreType.DMA((13,))]
        if gather:
            self.scratch += [half, pltpu.SemaphoreType.DMA((7, 2))]
        if back:
            self.scratch.append(pltpu.VMEM((1, D), F32))
        if low:
            self.outs.append(jax.ShapeDtypeStruct((2, chunk, D), BF))
            self.scratch.append(half)
        if maker is not Rows:
            width = weight.shape[1] if flip else weight.shape[0]
            more, more_scratch = maker.extras(2 * TP * chunk, width)
            self.outs += more
            self.scratch += more_scratch

    def bind(self, ins, outs, scratch):
        maker = self.maker
        made_outs = [outs.pop() for _ in range(maker.n_outs)][::-1]
        made_scratch = [scratch.pop() for _ in range(maker.n_scratch)][::-1]
        self.left = maker(ins, made_outs, made_scratch, self.chunk)
        self.w_in, self.resid_in = ins.pop(0), ins.pop(0)
        self.gain_in = ins.pop(0) if (self.back or self.gather == "norm") else None
        self.x_in = ins.pop(0) if self.back else None
        self.given_in = ins.pop(0) if self.gather == "given" else None
        self.y_out = outs.pop(0)
        gath_ref = outs.pop(0) if self.gather else None
        self.dgain_out = outs.pop(0) if self.back else None
        self.low_out = outs.pop(0) if self.low else None
        self.s_far, self.r_far, self.s_x, self.r_x, self.s_core, self.r_core = scratch[:6]
        self.keep, self.own, self.y_ref, self.sems = scratch[6:10]
        scratch = scratch[10:]
        self.ids = group_ids()
        self.g = None
        if self.gather:
            self.g = Gatherer(gath_ref, scratch.pop(0), scratch.pop(0), self.chunk, self.ids)
        self.dgain_ref = scratch.pop(0) if self.back else None
        self.low_ref = scratch.pop(0) if self.low else None
        self.slots, self.stores = [0, 1, 2, 3], []

    def load(self):
        me, core, across, far = self.ids
        for rows in self.left.by_rows:
            rows.start((far, across, core, me))

    def partial(self, owner, ref):
        slot, chunk, left = self.slots.pop(0), self.chunk, self.left
        for rows in left.by_rows:
            rows.wait(owner, slot)
        pair = [
            pl.ds(pl.multiple_of((TP * j + owner) * chunk, chunk), chunk) for j in range(2)
        ]
        left.make(pair, slot)
        a = left.pick(left.ref, pair)

        @pl.loop(0, D // 256)
        def _(n):
            cols = pl.ds(pl.multiple_of(n * 256, 256), 256)
            total = mm_nt(a, self.w_ref[cols, :]) if self.flip else mm(a, self.w_ref[:, cols])
            for j in range(2):
                ref[j, :, cols] = total[j * chunk : (j + 1) * chunk].astype(ref.dtype)

    def first(self, met):
        me, core, across, far = self.ids
        sems = self.sems
        self.left.prepare()
        self.w_ref = self.w_in.get()
        self.partial(far, self.s_far)
        met()
        self.c_far = send(self.s_far, self.r_far, sems.at[0], sems.at[1], core)
        self.c_far.start()
        if self.gather == "given":
            given_ref = self.given_in.get()
            for j in range(2):
                self.g.put(j, given_ref[j])
        self.partial(across, self.keep)
        self.c_far.wait_recv()
        self.c_x = []
        for j in range(2):
            self.s_x[j] = (self.keep[j] + self.r_far[j].astype(F32)).astype(BF)
            copy = send(self.s_x.at[j], self.r_x.at[j], sems.at[2 + j], sems.at[4 + j], across)
            copy.start()
            self.c_x.append(copy)
        self.partial(core, self.s_core)
        self.c_core = send(self.s_core, self.r_core, sems.at[6], sems.at[7], core)
        self.c_core.start()
        self.partial(me, self.own)

    def keep_out(self, src, dst, sem):
        copy = pltpu.make_async_copy(src, dst, self.sems.at[sem])
        copy.start()
        self.stores.append(copy)

    def second(self, between):
        self.c_core.wait_recv()
        resid_ref = self.resid_in.get()
        x_ref = self.x_in.get() if self.back else None
        gains = self.gain_in.get()[...] if self.gain_in else None
        if self.gather == "given":
            for j in range(2):
                self.g.forward(j)
        for j in range(2):
            self.c_x[j].wait_recv()
            if j == 1:
                between()
            total = self.own[j] + self.r_core[j].astype(F32) + self.r_x[j].astype(F32)
            if self.back:
                x = x_ref[j].astype(F32)
                r = lax.rsqrt(jnp.mean(x * x, axis=-1, keepdims=True) + EPS)
                scaled = total * gains
                inner = jnp.mean(scaled * x, axis=-1, keepdims=True)
                y = resid_ref[j].astype(F32) + r * scaled - x * (r * r * r * inner)
                dgain = jnp.sum(total * x * r, axis=0, keepdims=True)
                if j == 0:
                    self.dgain_ref[...] = dgain
                else:
                    self.dgain_ref[...] += dgain
            else:
                y = resid_ref[j].astype(F32) + total
            if self.gather == "norm":
                self.g.put(j, normed(y, gains).astype(BF))
            elif self.gather == "low":
                self.g.put(j, y.astype(BF))
            self.y_ref[j] = y.astype(self.y_ref.dtype)
            self.keep_out(self.y_ref.at[j], self.y_out.at[j], 8 + j)
            if self.low:
                self.low_ref[j] = y.astype(BF)
                self.keep_out(self.low_ref.at[j], self.low_out.at[j], 11 + j)
        if self.back:
            self.keep_out(self.dgain_ref, self.dgain_out, 10)

    def third(self):
        if self.gather in ("norm", "low"):
            for j in range(2):
                self.g.forward(j)

    def last(self):
        if self.gather:
            self.g.finish()
        for copy in [self.c_far, self.c_core] + self.c_x:
            copy.wait_send()
        for copy in self.stores:
            copy.wait()
        self.left.finish()


def stage(number, planes, stages, jobs=(), filler=None, share=SHARE):
    operands = [v for st in stages for v in st.operands]
    outs = [v for st in stages for v in st.outs]
    scratch = [v for st in stages for v in st.scratch]
    by_rows, base = [], 0
    for st in stages:
        by_rows += [base + i for i in st.by_rows]
        base += len(st.operands)

    def kernel(shipper, ins, results, refs, filler):
        for st in stages:
            parts = []
            for have, n in ((ins, st.operands), (results, st.outs), (refs, st.scratch)):
                parts.append(have[: len(n)])
                del have[: len(n)]
            st.bind(*parts)
            st.load()
        shipper.signal()

        def met():
            shipper.met()
            shipper.start()

        for n, st in enumerate(stages):
            st.first(met if n == 0 else (lambda: None))
        filler.prefetch()
        filler.begin()
        filler.advance(share[0])
        for n, st in enumerate(stages):
            st.second(lambda: filler.advance(share[1]) if n == 0 else None)
        filler.advance(share[2])
        for st in stages:
            st.third()
        filler.advance(1.0)
        filler.end()
        for st in stages:
            st.last()
        shipper.finish()

    cost = sum(st.cost for st in stages)
    got, moved, made = call_with_jobs(
        kernel, number, planes, jobs, operands, outs, scratch, "stage", cost, filler, tuple(by_rows)
    )
    got = list(got)
    each = []
    for st in stages:
        each.append(got[: len(st.outs)])
        del got[: len(st.outs)]
    return each, moved, made


class Attention:
    def __init__(self, parts, q, kv, bias, mkv, causal):
        self.parts, self.causal = parts, causal
        self.q_shape, self.kv_shape = q.shape, kv.shape
        self.rows, self.keys = q.shape[0], kv.shape[0]
        self.chunk = self.rows // (2 * TP)
        self.joint = q is kv
        self.extra = 0 if mkv is None else mkv.shape[0]
        self.total = self.keys + self.extra
        self.bias = bias
        self.size = 2 * self.chunk
        self.blocks = self.rows // self.size
        self.n_steps = 2 * HQ
        self.loads = [q] + ([] if self.joint else [kv])
        self.mem = [mkv] if self.extra else []
        self.raws = []

    def heads(self, *widths_dtypes):
        return [pltpu.VMEM((HQ, n, DH), dtype) for n, dtype in widths_dtypes]

    def split_qkv(self, q_ref, kv_ref, loads, qs, ks, vs):
        at = QC if self.joint else 0
        keys = self.keys
        for i in range(HQ):
            qs[i] = q_ref[:, DH * i : DH * (i + 1)]
            ks[i, :keys] = kv_ref[:, at + DH * i : at + DH * (i + 1)]
            vs[i, :keys] = kv_ref[:, at + QC + DH * i : at + QC + DH * (i + 1)]
        if self.extra:
            mkv_ref = loads.pop(0).get()
            for i in range(HQ):
                ks[i, keys:] = mkv_ref[:, DH * i : DH * (i + 1)]
                vs[i, keys:] = mkv_ref[:, QC + DH * i : QC + DH * (i + 1)]

    def place(self, row_chunk):
        upper = row_chunk // TP
        part = lax.axis_index("part") if self.parts > 1 else 0
        return (upper * (TP * self.parts) + TP * part + (row_chunk - TP * upper)) * self.chunk

    def halves(self, low, high):
        for half in range(2):
            first = max(low - HQ * half, 0)
            last = min(high - HQ * half, HQ)
            if first < last:
                n = self.blocks // 2
                yield half, range(half * n, (half + 1) * n), first, last

    def width(self, b):
        if self.causal and self.parts == 1:
            return (b + 1) * self.size
        return self.total

    def block(self, b):
        return pl.ds(b * self.size, self.size)

    def diagonal(self, b, u):
        keys = min(self.width(b), self.keys)
        start = self.keys - self.place(2 * b + u)
        return pl.ds(start if isinstance(start, int) else pl.multiple_of(start, 128), keys)


class AttentionForward(Attention):
    def __init__(self, parts, q, kv, segq, segk, bvec, mkv, causal, products=None):
        super().__init__(parts, q, kv, bvec is not None, mkv, causal)
        self.products = products
        if products:
            self.loads = [v for pair in products for v in pair]
        self.loads += self.mem + [segq, segk] + ([bvec] if self.bias else [])
        self.outs = [
            jax.ShapeDtypeStruct((self.rows, QC), BF),
            jax.ShapeDtypeStruct((HQ, self.rows, self.total), BF),
        ]
        self.scratch = self.heads((self.rows, BF), (self.total, BF), (self.total, BF), (self.rows, BF))
        self.scratch += [
            pltpu.VMEM((self.blocks, self.size, self.total), BF),
            pltpu.VMEM((self.rows, QC), BF),
            pltpu.SemaphoreType.DMA((3 + self.blocks,)),
        ]
        if self.bias:
            self.scratch.append(pltpu.VMEM((self.chunk, 2 * self.keys), F32))
        if products:
            for x, w in products:
                self.outs.append(jax.ShapeDtypeStruct((x.shape[0], w.shape[1]), BF))
                self.scratch.append(pltpu.VMEM((x.shape[0], w.shape[1]), BF))

    def begin(self, loads, raws, outs, scratch):
        self.att_out, self.p_out = outs[:2]
        self.qs, self.ks, self.vs, self.os, self.p_buf, self.att, self.sems = scratch[:7]
        self.toep = scratch[7] if self.bias else None
        loads = list(loads)
        self.copies = []
        if self.products:
            made = scratch[-len(self.products) :]
            for n, (out, to) in enumerate(zip(made, outs[2:])):
                x, w = loads.pop(0).get(), loads.pop(0).get()

                @pl.loop(0, x.shape[0] // 256)
                def _(r):
                    rows = pl.ds(pl.multiple_of(r * 256, 256), 256)
                    out[rows] = mm(x[rows], w[...]).astype(BF)

                self.copies.append(pltpu.make_async_copy(out, to, self.sems.at[1 + n]))
                self.copies[-1].start()
            q_ref, kv_ref = made[0], made[-1]
        else:
            q_ref = loads.pop(0).get()
            kv_ref = q_ref if self.joint else loads.pop(0).get()
        self.split_qkv(q_ref, kv_ref, loads, self.qs, self.ks, self.vs)
        self.segq, self.segk = loads.pop(0).get(), loads.pop(0).get()
        self.bvec = loads.pop(0).get() if self.bias else None

    def slot(self, h, b):
        n = self.blocks // 2
        return n * lax.rem(h + (b // n) * HQ, 2) + b % n

    def keep(self, h, b):
        wide, slot = pl.ds(0, self.width(b)), self.slot(h, b)
        return pltpu.make_async_copy(
            self.p_buf.at[slot, :, wide], self.p_out.at[h, self.block(b), wide], self.sems.at[3 + slot]
        )

    def one_block(self, h, b):
        wide, chunk, rows = self.width(b), self.chunk, self.block(b)
        keys = min(wide, self.keys)
        s = mm_nt(self.qs[h, rows], self.ks[h, :wide])
        if self.bias:
            parts = [self.toep[:, self.diagonal(b, u)] for u in range(2)]
            biased = s[:, :keys] + jnp.concatenate(parts, axis=0)
            s = jnp.concatenate([biased, s[:, keys:]], axis=1) if self.extra else biased
        allowed = self.segq[rows] == self.segk[:, :wide]
        s = jnp.where(allowed, s, MASKED)
        if self.causal:
            row = lax.broadcasted_iota(jnp.int32, (chunk, 1), 0)
            places = jnp.concatenate([row + self.place(2 * b + u) for u in range(2)], axis=0)
            seen = wide - self.size if self.parts == 1 else 0
            later = lax.broadcasted_iota(jnp.int32, (1, wide - seen), 1) + seen
            last = jnp.where(later <= places, s[:, seen:], MASKED)
            s = jnp.concatenate([s[:, :seen], last], axis=1) if seen else last
        top = jnp.max(s, axis=-1, keepdims=True)
        e = jnp.exp(s - top)
        p = (e * (1.0 / jnp.sum(e, axis=-1, keepdims=True))).astype(BF)
        self.p_buf[self.slot(h, b), :, :wide] = p
        self.keep(h, b).start()
        self.os[h, rows] = mm(p, self.vs[h, :wide]).astype(BF)

    def run(self, low, high):
        for half, blocks, first, last in self.halves(low, high):

            @pl.loop(first, last)
            def _(h):
                if self.bias:
                    row = jnp.broadcast_to(self.bvec[h], (self.chunk, 2 * self.keys))
                    self.toep[...] = pltpu.roll(row, 0, 1, stride=1, stride_axis=0)

                @pl.when(h >= 2)
                def _():
                    for b in blocks:
                        self.keep(h - 2, b).wait()

                if half == 1:

                    @pl.when(h < 2)
                    def _():
                        for b in range(self.blocks // 2):
                            self.keep(h + 1, b).wait()

                for b in blocks:
                    self.one_block(h, b)

    def end(self):
        for i in range(HQ):
            self.att[:, DH * i : DH * (i + 1)] = self.os[i]
        out = pltpu.make_async_copy(self.att, self.att_out, self.sems.at[0])
        out.start()
        for h in (HQ - 2, HQ - 1):
            for b in range(self.blocks // 2, self.blocks):
                self.keep(h, b).wait()
        out.wait()
        for copy in self.copies:
            copy.wait()


class AttentionBackward(Attention):
    def __init__(self, parts, p, q, kv, up, w_proj, att, bias, mkv, xs, proj=True, causal=False):
        super().__init__(parts, q, kv, bias, mkv, causal)
        self.xs, self.proj = xs if parts == 1 else [], proj
        self.loads += self.mem + [up, w_proj, att] + self.xs
        self.raws = [p]
        rows, total, keys = self.rows, self.total, self.keys
        if self.joint:
            self.outs = [jax.ShapeDtypeStruct((rows, 3 * QC), BF)]
        else:
            kv_type = BF if parts == 1 else F32
            self.outs = [
                jax.ShapeDtypeStruct((rows, QC), BF),
                jax.ShapeDtypeStruct((keys, 2 * QC), kv_type),
            ]
        if bias:
            self.outs.append(jax.ShapeDtypeStruct((HQ, 1, 2 * keys), F32))
        if self.extra:
            self.outs.append(jax.ShapeDtypeStruct((self.extra, 2 * QC), BF))
        if proj:
            self.outs.append(jax.ShapeDtypeStruct((QC, D), BF))
        for n in range(len(self.xs)):
            self.outs.append(jax.ShapeDtypeStruct((D, self.outs[n].shape[1]), BF))
        self.scratch = self.heads(
            (rows, BF), (total, BF), (total, BF), (rows, BF), (rows, BF), (total, F32), (total, F32)
        )
        self.scratch += [
            pltpu.VMEM((HQ, rows, 1), F32),
            pltpu.VMEM((self.blocks, self.size, total), BF),
            pltpu.SemaphoreType.DMA((self.blocks + len(self.outs),)),
        ]
        self.scratch += [pltpu.VMEM(o.shape, o.dtype) for o in self.outs]
        if bias:
            self.scratch.append(pltpu.VMEM((HQ, self.chunk, 2 * keys), F32))

    def fetch(self, h, b):
        n = self.blocks // 2
        slot = n * lax.rem(h + (b // n) * HQ, 2) + b % n
        wide = pl.ds(0, self.width(b))
        return pltpu.make_async_copy(
            self.p_in.at[h, self.block(b), wide], self.p_buf.at[slot, :, wide], self.sems.at[slot]
        )

    def begin(self, loads, raws, outs, scratch):
        self.results, (self.p_in,) = outs, raws
        scratch, loads = list(scratch), list(loads)
        self.qs, self.ks, self.vs, self.dos, self.dqs, self.dks, self.dvs = scratch[:7]
        self.rds, self.p_buf, self.sems = scratch[7:10]
        self.made = scratch[10 : 10 + len(outs)]
        self.diag = scratch[-1] if self.bias else None
        for b in range(self.blocks // 2):
            self.fetch(0, b).start()
        q_ref = loads.pop(0).get()
        kv_ref = q_ref if self.joint else loads.pop(0).get()
        self.split_qkv(q_ref, kv_ref, loads, self.qs, self.ks, self.vs)
        up_ref, w_ref, att_ref = (loads.pop(0).get() for _ in range(3))

        @pl.loop(0, self.rows // 256)
        def _(r):
            rows = pl.ds(pl.multiple_of(r * 256, 256), 256)
            grads = mm_nt(up_ref[rows], w_ref[...]).astype(BF)
            att = att_ref[rows]
            for i in range(HQ):
                span = slice(DH * i, DH * (i + 1))
                self.dos[i, rows] = grads[:, span]
                dots = grads[:, span].astype(F32) * att[:, span].astype(F32)
                self.rds[i, rows] = jnp.sum(dots, axis=-1, keepdims=True)

        made = list(self.made)
        self.dq = made.pop(0)
        self.dkv = self.dq if self.joint else made.pop(0)
        self.dbvec = made.pop(0) if self.bias else None
        self.dmkv = made.pop(0) if self.extra else None
        g_proj = made.pop(0) if self.proj else None
        self.g_rows, self.x_loads = made, loads
        if self.proj:

            @pl.loop(0, D // 256)
            def _(n):
                cols = pl.ds(pl.multiple_of(n * 256, 256), 256)
                g_proj[:, cols] = mm_tn(att_ref[...], up_ref[:, cols]).astype(BF)

    def run(self, low, high):
        keys, chunk, n = self.keys, self.chunk, self.blocks // 2
        for half, blocks, first, last in self.halves(low, high):

            @pl.loop(first, last)
            def _(h):
                for b in blocks:
                    self.fetch(h, b).wait()

                @pl.when(h + 1 < HQ)
                def _():
                    for b in blocks:
                        self.fetch(h + 1, b).start()

                if half == 0:

                    @pl.when(h + 1 == HQ)
                    def _():
                        for b in range(n, 2 * n):
                            self.fetch(0, b).start()

                    self.dks[h] = jnp.zeros(self.dks.shape[1:], F32)
                    self.dvs[h] = jnp.zeros(self.dvs.shape[1:], F32)
                    if self.bias:
                        self.diag[h] = jnp.zeros(self.diag.shape[1:], F32)
                for b in blocks:
                    wide, rows = self.width(b), self.block(b)
                    slot = n * lax.rem(h + half * HQ, 2) + b % n
                    q, grad, p = self.qs[h, rows], self.dos[h, rows], self.p_buf[slot, :, :wide]
                    dp = mm_nt(grad, self.vs[h, :wide])
                    ds = (p.astype(F32) * (dp - self.rds[h, rows])).astype(BF)
                    self.dqs[h, rows] = mm(ds, self.ks[h, :wide]).astype(BF)
                    self.dks[h, :wide] += mm_tn(ds, q)
                    self.dvs[h, :wide] += mm_tn(p, grad)
                    if self.bias:
                        for u in range(2):
                            part = ds[u * chunk : (u + 1) * chunk, : min(wide, keys)]
                            self.diag[h, :, self.diagonal(b, u)] += part.astype(F32)
                if self.bias and half == 1:
                    x = self.diag[h]
                    size = chunk
                    while size > 1:
                        size //= 2
                        x = x[:size] + pltpu.roll(x[size:], 2 * keys - size, 1)
                    self.dbvec[h] = x

    def end(self):
        keys = self.keys
        to = QC if self.joint else 0
        for i in range(HQ):
            self.dq[:, DH * i : DH * (i + 1)] = self.dqs[i]
            at = to + DH * i
            self.dkv[:, at : at + DH] = self.dks[i, :keys].astype(self.dkv.dtype)
            self.dkv[:, at + QC : at + QC + DH] = self.dvs[i, :keys].astype(self.dkv.dtype)
            if self.extra:
                self.dmkv[:, DH * i : DH * (i + 1)] = self.dks[i, keys:].astype(BF)
                self.dmkv[:, QC + DH * i : QC + DH * (i + 1)] = self.dvs[i, keys:].astype(BF)
        for load, out, grad in zip(self.x_loads, self.g_rows, (self.dq, self.dkv)):
            x_ref = load.get()

            @pl.loop(0, D // 256)
            def _(n):
                cols = pl.ds(pl.multiple_of(n * 256, 256), 256)
                out[cols] = mm_tn(x_ref[:, cols], grad[...]).astype(BF)

        copies = [
            pltpu.make_async_copy(src, dst, self.sems.at[self.blocks + n])
            for n, (src, dst) in enumerate(zip(self.made, self.results))
        ]
        for copy in copies:
            copy.start()
        for copy in copies:
            copy.wait()


class FeedForwardGrads:
    n_steps = 6

    def __init__(self, at_stage, act, x):
        self.at_stage, self.loads, self.raws = at_stage, [act, x], []
        self.outs = [jax.ShapeDtypeStruct((v.shape[1], D), BF) for v in (act, x)]
        self.outs[1] = jax.ShapeDtypeStruct((x.shape[1], act.shape[1]), BF)
        self.scratch = [pltpu.VMEM(o.shape, BF) for o in self.outs] + [pltpu.SemaphoreType.DMA((2,))]

    def begin(self, loads, raws, outs, scratch):
        self.left = [load.get() for load in loads]
        self.right = [self.at_stage.left.rows.ref, self.at_stage.left.ref]
        self.made, self.results, self.sems = scratch[:2], outs, scratch[2]

    def run(self, low, high):
        for n in range(2):
            first, last = max(low - 3 * n, 0), min(high - 3 * n, 3)
            if first < last:

                @pl.loop(first, last)
                def _(i):
                    cols = pl.ds(pl.multiple_of(i * 256, 256), 256)
                    self.made[n][cols] = mm_tn(self.left[n][:, cols], self.right[n][...]).astype(BF)

    def end(self):
        copies = [
            pltpu.make_async_copy(self.made[n], self.results[n], self.sems.at[n]) for n in range(2)
        ]
        for copy in copies:
            copy.start()
        for copy in copies:
            copy.wait()


class Idle:
    n_steps, loads, raws, outs, scratch = 0, [], [], [], []

    def begin(self, loads, raws, outs, scratch):
        pass

    def run(self, low, high):
        pass

    def end(self):
        pass


def attend(number, planes, filler, jobs):
    def kernel(shipper, ins, outs, scratch, filler):
        filler.prefetch()
        shipper.greet(())
        shipper.start()
        filler.begin()
        filler.run(0, filler.n_steps)
        filler.end()
        shipper.finish()

    _, moved, made = call_with_jobs(
        kernel, number, planes, jobs, [], [], [], "attend", 4 * 10**9, filler
    )
    return made, moved


class Chain:
    def __init__(self, value, steps, width):
        self.value, self.steps, self.width = value, steps, width


ALL = ("seq", "part", "tp", "fsdp")
CTX = ("seq", "part", "tp")


def per_device(
    parts,
    planes,
    enc_input,
    dec_input,
    segments,
    prefix_rows,
    buckets,
    memory,
    enc_gain,
    enc_qkv,
    enc_rel,
    enc_proj,
    enc_ffnorm,
    enc_ffin,
    enc_ffout,
    dec_gain,
    dec_qkv,
    dec_rel,
    dec_proj,
    cross_gain,
    cross_query,
    cross_kv,
    cross_proj,
    dec_ffnorm,
    dec_ffin,
    dec_ffout,
    enc_cotan,
    dec_cotan,
):
    seq, part, tp, plane = (lax.axis_index(name) for name in ALL)
    chunk = enc_input.shape[1]
    length = buckets.shape[0] // 2
    docs, prefix = prefix_rows.shape[1:]

    first = seq == 0
    split = planes * 2

    def joined(x, came):
        mine = lax.dynamic_index_in_dim(x, seq, 0, keepdims=False)
        came = came.astype(x.dtype)
        return jnp.stack([jnp.where(first, mine, came), jnp.where(first, came, mine)])

    def cols(w, start, width=QC):
        return lax.dynamic_slice_in_dim(w, start + width * tp, width, 1)

    def halved(w):
        rows = w.shape[0] // 2
        return lax.dynamic_slice_in_dim(w, rows * seq, rows, 0)

    def qkv_part(w):
        w = halved(w)
        return jnp.concatenate([cols(w, D * i) for i in range(w.shape[1] // D)], axis=1)

    hidden = enc_ffout.shape[0] // TP

    def ffin_part(w):
        w = halved(w)
        return jnp.concatenate(
            [cols(w, hidden * TP * i, hidden) for i in range(planes)], axis=1
        )

    def ffout_part(w):
        rows = hidden // 2
        return lax.dynamic_slice_in_dim(w, hidden * tp + rows * seq, rows, 0)

    def over_planes(w):
        return gather_job("fsdp", w, planes)

    def over_seq(w):
        return gather_job("seq", w, 2, 1)

    def matrix(w):
        return w.reshape(-1, w.shape[-1])

    gains = (enc_gain, enc_ffnorm, dec_gain, cross_gain, dec_ffnorm)
    which = jnp.arange(len(gains), dtype=jnp.int32)[:, None]
    gain_stack = sum(jnp.where(which == i, v.astype(F32)[None], 0.0) for i, v in enumerate(gains))
    which = jnp.arange(2, dtype=jnp.int32)[:, None, None]
    rel_stack = jnp.where(which == 0, enc_rel.astype(F32)[None], dec_rel.astype(F32)[None])
    segments = segments.reshape(2, 1, chunk)
    first_jobs = [
        swap_job(enc_input),
        gather_job("fsdp", gain_stack, planes),
        gather_job("fsdp", rel_stack, planes),
        over_planes(qkv_part(enc_qkv)),
        over_planes(qkv_part(memory)),
        swap_job(dec_input),
    ]
    if parts == 1:
        first_jobs.append(block_job(segments))
    xe, gain_stack, rel_stack, w_eqkv, table, xd, *segs = ship(0, planes, first_jobs)
    xe, xd = joined(enc_input, xe), joined(dec_input, xd)
    if parts == 1:
        seg = segs[0].reshape(-1)
    else:
        segs = lax.all_gather(segments.reshape(2, chunk), CTX, axis=1, tiled=True)
        seg = lax.dynamic_index_in_dim(segs, seq, 0, keepdims=False)
    per, per_rel = enc_gain.shape[0], enc_rel.size
    g_enc, g_effn, g_dec, g_cross, g_dffn = [
        gain_stack[:, i].reshape(1, D) for i in range(len(gains))
    ]
    rels = [rel_stack[:, i].reshape(BUCKETS, HEADS) for i in range(2)]
    onehot = (buckets[:, None] == jnp.arange(BUCKETS, dtype=jnp.int32)[None, :]).astype(BF)

    def bias_vector(rel):
        own = lax.dynamic_slice_in_dim(rel, HQ * tp, HQ, 1).astype(BF)
        return lax.dot_general(
            own, onehot, (((0,), (1,)), ((), ())), preferred_element_type=F32
        ).reshape(HQ, 1, 2 * length)

    turned = planes == TP

    def proj_jobs(w):
        return [turn_job(w)] if turned else []

    def proj_of(got, w):
        if turned:
            return got.pop()
        full = lax.all_gather(w, "fsdp", axis=0, tiled=True)
        return lax.dynamic_slice_in_dim(full, QC * tp, QC, 0)

    ((en,), (dn,)), (w_eqkv, table, w_dqkv, w_effin), _ = stage(
        1,
        planes,
        [GatherNormed(xe, g_enc), GatherNormed(xd, g_dec)],
        jobs=[
            over_seq(w_eqkv),
            over_seq(table),
            over_planes(qkv_part(dec_qkv)),
            over_planes(ffin_part(enc_ffin)),
        ],
    )
    w_eqkv, table = matrix(w_eqkv), matrix(table)

    segq = lax.dynamic_index_in_dim(seg.reshape(2, parts, TP * chunk), part, 1, keepdims=False)
    segq = segq.reshape(-1, 1)
    segk = seg.reshape(1, length)
    ids = lax.dynamic_index_in_dim(prefix_rows, seq, 0, keepdims=False).reshape(-1)
    extra = -(-(docs * prefix) // 256) * 256
    ids = jnp.concatenate([ids, jnp.full((extra - docs * prefix,), -1, jnp.int32)])
    mem_doc = np.full((extra,), -1, np.int32)
    mem_doc[: docs * prefix] = np.arange(docs * prefix) // prefix
    segk_mem = jnp.concatenate([segk, jnp.asarray(mem_doc)[None]], axis=1)
    pick = (ids[:, None] == jnp.arange(table.shape[0], dtype=jnp.int32)[None, :]).astype(BF)
    mkv = mm(pick, table).astype(BF)

    def spread(kv):
        if parts == 1:
            return kv
        got = lax.all_gather(kv, "part", axis=0)
        return got.reshape(parts, 2, TP * chunk, -1).transpose(1, 0, 2, 3).reshape(length, -1)

    def collect(dkv):
        if parts == 1:
            return dkv
        split = dkv.reshape(2, parts, TP * chunk, -1).transpose(1, 0, 2, 3)
        split = split.reshape(parts * 2 * TP * chunk, -1)
        return lax.psum_scatter(split, "part", scatter_dimension=0, tiled=True).astype(BF)

    def self_kv(rows):
        return (rows, rows) if parts == 1 else (rows[:, :QC], spread(rows[:, QC:]))

    def joint_grad(got):
        if parts == 1:
            return got.pop(0)
        return jnp.concatenate([got.pop(0), collect(got.pop(0))], axis=1)

    def self_fill(x, w, segk_now, bvec, mem, causal):
        if parts == 1:
            rows = jax.ShapeDtypeStruct((x.shape[0], w.shape[1]), BF)
            return AttentionForward(
                parts, rows, rows, segq, segk_now, bvec, mem, causal, [(x, w)]
            ), None
        rows = self_kv(mm(x, w).astype(BF))
        return AttentionForward(parts, *rows, segq, segk_now, bvec, mem, causal), rows

    def self_made(got, rows):
        return got[0], got[1], rows or (got[2], got[2])

    e_fill, e_qkv = self_fill(en, w_eqkv, segk_mem, bias_vector(rels[0]), mkv, False)
    made, (w_dqkv, w_effin, w_effout, *got) = attend(
        2,
        planes,
        e_fill,
        [over_seq(w_dqkv), over_seq(w_effin), over_planes(ffout_part(enc_ffout))]
        + proj_jobs(enc_proj),
    )
    e_att, e_p, e_qkv = self_made(made, e_qkv)
    w_eproj = proj_of(got, enc_proj)
    w_dqkv, w_effin = matrix(w_dqkv), matrix(w_effin)
    d_fill, d_qkv = self_fill(dn, w_dqkv, segk, bias_vector(rels[1]), None, True)
    ((e_mid, e_fn),), (w_effout, w_cq, w_ckv, *got), made = stage(
        3,
        planes,
        [Stage([e_att], w_eproj, xe, gather="norm", gain=g_effn)],
        [
            over_seq(w_effout),
            over_planes(qkv_part(cross_query)),
            over_planes(qkv_part(cross_kv)),
        ]
        + proj_jobs(dec_proj),
        d_fill,
    )
    d_att, d_p, d_qkv = self_made(made, d_qkv)
    w_dproj = proj_of(got, dec_proj)
    w_effout = matrix(w_effout)
    ((d_mid, c_n), (e_low, e_gath, e_pre, e_act)), moved, _ = stage(
        4,
        planes,
        [
            Stage([d_att], w_dproj, xd, gather="norm", gain=g_cross),
            Stage(
                [e_fn, w_effin], w_effout, e_mid, maker=FeedForward, gather="low", dtype=BF
            ),
        ],
        [
            over_seq(w_cq),
            over_seq(w_ckv),
            over_planes(ffin_part(dec_ffin)),
            over_planes(ffout_part(dec_ffout)),
            swap_job(dec_cotan),
        ],
    )
    w_cq, w_ckv, w_dffin, w_dffout, xdc = moved
    w_cq, w_ckv = matrix(w_cq), matrix(w_ckv)
    xdc = joined(dec_cotan, xdc)
    products = None
    if parts == 1:
        c_q = jax.ShapeDtypeStruct((c_n.shape[0], QC), BF)
        c_kv = jax.ShapeDtypeStruct((e_gath.shape[0], 2 * QC), BF)
        products = [(c_n, w_cq), (e_gath, w_ckv)]
    else:
        c_q = mm(c_n, w_cq).astype(BF)
        c_kv = spread(mm(e_gath, w_ckv).astype(BF))
    c_fill = AttentionForward(parts, c_q, c_kv, segq, segk, None, None, False, products)
    (c_att, c_p, *made), (w_dffin, *got) = attend(
        5, planes, c_fill, [over_seq(w_dffin)] + proj_jobs(cross_proj)
    )
    w_cproj = proj_of(got, cross_proj)
    if parts == 1:
        c_q, c_kv = made
    ((d_cross, d_fn),), (w_dffout, came, xec), _ = stage(
        6,
        planes,
        [Stage([c_att], w_cproj, d_mid, gather="norm", gain=g_dffn)],
        [over_seq(w_dffout), swap_job(e_low), swap_job(enc_cotan)],
    )
    enc_output, xec = joined(e_low, came), joined(enc_cotan, xec)
    w_dffin, w_dffout = matrix(w_dffin), matrix(w_dffout)
    ((d_low, up_g, d_pre, d_act),), _, _ = stage(
        7,
        planes,
        [
            Stage(
                [d_fn, w_dffin],
                w_dffout,
                d_cross,
                maker=FeedForward,
                gather="given",
                given=xdc,
                dtype=BF,
            )
        ],
    )

    def pieces(g):
        if parts > 1:
            g = lax.psum(g, "part")
        return g.reshape(planes, 2, g.shape[0] // split, g.shape[1])

    to_ctx = [
        lambda g: gather_job("across", g),
        lambda g: gather_job("seq", g),
        lambda g: gather_job("core", g, 2, 2),
    ]
    to_ctx_seq = [
        lambda g: gather_job("seq", g),
        lambda g: gather_job("across", g, 2, 1),
        lambda g: gather_job("core", g, 2, 2),
    ]

    def chain(g, width, seq_first=False):
        steps = [lambda g: swap_job(g, 1, True), lambda g: deal_job("fsdp", g)]
        return Chain(pieces(g), steps + (to_ctx_seq if seq_first else to_ctx), width)

    def proj_chain(g):
        if not turned:
            return Chain(g, [], -1)
        steps = [lambda g: swap_job(g, "cols", True), lambda g: deal_job("fsdp", g), turn_job]
        return Chain(g.reshape(planes, -1, D), steps + to_ctx, -1)

    def steps_of(chains):
        return [c.steps[0](c.value) for c in chains if c.steps]

    def hurry(chains):
        for c in chains:
            if len(c.steps) == 3:
                c.steps = [spread_job]

    def settle(chains, got):
        got = list(got)
        for c in chains:
            if c.steps:
                c.value = got.pop(0)
                c.steps.pop(0)
        return got

    at = Stage(
        [up_g, d_pre, w_dffout],
        w_dffin,
        xdc,
        flip=True,
        maker=FeedForwardBack,
        back=(d_cross, g_dffn),
        gather="low",
    )
    ((up, up_rows, dg_dffn, _),), (came,), made = stage(
        8, planes, [at], [swap_job(d_low)], FeedForwardGrads(at, d_act, d_fn)
    )
    dec_output = joined(d_low, came)
    k_dffout, k_dffin = chain(made[0], 0, True), chain(made[1], hidden, True)
    c_fill = AttentionBackward(
        parts, c_p, c_q, c_kv, up_rows, w_cproj, c_att, False, None, [c_n, e_gath]
    )
    moving = [k_dffout]
    (c_dq, c_dkv, g_cproj, *made), got = attend(9, planes, c_fill, steps_of(moving))
    settle(moving, got)
    c_dkv = collect(c_dkv)
    if parts > 1:
        made = [mm_tn(c_n, c_dq).astype(BF), mm_tn(e_gath, c_dkv).astype(BF)]
    k_cproj, k_cq, k_ckv = proj_chain(g_cproj), chain(made[0], QC, True), chain(made[1], QC, True)
    moving = [k_dffout, k_cq, k_ckv, k_cproj]
    ((up, up_rows, dg_cross),), got, _ = stage(
        10,
        planes,
        [Stage([c_dq], w_cq, up, flip=True, back=(d_mid, g_cross), gather="low")],
        steps_of(moving),
    )
    settle(moving, got)

    def self_grads(made, x):
        grad = joint_grad(made)
        g_rows = made.pop() if parts == 1 else mm_tn(x, grad).astype(BF)
        return grad, chain(g_rows, QC, True), made

    d_fill = AttentionBackward(
        parts, d_p, *d_qkv, up_rows, w_dproj, d_att, True, None, [dn], causal=True
    )
    moving = [k_dffin, k_cq, k_ckv, k_cproj]
    ((e_up, e_up_rows),), got, made = stage(
        16,
        planes,
        [Stage([c_dkv], w_ckv, xec, flip=True, gather="low")],
        steps_of(moving),
        d_fill,
    )
    settle(moving, got)
    d_rows_grad, k_dqkv, (d_dbv, g_dproj) = self_grads(made, dn)
    k_dproj = proj_chain(g_dproj)
    k_effout = chain(mm_tn(e_act, e_up_rows).astype(BF), 0, True)
    moving = [k_dffin, k_dffout, k_cproj, k_dqkv, k_dproj, k_effout]
    ((e_up, e_up_rows, dg_effn, pre_grad),), got, _ = stage(
        12,
        planes,
        [
            Stage(
                [e_up_rows, e_pre, w_effout],
                w_effin,
                e_up,
                flip=True,
                maker=FeedForwardBack,
                back=(e_mid, g_effn),
                gather="low",
            )
        ],
        steps_of(moving),
    )
    settle(moving, got)
    k_effin = chain(mm_tn(e_fn, pre_grad).astype(BF), hidden)
    k_eproj = proj_chain(mm_tn(e_att, e_up_rows).astype(BF))
    e_fill = AttentionBackward(
        parts, e_p, *e_qkv, e_up_rows, w_eproj, e_att, True, mkv, [en], False
    )
    moving += [k_cq, k_ckv, k_effin, k_eproj]
    ((d_in, dg_dec, d_in_low),), got, made = stage(
        11,
        planes,
        [Stage([d_rows_grad], w_dqkv, up, flip=True, back=(xd, g_dec), low=True)],
        steps_of(moving),
        e_fill,
    )
    settle(moving, got)
    e_rows_grad, k_eqkv, (e_dbv, d_mkv) = self_grads(made, en)
    k_table = chain(mm_tn(pick, d_mkv).astype(BF), QC)
    moving += [k_eqkv, k_table]
    ((e_in, dg_enc, e_in_low),), got, _ = stage(
        13,
        planes,
        [Stage([e_rows_grad], w_eqkv, e_up, flip=True, back=(xe, g_enc), low=True)],
        steps_of(moving) + [swap_job(d_in_low)],
    )
    (came,) = settle(moving, got)
    dec_ingrad = joined(d_in, came)

    def rel_grads(*dbvs):
        own = lax.dot_general(
            onehot.astype(F32),
            jnp.concatenate(dbvs, axis=0).reshape(len(dbvs) * HQ, -1),
            (((0,), (1,)), ((), ())),
            precision=lax.Precision.HIGHEST,
            preferred_element_type=F32,
        )
        heads = jnp.arange(HEADS, dtype=jnp.int32)[None, :] // HQ == tp
        return [
            jnp.where(heads, jnp.tile(own[:, HQ * i : HQ * (i + 1)], (1, TP)), 0.0)
            for i in range(len(dbvs))
        ]

    tiny = [v.reshape(planes, -1) for v in (dg_enc, dg_effn, dg_dec, dg_cross, dg_dffn)]
    tiny += [v.reshape(planes, -1) for v in rel_grads(e_dbv, d_dbv)]
    tiny = jnp.concatenate(tiny, axis=1).reshape(-1, 128)
    if parts > 1:
        tiny = lax.psum(tiny, "part")
    hurry(moving)
    tiny, came, *got = ship(
        14,
        planes,
        [total_job("fsdp", tiny, planes), swap_job(e_in_low)] + steps_of(moving),
    )
    enc_ingrad = joined(e_in, came)
    settle(moving, got)
    hurry(moving)
    tiny, *got = ship(15, planes, [spread_job(tiny, True)] + steps_of(moving))
    settle(moving, got)

    def proj_rows(k):
        full = lax.dynamic_update_slice_in_dim(jnp.zeros((D, D), BF), k.value, QC * tp, 0)
        full = lax.psum_scatter(full, "fsdp", scatter_dimension=0, tiled=True)
        return lax.psum(full.astype(F32), CTX)

    ready = [k_dffin, k_dffout, k_effin, k_effout, k_cq, k_ckv, k_dqkv, k_eqkv, k_table]
    k_projs = [k_eproj, k_dproj, k_cproj]
    if turned:
        ready += k_projs
    results = laid_out([k.value for k in ready], [k.width for k in ready])
    o_eproj, o_dproj, o_cproj = results[9:] if turned else [proj_rows(k) for k in k_projs]
    o_dffin, o_dffout, o_effin, o_effout, o_cq, o_ckv, o_dqkv, o_eqkv, o_table = results[:9]
    tiny = lax.dynamic_index_in_dim(tiny.reshape(planes, -1), plane, 0, keepdims=False)
    o_gains = [tiny[per * i : per * (i + 1)] for i in range(5)]
    o_rels = [
        tiny[5 * per + per_rel * i : 5 * per + per_rel * (i + 1)].reshape(-1, HEADS)
        for i in range(2)
    ]
    return (
        enc_output,
        dec_output,
        enc_ingrad,
        dec_ingrad,
        o_table,
        o_gains[0],
        o_eqkv,
        o_rels[0],
        o_eproj,
        o_gains[1],
        o_effin,
        o_effout,
        o_gains[2],
        o_dqkv,
        o_rels[1],
        o_dproj,
        o_gains[3],
        o_cq,
        o_ckv,
        o_cproj,
        o_gains[4],
        o_dffin,
        o_dffout,
    )


def solution(mesh):
    ctx, planes = mesh.shape["ctx"], mesh.shape["fsdp"]
    parts = ctx // (2 * TP)
    inner = Mesh(np.asarray(mesh.devices).reshape(2, parts, TP, planes), ALL)
    rows3 = P("fsdp", CTX, None)
    mat, vec = P("fsdp", None), P("fsdp")
    args = (
        (rows3, rows3, P("fsdp", CTX), P("fsdp", None, None), P(), mat)
        + (vec, mat, mat, mat, vec, mat, mat)
        + (vec, mat, mat, mat)
        + (vec, mat, mat, mat)
        + (vec, mat, mat)
        + (rows3, rows3)
    )
    outs = (
        (rows3, rows3, rows3, rows3, mat)
        + (vec, mat, mat, mat, vec, mat, mat)
        + (vec, mat, mat, mat)
        + (vec, mat, mat, mat)
        + (vec, mat, mat)
    )
    return jax.shard_map(
        functools.partial(per_device, parts, planes),
        mesh=inner,
        in_specs=args,
        out_specs=outs,
        check_vma=False,
    )
```

```python
import collections
import functools

import jax
import jax.numpy as jnp
import numpy as np
from jax import lax
from jax.experimental import pallas as pl
from jax.experimental.pallas import tpu as pltpu
from jax.sharding import Mesh
from jax.sharding import PartitionSpec as P

D = 768
HEADS = 12
DH = 64
BUCKETS = 32
EPS = 1e-06
MASKED = -1e30
TP = 4
HQ = HEADS // TP
QC = HQ * DH
BF = jnp.bfloat16
F32 = jnp.float32
MESH_ID = pl.DeviceIdType.MESH
MB = 1024 * 1024
VMEM_LIMIT = 60 * MB
SHARE = (0.25, 0.34, 0.75)


def mm(a, b):
    return jnp.dot(a, b, preferred_element_type=F32)


def mm_tn(a, b):
    return lax.dot_general(a, b, (((0,), (0,)), ((), ())), preferred_element_type=F32)


def mm_nt(a, b):
    return lax.dot_general(a, b, (((1,), (1,)), ((), ())), preferred_element_type=F32)


def gelu(v):
    return jax.nn.gelu(v, approximate=True)


def gelu_back(pre, grad):
    return jax.vjp(gelu, pre)[1](grad)[0]


def group_ids():
    me = lax.axis_index("tp")
    core = me + 1 - 2 * lax.rem(me, 2)
    across = lax.rem(me + 2, TP)
    far = lax.rem(core + 2, TP)
    return me, core, across, far


def send(src, dst, send_sem, recv_sem, peer):
    return pltpu.make_async_remote_copy(
        src_ref=src,
        dst_ref=dst,
        send_sem=send_sem,
        recv_sem=recv_sem,
        device_id={"tp": peer},
        device_id_type=MESH_ID,
    )


def normed(values, gains):
    return values * lax.rsqrt(jnp.mean(values * values, axis=-1, keepdims=True) + EPS) * gains


class Gatherer:
    def __init__(self, buf, stage, sems, chunk, ids):
        self.buf, self.stage, self.sems, self.chunk, self.ids = buf, stage, sems, chunk, ids
        self.sends, self.own = [], []

    def rows(self, j, owner):
        return self.buf.at[pl.ds(pl.multiple_of((TP * j + owner) * self.chunk, self.chunk), self.chunk)]

    def put(self, j, value):
        me, core, across, far = self.ids
        mine = self.stage.at[j]
        mine[...] = value
        x_copy = send(mine, self.rows(j, me), self.sems.at[0, j], self.sems.at[1, j], across)
        x_copy.start()
        c_copy = send(mine, self.rows(j, me), self.sems.at[2, j], self.sems.at[3, j], core)
        c_copy.start()
        self.sends += [x_copy, c_copy]
        own = pltpu.make_async_copy(mine, self.rows(j, me), self.sems.at[6, j])
        own.start()
        self.own.append(own)

    def forward(self, j):
        me, core, across, far = self.ids
        theirs = self.rows(j, across)
        send(theirs, theirs, self.sems.at[0, j], self.sems.at[1, j], across).wait_recv()
        f_copy = send(theirs, theirs, self.sems.at[4, j], self.sems.at[5, j], core)
        f_copy.start()
        self.sends.append(f_copy)

    def finish(self):
        me, core, across, far = self.ids
        for j in range(2):
            a = self.rows(j, core)
            send(a, a, self.sems.at[2, j], self.sems.at[3, j], core).wait_recv()
            b = self.rows(j, far)
            send(b, b, self.sems.at[4, j], self.sems.at[5, j], core).wait_recv()
        for copy in self.sends:
            copy.wait_send()
        for copy in self.own:
            copy.wait()


Job = collections.namedtuple("Job", ["axis", "src_axis", "dst_axis", "local", "src", "shape", "finish"])


def gather_job(axis, src, size=2, at=0):
    shape = src.shape[:at] + (size,) + src.shape[at:]
    return Job(axis, None, at, True, src, shape, None)


def total_job(axis, src, size=2):
    return gather_job(axis, src, size)._replace(finish="sum")


def deal_job(axis, src):
    return Job(axis, 0, 0, True, src, src.shape, "sum")


def swap_job(src, at=0, add=False):
    if at == "cols":
        shape = src.shape[:-1] + (src.shape[-1] // 2,)
    else:
        shape = src.shape[:at] + src.shape[at + 1 :]
    return Job("seq", at, None, add, src, shape, "add" if add else None)


def turn_job(src):
    return Job("turn", None, None, True, src, src.shape, None)


def block_job(src):
    return Job("ctx", 0, 0, True, src, (2 * TP,) + src.shape[1:], None)


def spread_job(src, add=False):
    return Job("all", None, None, True, src, (2, 2, 2) + src.shape, "sum3" if add else None)


def result_of(job):
    skip = {"sum": 1, "sum3": 3}.get(job.finish, 0)
    return job.shape[skip:], job.src.dtype


def entry(ref, axis, index):
    if axis == "cols":
        half = ref.shape[-1] // 2
        return ref.at[:, :, pl.ds(pl.multiple_of(index * half, half), half)]
    return ref if axis is None else ref.at[(slice(None),) * axis + (index,)]


class Shipper:
    def __init__(self, jobs, planes, srcs, outs, scratch, sems):
        self.jobs, self.planes, self.srcs, self.outs, self.sems = jobs, planes, srcs, outs, sems
        self.tp, self.seq, self.plane = (lax.axis_index(n) for n in ("tp", "seq", "fsdp"))
        self.dsts, self.bounce, self.made = [], [], []
        for job, out in zip(jobs, outs):
            if job.finish:
                self.dsts.append(scratch.pop(0))
                self.bounce.append(scratch.pop(0) if job.finish == "add" else None)
                self.made.append(scratch.pop(0) if job.finish != "add" else None)
            else:
                self.dsts.append(out)
                self.bounce.append(scratch.pop(0) if job.local else None)
                self.made.append(None)

    @staticmethod
    def scratch(jobs):
        shapes = []
        for job in jobs:
            dtype = job.src.dtype
            if job.finish:
                shapes.append(pltpu.VMEM(job.shape, dtype))
                if job.finish == "add":
                    shapes.append(pltpu.VMEM(job.shape, dtype))
                else:
                    shapes.append(pltpu.VMEM(*result_of(job)))
            elif job.axis == "all":
                shapes.append(pltpu.VMEM(job.src.shape, dtype))
            elif job.local:
                drop = job.dst_axis
                own = job.shape if drop is None else job.shape[:drop] + job.shape[drop + 1 :]
                shapes.append(pltpu.VMEM(own, dtype))
        return shapes

    @staticmethod
    def count(jobs, planes):
        return sum(2 * Shipper.n_peers(job, planes) + 2 for job in jobs)

    @staticmethod
    def n_peers(job, planes):
        return {"fsdp": planes - 1, "ctx": 2 * TP - 1, "all": 2 * TP - 1}.get(job.axis, 1)

    def coord(self, axis):
        half = self.tp // 2
        return {
            "fsdp": self.plane,
            "seq": self.seq,
            "across": half,
            "core": self.tp - 2 * half,
            "ctx": TP * self.seq + self.tp,
            "turn": None,
        }[axis]

    def peers(self, axis):
        if axis == "fsdp":
            n, z = self.planes, self.plane
            for k in range(1, n):
                to = lax.rem(z + k, n)
                yield to, {"fsdp": to}, lax.rem(z + (n - k), n)
        elif axis == "ctx":
            for k in range(1, 2 * TP):
                to = lax.rem(self.seq + k // TP, 2)
                to_tp = lax.rem(self.tp + k % TP, TP)
                from_seq = lax.rem(self.seq + (2 - k // TP), 2)
                from_tp = lax.rem(self.tp + (TP - k % TP), TP)
                yield to, {"seq": to, "tp": to_tp}, TP * from_seq + from_tp
        elif axis == "seq":
            yield 1 - self.seq, {"seq": 1 - self.seq}, 1 - self.seq
        elif axis == "turn":
            yield None, {"fsdp": self.tp, "tp": self.plane}, None
        else:
            to = lax.rem(self.tp + 2, TP) if axis == "across" else self.tp + 1 - 2 * lax.rem(self.tp, 2)
            other = 1 - self.coord(axis)
            yield other, {"tp": to}, other

    def signal(self, always=("core", "across")):
        wanted = {job.axis for job in self.jobs}
        if "all" in wanted:
            wanted = (wanted - {"all"}) | {"seq", "across", "core"}
        axes = list(always) + sorted(wanted - set(always))
        barrier = pltpu.get_barrier_semaphore()
        self.expected, self.turns = 0, "turn" in axes
        for axis in axes:
            for _, device, _ in self.peers(axis):
                if axis == "turn":

                    @pl.when(self.plane != self.tp)
                    def _():
                        pl.semaphore_signal(
                            barrier, inc=1, device_id=device, device_id_type=MESH_ID
                        )

                    continue
                pl.semaphore_signal(barrier, inc=1, device_id=device, device_id_type=MESH_ID)
                self.expected += 1

    def met(self):
        barrier = pltpu.get_barrier_semaphore()
        if self.turns:
            moves = self.plane != self.tp

            @pl.when(moves)
            def _():
                pl.semaphore_wait(barrier, self.expected + 1)

            @pl.when(jnp.logical_not(moves))
            def _():
                pl.semaphore_wait(barrier, self.expected)
        else:
            pl.semaphore_wait(barrier, self.expected)

    def greet(self, always=("core", "across")):
        self.signal(always)
        self.met()

    def each(self, act_remote, act_local):
        base = 0
        for n, (job, src, dst) in enumerate(zip(self.jobs, self.srcs, self.dsts)):
            if job.axis == "all":
                base += 2 * self.n_peers(job, self.planes) + 2
                continue
            mine = self.coord(job.axis)
            peers = list(self.peers(job.axis))
            for i, (to, device, source) in enumerate(peers):
                sems = (self.sems.at[base + 2 * i], self.sems.at[base + 2 * i + 1])

                def copy_into(slot, to=to, device=device, sems=sems, src=src, dst=dst, job=job):
                    return pltpu.make_async_remote_copy(
                        src_ref=entry(src, job.src_axis, to),
                        dst_ref=entry(dst, job.dst_axis, slot),
                        send_sem=sems[0],
                        recv_sem=sems[1],
                        device_id=device,
                        device_id_type=MESH_ID,
                    )

                def remote(copy_into=copy_into, source=source, mine=mine):
                    act_remote(copy_into, mine, source)

                if job.axis == "turn":
                    pl.when(self.plane != self.tp)(remote)
                else:
                    remote()
            if job.local:
                own = self.seq if job.axis == "ctx" else mine

                def local(n=n, job=job, src=src, dst=dst, own=own, mine=mine, sem=base + 2 * len(peers)):
                    here, there = entry(src, job.src_axis, own), entry(dst, job.dst_axis, mine)
                    bounce = self.bounce[n]
                    if bounce is None:
                        act_local([(here, there)], self.sems.at[sem])
                    elif job.finish == "add":
                        act_local([(here, bounce)], self.sems.at[sem])
                    else:
                        act_local([(here, bounce), (bounce, there)], self.sems.at[sem])

                if job.axis == "turn":
                    pl.when(self.plane == self.tp)(local)
                else:
                    local()
            base += 2 * len(peers) + 2
        return base

    def spreads(self):
        s, x, c = self.coord("seq"), self.coord("across"), self.coord("core")
        seq, across, core = (next(self.peers(axis))[1] for axis in ("seq", "across", "core"))
        moves = [
            ((s, x, c), across, (s, 1 - x, c)),
            ((s, x, c), seq, (1 - s, x, c)),
            ((s, x, c), core, (s, x, 1 - c)),
            ((s, 1 - x, c), seq, (1 - s, 1 - x, c)),
            ((s, 1 - x, c), core, (s, 1 - x, 1 - c)),
            ((1 - s, x, c), core, (1 - s, x, 1 - c)),
            ((1 - s, 1 - x, c), core, (1 - s, 1 - x, 1 - c)),
        ]
        base = 0
        for job, src, dst, bounce in zip(self.jobs, self.srcs, self.dsts, self.bounce):
            if job.axis == "all":

                def copy(k, arrives=False, src=src, dst=dst, base=base):
                    what, device, other = moves[k]
                    return pltpu.make_async_remote_copy(
                        src_ref=src if k < 3 else dst.at[what],
                        dst_ref=dst.at[other if arrives else what],
                        send_sem=self.sems.at[base + 2 * k],
                        recv_sem=self.sems.at[base + 2 * k + 1],
                        device_id=device,
                        device_id_type=MESH_ID,
                    )

                own = dst.at[s, x, c]
                legs = [(src, own)] if bounce is None else [(src, bounce), (bounce, own)]
                legs = [
                    pltpu.make_async_copy(*leg, self.sems.at[base + 14 + n])
                    for n, leg in enumerate(legs)
                ]
                yield copy, legs
            base += 2 * self.n_peers(job, self.planes) + 2

    def start_spreads(self):
        for copy, legs in self.spreads():
            for k in range(3):
                copy(k).start()
            legs[0].start()

    def finish_spreads(self):
        jobs = list(self.spreads())
        for copy, legs in jobs:
            if len(legs) > 1:
                legs[0].wait()
                legs[1].start()
        for first, then in ((0, (3, 4)), (1, (5,)), (3, (6,))):
            for copy, legs in jobs:
                copy(first, True).wait_recv()
                for k in then:
                    copy(k).start()
        for copy, legs in jobs:
            for k in (2, 4, 5, 6):
                copy(k, True).wait_recv()
            for k in range(7):
                copy(k).wait_send()
            legs[-1].wait()

    def start(self):
        if any(job.axis == "all" for job in self.jobs):
            self.start_spreads()
        self.each(
            lambda copy_into, mine, source: copy_into(mine).start(),
            lambda legs, sem: pltpu.make_async_copy(*legs[0], sem).start(),
        )

    def finish(self):
        def turn_round(legs, sem):
            if len(legs) > 1:
                pltpu.make_async_copy(*legs[0], sem).wait()
                pltpu.make_async_copy(*legs[1], sem).start()

        def remote(copy_into, mine, source):
            copy_into(source).wait_recv()
            copy_into(mine).wait_send()

        if any(job.axis == "all" for job in self.jobs):
            self.finish_spreads()
        self.each(lambda *_: None, turn_round)
        self.each(remote, lambda legs, sem: pltpu.make_async_copy(*legs[-1], sem).wait())
        stores, base = [], 0
        for job, dst, bounce, made, out in zip(
            self.jobs, self.dsts, self.bounce, self.made, self.outs
        ):
            base += 2 * self.n_peers(job, self.planes) + 2
            if not job.finish:
                continue
            if job.finish == "add":
                made = bounce

                @pl.loop(0, dst.shape[0])
                def _(i):
                    bounce[i] = (bounce[i].astype(F32) + dst[i].astype(F32)).astype(bounce.dtype)

            else:
                pieces = [dst.at[i] for i in range(dst.shape[0])]
                if job.finish == "sum3":
                    pieces = [dst.at[i, j, k] for i in range(2) for j in range(2) for k in range(2)]
                total = pieces[0][...].astype(F32)
                for piece in pieces[1:]:
                    total = total + piece[...].astype(F32)
                made[...] = total.astype(made.dtype)
            store = pltpu.make_async_copy(made, out, self.sems.at[base - 1])
            store.start()
            stores.append(store)
        for store in stores:
            store.wait()


def lay_out(src, dst, width):
    seqs, halves, cores, rows, cols = src.shape
    if width < 0:
        for i in range(seqs):
            for q in range(TP):
                block = slice(i * cols, (i + 1) * cols)
                dst[q * rows : (q + 1) * rows, block] = src[i, q // 2, q % 2].astype(F32)
        return

    @pl.loop(0, seqs)
    def _(i):
        if not width:
            for q in range(TP):
                at = pl.multiple_of((q * seqs + i) * rows, rows)
                dst[pl.ds(at, rows)] = src[i, q // 2, q % 2].astype(F32)
        else:
            at = pl.multiple_of(i * rows, rows)
            for n in range(cols // width):
                span = slice(n * width, (n + 1) * width)
                parts = [src[i, q // 2, q % 2, :, span].astype(F32) for q in range(TP)]
                block = slice(n * width * TP, (n + 1) * width * TP)
                dst[pl.ds(at, rows), block] = jnp.concatenate(parts, axis=1)


def laid_out(pieces, widths):
    shapes = []
    for p, width in zip(pieces, widths):
        seqs, halves, cores, rows, cols = p.shape
        if width < 0:
            shapes.append((halves * cores * rows, seqs * cols))
        elif width:
            shapes.append((seqs * rows, halves * cores * cols))
        else:
            shapes.append((seqs * halves * cores * rows, cols))
    n = len(pieces)

    def body(*refs):
        srcs, outs, got, made, sems = refs[:n], refs[n : 2 * n], refs[2 * n : 3 * n], refs[3 * n : 4 * n], refs[4 * n]
        loads = [pltpu.make_async_copy(srcs[i], got[i], sems.at[0, i]) for i in range(n)]
        stores = [pltpu.make_async_copy(made[i], outs[i], sems.at[1, i]) for i in range(n)]
        for load in loads:
            load.start()
        for i in range(n):
            loads[i].wait()
            lay_out(got[i], made[i], widths[i])
            stores[i].start()
        for store in stores:
            store.wait()

    return pl.pallas_call(
        body,
        out_shape=tuple(jax.ShapeDtypeStruct(shape, F32) for shape in shapes),
        in_specs=[HBM_SPEC] * n,
        out_specs=(HBM_SPEC,) * n,
        scratch_shapes=[pltpu.VMEM(p.shape, p.dtype) for p in pieces]
        + [pltpu.VMEM(shape, F32) for shape in shapes]
        + [pltpu.SemaphoreType.DMA((2, n))],
        compiler_params=pltpu.CompilerParams(vmem_limit_bytes=VMEM_LIMIT),
        name="lay_out",
    )(*pieces)


HBM_SPEC = pl.BlockSpec(memory_space=pltpu.HBM)


class Loaded:
    def __init__(self, src, dst, sem, start=True):
        self.copy, self.ref, self.waited = pltpu.make_async_copy(src, dst, sem), dst, False
        if start:
            self.copy.start()

    def get(self):
        if not self.waited:
            self.copy.wait()
            self.waited = True
        return self.ref


class LoadedRows:
    def __init__(self, src, dst, sems, chunk):
        self.src, self.ref, self.sems, self.chunk = src, dst, sems, chunk

    def copies(self, owner, slot):
        for j in range(2):
            at = pl.multiple_of((TP * j + owner) * self.chunk, self.chunk)
            rows = pl.ds(at, self.chunk)
            yield pltpu.make_async_copy(
                self.src.at[rows], self.ref.at[rows], self.sems.at[2 * slot + j]
            )

    def start(self, owners):
        for slot, owner in enumerate(owners):
            for copy in self.copies(owner, slot):
                copy.start()

    def wait(self, owner, slot):
        for copy in self.copies(owner, slot):
            copy.wait()


def call_with_jobs(
    kernel, number, planes, jobs, operands, outs, scratch, name, cost, filler=None, by_rows=()
):
    filler = filler or Idle()
    jobs = list(jobs)
    n_in, n_out, n_job = len(operands), len(outs), len(jobs)
    n_load, n_raw, n_fill = len(filler.loads), len(filler.raws), len(filler.outs)
    loads, raws = list(filler.loads), list(filler.raws)
    n_sems = max(Shipper.count(jobs, planes), 1)
    plain = [job._replace(src=jax.ShapeDtypeStruct(job.src.shape, job.src.dtype)) for job in jobs]
    job_scratch = Shipper.scratch(jobs)
    n_scratch = len(filler.scratch)

    def body(*refs):
        refs = list(refs)

        def take(n):
            out = refs[:n]
            del refs[:n]
            return out

        ins, srcs, fills, raw = take(n_in), take(n_job), take(n_load), take(n_raw)
        results, dsts, fill_outs = take(n_out), take(n_job), take(n_fill)
        sems, in_sems, row_sems = take(3)
        loaded = []
        for i, src in enumerate(ins):
            if i in by_rows:
                rows = row_sems.at[by_rows.index(i)]
                loaded.append(LoadedRows(src, refs.pop(0), rows, src.shape[0] // (2 * TP)))
            else:
                loaded.append(Loaded(src, refs.pop(0), in_sems.at[i]))
        fill_loads = [
            Loaded(src, refs.pop(0), in_sems.at[n_in + i], False) for i, src in enumerate(fills)
        ]
        shipper = Shipper(plain, planes, srcs, dsts, take(len(job_scratch)), sems)
        begin = functools.partial(filler.begin, fill_loads, raw, fill_outs, take(n_scratch))
        kernel(shipper, loaded, list(results), refs, Running(filler, begin, fill_loads))

    results = [result_of(job) for job in jobs]
    got = pl.pallas_call(
        body,
        out_shape=tuple(outs)
        + tuple(jax.ShapeDtypeStruct(*r) for r in results)
        + tuple(filler.outs),
        in_specs=[HBM_SPEC] * (n_in + n_job + n_load + n_raw),
        out_specs=(HBM_SPEC,) * (n_out + n_job + n_fill),
        scratch_shapes=[
            pltpu.SemaphoreType.DMA((n_sems,)),
            pltpu.SemaphoreType.DMA((max(n_in + n_load, 1),)),
            pltpu.SemaphoreType.DMA((max(len(by_rows), 1), 2 * TP)),
        ]
        + [pltpu.VMEM(v.shape, v.dtype) for v in operands + loads]
        + job_scratch
        + list(filler.scratch)
        + scratch,
        compiler_params=pltpu.CompilerParams(
            collective_id=number, has_side_effects=True, vmem_limit_bytes=VMEM_LIMIT
        ),
        cost_estimate=pl.CostEstimate(flops=cost, bytes_accessed=8 * MB, transcendentals=0),
        name=name,
    )(*operands, *[job.src for job in jobs], *loads, *raws)
    return got[:n_out], list(got[n_out : n_out + n_job]), list(got[n_out + n_job :])


class Running:
    def __init__(self, filler, begin, loads):
        self.begin, self.run, self.end, self.loads = begin, filler.run, filler.end, loads
        self.n_steps, self.done = filler.n_steps, 0

    def prefetch(self):
        for load in self.loads:
            load.copy.start()

    def advance(self, share):
        high = int(round(share * self.n_steps))
        if high > self.done:
            self.run(self.done, high)
            self.done = high


def ship(number, planes, jobs):
    def kernel(shipper, ins, outs, scratch, filler):
        shipper.greet(())
        shipper.start()
        shipper.finish()

    return call_with_jobs(kernel, number, planes, jobs, [], [], [], "ship", 0)[1]


class GatherNormed:
    by_rows = ()

    def __init__(self, x, gain):
        self.chunk = x.shape[1]
        self.operands, self.cost = [x, gain], 10**6
        self.outs = [jax.ShapeDtypeStruct((2 * TP * self.chunk, D), BF)]
        self.scratch = [pltpu.VMEM((2, self.chunk, D), BF), pltpu.SemaphoreType.DMA((7, 2))]

    def bind(self, ins, outs, scratch):
        self.x, self.gain = ins
        self.g = Gatherer(outs[0], scratch[0], scratch[1], self.chunk, group_ids())

    def load(self):
        pass

    def first(self, met):
        x_ref, gain_ref = self.x.get(), self.gain.get()
        met()
        for j in range(2):
            self.g.put(j, normed(x_ref[j].astype(F32), gain_ref[...]).astype(BF))

    def second(self, between):
        between()

    def third(self):
        for j in range(2):
            self.g.forward(j)

    def last(self):
        self.g.finish()


GELU_C = float(np.sqrt(2.0 / np.pi))


def gelu_parts(v):
    tanh = jnp.tanh(GELU_C * (v + 0.044715 * v * v * v))
    return tanh, 0.5 * (1.0 + tanh)


def gelu_slope(v):
    tanh, half = gelu_parts(v)
    return half + 0.5 * v * (1.0 - tanh * tanh) * (GELU_C * (1.0 + 3 * 0.044715 * v * v))


class Rows:
    n_operands, n_outs, n_scratch = 1, 0, 0

    def __init__(self, ins, outs, scratch, chunk):
        self.rows, self.chunk = ins.pop(0), chunk
        self.by_rows = [self.rows]

    def prepare(self):
        self.ref = self.rows.ref

    def make(self, pair, slot):
        pass

    def finish(self):
        pass

    def pick(self, ref, pair):
        return jnp.concatenate([ref[rows] for rows in pair], axis=0)


class MadeRows(Rows):
    def write(self, index, ref, out, slot, pair):
        for j, rows in enumerate(pair):
            copy = pltpu.make_async_copy(ref.at[rows], out.at[rows], self.sems.at[index, 2 * slot + j])
            copy.start()
            self.copies.append(copy)

    def finish(self):
        for copy in self.copies:
            copy.wait()

    def tiles(self, body):
        @pl.loop(0, self.ref.shape[1] // 256)
        def _(n):
            body(pl.ds(pl.multiple_of(n * 256, 256), 256))


class FeedForward(MadeRows):
    n_operands, n_outs, n_scratch = 2, 2, 3

    def __init__(self, ins, outs, scratch, chunk):
        self.rows, self.w_in, self.chunk, self.copies = ins.pop(0), ins.pop(0), chunk, []
        self.by_rows = [self.rows]
        self.pre_out, self.act_out = outs.pop(0), outs.pop(0)
        self.pre, self.ref, self.sems = scratch.pop(0), scratch.pop(0), scratch.pop(0)

    @staticmethod
    def extras(n_rows, width):
        shapes = [((n_rows, width), F32), ((n_rows, width), BF)]
        scratch = [pltpu.VMEM(*v) for v in shapes] + [pltpu.SemaphoreType.DMA((2, 2 * TP))]
        return [jax.ShapeDtypeStruct(*v) for v in shapes], scratch

    def prepare(self):
        self.w_in = self.w_in.get()

    def make(self, pair, slot):
        x = self.pick(self.rows.ref, pair)

        def tile(cols):
            v = mm(x, self.w_in[:, cols])
            act = (v * gelu_parts(v)[1]).astype(BF)
            for j, rows in enumerate(pair):
                self.pre[rows, cols] = v[j * self.chunk : (j + 1) * self.chunk]
                self.ref[rows, cols] = act[j * self.chunk : (j + 1) * self.chunk]

        self.tiles(tile)
        self.write(0, self.pre, self.pre_out, slot, pair)
        self.write(1, self.ref, self.act_out, slot, pair)


class FeedForwardBack(MadeRows):
    n_operands, n_outs, n_scratch = 3, 1, 2

    def __init__(self, ins, outs, scratch, chunk):
        self.rows, self.pre, self.w_out = ins.pop(0), ins.pop(0), ins.pop(0)
        self.chunk, self.copies = chunk, []
        self.by_rows = [self.rows, self.pre]
        self.out, self.ref, self.sems = outs.pop(0), scratch.pop(0), scratch.pop(0)

    @staticmethod
    def extras(n_rows, width):
        shape = ((n_rows, width), BF)
        scratch = [pltpu.VMEM(*shape), pltpu.SemaphoreType.DMA((1, 2 * TP))]
        return [jax.ShapeDtypeStruct(*shape)], scratch

    def prepare(self):
        self.w_out = self.w_out.get()

    def make(self, pair, slot):
        x = self.pick(self.rows.ref, pair)

        def tile(cols):
            grad = mm_nt(x, self.w_out[cols, :])
            for j, rows in enumerate(pair):
                back = gelu_slope(self.pre.ref[rows, cols]) * grad[j * self.chunk : (j + 1) * self.chunk]
                self.ref[rows, cols] = back.astype(BF)

        self.tiles(tile)
        self.write(0, self.ref, self.out, slot, pair)


class Stage:
    def __init__(
        self,
        left,
        weight,
        resid,
        *,
        flip=False,
        maker=Rows,
        back=None,
        gather=None,
        gain=None,
        given=None,
        dtype=F32,
        low=False,
    ):
        self.maker, self.flip, self.back, self.gather, self.low = maker, flip, bool(back), gather, low
        self.chunk = chunk = resid.shape[1]
        self.operands = list(left) + [weight, resid]
        self.cost = 4 * left[0].shape[0] * D * D
        self.by_rows = {Rows: (0,), FeedForward: (0,), FeedForwardBack: (0, 1)}[maker]
        if back:
            self.operands += [back[1], back[0]]
        elif gather == "norm":
            self.operands.append(gain)
        if gather == "given":
            self.operands.append(given)
        self.outs = [jax.ShapeDtypeStruct((2, chunk, D), dtype)]
        if gather:
            self.outs.append(jax.ShapeDtypeStruct((2 * TP * chunk, D), BF))
        if back:
            self.outs.append(jax.ShapeDtypeStruct((1, D), F32))
        half = pltpu.VMEM((2, chunk, D), BF)
        full = pltpu.VMEM((2, chunk, D), F32)
        self.scratch = [half] * 6 + [full] * 2
        self.scratch += [pltpu.VMEM((2, chunk, D), dtype), pltpu.SemaphoreType.DMA((13,))]
        if gather:
            self.scratch += [half, pltpu.SemaphoreType.DMA((7, 2))]
        if back:
            self.scratch.append(pltpu.VMEM((1, D), F32))
        if low:
            self.outs.append(jax.ShapeDtypeStruct((2, chunk, D), BF))
            self.scratch.append(half)
        if maker is not Rows:
            width = weight.shape[1] if flip else weight.shape[0]
            more, more_scratch = maker.extras(2 * TP * chunk, width)
            self.outs += more
            self.scratch += more_scratch

    def bind(self, ins, outs, scratch):
        maker = self.maker
        made_outs = [outs.pop() for _ in range(maker.n_outs)][::-1]
        made_scratch = [scratch.pop() for _ in range(maker.n_scratch)][::-1]
        self.left = maker(ins, made_outs, made_scratch, self.chunk)
        self.w_in, self.resid_in = ins.pop(0), ins.pop(0)
        self.gain_in = ins.pop(0) if (self.back or self.gather == "norm") else None
        self.x_in = ins.pop(0) if self.back else None
        self.given_in = ins.pop(0) if self.gather == "given" else None
        self.y_out = outs.pop(0)
        gath_ref = outs.pop(0) if self.gather else None
        self.dgain_out = outs.pop(0) if self.back else None
        self.low_out = outs.pop(0) if self.low else None
        self.s_far, self.r_far, self.s_x, self.r_x, self.s_core, self.r_core = scratch[:6]
        self.keep, self.own, self.y_ref, self.sems = scratch[6:10]
        scratch = scratch[10:]
        self.ids = group_ids()
        self.g = None
        if self.gather:
            self.g = Gatherer(gath_ref, scratch.pop(0), scratch.pop(0), self.chunk, self.ids)
        self.dgain_ref = scratch.pop(0) if self.back else None
        self.low_ref = scratch.pop(0) if self.low else None
        self.slots, self.stores = [0, 1, 2, 3], []

    def load(self):
        me, core, across, far = self.ids
        for rows in self.left.by_rows:
            rows.start((far, across, core, me))

    def partial(self, owner, ref):
        slot, chunk, left = self.slots.pop(0), self.chunk, self.left
        for rows in left.by_rows:
            rows.wait(owner, slot)
        pair = [
            pl.ds(pl.multiple_of((TP * j + owner) * chunk, chunk), chunk) for j in range(2)
        ]
        left.make(pair, slot)
        a = left.pick(left.ref, pair)

        @pl.loop(0, D // 256)
        def _(n):
            cols = pl.ds(pl.multiple_of(n * 256, 256), 256)
            total = mm_nt(a, self.w_ref[cols, :]) if self.flip else mm(a, self.w_ref[:, cols])
            for j in range(2):
                ref[j, :, cols] = total[j * chunk : (j + 1) * chunk].astype(ref.dtype)

    def first(self, met):
        me, core, across, far = self.ids
        sems = self.sems
        self.left.prepare()
        self.w_ref = self.w_in.get()
        self.partial(far, self.s_far)
        met()
        self.c_far = send(self.s_far, self.r_far, sems.at[0], sems.at[1], core)
        self.c_far.start()
        if self.gather == "given":
            given_ref = self.given_in.get()
            for j in range(2):
                self.g.put(j, given_ref[j])
        self.partial(across, self.keep)
        self.c_far.wait_recv()
        self.c_x = []
        for j in range(2):
            self.s_x[j] = (self.keep[j] + self.r_far[j].astype(F32)).astype(BF)
            copy = send(self.s_x.at[j], self.r_x.at[j], sems.at[2 + j], sems.at[4 + j], across)
            copy.start()
            self.c_x.append(copy)
        self.partial(core, self.s_core)
        self.c_core = send(self.s_core, self.r_core, sems.at[6], sems.at[7], core)
        self.c_core.start()
        self.partial(me, self.own)

    def keep_out(self, src, dst, sem):
        copy = pltpu.make_async_copy(src, dst, self.sems.at[sem])
        copy.start()
        self.stores.append(copy)

    def second(self, between):
        self.c_core.wait_recv()
        resid_ref = self.resid_in.get()
        x_ref = self.x_in.get() if self.back else None
        gains = self.gain_in.get()[...] if self.gain_in else None
        if self.gather == "given":
            for j in range(2):
                self.g.forward(j)
        for j in range(2):
            self.c_x[j].wait_recv()
            if j == 1:
                between()
            total = self.own[j] + self.r_core[j].astype(F32) + self.r_x[j].astype(F32)
            if self.back:
                x = x_ref[j].astype(F32)
                r = lax.rsqrt(jnp.mean(x * x, axis=-1, keepdims=True) + EPS)
                scaled = total * gains
                inner = jnp.mean(scaled * x, axis=-1, keepdims=True)
                y = resid_ref[j].astype(F32) + r * scaled - x * (r * r * r * inner)
                dgain = jnp.sum(total * x * r, axis=0, keepdims=True)
                if j == 0:
                    self.dgain_ref[...] = dgain
                else:
                    self.dgain_ref[...] += dgain
            else:
                y = resid_ref[j].astype(F32) + total
            if self.gather == "norm":
                self.g.put(j, normed(y, gains).astype(BF))
            elif self.gather == "low":
                self.g.put(j, y.astype(BF))
            self.y_ref[j] = y.astype(self.y_ref.dtype)
            self.keep_out(self.y_ref.at[j], self.y_out.at[j], 8 + j)
            if self.low:
                self.low_ref[j] = y.astype(BF)
                self.keep_out(self.low_ref.at[j], self.low_out.at[j], 11 + j)
        if self.back:
            self.keep_out(self.dgain_ref, self.dgain_out, 10)

    def third(self):
        if self.gather in ("norm", "low"):
            for j in range(2):
                self.g.forward(j)

    def last(self):
        if self.gather:
            self.g.finish()
        for copy in [self.c_far, self.c_core] + self.c_x:
            copy.wait_send()
        for copy in self.stores:
            copy.wait()
        self.left.finish()


def stage(number, planes, stages, jobs=(), filler=None, share=SHARE):
    operands = [v for st in stages for v in st.operands]
    outs = [v for st in stages for v in st.outs]
    scratch = [v for st in stages for v in st.scratch]
    by_rows, base = [], 0
    for st in stages:
        by_rows += [base + i for i in st.by_rows]
        base += len(st.operands)

    def kernel(shipper, ins, results, refs, filler):
        for st in stages:
            parts = []
            for have, n in ((ins, st.operands), (results, st.outs), (refs, st.scratch)):
                parts.append(have[: len(n)])
                del have[: len(n)]
            st.bind(*parts)
            st.load()
        shipper.signal()

        def met():
            shipper.met()
            shipper.start()

        for n, st in enumerate(stages):
            st.first(met if n == 0 else (lambda: None))
        filler.prefetch()
        filler.begin()
        filler.advance(share[0])
        for n, st in enumerate(stages):
            st.second(lambda: filler.advance(share[1]) if n == 0 else None)
        filler.advance(share[2])
        for st in stages:
            st.third()
        filler.advance(1.0)
        filler.end()
        for st in stages:
            st.last()
        shipper.finish()

    cost = sum(st.cost for st in stages)
    got, moved, made = call_with_jobs(
        kernel, number, planes, jobs, operands, outs, scratch, "stage", cost, filler, tuple(by_rows)
    )
    got = list(got)
    each = []
    for st in stages:
        each.append(got[: len(st.outs)])
        del got[: len(st.outs)]
    return each, moved, made


class Attention:
    def __init__(self, parts, q, kv, bias, mkv, causal):
        self.parts, self.causal = parts, causal
        self.q_shape, self.kv_shape = q.shape, kv.shape
        self.rows, self.keys = q.shape[0], kv.shape[0]
        self.chunk = self.rows // (2 * TP)
        self.joint = q is kv
        self.extra = 0 if mkv is None else mkv.shape[0]
        self.total = self.keys + self.extra
        self.bias = bias
        self.size = 2 * self.chunk
        self.blocks = self.rows // self.size
        self.n_steps = 2 * HQ
        self.loads = [q] + ([] if self.joint else [kv])
        self.mem = [mkv] if self.extra else []
        self.raws = []

    def heads(self, *widths_dtypes):
        return [pltpu.VMEM((HQ, n, DH), dtype) for n, dtype in widths_dtypes]

    def split_qkv(self, q_ref, kv_ref, loads, qs, ks, vs):
        at = QC if self.joint else 0
        keys = self.keys
        for i in range(HQ):
            qs[i] = q_ref[:, DH * i : DH * (i + 1)]
            ks[i, :keys] = kv_ref[:, at + DH * i : at + DH * (i + 1)]
            vs[i, :keys] = kv_ref[:, at + QC + DH * i : at + QC + DH * (i + 1)]
        if self.extra:
            mkv_ref = loads.pop(0).get()
            for i in range(HQ):
                ks[i, keys:] = mkv_ref[:, DH * i : DH * (i + 1)]
                vs[i, keys:] = mkv_ref[:, QC + DH * i : QC + DH * (i + 1)]

    def place(self, row_chunk):
        upper = row_chunk // TP
        part = lax.axis_index("part") if self.parts > 1 else 0
        return (upper * (TP * self.parts) + TP * part + (row_chunk - TP * upper)) * self.chunk

    def halves(self, low, high):
        for half in range(2):
            first = max(low - HQ * half, 0)
            last = min(high - HQ * half, HQ)
            if first < last:
                n = self.blocks // 2
                yield half, range(half * n, (half + 1) * n), first, last

    def width(self, b):
        if self.causal and self.parts == 1:
            return (b + 1) * self.size
        return self.total

    def block(self, b):
        return pl.ds(b * self.size, self.size)

    def diagonal(self, b, u):
        keys = min(self.width(b), self.keys)
        start = self.keys - self.place(2 * b + u)
        return pl.ds(start if isinstance(start, int) else pl.multiple_of(start, 128), keys)


class AttentionForward(Attention):
    def __init__(self, parts, q, kv, segq, segk, bvec, mkv, causal, products=None):
        super().__init__(parts, q, kv, bvec is not None, mkv, causal)
        self.products = products
        if products:
            self.loads = [v for pair in products for v in pair]
        self.loads += self.mem + [segq, segk] + ([bvec] if self.bias else [])
        self.outs = [
            jax.ShapeDtypeStruct((self.rows, QC), BF),
            jax.ShapeDtypeStruct((HQ, self.rows, self.total), BF),
        ]
        self.scratch = self.heads((self.rows, BF), (self.total, BF), (self.total, BF), (self.rows, BF))
        self.scratch += [
            pltpu.VMEM((self.blocks, self.size, self.total), BF),
            pltpu.VMEM((self.rows, QC), BF),
            pltpu.SemaphoreType.DMA((3 + self.blocks,)),
        ]
        if self.bias:
            self.scratch.append(pltpu.VMEM((self.chunk, 2 * self.keys), F32))
        if products:
            for x, w in products:
                self.outs.append(jax.ShapeDtypeStruct((x.shape[0], w.shape[1]), BF))
                self.scratch.append(pltpu.VMEM((x.shape[0], w.shape[1]), BF))

    def begin(self, loads, raws, outs, scratch):
        self.att_out, self.p_out = outs[:2]
        self.qs, self.ks, self.vs, self.os, self.p_buf, self.att, self.sems = scratch[:7]
        self.toep = scratch[7] if self.bias else None
        loads = list(loads)
        self.copies = []
        if self.products:
            made = scratch[-len(self.products) :]
            for n, (out, to) in enumerate(zip(made, outs[2:])):
                x, w = loads.pop(0).get(), loads.pop(0).get()

                @pl.loop(0, x.shape[0] // 256)
                def _(r):
                    rows = pl.ds(pl.multiple_of(r * 256, 256), 256)
                    out[rows] = mm(x[rows], w[...]).astype(BF)

                self.copies.append(pltpu.make_async_copy(out, to, self.sems.at[1 + n]))
                self.copies[-1].start()
            q_ref, kv_ref = made[0], made[-1]
        else:
            q_ref = loads.pop(0).get()
            kv_ref = q_ref if self.joint else loads.pop(0).get()
        self.split_qkv(q_ref, kv_ref, loads, self.qs, self.ks, self.vs)
        self.segq, self.segk = loads.pop(0).get(), loads.pop(0).get()
        self.bvec = loads.pop(0).get() if self.bias else None

    def slot(self, h, b):
        n = self.blocks // 2
        return n * lax.rem(h + (b // n) * HQ, 2) + b % n

    def keep(self, h, b):
        wide, slot = pl.ds(0, self.width(b)), self.slot(h, b)
        return pltpu.make_async_copy(
            self.p_buf.at[slot, :, wide], self.p_out.at[h, self.block(b), wide], self.sems.at[3 + slot]
        )

    def one_block(self, h, b):
        wide, chunk, rows = self.width(b), self.chunk, self.block(b)
        keys = min(wide, self.keys)
        s = mm_nt(self.qs[h, rows], self.ks[h, :wide])
        if self.bias:
            parts = [self.toep[:, self.diagonal(b, u)] for u in range(2)]
            biased = s[:, :keys] + jnp.concatenate(parts, axis=0)
            s = jnp.concatenate([biased, s[:, keys:]], axis=1) if self.extra else biased
        allowed = self.segq[rows] == self.segk[:, :wide]
        s = jnp.where(allowed, s, MASKED)
        if self.causal:
            row = lax.broadcasted_iota(jnp.int32, (chunk, 1), 0)
            places = jnp.concatenate([row + self.place(2 * b + u) for u in range(2)], axis=0)
            seen = wide - self.size if self.parts == 1 else 0
            later = lax.broadcasted_iota(jnp.int32, (1, wide - seen), 1) + seen
            last = jnp.where(later <= places, s[:, seen:], MASKED)
            s = jnp.concatenate([s[:, :seen], last], axis=1) if seen else last
        top = jnp.max(s, axis=-1, keepdims=True)
        e = jnp.exp(s - top)
        p = (e * (1.0 / jnp.sum(e, axis=-1, keepdims=True))).astype(BF)
        self.p_buf[self.slot(h, b), :, :wide] = p
        self.keep(h, b).start()
        self.os[h, rows] = mm(p, self.vs[h, :wide]).astype(BF)

    def run(self, low, high):
        for half, blocks, first, last in self.halves(low, high):

            @pl.loop(first, last)
            def _(h):
                if self.bias:
                    row = jnp.broadcast_to(self.bvec[h], (self.chunk, 2 * self.keys))
                    self.toep[...] = pltpu.roll(row, 0, 1, stride=1, stride_axis=0)

                @pl.when(h >= 2)
                def _():
                    for b in blocks:
                        self.keep(h - 2, b).wait()

                if half == 1:

                    @pl.when(h < 2)
                    def _():
                        for b in range(self.blocks // 2):
                            self.keep(h + 1, b).wait()

                for b in blocks:
                    self.one_block(h, b)

    def end(self):
        for i in range(HQ):
            self.att[:, DH * i : DH * (i + 1)] = self.os[i]
        out = pltpu.make_async_copy(self.att, self.att_out, self.sems.at[0])
        out.start()
        for h in (HQ - 2, HQ - 1):
            for b in range(self.blocks // 2, self.blocks):
                self.keep(h, b).wait()
        out.wait()
        for copy in self.copies:
            copy.wait()


class AttentionBackward(Attention):
    def __init__(self, parts, p, q, kv, up, w_proj, att, bias, mkv, xs, proj=True, causal=False):
        super().__init__(parts, q, kv, bias, mkv, causal)
        self.xs, self.proj = xs if parts == 1 else [], proj
        self.loads += self.mem + [up, w_proj, att] + self.xs
        self.raws = [p]
        rows, total, keys = self.rows, self.total, self.keys
        if self.joint:
            self.outs = [jax.ShapeDtypeStruct((rows, 3 * QC), BF)]
        else:
            kv_type = BF if parts == 1 else F32
            self.outs = [
                jax.ShapeDtypeStruct((rows, QC), BF),
                jax.ShapeDtypeStruct((keys, 2 * QC), kv_type),
            ]
        if bias:
            self.outs.append(jax.ShapeDtypeStruct((HQ, 1, 2 * keys), F32))
        if self.extra:
            self.outs.append(jax.ShapeDtypeStruct((self.extra, 2 * QC), BF))
        if proj:
            self.outs.append(jax.ShapeDtypeStruct((QC, D), BF))
        for n in range(len(self.xs)):
            self.outs.append(jax.ShapeDtypeStruct((D, self.outs[n].shape[1]), BF))
        self.scratch = self.heads(
            (rows, BF), (total, BF), (total, BF), (rows, BF), (rows, BF), (total, F32), (total, F32)
        )
        self.scratch += [
            pltpu.VMEM((HQ, rows, 1), F32),
            pltpu.VMEM((self.blocks, self.size, total), BF),
            pltpu.SemaphoreType.DMA((self.blocks + len(self.outs),)),
        ]
        self.scratch += [pltpu.VMEM(o.shape, o.dtype) for o in self.outs]
        if bias:
            self.scratch.append(pltpu.VMEM((HQ, self.chunk, 2 * keys), F32))

    def fetch(self, h, b):
        n = self.blocks // 2
        slot = n * lax.rem(h + (b // n) * HQ, 2) + b % n
        wide = pl.ds(0, self.width(b))
        return pltpu.make_async_copy(
            self.p_in.at[h, self.block(b), wide], self.p_buf.at[slot, :, wide], self.sems.at[slot]
        )

    def begin(self, loads, raws, outs, scratch):
        self.results, (self.p_in,) = outs, raws
        scratch, loads = list(scratch), list(loads)
        self.qs, self.ks, self.vs, self.dos, self.dqs, self.dks, self.dvs = scratch[:7]
        self.rds, self.p_buf, self.sems = scratch[7:10]
        self.made = scratch[10 : 10 + len(outs)]
        self.diag = scratch[-1] if self.bias else None
        for b in range(self.blocks // 2):
            self.fetch(0, b).start()
        q_ref = loads.pop(0).get()
        kv_ref = q_ref if self.joint else loads.pop(0).get()
        self.split_qkv(q_ref, kv_ref, loads, self.qs, self.ks, self.vs)
        up_ref, w_ref, att_ref = (loads.pop(0).get() for _ in range(3))

        @pl.loop(0, self.rows // 256)
        def _(r):
            rows = pl.ds(pl.multiple_of(r * 256, 256), 256)
            grads = mm_nt(up_ref[rows], w_ref[...]).astype(BF)
            att = att_ref[rows]
            for i in range(HQ):
                span = slice(DH * i, DH * (i + 1))
                self.dos[i, rows] = grads[:, span]
                dots = grads[:, span].astype(F32) * att[:, span].astype(F32)
                self.rds[i, rows] = jnp.sum(dots, axis=-1, keepdims=True)

        made = list(self.made)
        self.dq = made.pop(0)
        self.dkv = self.dq if self.joint else made.pop(0)
        self.dbvec = made.pop(0) if self.bias else None
        self.dmkv = made.pop(0) if self.extra else None
        g_proj = made.pop(0) if self.proj else None
        self.g_rows, self.x_loads = made, loads
        if self.proj:

            @pl.loop(0, D // 256)
            def _(n):
                cols = pl.ds(pl.multiple_of(n * 256, 256), 256)
                g_proj[:, cols] = mm_tn(att_ref[...], up_ref[:, cols]).astype(BF)

    def run(self, low, high):
        keys, chunk, n = self.keys, self.chunk, self.blocks // 2
        for half, blocks, first, last in self.halves(low, high):

            @pl.loop(first, last)
            def _(h):
                for b in blocks:
                    self.fetch(h, b).wait()

                @pl.when(h + 1 < HQ)
                def _():
                    for b in blocks:
                        self.fetch(h + 1, b).start()

                if half == 0:

                    @pl.when(h + 1 == HQ)
                    def _():
                        for b in range(n, 2 * n):
                            self.fetch(0, b).start()

                    self.dks[h] = jnp.zeros(self.dks.shape[1:], F32)
                    self.dvs[h] = jnp.zeros(self.dvs.shape[1:], F32)
                    if self.bias:
                        self.diag[h] = jnp.zeros(self.diag.shape[1:], F32)
                for b in blocks:
                    wide, rows = self.width(b), self.block(b)
                    slot = n * lax.rem(h + half * HQ, 2) + b % n
                    q, grad, p = self.qs[h, rows], self.dos[h, rows], self.p_buf[slot, :, :wide]
                    dp = mm_nt(grad, self.vs[h, :wide])
                    ds = (p.astype(F32) * (dp - self.rds[h, rows])).astype(BF)
                    self.dqs[h, rows] = mm(ds, self.ks[h, :wide]).astype(BF)
                    self.dks[h, :wide] += mm_tn(ds, q)
                    self.dvs[h, :wide] += mm_tn(p, grad)
                    if self.bias:
                        for u in range(2):
                            part = ds[u * chunk : (u + 1) * chunk, : min(wide, keys)]
                            self.diag[h, :, self.diagonal(b, u)] += part.astype(F32)
                if self.bias and half == 1:
                    x = self.diag[h]
                    size = chunk
                    while size > 1:
                        size //= 2
                        x = x[:size] + pltpu.roll(x[size:], 2 * keys - size, 1)
                    self.dbvec[h] = x

    def end(self):
        keys = self.keys
        to = QC if self.joint else 0
        for i in range(HQ):
            self.dq[:, DH * i : DH * (i + 1)] = self.dqs[i]
            at = to + DH * i
            self.dkv[:, at : at + DH] = self.dks[i, :keys].astype(self.dkv.dtype)
            self.dkv[:, at + QC : at + QC + DH] = self.dvs[i, :keys].astype(self.dkv.dtype)
            if self.extra:
                self.dmkv[:, DH * i : DH * (i + 1)] = self.dks[i, keys:].astype(BF)
                self.dmkv[:, QC + DH * i : QC + DH * (i + 1)] = self.dvs[i, keys:].astype(BF)
        for load, out, grad in zip(self.x_loads, self.g_rows, (self.dq, self.dkv)):
            x_ref = load.get()

            @pl.loop(0, D // 256)
            def _(n):
                cols = pl.ds(pl.multiple_of(n * 256, 256), 256)
                out[cols] = mm_tn(x_ref[:, cols], grad[...]).astype(BF)

        copies = [
            pltpu.make_async_copy(src, dst, self.sems.at[self.blocks + n])
            for n, (src, dst) in enumerate(zip(self.made, self.results))
        ]
        for copy in copies:
            copy.start()
        for copy in copies:
            copy.wait()


class FeedForwardGrads:
    n_steps = 6

    def __init__(self, at_stage, act, x):
        self.at_stage, self.loads, self.raws = at_stage, [act, x], []
        self.outs = [jax.ShapeDtypeStruct((v.shape[1], D), BF) for v in (act, x)]
        self.outs[1] = jax.ShapeDtypeStruct((x.shape[1], act.shape[1]), BF)
        self.scratch = [pltpu.VMEM(o.shape, BF) for o in self.outs] + [pltpu.SemaphoreType.DMA((2,))]

    def begin(self, loads, raws, outs, scratch):
        self.left = [load.get() for load in loads]
        self.right = [self.at_stage.left.rows.ref, self.at_stage.left.ref]
        self.made, self.results, self.sems = scratch[:2], outs, scratch[2]

    def run(self, low, high):
        for n in range(2):
            first, last = max(low - 3 * n, 0), min(high - 3 * n, 3)
            if first < last:

                @pl.loop(first, last)
                def _(i):
                    cols = pl.ds(pl.multiple_of(i * 256, 256), 256)
                    self.made[n][cols] = mm_tn(self.left[n][:, cols], self.right[n][...]).astype(BF)

    def end(self):
        copies = [
            pltpu.make_async_copy(self.made[n], self.results[n], self.sems.at[n]) for n in range(2)
        ]
        for copy in copies:
            copy.start()
        for copy in copies:
            copy.wait()


class Idle:
    n_steps, loads, raws, outs, scratch = 0, [], [], [], []

    def begin(self, loads, raws, outs, scratch):
        pass

    def run(self, low, high):
        pass

    def end(self):
        pass


def attend(number, planes, filler, jobs):
    def kernel(shipper, ins, outs, scratch, filler):
        filler.prefetch()
        shipper.greet(())
        shipper.start()
        filler.begin()
        filler.run(0, filler.n_steps)
        filler.end()
        shipper.finish()

    _, moved, made = call_with_jobs(
        kernel, number, planes, jobs, [], [], [], "attend", 4 * 10**9, filler
    )
    return made, moved


def stacked(gains, rels):
    n = len(gains)

    def body(*refs):
        rows, table = refs[-2:]
        for i in range(n):
            rows[i : i + 1] = refs[i][...].astype(F32).reshape(1, -1)
        for i in range(len(rels)):
            table[i] = refs[n + i][...].astype(F32)

    return pl.pallas_call(
        body,
        out_shape=(
            jax.ShapeDtypeStruct((n, gains[0].shape[0]), F32),
            jax.ShapeDtypeStruct((len(rels),) + rels[0].shape, F32),
        ),
        name="stacked",
    )(*gains, *rels)


class Chain:
    def __init__(self, value, steps, width):
        self.value, self.steps, self.width = value, steps, width


ALL = ("seq", "part", "tp", "fsdp")
CTX = ("seq", "part", "tp")


def per_device(
    parts,
    planes,
    enc_input,
    dec_input,
    segments,
    prefix_rows,
    buckets,
    memory,
    enc_gain,
    enc_qkv,
    enc_rel,
    enc_proj,
    enc_ffnorm,
    enc_ffin,
    enc_ffout,
    dec_gain,
    dec_qkv,
    dec_rel,
    dec_proj,
    cross_gain,
    cross_query,
    cross_kv,
    cross_proj,
    dec_ffnorm,
    dec_ffin,
    dec_ffout,
    enc_cotan,
    dec_cotan,
):
    seq, part, tp, plane = (lax.axis_index(name) for name in ALL)
    chunk = enc_input.shape[1]
    length = buckets.shape[0] // 2
    docs, prefix = prefix_rows.shape[1:]

    first = seq == 0
    split = planes * 2

    def joined(x, came):
        mine = lax.dynamic_index_in_dim(x, seq, 0, keepdims=False)
        came = came.astype(x.dtype)
        return jnp.stack([jnp.where(first, mine, came), jnp.where(first, came, mine)])

    def cols(w, start, width=QC):
        return lax.dynamic_slice_in_dim(w, start + width * tp, width, 1)

    def halved(w):
        rows = w.shape[0] // 2
        return lax.dynamic_slice_in_dim(w, rows * seq, rows, 0)

    def qkv_part(w):
        w = halved(w)
        return jnp.concatenate([cols(w, D * i) for i in range(w.shape[1] // D)], axis=1)

    hidden = enc_ffout.shape[0] // TP

    def ffin_part(w):
        w = halved(w)
        return jnp.concatenate(
            [cols(w, hidden * TP * i, hidden) for i in range(planes)], axis=1
        )

    def ffout_part(w):
        rows = hidden // 2
        return lax.dynamic_slice_in_dim(w, hidden * tp + rows * seq, rows, 0)

    def over_planes(w):
        return gather_job("fsdp", w, planes)

    def over_seq(w):
        return gather_job("seq", w, 2, 1)

    def matrix(w):
        return w.reshape(-1, w.shape[-1])

    gains = (enc_gain, enc_ffnorm, dec_gain, cross_gain, dec_ffnorm)
    gain_stack, rel_stack = stacked(gains, (enc_rel, dec_rel))
    segments = segments.reshape(2, 1, chunk)
    first_jobs = [
        swap_job(enc_input),
        gather_job("fsdp", gain_stack, planes),
        gather_job("fsdp", rel_stack, planes),
        over_planes(qkv_part(enc_qkv)),
        over_planes(qkv_part(memory)),
        swap_job(dec_input),
    ]
    if parts == 1:
        first_jobs.append(block_job(segments))
    xe, gain_stack, rel_stack, w_eqkv, table, xd, *segs = ship(0, planes, first_jobs)
    xe, xd = joined(enc_input, xe), joined(dec_input, xd)
    if parts == 1:
        seg = segs[0].reshape(-1)
    else:
        segs = lax.all_gather(segments.reshape(2, chunk), CTX, axis=1, tiled=True)
        seg = lax.dynamic_index_in_dim(segs, seq, 0, keepdims=False)
    per, per_rel = enc_gain.shape[0], enc_rel.size
    g_enc, g_effn, g_dec, g_cross, g_dffn = [
        gain_stack[:, i].reshape(1, D) for i in range(len(gains))
    ]
    rels = [rel_stack[:, i].reshape(BUCKETS, HEADS) for i in range(2)]
    onehot = (buckets[:, None] == jnp.arange(BUCKETS, dtype=jnp.int32)[None, :]).astype(BF)

    def bias_vector(rel):
        own = lax.dynamic_slice_in_dim(rel, HQ * tp, HQ, 1).astype(BF)
        return lax.dot_general(
            own, onehot, (((0,), (1,)), ((), ())), preferred_element_type=F32
        ).reshape(HQ, 1, 2 * length)

    turned = planes == TP

    def proj_jobs(w):
        return [turn_job(w)] if turned else []

    def proj_of(got, w):
        if turned:
            return got.pop()
        full = lax.all_gather(w, "fsdp", axis=0, tiled=True)
        return lax.dynamic_slice_in_dim(full, QC * tp, QC, 0)

    ((en,), (dn,)), (w_eqkv, table, w_dqkv, w_effin), _ = stage(
        1,
        planes,
        [GatherNormed(xe, g_enc), GatherNormed(xd, g_dec)],
        jobs=[
            over_seq(w_eqkv),
            over_seq(table),
            over_planes(qkv_part(dec_qkv)),
            over_planes(ffin_part(enc_ffin)),
        ],
    )
    w_eqkv, table = matrix(w_eqkv), matrix(table)

    segq = lax.dynamic_index_in_dim(seg.reshape(2, parts, TP * chunk), part, 1, keepdims=False)
    segq = segq.reshape(-1, 1)
    segk = seg.reshape(1, length)
    ids = lax.dynamic_index_in_dim(prefix_rows, seq, 0, keepdims=False).reshape(-1)
    extra = -(-(docs * prefix) // 256) * 256
    ids = jnp.concatenate([ids, jnp.full((extra - docs * prefix,), -1, jnp.int32)])
    mem_doc = np.full((extra,), -1, np.int32)
    mem_doc[: docs * prefix] = np.arange(docs * prefix) // prefix
    segk_mem = jnp.concatenate([segk, jnp.asarray(mem_doc)[None]], axis=1)
    pick = (ids[:, None] == jnp.arange(table.shape[0], dtype=jnp.int32)[None, :]).astype(BF)
    mkv = mm(pick, table).astype(BF)

    def spread(kv):
        if parts == 1:
            return kv
        got = lax.all_gather(kv, "part", axis=0)
        return got.reshape(parts, 2, TP * chunk, -1).transpose(1, 0, 2, 3).reshape(length, -1)

    def collect(dkv):
        if parts == 1:
            return dkv
        split = dkv.reshape(2, parts, TP * chunk, -1).transpose(1, 0, 2, 3)
        split = split.reshape(parts * 2 * TP * chunk, -1)
        return lax.psum_scatter(split, "part", scatter_dimension=0, tiled=True).astype(BF)

    def self_kv(rows):
        return (rows, rows) if parts == 1 else (rows[:, :QC], spread(rows[:, QC:]))

    def joint_grad(got):
        if parts == 1:
            return got.pop(0)
        return jnp.concatenate([got.pop(0), collect(got.pop(0))], axis=1)

    def self_fill(x, w, segk_now, bvec, mem, causal):
        if parts == 1:
            rows = jax.ShapeDtypeStruct((x.shape[0], w.shape[1]), BF)
            return AttentionForward(
                parts, rows, rows, segq, segk_now, bvec, mem, causal, [(x, w)]
            ), None
        rows = self_kv(mm(x, w).astype(BF))
        return AttentionForward(parts, *rows, segq, segk_now, bvec, mem, causal), rows

    def self_made(got, rows):
        return got[0], got[1], rows or (got[2], got[2])

    e_fill, e_qkv = self_fill(en, w_eqkv, segk_mem, bias_vector(rels[0]), mkv, False)
    made, (w_dqkv, w_effout, *got) = attend(
        2,
        planes,
        e_fill,
        [over_seq(w_dqkv), over_planes(ffout_part(enc_ffout))]
        + proj_jobs(enc_proj),
    )
    e_att, e_p, e_qkv = self_made(made, e_qkv)
    w_eproj = proj_of(got, enc_proj)
    w_dqkv = matrix(w_dqkv)
    d_fill, d_qkv = self_fill(dn, w_dqkv, segk, bias_vector(rels[1]), None, True)
    ((e_mid, e_fn),), (w_effin, w_effout, w_cq, w_ckv, *got), made = stage(
        3,
        planes,
        [Stage([e_att], w_eproj, xe, gather="norm", gain=g_effn)],
        [
            over_seq(w_effin),
            over_seq(w_effout),
            over_planes(qkv_part(cross_query)),
            over_planes(qkv_part(cross_kv)),
        ]
        + proj_jobs(dec_proj),
        d_fill,
    )
    d_att, d_p, d_qkv = self_made(made, d_qkv)
    w_dproj = proj_of(got, dec_proj)
    w_effin, w_effout = matrix(w_effin), matrix(w_effout)
    ((d_mid, c_n), (e_low, e_gath, e_pre, e_act)), moved, _ = stage(
        4,
        planes,
        [
            Stage([d_att], w_dproj, xd, gather="norm", gain=g_cross),
            Stage(
                [e_fn, w_effin], w_effout, e_mid, maker=FeedForward, gather="low", dtype=BF
            ),
        ],
        [
            over_seq(w_cq),
            over_seq(w_ckv),
            over_planes(ffin_part(dec_ffin)),
            over_planes(ffout_part(dec_ffout)),
            swap_job(dec_cotan),
        ],
    )
    w_cq, w_ckv, w_dffin, w_dffout, xdc = moved
    w_cq, w_ckv = matrix(w_cq), matrix(w_ckv)
    xdc = joined(dec_cotan, xdc)
    products = None
    if parts == 1:
        c_q = jax.ShapeDtypeStruct((c_n.shape[0], QC), BF)
        c_kv = jax.ShapeDtypeStruct((e_gath.shape[0], 2 * QC), BF)
        products = [(c_n, w_cq), (e_gath, w_ckv)]
    else:
        c_q = mm(c_n, w_cq).astype(BF)
        c_kv = spread(mm(e_gath, w_ckv).astype(BF))
    c_fill = AttentionForward(parts, c_q, c_kv, segq, segk, None, None, False, products)
    (c_att, c_p, *made), (w_dffin, *got) = attend(
        5, planes, c_fill, [over_seq(w_dffin)] + proj_jobs(cross_proj)
    )
    w_cproj = proj_of(got, cross_proj)
    if parts == 1:
        c_q, c_kv = made
    ((d_cross, d_fn),), (w_dffout, came, xec), _ = stage(
        6,
        planes,
        [Stage([c_att], w_cproj, d_mid, gather="norm", gain=g_dffn)],
        [over_seq(w_dffout), swap_job(e_low), swap_job(enc_cotan)],
    )
    enc_output, xec = joined(e_low, came), joined(enc_cotan, xec)
    w_dffin, w_dffout = matrix(w_dffin), matrix(w_dffout)
    ((d_low, up_g, d_pre, d_act),), _, _ = stage(
        7,
        planes,
        [
            Stage(
                [d_fn, w_dffin],
                w_dffout,
                d_cross,
                maker=FeedForward,
                gather="given",
                given=xdc,
                dtype=BF,
            )
        ],
    )

    def pieces(g):
        if parts > 1:
            g = lax.psum(g, "part")
        return g.reshape(planes, 2, g.shape[0] // split, g.shape[1])

    to_ctx = [
        lambda g: gather_job("across", g),
        lambda g: gather_job("seq", g),
        lambda g: gather_job("core", g, 2, 2),
    ]
    to_ctx_seq = [
        lambda g: gather_job("seq", g),
        lambda g: gather_job("across", g, 2, 1),
        lambda g: gather_job("core", g, 2, 2),
    ]

    def chain(g, width, seq_first=False):
        steps = [lambda g: swap_job(g, 1, True), lambda g: deal_job("fsdp", g)]
        return Chain(pieces(g), steps + (to_ctx_seq if seq_first else to_ctx), width)

    def proj_chain(g):
        if not turned:
            return Chain(g, [], -1)
        steps = [lambda g: swap_job(g, "cols", True), lambda g: deal_job("fsdp", g), turn_job]
        return Chain(g.reshape(planes, -1, D), steps + to_ctx, -1)

    def steps_of(chains):
        return [c.steps[0](c.value) for c in chains if c.steps]

    def hurry(chains):
        for c in chains:
            if len(c.steps) == 3:
                c.steps = [spread_job]

    def settle(chains, got):
        got = list(got)
        for c in chains:
            if c.steps:
                c.value = got.pop(0)
                c.steps.pop(0)
        return got

    at = Stage(
        [up_g, d_pre, w_dffout],
        w_dffin,
        xdc,
        flip=True,
        maker=FeedForwardBack,
        back=(d_cross, g_dffn),
        gather="low",
    )
    ((up, up_rows, dg_dffn, _),), (came,), made = stage(
        8, planes, [at], [swap_job(d_low)], FeedForwardGrads(at, d_act, d_fn)
    )
    dec_output = joined(d_low, came)
    k_dffout, k_dffin = chain(made[0], 0, True), chain(made[1], hidden, True)
    c_fill = AttentionBackward(
        parts, c_p, c_q, c_kv, up_rows, w_cproj, c_att, False, None, [c_n, e_gath]
    )
    moving = [k_dffout]
    (c_dq, c_dkv, g_cproj, *made), got = attend(9, planes, c_fill, steps_of(moving))
    settle(moving, got)
    c_dkv = collect(c_dkv)
    if parts > 1:
        made = [mm_tn(c_n, c_dq).astype(BF), mm_tn(e_gath, c_dkv).astype(BF)]
    k_cproj, k_cq, k_ckv = proj_chain(g_cproj), chain(made[0], QC, True), chain(made[1], QC, True)
    moving = [k_dffout, k_cq, k_ckv, k_cproj]
    ((up, up_rows, dg_cross),), got, _ = stage(
        10,
        planes,
        [Stage([c_dq], w_cq, up, flip=True, back=(d_mid, g_cross), gather="low")],
        steps_of(moving),
    )
    settle(moving, got)

    def self_grads(made, x):
        grad = joint_grad(made)
        g_rows = made.pop() if parts == 1 else mm_tn(x, grad).astype(BF)
        return grad, chain(g_rows, QC, True), made

    d_fill = AttentionBackward(
        parts, d_p, *d_qkv, up_rows, w_dproj, d_att, True, None, [dn], causal=True
    )
    moving = [k_dffin, k_cq, k_ckv, k_cproj]
    ((e_up, e_up_rows),), got, made = stage(
        16,
        planes,
        [Stage([c_dkv], w_ckv, xec, flip=True, gather="low")],
        steps_of(moving),
        d_fill,
    )
    settle(moving, got)
    d_rows_grad, k_dqkv, (d_dbv, g_dproj) = self_grads(made, dn)
    k_dproj = proj_chain(g_dproj)
    k_effout = chain(mm_tn(e_act, e_up_rows).astype(BF), 0, True)
    moving = [k_dffin, k_dffout, k_cproj, k_dqkv, k_effout]
    ((e_up, e_up_rows, dg_effn, pre_grad),), got, _ = stage(
        12,
        planes,
        [
            Stage(
                [e_up_rows, e_pre, w_effout],
                w_effin,
                e_up,
                flip=True,
                maker=FeedForwardBack,
                back=(e_mid, g_effn),
                gather="low",
            )
        ],
        steps_of(moving),
    )
    settle(moving, got)
    k_effin = chain(mm_tn(e_fn, pre_grad).astype(BF), hidden)
    k_eproj = proj_chain(mm_tn(e_att, e_up_rows).astype(BF))
    e_fill = AttentionBackward(
        parts, e_p, *e_qkv, e_up_rows, w_eproj, e_att, True, mkv, [en], False
    )
    moving += [k_cq, k_ckv, k_dproj, k_effin, k_eproj]
    ((d_in, dg_dec, d_in_low),), got, made = stage(
        11,
        planes,
        [Stage([d_rows_grad], w_dqkv, up, flip=True, back=(xd, g_dec), low=True)],
        steps_of(moving),
        e_fill,
    )
    settle(moving, got)
    e_rows_grad, k_eqkv, (e_dbv, d_mkv) = self_grads(made, en)
    k_table = chain(mm_tn(pick, d_mkv).astype(BF), QC)
    moving += [k_eqkv, k_table]
    ((e_in, dg_enc, e_in_low),), got, _ = stage(
        13,
        planes,
        [Stage([e_rows_grad], w_eqkv, e_up, flip=True, back=(xe, g_enc), low=True)],
        steps_of(moving),
    )
    settle(moving, got)

    def rel_grads(*dbvs):
        own = lax.dot_general(
            onehot.astype(F32),
            jnp.concatenate(dbvs, axis=0).reshape(len(dbvs) * HQ, -1),
            (((0,), (1,)), ((), ())),
            precision=lax.Precision.HIGHEST,
            preferred_element_type=F32,
        )
        heads = jnp.arange(HEADS, dtype=jnp.int32)[None, :] // HQ == tp
        return [
            jnp.where(heads, jnp.tile(own[:, HQ * i : HQ * (i + 1)], (1, TP)), 0.0)
            for i in range(len(dbvs))
        ]

    tiny = [v.reshape(planes, -1) for v in (dg_enc, dg_effn, dg_dec, dg_cross, dg_dffn)]
    tiny += [v.reshape(planes, -1) for v in rel_grads(e_dbv, d_dbv)]
    tiny = jnp.concatenate(tiny, axis=1).reshape(-1, 128)
    if parts > 1:
        tiny = lax.psum(tiny, "part")
    hurry(moving)
    tiny, came, d_came, *got = ship(
        14,
        planes,
        [total_job("fsdp", tiny, planes), swap_job(e_in_low), swap_job(d_in_low)]
        + steps_of(moving),
    )
    enc_ingrad, dec_ingrad = joined(e_in, came), joined(d_in, d_came)
    settle(moving, got)
    hurry(moving)
    tiny, *got = ship(15, planes, [spread_job(tiny, True)] + steps_of(moving))
    settle(moving, got)

    def proj_rows(k):
        full = lax.dynamic_update_slice_in_dim(jnp.zeros((D, D), BF), k.value, QC * tp, 0)
        full = lax.psum_scatter(full, "fsdp", scatter_dimension=0, tiled=True)
        return lax.psum(full.astype(F32), CTX)

    ready = [k_dffin, k_dffout, k_effin, k_effout, k_cq, k_ckv, k_dqkv, k_eqkv, k_table]
    k_projs = [k_eproj, k_dproj, k_cproj]
    if turned:
        ready += k_projs
    results = laid_out([k.value for k in ready], [k.width for k in ready])
    o_eproj, o_dproj, o_cproj = results[9:] if turned else [proj_rows(k) for k in k_projs]
    o_dffin, o_dffout, o_effin, o_effout, o_cq, o_ckv, o_dqkv, o_eqkv, o_table = results[:9]
    tiny = lax.dynamic_index_in_dim(tiny.reshape(planes, -1), plane, 0, keepdims=False)
    o_gains = [tiny[per * i : per * (i + 1)] for i in range(5)]
    o_rels = [
        tiny[5 * per + per_rel * i : 5 * per + per_rel * (i + 1)].reshape(-1, HEADS)
        for i in range(2)
    ]
    return (
        enc_output,
        dec_output,
        enc_ingrad,
        dec_ingrad,
        o_table,
        o_gains[0],
        o_eqkv,
        o_rels[0],
        o_eproj,
        o_gains[1],
        o_effin,
        o_effout,
        o_gains[2],
        o_dqkv,
        o_rels[1],
        o_dproj,
        o_gains[3],
        o_cq,
        o_ckv,
        o_cproj,
        o_gains[4],
        o_dffin,
        o_dffout,
    )


def solution(mesh):
    ctx, planes = mesh.shape["ctx"], mesh.shape["fsdp"]
    parts = ctx // (2 * TP)
    inner = Mesh(np.asarray(mesh.devices).reshape(2, parts, TP, planes), ALL)
    rows3 = P("fsdp", CTX, None)
    mat, vec = P("fsdp", None), P("fsdp")
    args = (
        (rows3, rows3, P("fsdp", CTX), P("fsdp", None, None), P(), mat)
        + (vec, mat, mat, mat, vec, mat, mat)
        + (vec, mat, mat, mat)
        + (vec, mat, mat, mat)
        + (vec, mat, mat)
        + (rows3, rows3)
    )
    outs = (
        (rows3, rows3, rows3, rows3, mat)
        + (vec, mat, mat, mat, vec, mat, mat)
        + (vec, mat, mat, mat)
        + (vec, mat, mat, mat)
        + (vec, mat, mat)
    )
    return jax.shard_map(
        functools.partial(per_device, parts, planes),
        mesh=inner,
        in_specs=args,
        out_specs=outs,
        check_vma=False,
    )
```

```python
import collections
import functools

import jax
import jax.numpy as jnp
import numpy as np
from jax import lax
from jax.experimental import pallas as pl
from jax.experimental.pallas import tpu as pltpu
from jax.sharding import Mesh
from jax.sharding import PartitionSpec as P

D = 768
HEADS = 12
DH = 64
BUCKETS = 32
EPS = 1e-06
MASKED = -1e30
TP = 4
HQ = HEADS // TP
QC = HQ * DH
BF = jnp.bfloat16
F32 = jnp.float32
MESH_ID = pl.DeviceIdType.MESH
MB = 1024 * 1024
VMEM_LIMIT = 60 * MB
SHARE = (0.25, 0.34, 0.75)


def mm(a, b):
    return jnp.dot(a, b, preferred_element_type=F32)


def mm_tn(a, b):
    return lax.dot_general(a, b, (((0,), (0,)), ((), ())), preferred_element_type=F32)


def mm_nt(a, b):
    return lax.dot_general(a, b, (((1,), (1,)), ((), ())), preferred_element_type=F32)


def gelu(v):
    return jax.nn.gelu(v, approximate=True)


def gelu_back(pre, grad):
    return jax.vjp(gelu, pre)[1](grad)[0]


def group_ids():
    me = lax.axis_index("tp")
    core = me + 1 - 2 * lax.rem(me, 2)
    across = lax.rem(me + 2, TP)
    far = lax.rem(core + 2, TP)
    return me, core, across, far


def send(src, dst, send_sem, recv_sem, peer):
    return pltpu.make_async_remote_copy(
        src_ref=src,
        dst_ref=dst,
        send_sem=send_sem,
        recv_sem=recv_sem,
        device_id={"tp": peer},
        device_id_type=MESH_ID,
    )


def normed(values, gains):
    return values * lax.rsqrt(jnp.mean(values * values, axis=-1, keepdims=True) + EPS) * gains


class Gatherer:
    def __init__(self, buf, stage, sems, chunk, ids):
        self.buf, self.stage, self.sems, self.chunk, self.ids = buf, stage, sems, chunk, ids
        self.sends, self.own = [], []

    def rows(self, j, owner):
        return self.buf.at[pl.ds(pl.multiple_of((TP * j + owner) * self.chunk, self.chunk), self.chunk)]

    def put(self, j, value):
        me, core, across, far = self.ids
        mine = self.stage.at[j]
        mine[...] = value
        x_copy = send(mine, self.rows(j, me), self.sems.at[0, j], self.sems.at[1, j], across)
        x_copy.start()
        c_copy = send(mine, self.rows(j, me), self.sems.at[2, j], self.sems.at[3, j], core)
        c_copy.start()
        self.sends += [x_copy, c_copy]
        own = pltpu.make_async_copy(mine, self.rows(j, me), self.sems.at[6, j])
        own.start()
        self.own.append(own)

    def forward(self, j):
        me, core, across, far = self.ids
        theirs = self.rows(j, across)
        send(theirs, theirs, self.sems.at[0, j], self.sems.at[1, j], across).wait_recv()
        f_copy = send(theirs, theirs, self.sems.at[4, j], self.sems.at[5, j], core)
        f_copy.start()
        self.sends.append(f_copy)

    def finish(self):
        me, core, across, far = self.ids
        for j in range(2):
            a = self.rows(j, core)
            send(a, a, self.sems.at[2, j], self.sems.at[3, j], core).wait_recv()
            b = self.rows(j, far)
            send(b, b, self.sems.at[4, j], self.sems.at[5, j], core).wait_recv()
        for copy in self.sends:
            copy.wait_send()
        for copy in self.own:
            copy.wait()


Job = collections.namedtuple("Job", ["axis", "src_axis", "dst_axis", "local", "src", "shape", "finish"])


def gather_job(axis, src, size=2, at=0):
    shape = src.shape[:at] + (size,) + src.shape[at:]
    return Job(axis, None, at, True, src, shape, None)


def total_job(axis, src, size=2):
    return gather_job(axis, src, size)._replace(finish="sum")


def deal_job(axis, src):
    return Job(axis, 0, 0, True, src, src.shape, "sum")


def swap_job(src, at=0, add=False):
    if at == "cols":
        shape = src.shape[:-1] + (src.shape[-1] // 2,)
    else:
        shape = src.shape[:at] + src.shape[at + 1 :]
    return Job("seq", at, None, add, src, shape, "add" if add else None)


def turn_job(src):
    return Job("turn", None, None, True, src, src.shape, None)


def block_job(src):
    return Job("ctx", 0, 0, True, src, (2 * TP,) + src.shape[1:], None)


def spread_job(src, add=False):
    return Job("all", None, None, True, src, (2, 2, 2) + src.shape, "sum3" if add else None)


def result_of(job):
    skip = {"sum": 1, "sum3": 3}.get(job.finish, 0)
    return job.shape[skip:], job.src.dtype


def entry(ref, axis, index):
    if axis == "cols":
        half = ref.shape[-1] // 2
        return ref.at[:, :, pl.ds(pl.multiple_of(index * half, half), half)]
    return ref if axis is None else ref.at[(slice(None),) * axis + (index,)]


class Shipper:
    def __init__(self, jobs, planes, srcs, outs, scratch, sems):
        self.jobs, self.planes, self.srcs, self.outs, self.sems = jobs, planes, srcs, outs, sems
        self.tp, self.seq, self.plane = (lax.axis_index(n) for n in ("tp", "seq", "fsdp"))
        self.dsts, self.bounce, self.made = [], [], []
        for job, out in zip(jobs, outs):
            if job.finish:
                self.dsts.append(scratch.pop(0))
                self.bounce.append(scratch.pop(0) if job.finish == "add" else None)
                self.made.append(scratch.pop(0) if job.finish != "add" else None)
            else:
                self.dsts.append(out)
                self.bounce.append(scratch.pop(0) if job.local else None)
                self.made.append(None)

    @staticmethod
    def scratch(jobs):
        shapes = []
        for job in jobs:
            dtype = job.src.dtype
            if job.finish:
                shapes.append(pltpu.VMEM(job.shape, dtype))
                if job.finish == "add":
                    shapes.append(pltpu.VMEM(job.shape, dtype))
                else:
                    shapes.append(pltpu.VMEM(*result_of(job)))
            elif job.axis == "all":
                shapes.append(pltpu.VMEM(job.src.shape, dtype))
            elif job.local:
                drop = job.dst_axis
                own = job.shape if drop is None else job.shape[:drop] + job.shape[drop + 1 :]
                shapes.append(pltpu.VMEM(own, dtype))
        return shapes

    @staticmethod
    def count(jobs, planes):
        return sum(2 * Shipper.n_peers(job, planes) + 2 for job in jobs)

    @staticmethod
    def n_peers(job, planes):
        return {"fsdp": planes - 1, "ctx": 2 * TP - 1, "all": 2 * TP - 1}.get(job.axis, 1)

    def coord(self, axis):
        half = self.tp // 2
        return {
            "fsdp": self.plane,
            "seq": self.seq,
            "across": half,
            "core": self.tp - 2 * half,
            "ctx": TP * self.seq + self.tp,
            "turn": None,
        }[axis]

    def peers(self, axis):
        if axis == "fsdp":
            n, z = self.planes, self.plane
            for k in range(1, n):
                to = lax.rem(z + k, n)
                yield to, {"fsdp": to}, lax.rem(z + (n - k), n)
        elif axis == "ctx":
            for k in range(1, 2 * TP):
                to = lax.rem(self.seq + k // TP, 2)
                to_tp = lax.rem(self.tp + k % TP, TP)
                from_seq = lax.rem(self.seq + (2 - k // TP), 2)
                from_tp = lax.rem(self.tp + (TP - k % TP), TP)
                yield to, {"seq": to, "tp": to_tp}, TP * from_seq + from_tp
        elif axis == "seq":
            yield 1 - self.seq, {"seq": 1 - self.seq}, 1 - self.seq
        elif axis == "turn":
            yield None, {"fsdp": self.tp, "tp": self.plane}, None
        else:
            to = lax.rem(self.tp + 2, TP) if axis == "across" else self.tp + 1 - 2 * lax.rem(self.tp, 2)
            other = 1 - self.coord(axis)
            yield other, {"tp": to}, other

    def signal(self, always=("core", "across")):
        wanted = {job.axis for job in self.jobs}
        if "all" in wanted:
            wanted = (wanted - {"all"}) | {"seq", "across", "core"}
        axes = list(always) + sorted(wanted - set(always))
        barrier = pltpu.get_barrier_semaphore()
        self.expected, self.turns = 0, "turn" in axes
        for axis in axes:
            for _, device, _ in self.peers(axis):
                if axis == "turn":

                    @pl.when(self.plane != self.tp)
                    def _():
                        pl.semaphore_signal(
                            barrier, inc=1, device_id=device, device_id_type=MESH_ID
                        )

                    continue
                pl.semaphore_signal(barrier, inc=1, device_id=device, device_id_type=MESH_ID)
                self.expected += 1

    def met(self):
        barrier = pltpu.get_barrier_semaphore()
        if self.turns:
            moves = self.plane != self.tp

            @pl.when(moves)
            def _():
                pl.semaphore_wait(barrier, self.expected + 1)

            @pl.when(jnp.logical_not(moves))
            def _():
                pl.semaphore_wait(barrier, self.expected)
        else:
            pl.semaphore_wait(barrier, self.expected)

    def greet(self, always=("core", "across")):
        self.signal(always)
        self.met()

    def each(self, act_remote, act_local):
        base = 0
        for n, (job, src, dst) in enumerate(zip(self.jobs, self.srcs, self.dsts)):
            if job.axis == "all":
                base += 2 * self.n_peers(job, self.planes) + 2
                continue
            mine = self.coord(job.axis)
            peers = list(self.peers(job.axis))
            for i, (to, device, source) in enumerate(peers):
                sems = (self.sems.at[base + 2 * i], self.sems.at[base + 2 * i + 1])

                def copy_into(slot, to=to, device=device, sems=sems, src=src, dst=dst, job=job):
                    return pltpu.make_async_remote_copy(
                        src_ref=entry(src, job.src_axis, to),
                        dst_ref=entry(dst, job.dst_axis, slot),
                        send_sem=sems[0],
                        recv_sem=sems[1],
                        device_id=device,
                        device_id_type=MESH_ID,
                    )

                def remote(copy_into=copy_into, source=source, mine=mine):
                    act_remote(copy_into, mine, source)

                if job.axis == "turn":
                    pl.when(self.plane != self.tp)(remote)
                else:
                    remote()
            if job.local:
                own = self.seq if job.axis == "ctx" else mine

                def local(n=n, job=job, src=src, dst=dst, own=own, mine=mine, sem=base + 2 * len(peers)):
                    here, there = entry(src, job.src_axis, own), entry(dst, job.dst_axis, mine)
                    bounce = self.bounce[n]
                    if bounce is None:
                        act_local([(here, there)], self.sems.at[sem])
                    elif job.finish == "add":
                        act_local([(here, bounce)], self.sems.at[sem])
                    else:
                        act_local([(here, bounce), (bounce, there)], self.sems.at[sem])

                if job.axis == "turn":
                    pl.when(self.plane == self.tp)(local)
                else:
                    local()
            base += 2 * len(peers) + 2
        return base

    def spreads(self):
        s, x, c = self.coord("seq"), self.coord("across"), self.coord("core")
        seq, across, core = (next(self.peers(axis))[1] for axis in ("seq", "across", "core"))
        moves = [
            ((s, x, c), across, (s, 1 - x, c)),
            ((s, x, c), seq, (1 - s, x, c)),
            ((s, x, c), core, (s, x, 1 - c)),
            ((s, 1 - x, c), seq, (1 - s, 1 - x, c)),
            ((s, 1 - x, c), core, (s, 1 - x, 1 - c)),
            ((1 - s, x, c), core, (1 - s, x, 1 - c)),
            ((1 - s, 1 - x, c), core, (1 - s, 1 - x, 1 - c)),
        ]
        base = 0
        for job, src, dst, bounce in zip(self.jobs, self.srcs, self.dsts, self.bounce):
            if job.axis == "all":

                def copy(k, arrives=False, src=src, dst=dst, base=base):
                    what, device, other = moves[k]
                    return pltpu.make_async_remote_copy(
                        src_ref=src if k < 3 else dst.at[what],
                        dst_ref=dst.at[other if arrives else what],
                        send_sem=self.sems.at[base + 2 * k],
                        recv_sem=self.sems.at[base + 2 * k + 1],
                        device_id=device,
                        device_id_type=MESH_ID,
                    )

                own = dst.at[s, x, c]
                legs = [(src, own)] if bounce is None else [(src, bounce), (bounce, own)]
                legs = [
                    pltpu.make_async_copy(*leg, self.sems.at[base + 14 + n])
                    for n, leg in enumerate(legs)
                ]
                yield copy, legs
            base += 2 * self.n_peers(job, self.planes) + 2

    def start_spreads(self):
        for copy, legs in self.spreads():
            for k in range(3):
                copy(k).start()
            legs[0].start()

    def finish_spreads(self):
        jobs = list(self.spreads())
        for copy, legs in jobs:
            if len(legs) > 1:
                legs[0].wait()
                legs[1].start()
        for first, then in ((0, (3, 4)), (1, (5,)), (3, (6,))):
            for copy, legs in jobs:
                copy(first, True).wait_recv()
                for k in then:
                    copy(k).start()
        for copy, legs in jobs:
            for k in (2, 4, 5, 6):
                copy(k, True).wait_recv()
            for k in range(7):
                copy(k).wait_send()
            legs[-1].wait()

    def start(self):
        if any(job.axis == "all" for job in self.jobs):
            self.start_spreads()
        self.each(
            lambda copy_into, mine, source: copy_into(mine).start(),
            lambda legs, sem: pltpu.make_async_copy(*legs[0], sem).start(),
        )

    def finish(self):
        def turn_round(legs, sem):
            if len(legs) > 1:
                pltpu.make_async_copy(*legs[0], sem).wait()
                pltpu.make_async_copy(*legs[1], sem).start()

        def remote(copy_into, mine, source):
            copy_into(source).wait_recv()
            copy_into(mine).wait_send()

        if any(job.axis == "all" for job in self.jobs):
            self.finish_spreads()
        self.each(lambda *_: None, turn_round)
        self.each(remote, lambda legs, sem: pltpu.make_async_copy(*legs[-1], sem).wait())
        stores, base = [], 0
        for job, dst, bounce, made, out in zip(
            self.jobs, self.dsts, self.bounce, self.made, self.outs
        ):
            base += 2 * self.n_peers(job, self.planes) + 2
            if not job.finish:
                continue
            if job.finish == "add":
                made = bounce

                @pl.loop(0, dst.shape[0])
                def _(i):
                    bounce[i] = (bounce[i].astype(F32) + dst[i].astype(F32)).astype(bounce.dtype)

            else:
                pieces = [dst.at[i] for i in range(dst.shape[0])]
                if job.finish == "sum3":
                    pieces = [dst.at[i, j, k] for i in range(2) for j in range(2) for k in range(2)]
                total = pieces[0][...].astype(F32)
                for piece in pieces[1:]:
                    total = total + piece[...].astype(F32)
                made[...] = total.astype(made.dtype)
            store = pltpu.make_async_copy(made, out, self.sems.at[base - 1])
            store.start()
            stores.append(store)
        for store in stores:
            store.wait()


def lay_out(src, dst, width):
    seqs, halves, cores, rows, cols = src.shape
    if width < 0:
        for i in range(seqs):
            for q in range(TP):
                block = slice(i * cols, (i + 1) * cols)
                dst[q * rows : (q + 1) * rows, block] = src[i, q // 2, q % 2].astype(F32)
        return

    @pl.loop(0, seqs)
    def _(i):
        if not width:
            for q in range(TP):
                at = pl.multiple_of((q * seqs + i) * rows, rows)
                dst[pl.ds(at, rows)] = src[i, q // 2, q % 2].astype(F32)
        else:
            at = pl.multiple_of(i * rows, rows)
            for n in range(cols // width):
                span = slice(n * width, (n + 1) * width)
                parts = [src[i, q // 2, q % 2, :, span].astype(F32) for q in range(TP)]
                block = slice(n * width * TP, (n + 1) * width * TP)
                dst[pl.ds(at, rows), block] = jnp.concatenate(parts, axis=1)


def laid_out(pieces, widths):
    shapes = []
    for p, width in zip(pieces, widths):
        seqs, halves, cores, rows, cols = p.shape
        if width < 0:
            shapes.append((halves * cores * rows, seqs * cols))
        elif width:
            shapes.append((seqs * rows, halves * cores * cols))
        else:
            shapes.append((seqs * halves * cores * rows, cols))
    n = len(pieces)

    def body(*refs):
        srcs, outs, got, made, sems = refs[:n], refs[n : 2 * n], refs[2 * n : 3 * n], refs[3 * n : 4 * n], refs[4 * n]
        loads = [pltpu.make_async_copy(srcs[i], got[i], sems.at[0, i]) for i in range(n)]
        stores = [pltpu.make_async_copy(made[i], outs[i], sems.at[1, i]) for i in range(n)]
        for load in loads:
            load.start()
        for i in range(n):
            loads[i].wait()
            lay_out(got[i], made[i], widths[i])
            stores[i].start()
        for store in stores:
            store.wait()

    return pl.pallas_call(
        body,
        out_shape=tuple(jax.ShapeDtypeStruct(shape, F32) for shape in shapes),
        in_specs=[HBM_SPEC] * n,
        out_specs=(HBM_SPEC,) * n,
        scratch_shapes=[pltpu.VMEM(p.shape, p.dtype) for p in pieces]
        + [pltpu.VMEM(shape, F32) for shape in shapes]
        + [pltpu.SemaphoreType.DMA((2, n))],
        compiler_params=pltpu.CompilerParams(vmem_limit_bytes=VMEM_LIMIT),
        name="lay_out",
    )(*pieces)


HBM_SPEC = pl.BlockSpec(memory_space=pltpu.HBM)


class Loaded:
    def __init__(self, src, dst, sem, start=True):
        self.copy, self.ref, self.waited = pltpu.make_async_copy(src, dst, sem), dst, False
        if start:
            self.copy.start()

    def get(self):
        if not self.waited:
            self.copy.wait()
            self.waited = True
        return self.ref


class LoadedRows:
    def __init__(self, src, dst, sems, chunk):
        self.src, self.ref, self.sems, self.chunk = src, dst, sems, chunk

    def copies(self, owner, slot):
        for j in range(2):
            at = pl.multiple_of((TP * j + owner) * self.chunk, self.chunk)
            rows = pl.ds(at, self.chunk)
            yield pltpu.make_async_copy(
                self.src.at[rows], self.ref.at[rows], self.sems.at[2 * slot + j]
            )

    def start(self, owners):
        for slot, owner in enumerate(owners):
            for copy in self.copies(owner, slot):
                copy.start()

    def wait(self, owner, slot):
        for copy in self.copies(owner, slot):
            copy.wait()


def call_with_jobs(
    kernel, number, planes, jobs, operands, outs, scratch, name, cost, filler=None, by_rows=()
):
    filler = filler or Idle()
    jobs = list(jobs)
    n_in, n_out, n_job = len(operands), len(outs), len(jobs)
    n_load, n_raw, n_fill = len(filler.loads), len(filler.raws), len(filler.outs)
    loads, raws = list(filler.loads), list(filler.raws)
    n_sems = max(Shipper.count(jobs, planes), 1)
    plain = [job._replace(src=jax.ShapeDtypeStruct(job.src.shape, job.src.dtype)) for job in jobs]
    job_scratch = Shipper.scratch(jobs)
    n_scratch = len(filler.scratch)

    def body(*refs):
        refs = list(refs)

        def take(n):
            out = refs[:n]
            del refs[:n]
            return out

        ins, srcs, fills, raw = take(n_in), take(n_job), take(n_load), take(n_raw)
        results, dsts, fill_outs = take(n_out), take(n_job), take(n_fill)
        sems, in_sems, row_sems = take(3)
        loaded = []
        for i, src in enumerate(ins):
            if i in by_rows:
                rows = row_sems.at[by_rows.index(i)]
                loaded.append(LoadedRows(src, refs.pop(0), rows, src.shape[0] // (2 * TP)))
            else:
                loaded.append(Loaded(src, refs.pop(0), in_sems.at[i]))
        fill_loads = [
            Loaded(src, refs.pop(0), in_sems.at[n_in + i], False) for i, src in enumerate(fills)
        ]
        shipper = Shipper(plain, planes, srcs, dsts, take(len(job_scratch)), sems)
        begin = functools.partial(filler.begin, fill_loads, raw, fill_outs, take(n_scratch))
        kernel(shipper, loaded, list(results), refs, Running(filler, begin, fill_loads))

    results = [result_of(job) for job in jobs]
    got = pl.pallas_call(
        body,
        out_shape=tuple(outs)
        + tuple(jax.ShapeDtypeStruct(*r) for r in results)
        + tuple(filler.outs),
        in_specs=[HBM_SPEC] * (n_in + n_job + n_load + n_raw),
        out_specs=(HBM_SPEC,) * (n_out + n_job + n_fill),
        scratch_shapes=[
            pltpu.SemaphoreType.DMA((n_sems,)),
            pltpu.SemaphoreType.DMA((max(n_in + n_load, 1),)),
            pltpu.SemaphoreType.DMA((max(len(by_rows), 1), 2 * TP)),
        ]
        + [pltpu.VMEM(v.shape, v.dtype) for v in operands + loads]
        + job_scratch
        + list(filler.scratch)
        + scratch,
        compiler_params=pltpu.CompilerParams(
            collective_id=number, has_side_effects=True, vmem_limit_bytes=VMEM_LIMIT
        ),
        cost_estimate=pl.CostEstimate(flops=cost, bytes_accessed=8 * MB, transcendentals=0),
        name=name,
    )(*operands, *[job.src for job in jobs], *loads, *raws)
    return got[:n_out], list(got[n_out : n_out + n_job]), list(got[n_out + n_job :])


class Running:
    def __init__(self, filler, begin, loads):
        self.begin, self.run, self.end, self.loads = begin, filler.run, filler.end, loads
        self.n_steps, self.done = filler.n_steps, 0

    def prefetch(self):
        for load in self.loads:
            load.copy.start()

    def advance(self, share):
        high = int(round(share * self.n_steps))
        if high > self.done:
            self.run(self.done, high)
            self.done = high


def ship(number, planes, jobs):
    def kernel(shipper, ins, outs, scratch, filler):
        shipper.greet(())
        shipper.start()
        shipper.finish()

    return call_with_jobs(kernel, number, planes, jobs, [], [], [], "ship", 0)[1]


class GatherNormed:
    by_rows = ()

    def __init__(self, x, gain):
        self.chunk = x.shape[1]
        self.operands, self.cost = [x, gain], 10**6
        self.outs = [jax.ShapeDtypeStruct((2 * TP * self.chunk, D), BF)]
        self.scratch = [pltpu.VMEM((2, self.chunk, D), BF), pltpu.SemaphoreType.DMA((7, 2))]

    def bind(self, ins, outs, scratch):
        self.x, self.gain = ins
        self.g = Gatherer(outs[0], scratch[0], scratch[1], self.chunk, group_ids())

    def load(self):
        pass

    def first(self, met):
        x_ref, gain_ref = self.x.get(), self.gain.get()
        met()
        for j in range(2):
            self.g.put(j, normed(x_ref[j].astype(F32), gain_ref[...]).astype(BF))

    def second(self, between):
        between()

    def third(self):
        for j in range(2):
            self.g.forward(j)

    def last(self):
        self.g.finish()


GELU_C = float(np.sqrt(2.0 / np.pi))


def gelu_parts(v):
    tanh = jnp.tanh(GELU_C * (v + 0.044715 * v * v * v))
    return tanh, 0.5 * (1.0 + tanh)


def gelu_slope(v):
    tanh, half = gelu_parts(v)
    return half + 0.5 * v * (1.0 - tanh * tanh) * (GELU_C * (1.0 + 3 * 0.044715 * v * v))


class Rows:
    n_operands, n_outs, n_scratch = 1, 0, 0

    def __init__(self, ins, outs, scratch, chunk):
        self.rows, self.chunk = ins.pop(0), chunk
        self.by_rows = [self.rows]

    def prepare(self):
        self.ref = self.rows.ref

    def make(self, pair, slot):
        pass

    def finish(self):
        pass

    def pick(self, ref, pair):
        return jnp.concatenate([ref[rows] for rows in pair], axis=0)


class MadeRows(Rows):
    def write(self, index, ref, out, slot, pair):
        for j, rows in enumerate(pair):
            copy = pltpu.make_async_copy(ref.at[rows], out.at[rows], self.sems.at[index, 2 * slot + j])
            copy.start()
            self.copies.append(copy)

    def finish(self):
        for copy in self.copies:
            copy.wait()

    def tiles(self, body):
        @pl.loop(0, self.ref.shape[1] // 256)
        def _(n):
            body(pl.ds(pl.multiple_of(n * 256, 256), 256))


class FeedForward(MadeRows):
    n_operands, n_outs, n_scratch = 2, 2, 3

    def __init__(self, ins, outs, scratch, chunk):
        self.rows, self.w_in, self.chunk, self.copies = ins.pop(0), ins.pop(0), chunk, []
        self.by_rows = [self.rows]
        self.pre_out, self.act_out = outs.pop(0), outs.pop(0)
        self.pre, self.ref, self.sems = scratch.pop(0), scratch.pop(0), scratch.pop(0)

    @staticmethod
    def extras(n_rows, width):
        shapes = [((n_rows, width), F32), ((n_rows, width), BF)]
        scratch = [pltpu.VMEM(*v) for v in shapes] + [pltpu.SemaphoreType.DMA((2, 2 * TP))]
        return [jax.ShapeDtypeStruct(*v) for v in shapes], scratch

    def prepare(self):
        self.w_in = self.w_in.get()

    def make(self, pair, slot):
        x = self.pick(self.rows.ref, pair)

        def tile(cols):
            v = mm(x, self.w_in[:, cols])
            act = (v * gelu_parts(v)[1]).astype(BF)
            for j, rows in enumerate(pair):
                self.pre[rows, cols] = v[j * self.chunk : (j + 1) * self.chunk]
                self.ref[rows, cols] = act[j * self.chunk : (j + 1) * self.chunk]

        self.tiles(tile)
        self.write(0, self.pre, self.pre_out, slot, pair)
        self.write(1, self.ref, self.act_out, slot, pair)


class FeedForwardBack(MadeRows):
    n_operands, n_outs, n_scratch = 3, 1, 2

    def __init__(self, ins, outs, scratch, chunk):
        self.rows, self.pre, self.w_out = ins.pop(0), ins.pop(0), ins.pop(0)
        self.chunk, self.copies = chunk, []
        self.by_rows = [self.rows, self.pre]
        self.out, self.ref, self.sems = outs.pop(0), scratch.pop(0), scratch.pop(0)

    @staticmethod
    def extras(n_rows, width):
        shape = ((n_rows, width), BF)
        scratch = [pltpu.VMEM(*shape), pltpu.SemaphoreType.DMA((1, 2 * TP))]
        return [jax.ShapeDtypeStruct(*shape)], scratch

    def prepare(self):
        self.w_out = self.w_out.get()

    def make(self, pair, slot):
        x = self.pick(self.rows.ref, pair)

        def tile(cols):
            grad = mm_nt(x, self.w_out[cols, :])
            for j, rows in enumerate(pair):
                back = gelu_slope(self.pre.ref[rows, cols]) * grad[j * self.chunk : (j + 1) * self.chunk]
                self.ref[rows, cols] = back.astype(BF)

        self.tiles(tile)
        self.write(0, self.ref, self.out, slot, pair)


class Stage:
    def __init__(
        self,
        left,
        weight,
        resid,
        *,
        flip=False,
        maker=Rows,
        back=None,
        gather=None,
        gain=None,
        given=None,
        dtype=F32,
        low=False,
    ):
        self.maker, self.flip, self.back, self.gather, self.low = maker, flip, bool(back), gather, low
        self.chunk = chunk = resid.shape[1]
        self.operands = list(left) + [weight, resid]
        self.cost = 4 * left[0].shape[0] * D * D
        self.by_rows = {Rows: (0,), FeedForward: (0,), FeedForwardBack: (0, 1)}[maker]
        if back:
            self.operands += [back[1], back[0]]
        elif gather == "norm":
            self.operands.append(gain)
        if gather == "given":
            self.operands.append(given)
        self.outs = [jax.ShapeDtypeStruct((2, chunk, D), dtype)]
        if gather:
            self.outs.append(jax.ShapeDtypeStruct((2 * TP * chunk, D), BF))
        if back:
            self.outs.append(jax.ShapeDtypeStruct((1, D), F32))
        half = pltpu.VMEM((2, chunk, D), BF)
        full = pltpu.VMEM((2, chunk, D), F32)
        self.scratch = [half] * 6 + [full] * 2
        self.scratch += [pltpu.VMEM((2, chunk, D), dtype), pltpu.SemaphoreType.DMA((13,))]
        if gather:
            self.scratch += [half, pltpu.SemaphoreType.DMA((7, 2))]
        if back:
            self.scratch.append(pltpu.VMEM((1, D), F32))
        if low:
            self.outs.append(jax.ShapeDtypeStruct((2, chunk, D), BF))
            self.scratch.append(half)
        if maker is not Rows:
            width = weight.shape[1] if flip else weight.shape[0]
            more, more_scratch = maker.extras(2 * TP * chunk, width)
            self.outs += more
            self.scratch += more_scratch

    def bind(self, ins, outs, scratch):
        maker = self.maker
        made_outs = [outs.pop() for _ in range(maker.n_outs)][::-1]
        made_scratch = [scratch.pop() for _ in range(maker.n_scratch)][::-1]
        self.left = maker(ins, made_outs, made_scratch, self.chunk)
        self.w_in, self.resid_in = ins.pop(0), ins.pop(0)
        self.gain_in = ins.pop(0) if (self.back or self.gather == "norm") else None
        self.x_in = ins.pop(0) if self.back else None
        self.given_in = ins.pop(0) if self.gather == "given" else None
        self.y_out = outs.pop(0)
        gath_ref = outs.pop(0) if self.gather else None
        self.dgain_out = outs.pop(0) if self.back else None
        self.low_out = outs.pop(0) if self.low else None
        self.s_far, self.r_far, self.s_x, self.r_x, self.s_core, self.r_core = scratch[:6]
        self.keep, self.own, self.y_ref, self.sems = scratch[6:10]
        scratch = scratch[10:]
        self.ids = group_ids()
        self.g = None
        if self.gather:
            self.g = Gatherer(gath_ref, scratch.pop(0), scratch.pop(0), self.chunk, self.ids)
        self.dgain_ref = scratch.pop(0) if self.back else None
        self.low_ref = scratch.pop(0) if self.low else None
        self.slots, self.stores = [0, 1, 2, 3], []

    def load(self):
        me, core, across, far = self.ids
        for rows in self.left.by_rows:
            rows.start((far, across, core, me))

    def partial(self, owner, ref):
        slot, chunk, left = self.slots.pop(0), self.chunk, self.left
        for rows in left.by_rows:
            rows.wait(owner, slot)
        pair = [
            pl.ds(pl.multiple_of((TP * j + owner) * chunk, chunk), chunk) for j in range(2)
        ]
        left.make(pair, slot)
        a = left.pick(left.ref, pair)

        @pl.loop(0, D // 256)
        def _(n):
            cols = pl.ds(pl.multiple_of(n * 256, 256), 256)
            total = mm_nt(a, self.w_ref[cols, :]) if self.flip else mm(a, self.w_ref[:, cols])
            for j in range(2):
                ref[j, :, cols] = total[j * chunk : (j + 1) * chunk].astype(ref.dtype)

    def first(self, met):
        me, core, across, far = self.ids
        sems = self.sems
        self.left.prepare()
        self.w_ref = self.w_in.get()
        self.partial(far, self.s_far)
        met()
        self.c_far = send(self.s_far, self.r_far, sems.at[0], sems.at[1], core)
        self.c_far.start()
        if self.gather == "given":
            given_ref = self.given_in.get()
            for j in range(2):
                self.g.put(j, given_ref[j])
        self.partial(across, self.keep)
        self.c_far.wait_recv()
        self.c_x = []
        for j in range(2):
            self.s_x[j] = (self.keep[j] + self.r_far[j].astype(F32)).astype(BF)
            copy = send(self.s_x.at[j], self.r_x.at[j], sems.at[2 + j], sems.at[4 + j], across)
            copy.start()
            self.c_x.append(copy)
        self.partial(core, self.s_core)
        self.c_core = send(self.s_core, self.r_core, sems.at[6], sems.at[7], core)
        self.c_core.start()
        self.partial(me, self.own)

    def keep_out(self, src, dst, sem):
        copy = pltpu.make_async_copy(src, dst, self.sems.at[sem])
        copy.start()
        self.stores.append(copy)

    def second(self, between):
        self.c_core.wait_recv()
        resid_ref = self.resid_in.get()
        x_ref = self.x_in.get() if self.back else None
        gains = self.gain_in.get()[...] if self.gain_in else None
        if self.gather == "given":
            for j in range(2):
                self.g.forward(j)
        for j in range(2):
            self.c_x[j].wait_recv()
            if j == 1:
                between()
            total = self.own[j] + self.r_core[j].astype(F32) + self.r_x[j].astype(F32)
            if self.back:
                x = x_ref[j].astype(F32)
                r = lax.rsqrt(jnp.mean(x * x, axis=-1, keepdims=True) + EPS)
                scaled = total * gains
                inner = jnp.mean(scaled * x, axis=-1, keepdims=True)
                y = resid_ref[j].astype(F32) + r * scaled - x * (r * r * r * inner)
                dgain = jnp.sum(total * x * r, axis=0, keepdims=True)
                if j == 0:
                    self.dgain_ref[...] = dgain
                else:
                    self.dgain_ref[...] += dgain
            else:
                y = resid_ref[j].astype(F32) + total
            if self.gather == "norm":
                self.g.put(j, normed(y, gains).astype(BF))
            elif self.gather == "low":
                self.g.put(j, y.astype(BF))
            self.y_ref[j] = y.astype(self.y_ref.dtype)
            self.keep_out(self.y_ref.at[j], self.y_out.at[j], 8 + j)
            if self.low:
                self.low_ref[j] = y.astype(BF)
                self.keep_out(self.low_ref.at[j], self.low_out.at[j], 11 + j)
        if self.back:
            self.keep_out(self.dgain_ref, self.dgain_out, 10)

    def third(self):
        if self.gather in ("norm", "low"):
            for j in range(2):
                self.g.forward(j)

    def last(self):
        if self.gather:
            self.g.finish()
        for copy in [self.c_far, self.c_core] + self.c_x:
            copy.wait_send()
        for copy in self.stores:
            copy.wait()
        self.left.finish()


def stage(number, planes, stages, jobs=(), filler=None, share=SHARE):
    operands = [v for st in stages for v in st.operands]
    outs = [v for st in stages for v in st.outs]
    scratch = [v for st in stages for v in st.scratch]
    by_rows, base = [], 0
    for st in stages:
        by_rows += [base + i for i in st.by_rows]
        base += len(st.operands)

    def kernel(shipper, ins, results, refs, filler):
        for st in stages:
            parts = []
            for have, n in ((ins, st.operands), (results, st.outs), (refs, st.scratch)):
                parts.append(have[: len(n)])
                del have[: len(n)]
            st.bind(*parts)
            st.load()
        shipper.signal()

        def met():
            shipper.met()
            shipper.start()

        for n, st in enumerate(stages):
            st.first(met if n == 0 else (lambda: None))
        filler.prefetch()
        filler.begin()
        filler.advance(share[0])
        for n, st in enumerate(stages):
            st.second(lambda: filler.advance(share[1]) if n == 0 else None)
        filler.advance(share[2])
        for st in stages:
            st.third()
        filler.advance(1.0)
        filler.end()
        for st in stages:
            st.last()
        shipper.finish()

    cost = sum(st.cost for st in stages)
    got, moved, made = call_with_jobs(
        kernel, number, planes, jobs, operands, outs, scratch, "stage", cost, filler, tuple(by_rows)
    )
    got = list(got)
    each = []
    for st in stages:
        each.append(got[: len(st.outs)])
        del got[: len(st.outs)]
    return each, moved, made


class Attention:
    def __init__(self, parts, q, kv, bias, mkv, causal):
        self.parts, self.causal = parts, causal
        self.q_shape, self.kv_shape = q.shape, kv.shape
        self.rows, self.keys = q.shape[0], kv.shape[0]
        self.chunk = self.rows // (2 * TP)
        self.joint = q is kv
        self.extra = 0 if mkv is None else mkv.shape[0]
        self.total = self.keys + self.extra
        self.bias = bias
        self.size = 2 * self.chunk
        self.blocks = self.rows // self.size
        self.n_steps = 2 * HQ
        self.loads = [q] + ([] if self.joint else [kv])
        self.mem = [mkv] if self.extra else []
        self.raws = []

    def heads(self, *widths_dtypes):
        return [pltpu.VMEM((HQ, n, DH), dtype) for n, dtype in widths_dtypes]

    def split_qkv(self, q_ref, kv_ref, loads, qs, ks, vs):
        at = QC if self.joint else 0
        keys = self.keys
        for i in range(HQ):
            qs[i] = q_ref[:, DH * i : DH * (i + 1)]
            ks[i, :keys] = kv_ref[:, at + DH * i : at + DH * (i + 1)]
            vs[i, :keys] = kv_ref[:, at + QC + DH * i : at + QC + DH * (i + 1)]
        if self.extra:
            mkv_ref = loads.pop(0).get()
            for i in range(HQ):
                ks[i, keys:] = mkv_ref[:, DH * i : DH * (i + 1)]
                vs[i, keys:] = mkv_ref[:, QC + DH * i : QC + DH * (i + 1)]

    def place(self, row_chunk):
        upper = row_chunk // TP
        part = lax.axis_index("part") if self.parts > 1 else 0
        return (upper * (TP * self.parts) + TP * part + (row_chunk - TP * upper)) * self.chunk

    def halves(self, low, high):
        for half in range(2):
            first = max(low - HQ * half, 0)
            last = min(high - HQ * half, HQ)
            if first < last:
                n = self.blocks // 2
                yield half, range(half * n, (half + 1) * n), first, last

    def width(self, b):
        if self.causal and self.parts == 1:
            return (b + 1) * self.size
        return self.total

    def block(self, b):
        return pl.ds(b * self.size, self.size)

    def diagonal(self, b, u):
        keys = min(self.width(b), self.keys)
        start = self.keys - self.place(2 * b + u)
        return pl.ds(start if isinstance(start, int) else pl.multiple_of(start, 128), keys)


class AttentionForward(Attention):
    def __init__(self, parts, q, kv, segq, segk, bvec, mkv, causal, products=None):
        super().__init__(parts, q, kv, bvec is not None, mkv, causal)
        self.products = products
        if products:
            self.loads = [v for pair in products for v in pair]
        self.loads += self.mem + [segq, segk] + ([bvec] if self.bias else [])
        self.outs = [
            jax.ShapeDtypeStruct((self.rows, QC), BF),
            jax.ShapeDtypeStruct((HQ, self.rows, self.total), BF),
        ]
        self.scratch = self.heads((self.rows, BF), (self.total, BF), (self.total, BF), (self.rows, BF))
        self.scratch += [
            pltpu.VMEM((self.blocks, self.size, self.total), BF),
            pltpu.VMEM((self.rows, QC), BF),
            pltpu.SemaphoreType.DMA((3 + self.blocks,)),
        ]
        if self.bias:
            self.scratch.append(pltpu.VMEM((self.chunk, 2 * self.keys), F32))
        if products:
            for x, w in products:
                self.outs.append(jax.ShapeDtypeStruct((x.shape[0], w.shape[1]), BF))
                self.scratch.append(pltpu.VMEM((x.shape[0], w.shape[1]), BF))

    def begin(self, loads, raws, outs, scratch):
        self.att_out, self.p_out = outs[:2]
        self.qs, self.ks, self.vs, self.os, self.p_buf, self.att, self.sems = scratch[:7]
        self.toep = scratch[7] if self.bias else None
        loads = list(loads)
        self.copies = []
        if self.products:
            made = scratch[-len(self.products) :]
            for n, (out, to) in enumerate(zip(made, outs[2:])):
                x, w = loads.pop(0).get(), loads.pop(0).get()

                @pl.loop(0, x.shape[0] // 256)
                def _(r):
                    rows = pl.ds(pl.multiple_of(r * 256, 256), 256)
                    out[rows] = mm(x[rows], w[...]).astype(BF)

                self.copies.append(pltpu.make_async_copy(out, to, self.sems.at[1 + n]))
                self.copies[-1].start()
            q_ref, kv_ref = made[0], made[-1]
        else:
            q_ref = loads.pop(0).get()
            kv_ref = q_ref if self.joint else loads.pop(0).get()
        self.split_qkv(q_ref, kv_ref, loads, self.qs, self.ks, self.vs)
        self.segq, self.segk = loads.pop(0).get(), loads.pop(0).get()
        self.bvec = loads.pop(0).get() if self.bias else None

    def slot(self, h, b):
        n = self.blocks // 2
        return n * lax.rem(h + (b // n) * HQ, 2) + b % n

    def keep(self, h, b):
        wide, slot = pl.ds(0, self.width(b)), self.slot(h, b)
        return pltpu.make_async_copy(
            self.p_buf.at[slot, :, wide], self.p_out.at[h, self.block(b), wide], self.sems.at[3 + slot]
        )

    def one_block(self, h, b):
        wide, chunk, rows = self.width(b), self.chunk, self.block(b)
        keys = min(wide, self.keys)
        s = mm_nt(self.qs[h, rows], self.ks[h, :wide])
        if self.bias:
            parts = [self.toep[:, self.diagonal(b, u)] for u in range(2)]
            biased = s[:, :keys] + jnp.concatenate(parts, axis=0)
            s = jnp.concatenate([biased, s[:, keys:]], axis=1) if self.extra else biased
        allowed = self.segq[rows] == self.segk[:, :wide]
        s = jnp.where(allowed, s, MASKED)
        if self.causal:
            row = lax.broadcasted_iota(jnp.int32, (chunk, 1), 0)
            places = jnp.concatenate([row + self.place(2 * b + u) for u in range(2)], axis=0)
            seen = wide - self.size if self.parts == 1 else 0
            later = lax.broadcasted_iota(jnp.int32, (1, wide - seen), 1) + seen
            last = jnp.where(later <= places, s[:, seen:], MASKED)
            s = jnp.concatenate([s[:, :seen], last], axis=1) if seen else last
        top = jnp.max(s, axis=-1, keepdims=True)
        e = jnp.exp(s - top)
        p = (e * (1.0 / jnp.sum(e, axis=-1, keepdims=True))).astype(BF)
        self.p_buf[self.slot(h, b), :, :wide] = p
        self.keep(h, b).start()
        self.os[h, rows] = mm(p, self.vs[h, :wide]).astype(BF)

    def run(self, low, high):
        for half, blocks, first, last in self.halves(low, high):

            @pl.loop(first, last)
            def _(h):
                if self.bias:
                    row = jnp.broadcast_to(self.bvec[h], (self.chunk, 2 * self.keys))
                    self.toep[...] = pltpu.roll(row, 0, 1, stride=1, stride_axis=0)

                @pl.when(h >= 2)
                def _():
                    for b in blocks:
                        self.keep(h - 2, b).wait()

                if half == 1:

                    @pl.when(h < 2)
                    def _():
                        for b in range(self.blocks // 2):
                            self.keep(h + 1, b).wait()

                for b in blocks:
                    self.one_block(h, b)

    def end(self):
        for i in range(HQ):
            self.att[:, DH * i : DH * (i + 1)] = self.os[i]
        out = pltpu.make_async_copy(self.att, self.att_out, self.sems.at[0])
        out.start()
        for h in (HQ - 2, HQ - 1):
            for b in range(self.blocks // 2, self.blocks):
                self.keep(h, b).wait()
        out.wait()
        for copy in self.copies:
            copy.wait()


class AttentionBackward(Attention):
    def __init__(self, parts, p, q, kv, up, w_proj, att, bias, mkv, xs, proj=True, causal=False):
        super().__init__(parts, q, kv, bias, mkv, causal)
        self.xs, self.proj = xs if parts == 1 else [], proj
        self.loads += self.mem + [up, w_proj, att] + self.xs
        self.raws = [p]
        rows, total, keys = self.rows, self.total, self.keys
        if self.joint:
            self.outs = [jax.ShapeDtypeStruct((rows, 3 * QC), BF)]
        else:
            kv_type = BF if parts == 1 else F32
            self.outs = [
                jax.ShapeDtypeStruct((rows, QC), BF),
                jax.ShapeDtypeStruct((keys, 2 * QC), kv_type),
            ]
        if bias:
            self.outs.append(jax.ShapeDtypeStruct((HQ, 1, 2 * keys), F32))
        if self.extra:
            self.outs.append(jax.ShapeDtypeStruct((self.extra, 2 * QC), BF))
        if proj:
            self.outs.append(jax.ShapeDtypeStruct((QC, D), BF))
        for n in range(len(self.xs)):
            self.outs.append(jax.ShapeDtypeStruct((D, self.outs[n].shape[1]), BF))
        self.scratch = self.heads(
            (rows, BF), (total, BF), (total, BF), (rows, BF), (rows, BF), (total, F32), (total, F32)
        )
        self.scratch += [
            pltpu.VMEM((HQ, rows, 1), F32),
            pltpu.VMEM((self.blocks, self.size, total), BF),
            pltpu.SemaphoreType.DMA((self.blocks + len(self.outs),)),
        ]
        self.scratch += [pltpu.VMEM(o.shape, o.dtype) for o in self.outs]
        if bias:
            self.scratch.append(pltpu.VMEM((HQ, self.chunk, 2 * keys), F32))

    def fetch(self, h, b):
        n = self.blocks // 2
        slot = n * lax.rem(h + (b // n) * HQ, 2) + b % n
        wide = pl.ds(0, self.width(b))
        return pltpu.make_async_copy(
            self.p_in.at[h, self.block(b), wide], self.p_buf.at[slot, :, wide], self.sems.at[slot]
        )

    def begin(self, loads, raws, outs, scratch):
        self.results, (self.p_in,) = outs, raws
        scratch, loads = list(scratch), list(loads)
        self.qs, self.ks, self.vs, self.dos, self.dqs, self.dks, self.dvs = scratch[:7]
        self.rds, self.p_buf, self.sems = scratch[7:10]
        self.made = scratch[10 : 10 + len(outs)]
        self.diag = scratch[-1] if self.bias else None
        for b in range(self.blocks // 2):
            self.fetch(0, b).start()
        q_ref = loads.pop(0).get()
        kv_ref = q_ref if self.joint else loads.pop(0).get()
        self.split_qkv(q_ref, kv_ref, loads, self.qs, self.ks, self.vs)
        up_ref, w_ref, att_ref = (loads.pop(0).get() for _ in range(3))

        @pl.loop(0, self.rows // 256)
        def _(r):
            rows = pl.ds(pl.multiple_of(r * 256, 256), 256)
            grads = mm_nt(up_ref[rows], w_ref[...]).astype(BF)
            att = att_ref[rows]
            for i in range(HQ):
                span = slice(DH * i, DH * (i + 1))
                self.dos[i, rows] = grads[:, span]
                dots = grads[:, span].astype(F32) * att[:, span].astype(F32)
                self.rds[i, rows] = jnp.sum(dots, axis=-1, keepdims=True)

        made = list(self.made)
        self.dq = made.pop(0)
        self.dkv = self.dq if self.joint else made.pop(0)
        self.dbvec = made.pop(0) if self.bias else None
        self.dmkv = made.pop(0) if self.extra else None
        g_proj = made.pop(0) if self.proj else None
        self.g_rows, self.x_loads = made, loads
        if self.proj:

            @pl.loop(0, D // 256)
            def _(n):
                cols = pl.ds(pl.multiple_of(n * 256, 256), 256)
                g_proj[:, cols] = mm_tn(att_ref[...], up_ref[:, cols]).astype(BF)

    def run(self, low, high):
        keys, chunk, n = self.keys, self.chunk, self.blocks // 2
        for half, blocks, first, last in self.halves(low, high):

            @pl.loop(first, last)
            def _(h):
                for b in blocks:
                    self.fetch(h, b).wait()

                @pl.when(h + 1 < HQ)
                def _():
                    for b in blocks:
                        self.fetch(h + 1, b).start()

                if half == 0:

                    @pl.when(h + 1 == HQ)
                    def _():
                        for b in range(n, 2 * n):
                            self.fetch(0, b).start()

                    self.dks[h] = jnp.zeros(self.dks.shape[1:], F32)
                    self.dvs[h] = jnp.zeros(self.dvs.shape[1:], F32)
                    if self.bias:
                        self.diag[h] = jnp.zeros(self.diag.shape[1:], F32)
                for b in blocks:
                    wide, rows = self.width(b), self.block(b)
                    slot = n * lax.rem(h + half * HQ, 2) + b % n
                    q, grad, p = self.qs[h, rows], self.dos[h, rows], self.p_buf[slot, :, :wide]
                    dp = mm_nt(grad, self.vs[h, :wide])
                    ds = (p.astype(F32) * (dp - self.rds[h, rows])).astype(BF)
                    self.dqs[h, rows] = mm(ds, self.ks[h, :wide]).astype(BF)
                    self.dks[h, :wide] += mm_tn(ds, q)
                    self.dvs[h, :wide] += mm_tn(p, grad)
                    if self.bias:
                        for u in range(2):
                            part = ds[u * chunk : (u + 1) * chunk, : min(wide, keys)]
                            self.diag[h, :, self.diagonal(b, u)] += part.astype(F32)
                if self.bias and half == 1:
                    x = self.diag[h]
                    size = chunk
                    while size > 1:
                        size //= 2
                        x = x[:size] + pltpu.roll(x[size:], 2 * keys - size, 1)
                    self.dbvec[h] = x

    def end(self):
        keys = self.keys
        to = QC if self.joint else 0
        for i in range(HQ):
            self.dq[:, DH * i : DH * (i + 1)] = self.dqs[i]
            at = to + DH * i
            self.dkv[:, at : at + DH] = self.dks[i, :keys].astype(self.dkv.dtype)
            self.dkv[:, at + QC : at + QC + DH] = self.dvs[i, :keys].astype(self.dkv.dtype)
            if self.extra:
                self.dmkv[:, DH * i : DH * (i + 1)] = self.dks[i, keys:].astype(BF)
                self.dmkv[:, QC + DH * i : QC + DH * (i + 1)] = self.dvs[i, keys:].astype(BF)
        for load, out, grad in zip(self.x_loads, self.g_rows, (self.dq, self.dkv)):
            x_ref = load.get()

            @pl.loop(0, D // 256)
            def _(n):
                cols = pl.ds(pl.multiple_of(n * 256, 256), 256)
                out[cols] = mm_tn(x_ref[:, cols], grad[...]).astype(BF)

        copies = [
            pltpu.make_async_copy(src, dst, self.sems.at[self.blocks + n])
            for n, (src, dst) in enumerate(zip(self.made, self.results))
        ]
        for copy in copies:
            copy.start()
        for copy in copies:
            copy.wait()


class FeedForwardGrads:
    def __init__(self, at_stage, act, x):
        self.at_stage, self.raws, self.both = at_stage, [], act is not None
        self.loads = ([act] if self.both else []) + [x]
        self.n_steps = 3 * len(self.loads)
        self.outs = [jax.ShapeDtypeStruct((v.shape[1], D), BF) for v in self.loads]
        self.scratch = [pltpu.VMEM(o.shape, BF) for o in self.outs] + [pltpu.SemaphoreType.DMA((2,))]

    def begin(self, loads, raws, outs, scratch):
        self.left = [load.get() for load in loads]
        self.right = [self.at_stage.left.rows.ref] if self.both else []
        self.right.append(self.at_stage.left.ref)
        self.made, self.results, self.sems = scratch[:-1], outs, scratch[-1]

    def run(self, low, high):
        for n in range(len(self.left)):
            first, last = max(low - 3 * n, 0), min(high - 3 * n, 3)
            if first < last:

                @pl.loop(first, last)
                def _(i):
                    cols = pl.ds(pl.multiple_of(i * 256, 256), 256)
                    self.made[n][cols] = mm_tn(self.left[n][:, cols], self.right[n][...]).astype(BF)

    def end(self):
        copies = [
            pltpu.make_async_copy(self.made[n], self.results[n], self.sems.at[n])
            for n in range(len(self.left))
        ]
        for copy in copies:
            copy.start()
        for copy in copies:
            copy.wait()


class Idle:
    n_steps, loads, raws, outs, scratch = 0, [], [], [], []

    def begin(self, loads, raws, outs, scratch):
        pass

    def run(self, low, high):
        pass

    def end(self):
        pass


def attend(number, planes, filler, jobs):
    def kernel(shipper, ins, outs, scratch, filler):
        filler.prefetch()
        shipper.greet(())
        shipper.start()
        filler.begin()
        filler.run(0, filler.n_steps)
        filler.end()
        shipper.finish()

    _, moved, made = call_with_jobs(
        kernel, number, planes, jobs, [], [], [], "attend", 4 * 10**9, filler
    )
    return made, moved


def stacked(gains, rels):
    n = len(gains)

    def body(*refs):
        rows, table = refs[-2:]
        for i in range(n):
            rows[i : i + 1] = refs[i][...].astype(F32).reshape(1, -1)
        for i in range(len(rels)):
            table[i] = refs[n + i][...].astype(F32)

    return pl.pallas_call(
        body,
        out_shape=(
            jax.ShapeDtypeStruct((n, gains[0].shape[0]), F32),
            jax.ShapeDtypeStruct((len(rels),) + rels[0].shape, F32),
        ),
        name="stacked",
    )(*gains, *rels)


class Chain:
    def __init__(self, value, steps, width):
        self.value, self.steps, self.width = value, steps, width


ALL = ("seq", "part", "tp", "fsdp")
CTX = ("seq", "part", "tp")


def per_device(
    parts,
    planes,
    enc_input,
    dec_input,
    segments,
    prefix_rows,
    buckets,
    memory,
    enc_gain,
    enc_qkv,
    enc_rel,
    enc_proj,
    enc_ffnorm,
    enc_ffin,
    enc_ffout,
    dec_gain,
    dec_qkv,
    dec_rel,
    dec_proj,
    cross_gain,
    cross_query,
    cross_kv,
    cross_proj,
    dec_ffnorm,
    dec_ffin,
    dec_ffout,
    enc_cotan,
    dec_cotan,
):
    seq, part, tp, plane = (lax.axis_index(name) for name in ALL)
    chunk = enc_input.shape[1]
    length = buckets.shape[0] // 2
    docs, prefix = prefix_rows.shape[1:]

    first = seq == 0
    split = planes * 2

    def joined(x, came):
        mine = lax.dynamic_index_in_dim(x, seq, 0, keepdims=False)
        came = came.astype(x.dtype)
        return jnp.stack([jnp.where(first, mine, came), jnp.where(first, came, mine)])

    def cols(w, start, width=QC):
        return lax.dynamic_slice_in_dim(w, start + width * tp, width, 1)

    def halved(w):
        rows = w.shape[0] // 2
        return lax.dynamic_slice_in_dim(w, rows * seq, rows, 0)

    def qkv_part(w):
        w = halved(w)
        return jnp.concatenate([cols(w, D * i) for i in range(w.shape[1] // D)], axis=1)

    hidden = enc_ffout.shape[0] // TP

    def ffin_part(w):
        w = halved(w)
        return jnp.concatenate(
            [cols(w, hidden * TP * i, hidden) for i in range(planes)], axis=1
        )

    def ffout_part(w):
        rows = hidden // 2
        return lax.dynamic_slice_in_dim(w, hidden * tp + rows * seq, rows, 0)

    def over_planes(w):
        return gather_job("fsdp", w, planes)

    def over_seq(w):
        return gather_job("seq", w, 2, 1)

    def matrix(w):
        return w.reshape(-1, w.shape[-1])

    gains = (enc_gain, enc_ffnorm, dec_gain, cross_gain, dec_ffnorm)
    gain_stack, rel_stack = stacked(gains, (enc_rel, dec_rel))
    segments = segments.reshape(2, 1, chunk)
    first_jobs = [
        swap_job(enc_input),
        gather_job("fsdp", gain_stack, planes),
        gather_job("fsdp", rel_stack, planes),
        over_planes(qkv_part(enc_qkv)),
        over_planes(qkv_part(memory)),
        swap_job(dec_input),
    ]
    if parts == 1:
        first_jobs.append(block_job(segments))
    xe, gain_stack, rel_stack, w_eqkv, table, xd, *segs = ship(0, planes, first_jobs)
    xe, xd = joined(enc_input, xe), joined(dec_input, xd)
    if parts == 1:
        seg = segs[0].reshape(-1)
    else:
        segs = lax.all_gather(segments.reshape(2, chunk), CTX, axis=1, tiled=True)
        seg = lax.dynamic_index_in_dim(segs, seq, 0, keepdims=False)
    per, per_rel = enc_gain.shape[0], enc_rel.size
    g_enc, g_effn, g_dec, g_cross, g_dffn = [
        gain_stack[:, i].reshape(1, D) for i in range(len(gains))
    ]
    rels = [rel_stack[:, i].reshape(BUCKETS, HEADS) for i in range(2)]
    onehot = (buckets[:, None] == jnp.arange(BUCKETS, dtype=jnp.int32)[None, :]).astype(BF)

    def bias_vector(rel):
        own = lax.dynamic_slice_in_dim(rel, HQ * tp, HQ, 1).astype(BF)
        return lax.dot_general(
            own, onehot, (((0,), (1,)), ((), ())), preferred_element_type=F32
        ).reshape(HQ, 1, 2 * length)

    turned = planes == TP

    def proj_jobs(w):
        return [turn_job(w)] if turned else []

    def proj_of(got, w):
        if turned:
            return got.pop()
        full = lax.all_gather(w, "fsdp", axis=0, tiled=True)
        return lax.dynamic_slice_in_dim(full, QC * tp, QC, 0)

    ((en,), (dn,)), (w_eqkv, table, w_dqkv, w_effin), _ = stage(
        1,
        planes,
        [GatherNormed(xe, g_enc), GatherNormed(xd, g_dec)],
        jobs=[
            over_seq(w_eqkv),
            over_seq(table),
            over_planes(qkv_part(dec_qkv)),
            over_planes(ffin_part(enc_ffin)),
        ],
    )
    w_eqkv, table = matrix(w_eqkv), matrix(table)

    segq = lax.dynamic_index_in_dim(seg.reshape(2, parts, TP * chunk), part, 1, keepdims=False)
    segq = segq.reshape(-1, 1)
    segk = seg.reshape(1, length)
    ids = lax.dynamic_index_in_dim(prefix_rows, seq, 0, keepdims=False).reshape(-1)
    extra = -(-(docs * prefix) // 256) * 256
    ids = jnp.concatenate([ids, jnp.full((extra - docs * prefix,), -1, jnp.int32)])
    mem_doc = np.full((extra,), -1, np.int32)
    mem_doc[: docs * prefix] = np.arange(docs * prefix) // prefix
    segk_mem = jnp.concatenate([segk, jnp.asarray(mem_doc)[None]], axis=1)
    pick = (ids[:, None] == jnp.arange(table.shape[0], dtype=jnp.int32)[None, :]).astype(BF)
    mkv = mm(pick, table).astype(BF)

    def spread(kv):
        if parts == 1:
            return kv
        got = lax.all_gather(kv, "part", axis=0)
        return got.reshape(parts, 2, TP * chunk, -1).transpose(1, 0, 2, 3).reshape(length, -1)

    def collect(dkv):
        if parts == 1:
            return dkv
        split = dkv.reshape(2, parts, TP * chunk, -1).transpose(1, 0, 2, 3)
        split = split.reshape(parts * 2 * TP * chunk, -1)
        return lax.psum_scatter(split, "part", scatter_dimension=0, tiled=True).astype(BF)

    def self_kv(rows):
        return (rows, rows) if parts == 1 else (rows[:, :QC], spread(rows[:, QC:]))

    def joint_grad(got):
        if parts == 1:
            return got.pop(0)
        return jnp.concatenate([got.pop(0), collect(got.pop(0))], axis=1)

    def self_fill(x, w, segk_now, bvec, mem, causal):
        if parts == 1:
            rows = jax.ShapeDtypeStruct((x.shape[0], w.shape[1]), BF)
            return AttentionForward(
                parts, rows, rows, segq, segk_now, bvec, mem, causal, [(x, w)]
            ), None
        rows = self_kv(mm(x, w).astype(BF))
        return AttentionForward(parts, *rows, segq, segk_now, bvec, mem, causal), rows

    def self_made(got, rows):
        return got[0], got[1], rows or (got[2], got[2])

    e_fill, e_qkv = self_fill(en, w_eqkv, segk_mem, bias_vector(rels[0]), mkv, False)
    made, (w_dqkv, w_effout, *got) = attend(
        2,
        planes,
        e_fill,
        [over_seq(w_dqkv), over_planes(ffout_part(enc_ffout))]
        + proj_jobs(enc_proj),
    )
    e_att, e_p, e_qkv = self_made(made, e_qkv)
    w_eproj = proj_of(got, enc_proj)
    w_dqkv = matrix(w_dqkv)
    d_fill, d_qkv = self_fill(dn, w_dqkv, segk, bias_vector(rels[1]), None, True)
    ((e_mid, e_fn),), (w_effin, w_effout, w_cq, w_ckv, *got), made = stage(
        3,
        planes,
        [Stage([e_att], w_eproj, xe, gather="norm", gain=g_effn)],
        [
            over_seq(w_effin),
            over_seq(w_effout),
            over_planes(qkv_part(cross_query)),
            over_planes(qkv_part(cross_kv)),
        ]
        + proj_jobs(dec_proj),
        d_fill,
    )
    d_att, d_p, d_qkv = self_made(made, d_qkv)
    w_dproj = proj_of(got, dec_proj)
    w_effin, w_effout = matrix(w_effin), matrix(w_effout)
    ((d_mid, c_n), (e_low, e_gath, e_pre, e_act)), moved, _ = stage(
        4,
        planes,
        [
            Stage([d_att], w_dproj, xd, gather="norm", gain=g_cross),
            Stage(
                [e_fn, w_effin], w_effout, e_mid, maker=FeedForward, gather="low", dtype=BF
            ),
        ],
        [
            over_seq(w_cq),
            over_seq(w_ckv),
            over_planes(ffin_part(dec_ffin)),
            over_planes(ffout_part(dec_ffout)),
            swap_job(dec_cotan),
        ],
    )
    w_cq, w_ckv, w_dffin, w_dffout, xdc = moved
    w_cq, w_ckv = matrix(w_cq), matrix(w_ckv)
    xdc = joined(dec_cotan, xdc)
    products = None
    if parts == 1:
        c_q = jax.ShapeDtypeStruct((c_n.shape[0], QC), BF)
        c_kv = jax.ShapeDtypeStruct((e_gath.shape[0], 2 * QC), BF)
        products = [(c_n, w_cq), (e_gath, w_ckv)]
    else:
        c_q = mm(c_n, w_cq).astype(BF)
        c_kv = spread(mm(e_gath, w_ckv).astype(BF))
    c_fill = AttentionForward(parts, c_q, c_kv, segq, segk, None, None, False, products)
    (c_att, c_p, *made), (w_dffin, *got) = attend(
        5, planes, c_fill, [over_seq(w_dffin)] + proj_jobs(cross_proj)
    )
    w_cproj = proj_of(got, cross_proj)
    if parts == 1:
        c_q, c_kv = made
    ((d_cross, d_fn),), (w_dffout, came, xec), _ = stage(
        6,
        planes,
        [Stage([c_att], w_cproj, d_mid, gather="norm", gain=g_dffn)],
        [over_seq(w_dffout), swap_job(e_low), swap_job(enc_cotan)],
    )
    enc_output, xec = joined(e_low, came), joined(enc_cotan, xec)
    w_dffin, w_dffout = matrix(w_dffin), matrix(w_dffout)
    ((d_low, up_g, d_pre, d_act),), _, _ = stage(
        7,
        planes,
        [
            Stage(
                [d_fn, w_dffin],
                w_dffout,
                d_cross,
                maker=FeedForward,
                gather="given",
                given=xdc,
                dtype=BF,
            )
        ],
    )

    def pieces(g):
        if parts > 1:
            g = lax.psum(g, "part")
        return g.reshape(planes, 2, g.shape[0] // split, g.shape[1])

    to_ctx = [
        lambda g: gather_job("across", g),
        lambda g: gather_job("seq", g),
        lambda g: gather_job("core", g, 2, 2),
    ]
    to_ctx_seq = [
        lambda g: gather_job("seq", g),
        lambda g: gather_job("across", g, 2, 1),
        lambda g: gather_job("core", g, 2, 2),
    ]

    def chain(g, width, seq_first=False):
        steps = [lambda g: swap_job(g, 1, True), lambda g: deal_job("fsdp", g)]
        return Chain(pieces(g), steps + (to_ctx_seq if seq_first else to_ctx), width)

    def proj_chain(g):
        if not turned:
            return Chain(g, [], -1)
        steps = [lambda g: swap_job(g, "cols", True), lambda g: deal_job("fsdp", g), turn_job]
        return Chain(g.reshape(planes, -1, D), steps + to_ctx, -1)

    def steps_of(chains):
        return [c.steps[0](c.value) for c in chains if c.steps]

    def hurry(chains):
        for c in chains:
            if len(c.steps) == 3:
                c.steps = [spread_job]

    def settle(chains, got):
        got = list(got)
        for c in chains:
            if c.steps:
                c.value = got.pop(0)
                c.steps.pop(0)
        return got

    at = Stage(
        [up_g, d_pre, w_dffout],
        w_dffin,
        xdc,
        flip=True,
        maker=FeedForwardBack,
        back=(d_cross, g_dffn),
        gather="low",
    )
    ((up, up_rows, dg_dffn, _),), (came,), made = stage(
        8, planes, [at], [swap_job(d_low)], FeedForwardGrads(at, d_act, d_fn)
    )
    dec_output = joined(d_low, came)
    k_dffout, k_dffin = chain(made[0], 0, True), chain(made[1], hidden, True)
    c_fill = AttentionBackward(
        parts, c_p, c_q, c_kv, up_rows, w_cproj, c_att, False, None, [c_n, e_gath]
    )
    moving = [k_dffout]
    (c_dq, c_dkv, g_cproj, *made), got = attend(9, planes, c_fill, steps_of(moving))
    settle(moving, got)
    c_dkv = collect(c_dkv)
    if parts > 1:
        made = [mm_tn(c_n, c_dq).astype(BF), mm_tn(e_gath, c_dkv).astype(BF)]
    k_cproj, k_cq, k_ckv = proj_chain(g_cproj), chain(made[0], QC, True), chain(made[1], QC, True)
    moving = [k_dffout, k_cq, k_ckv, k_cproj]
    ((up, up_rows, dg_cross),), got, _ = stage(
        10,
        planes,
        [Stage([c_dq], w_cq, up, flip=True, back=(d_mid, g_cross), gather="low")],
        steps_of(moving),
    )
    settle(moving, got)

    def self_grads(made, x):
        grad = joint_grad(made)
        g_rows = made.pop() if parts == 1 else mm_tn(x, grad).astype(BF)
        return grad, chain(g_rows, QC, True), made

    d_fill = AttentionBackward(
        parts, d_p, *d_qkv, up_rows, w_dproj, d_att, True, None, [dn], causal=True
    )
    moving = [k_dffin, k_cq, k_ckv, k_cproj]
    ((e_up, e_up_rows),), got, made = stage(
        16,
        planes,
        [Stage([c_dkv], w_ckv, xec, flip=True, gather="low")],
        steps_of(moving),
        d_fill,
    )
    settle(moving, got)
    d_rows_grad, k_dqkv, (d_dbv, g_dproj) = self_grads(made, dn)
    k_dproj = proj_chain(g_dproj)
    k_effout = chain(mm_tn(e_act, e_up_rows).astype(BF), 0, True)
    moving = [k_dffin, k_dffout, k_cproj, k_dqkv, k_effout]
    at = Stage(
        [e_up_rows, e_pre, w_effout],
        w_effin,
        e_up,
        flip=True,
        maker=FeedForwardBack,
        back=(e_mid, g_effn),
        gather="low",
    )
    ((e_up, e_up_rows, dg_effn, _),), got, made = stage(
        12, planes, [at], steps_of(moving), FeedForwardGrads(at, None, e_fn)
    )
    settle(moving, got)
    k_effin = chain(made[0], hidden)
    k_eproj = proj_chain(mm_tn(e_att, e_up_rows).astype(BF))
    e_fill = AttentionBackward(
        parts, e_p, *e_qkv, e_up_rows, w_eproj, e_att, True, mkv, [en], False
    )
    moving += [k_cq, k_ckv, k_dproj, k_effin, k_eproj]
    ((d_in, dg_dec, d_in_low),), got, made = stage(
        11,
        planes,
        [Stage([d_rows_grad], w_dqkv, up, flip=True, back=(xd, g_dec), low=True)],
        steps_of(moving),
        e_fill,
    )
    settle(moving, got)
    e_rows_grad, k_eqkv, (e_dbv, d_mkv) = self_grads(made, en)
    k_table = chain(mm_tn(pick, d_mkv).astype(BF), QC)
    moving += [k_eqkv, k_table]
    ((e_in, dg_enc, e_in_low),), got, _ = stage(
        13,
        planes,
        [Stage([e_rows_grad], w_eqkv, e_up, flip=True, back=(xe, g_enc), low=True)],
        steps_of(moving),
    )
    settle(moving, got)

    def rel_grads(*dbvs):
        own = lax.dot_general(
            onehot.astype(F32),
            jnp.concatenate(dbvs, axis=0).reshape(len(dbvs) * HQ, -1),
            (((0,), (1,)), ((), ())),
            precision=lax.Precision.HIGHEST,
            preferred_element_type=F32,
        )
        heads = jnp.arange(HEADS, dtype=jnp.int32)[None, :] // HQ == tp
        return [
            jnp.where(heads, jnp.tile(own[:, HQ * i : HQ * (i + 1)], (1, TP)), 0.0)
            for i in range(len(dbvs))
        ]

    tiny = [v.reshape(planes, -1) for v in (dg_enc, dg_effn, dg_dec, dg_cross, dg_dffn)]
    tiny += [v.reshape(planes, -1) for v in rel_grads(e_dbv, d_dbv)]
    tiny = jnp.concatenate(tiny, axis=1).reshape(-1, 128)
    if parts > 1:
        tiny = lax.psum(tiny, "part")
    hurry(moving)
    tiny, came, d_came, *got = ship(
        14,
        planes,
        [total_job("fsdp", tiny, planes), swap_job(e_in_low), swap_job(d_in_low)]
        + steps_of(moving),
    )
    enc_ingrad, dec_ingrad = joined(e_in, came), joined(d_in, d_came)
    settle(moving, got)
    hurry(moving)
    tiny, *got = ship(15, planes, [spread_job(tiny, True)] + steps_of(moving))
    settle(moving, got)

    def proj_rows(k):
        full = lax.dynamic_update_slice_in_dim(jnp.zeros((D, D), BF), k.value, QC * tp, 0)
        full = lax.psum_scatter(full, "fsdp", scatter_dimension=0, tiled=True)
        return lax.psum(full.astype(F32), CTX)

    ready = [k_dffin, k_dffout, k_effin, k_effout, k_cq, k_ckv, k_dqkv, k_eqkv, k_table]
    k_projs = [k_eproj, k_dproj, k_cproj]
    if turned:
        ready += k_projs
    results = laid_out([k.value for k in ready], [k.width for k in ready])
    o_eproj, o_dproj, o_cproj = results[9:] if turned else [proj_rows(k) for k in k_projs]
    o_dffin, o_dffout, o_effin, o_effout, o_cq, o_ckv, o_dqkv, o_eqkv, o_table = results[:9]
    tiny = lax.dynamic_index_in_dim(tiny.reshape(planes, -1), plane, 0, keepdims=False)
    o_gains = [tiny[per * i : per * (i + 1)] for i in range(5)]
    o_rels = [
        tiny[5 * per + per_rel * i : 5 * per + per_rel * (i + 1)].reshape(-1, HEADS)
        for i in range(2)
    ]
    return (
        enc_output,
        dec_output,
        enc_ingrad,
        dec_ingrad,
        o_table,
        o_gains[0],
        o_eqkv,
        o_rels[0],
        o_eproj,
        o_gains[1],
        o_effin,
        o_effout,
        o_gains[2],
        o_dqkv,
        o_rels[1],
        o_dproj,
        o_gains[3],
        o_cq,
        o_ckv,
        o_cproj,
        o_gains[4],
        o_dffin,
        o_dffout,
    )


def solution(mesh):
    ctx, planes = mesh.shape["ctx"], mesh.shape["fsdp"]
    parts = ctx // (2 * TP)
    inner = Mesh(np.asarray(mesh.devices).reshape(2, parts, TP, planes), ALL)
    rows3 = P("fsdp", CTX, None)
    mat, vec = P("fsdp", None), P("fsdp")
    args = (
        (rows3, rows3, P("fsdp", CTX), P("fsdp", None, None), P(), mat)
        + (vec, mat, mat, mat, vec, mat, mat)
        + (vec, mat, mat, mat)
        + (vec, mat, mat, mat)
        + (vec, mat, mat)
        + (rows3, rows3)
    )
    outs = (
        (rows3, rows3, rows3, rows3, mat)
        + (vec, mat, mat, mat, vec, mat, mat)
        + (vec, mat, mat, mat)
        + (vec, mat, mat, mat)
        + (vec, mat, mat)
    )
    return jax.shard_map(
        functools.partial(per_device, parts, planes),
        mesh=inner,
        in_specs=args,
        out_specs=outs,
        check_vma=False,
    )
```
